128 devices in a mesh: head: 2 (over z_lo), blk: 64 (over y, x, z_hi, core).
Axes of the slice: x: 4, y: 4, z: 4 (z_hi: 2, z_lo: 2; z = z_hi * 2 + z_lo), core: 2. Of those that a mesh axis runs over, the one named last changes fastest.
Arguments:
- tokens: bfloat16 [16384, 2048], P(('head', 'blk')), may hold values from -6 to 6
- norm_gain: float32 [2048], replicated, may hold values from 0.5 to 1.5
- w_query: bfloat16 [2048, 4096], P('blk', 'head'), may hold values from -0.125 to 0.125
- key_weight: bfloat16 [2048, 512], P('blk', 'head'), may hold values from -0.125 to 0.125
- value_weight: bfloat16 [2048, 512], P('blk', 'head'), may hold values from -0.125 to 0.125
- query_gain: float32 [128], replicated, may hold values from 0.25 to 1.75
- key_gain: float32 [128], replicated, may hold values from 0.25 to 1.75
- w_out: bfloat16 [4096, 2048], P('head', 'blk'), may hold values from -0.75 to 0.75
- mix_gain: float32 [2048], replicated, may hold values from 0.5 to 1.5
- w_router: bfloat16 [128, 2048], P('head', 'blk'), may hold values from -0.0625 to 0.0625
- expert_gate_up: bfloat16 [128, 2048, 1536], P(('head', 'blk')), may hold values from -0.125 to 0.125
- expert_down: bfloat16 [128, 768, 2048], P(('head', 'blk')), may hold values from -0.875 to 0.875
- lengths: int32 [16], replicated, may hold values from 1 to 4096, 16384 in all
- block_deal: int32 [64], replicated, may hold values from 0 to 63, each once
- routes: int32 [16384, 8], P(('head', 'blk')), may hold values from 0 to 127, all different within a row; in each aligned block of 128 rows (0 to 127, 128 to 255, ...) at most 8 rows name the same one
- cotangent: bfloat16 [16384, 2048], P(('head', 'blk')), may hold values from -6 to 6
Outputs:
- output: bfloat16 [16384, 2048], P(('head', 'blk'))
- grad_tokens: float32 [16384, 2048], P(('head', 'blk'))
- grad_norm_gain: float32 [2048], replicated
- grad_w_query: float32 [2048, 4096], P('blk', 'head')
- grad_w_key: float32 [2048, 512], P('blk', 'head')
- grad_w_value: float32 [2048, 512], P('blk', 'head')
- grad_query_gain: float32 [128], replicated
- grad_key_gain: float32 [128], replicated
- grad_w_out: float32 [4096, 2048], P('head', 'blk')
- grad_mix_gain: float32 [2048], replicated
- grad_w_router: float32 [128, 2048], P('head', 'blk')
- grad_expert_gate_up: float32 [128, 2048, 1536], P(('head', 'blk'))
- grad_expert_down: float32 [128, 768, 2048], P(('head', 'blk'))
The draws below stay inside these ranges and needn't reach their ends.
Inputs may be any that keep to these rules, and one draw needn't show every extreme that they name: `lengths`: they sum to 16384; the largest is exactly 4096. A permutation of the 64 stream blocks of 256 tokens; index b of blk holds block block_deal[b], head index 0 its first 128 tokens. `routes`: each row names 8 different experts; the 128 rows of one device name one expert at most 8 times.
All inputs are finite; a program needn't handle non-finite values.
Results may differ from the reference program's by a relative error of at most 0.03.
Values may be sent and summed in bfloat16 or wider, within the bound.
A program may use at most 704 MiB of HBM per device.

```python
import math
import jax
import jax.numpy as jnp
import numpy as np
from jax import lax

MODEL_DIMENSION = 2048
QUERY_HEADS = 32
KEY_VALUE_HEADS = 4
HEAD_DIMENSION = 128
FF = 768
TOPK = 8
TOK_DEV = 128
EXPERTS = 128
CYCLE = 64
BLOCK = 256
TOKEN_TOTAL = 16384
LONGEST_LENGTH = 4096
SEQS = 16
CAP = 8
N_HEAD = 2
N_BLK = 64


def level_of(stream_key, extent, pieces, least, largest):
    gain, own = 1.0, jax.random.fold_in(stream_key, 6)
    for position, blocks in pieces:
        heights = jnp.exp(jax.random.uniform(jax.random.fold_in(own, position), (blocks,), jnp.float32, least / len(pieces), largest / len(pieces)))
        gain = gain * jnp.repeat(heights, extent[position] // blocks).reshape([-1 if axis == position else 1 for axis in range(len(extent))])
    return gain


def length_profile(count, total, reach, slope):
    weights = [(1 << 20) // math.isqrt(standing ** slope) + 1 for standing in range(2, count + 1)]
    spare, given = total - reach - (count - 1), [1] * (count - 1)
    while spare > 0:
        candidates = [i for i in range(count - 1) if given[i] < reach]
        whole, budget = sum([weights[i] for i in candidates]), spare
        for i in candidates:
            addition = min(reach - given[i], max(1, budget * weights[i] // whole), spare)
            given[i] = given[i] + addition
            spare = spare - addition
    return np.array([reach] + given)


def ragged_sizes(rng, number_of, total, limit, lean):
    if number_of == 2:
        one = jax.random.randint(rng, (), max(1, total - limit), min(limit, total - 1) + 1)
        return jnp.stack([one, total - one])
    sizes = jnp.asarray(length_profile(number_of, total, limit, lean), jnp.int32)
    twos = (number_of - 1) // 2
    giver, receiver = sizes[1:1 + 2 * twos:2], sizes[2:2 + 2 * twos:2]
    margin = jnp.minimum(giver - 1, limit - receiver)
    moved = jax.random.randint(jax.random.fold_in(rng, 1), (twos,), 0, 1 << 20) % (margin + 1)
    sizes = sizes.at[1:1 + 2 * twos:2].set(giver - moved).at[2:2 + 2 * twos:2].set(receiver + moved)
    return sizes[jax.random.permutation(jax.random.fold_in(rng, 2), number_of)]


def routed_block(key, own, number, rows, count, top, bound, slope):
    order = jax.random.permutation(key, count)
    heavy_load, usual = shares(count, rows * top, bound, slope, True), shares(count, rows * top, bound, slope, False)
    places = jnp.arange(count)

    def named(sizes, rotation):
        used = int((sizes > 0).sum())
        fixed = max(1, used // 4)
        moved = fixed + (places - fixed + rotation * (used - fixed)) % max(1, count - fixed)
        return jnp.zeros((count,), jnp.int32).at[order[jnp.where(places < fixed, places, moved)]].set(jnp.asarray(sizes, jnp.int32))

    sizes = jnp.where(number % 4 == 0, named(heavy_load, number // 4), named(usual, number - number // 4 - 1))
    mixed = jax.random.permutation(jax.random.fold_in(own, 3), count)
    source_of, sink = mixed[0:count // 2 * 2:2], mixed[1:count // 2 * 2:2]
    room = jnp.minimum(sizes[source_of] - 1, bound - sizes[sink]) // 2
    room = jnp.where((source_of == order[0]) | (sink == order[0]) | (sizes[sink] == 0), 0, jnp.maximum(room, 0))
    moved = jax.random.randint(jax.random.fold_in(own, 4), (count // 2,), 0, 1 << 20) % (room + 1)
    sizes = sizes.at[source_of].add(-moved).at[sink].add(moved)
    members = jnp.searchsorted(jnp.cumsum(sizes), jnp.arange(rows * top), side="right").astype(jnp.int32)
    table = members.reshape(top, rows).T
    table = table[jax.random.permutation(jax.random.fold_in(own, 1), rows)]
    rotation = jax.random.randint(jax.random.fold_in(own, 2), (rows, 1), 0, top)
    return jnp.take_along_axis(table, (jnp.arange(top)[None, :] + rotation) % top, axis=1)


def shares(number_of, total, most, lean, full):
    loads = [(1 << 20) // math.isqrt(rank ** lean) + 1 for rank in range(1, number_of + 1)]
    largest = most if full else min(most, max(-(-total // number_of), total * loads[0] // sum(loads)))
    least = 1 if total - largest >= number_of - 1 else 0
    holding, spare = [largest] + [least] * (number_of - 1), total - largest - least * (number_of - 1)
    while spare > 0:
        candidates = [i for i in range(1, number_of) if holding[i] < largest] or [i for i in range(1, number_of) if holding[i] < most]
        whole, remaining = sum([loads[i] for i in candidates]), spare
        for i in candidates:
            addition = min(most - holding[i], max(1, remaining * loads[i] // whole), spare)
            holding[i] = holding[i] + addition
            spare = spare - addition
    return np.array(holding)


def gaussian(rng, dims, deviation, bound, pieces=(), kind=jnp.bfloat16):
    values = jax.random.normal(rng, dims, jnp.float32) * deviation
    if len(pieces) > 0:
        values = level_of(rng, dims, pieces, -0.22, 0.18) * values
    return jnp.clip(values, min=-bound, max=bound).astype(kind)


def setup_inputs(seed: int = 0) -> dict:
    key_list = jax.random.split(jax.random.key(seed), 17)
    tokens = gaussian(key_list[0], (TOKEN_TOTAL, MODEL_DIMENSION), 1.0, 6.0, ((0, 128),))
    norm_gain = jnp.clip(1.0 + 0.1 * jax.random.normal(key_list[1], (MODEL_DIMENSION,), jnp.float32), 0.5, 1.5)
    w_query = gaussian(key_list[2], (MODEL_DIMENSION, QUERY_HEADS * HEAD_DIMENSION), MODEL_DIMENSION ** -0.5, 0.125, ((0, 64), (1, 2)))
    key_weight = gaussian(key_list[3], (MODEL_DIMENSION, KEY_VALUE_HEADS * HEAD_DIMENSION), MODEL_DIMENSION ** -0.5, 0.125, ((0, 64), (1, 2)))
    value_weight = gaussian(key_list[4], (MODEL_DIMENSION, KEY_VALUE_HEADS * HEAD_DIMENSION), MODEL_DIMENSION ** -0.5, 0.125, ((0, 64), (1, 2)))
    query_gain = jnp.clip(1.0 + 0.15 * jax.random.normal(key_list[5], (HEAD_DIMENSION,), jnp.float32), 0.25, 1.75)
    key_gain = jnp.clip(1.0 + 0.15 * jax.random.normal(key_list[6], (HEAD_DIMENSION,), jnp.float32), 0.25, 1.75)
    w_out = gaussian(key_list[7], (QUERY_HEADS * HEAD_DIMENSION, MODEL_DIMENSION), (QUERY_HEADS * HEAD_DIMENSION // 64) ** -0.5, 0.75, ((0, 2), (1, 64)))
    mix_gain = jnp.clip(1.0 + 0.1 * jax.random.normal(key_list[8], (MODEL_DIMENSION,), jnp.float32), 0.5, 1.5)
    w_router = gaussian(key_list[9], (EXPERTS, MODEL_DIMENSION), (4 * MODEL_DIMENSION) ** -0.5, 0.0625, ((0, 2), (1, 64)))
    expert_gate_up = gaussian(key_list[10], (EXPERTS, MODEL_DIMENSION, 2 * FF), MODEL_DIMENSION ** -0.5, 0.125, ((0, 128),))
    expert_down = gaussian(key_list[11], (EXPERTS, FF, MODEL_DIMENSION), (FF // 16) ** -0.5, 0.875, ((0, 128),))
    lengths = ragged_sizes(key_list[12], SEQS, TOKEN_TOTAL, LONGEST_LENGTH, 2).astype(jnp.int32)
    block_deal = jax.random.permutation(key_list[13], CYCLE).astype(jnp.int32)
    routes_keys = jax.random.split(jax.random.fold_in(key_list[14], 1), TOKEN_TOTAL // TOK_DEV)
    routes_turns = jax.random.permutation(jax.random.fold_in(key_list[14], 3), TOKEN_TOTAL // TOK_DEV)
    routes = jax.vmap(lambda own, number: routed_block(jax.random.fold_in(key_list[14], 2), own, number, TOK_DEV, EXPERTS, TOPK, CAP, 2))(routes_keys, routes_turns).reshape((TOKEN_TOTAL, TOPK))
    cotangent = gaussian(key_list[15], (TOKEN_TOTAL, MODEL_DIMENSION), 1.0, 6.0, ((0, 128),))
    return dict(tokens=tokens, norm_gain=norm_gain, w_query=w_query, key_weight=key_weight, value_weight=value_weight, query_gain=query_gain, key_gain=key_gain, w_out=w_out, mix_gain=mix_gain, w_router=w_router, expert_gate_up=expert_gate_up, expert_down=expert_down, lengths=lengths, block_deal=block_deal, routes=routes, cotangent=cotangent)


@jax.custom_vjp
def lower_precision(v):
    return lax.optimization_barrier(v.astype(jnp.bfloat16)).astype(jnp.float32)

@jax.custom_vjp
def lower_backward(v):
    return v

def low_keep(v):
    return (lower_precision(v), None)

def low_pass(kept, grad):
    return (grad,)

def back_keep(v):
    return (v, None)

def back_low(kept, grad):
    return (lower_precision(grad),)
lower_precision.defvjp(low_keep, low_pass)
lower_backward.defvjp(back_keep, back_low)
eps_norm = 1e-06
rope_base = 1000000.0
big_negative = -1e+30
highest_precision = lax.Precision.HIGHEST

def rms_scale(values, gain_vec):
    return values * lax.rsqrt(lax.optimization_barrier(jnp.mean(values * values, axis=-1, keepdims=True)) + eps_norm) * gain_vec

def rope_turn(values, offsets):
    half_dim = values.shape[-1] // 2
    spacing = rope_base ** (-2.0 * jnp.arange(half_dim, dtype=jnp.float32) / values.shape[-1])
    angles = offsets[:, None] * spacing[None, :]
    cosine = jnp.cos(angles)[:, None, :]
    sine_part = jnp.sin(angles)[:, None, :]
    front_half = values[..., :half_dim]
    back_half = values[..., half_dim:]
    return jnp.concatenate([front_half * cosine - back_half * sine_part, back_half * cosine + front_half * sine_part], axis=-1)

def sequence_of(places, lengths):
    seq_ends = jnp.cumsum(lengths).astype(jnp.int32)
    passed = places[:, None] >= seq_ends[None, :]
    segment = lax.optimization_barrier(jnp.sum(passed.astype(jnp.int32), axis=1)).astype(jnp.int32)
    seq_begin = lax.optimization_barrier(jnp.sum(jnp.where(passed, lengths[None, :], 0), axis=1)).astype(jnp.int32)
    return (segment, places - seq_begin)

def route_targets(routes, devices_all):
    per_device = routes.reshape(devices_all, TOK_DEV * TOPK)
    onehot = (per_device[:, :, None] == jnp.arange(EXPERTS, dtype=jnp.int32)).astype(jnp.int32)
    earlier = (jnp.cumsum(onehot, axis=1) - onehot).astype(jnp.int32)
    slot_index = lax.optimization_barrier(jnp.sum(earlier * onehot, axis=2)).astype(jnp.int32)
    source = jnp.arange(devices_all, dtype=jnp.int32)[:, None]
    return (per_device * (devices_all * CAP) + source * CAP + slot_index).reshape(-1).astype(jnp.int32)

def attend_stream(query_rows, every_key, every_value, stream_segment):
    block_length = min(512, TOKEN_TOTAL)
    group_width = QUERY_HEADS // KEY_VALUE_HEADS
    score_scale = HEAD_DIMENSION ** (-0.5)
    window = LONGEST_LENGTH + block_length
    key_padded = jnp.concatenate([jnp.zeros((LONGEST_LENGTH, KEY_VALUE_HEADS, HEAD_DIMENSION), jnp.float32), every_key], axis=0)
    value_padded = jnp.concatenate([jnp.zeros((LONGEST_LENGTH, KEY_VALUE_HEADS, HEAD_DIMENSION), jnp.float32), every_value], axis=0)
    segment_pad = jnp.concatenate([jnp.full((LONGEST_LENGTH,), -1, jnp.int32), stream_segment])

    def one_block(leading_row):
        query_portion = lax.dynamic_slice_in_dim(query_rows, leading_row, block_length, 0).reshape(block_length, KEY_VALUE_HEADS, group_width, HEAD_DIMENSION)
        key_part = lax.dynamic_slice_in_dim(key_padded, leading_row, window, 0)
        value_part = lax.dynamic_slice_in_dim(value_padded, leading_row, window, 0)
        query_seg = lax.dynamic_slice_in_dim(stream_segment, leading_row, block_length, 0)
        key_seg = lax.dynamic_slice_in_dim(segment_pad, leading_row, window, 0)
        query_pos = leading_row + jnp.arange(block_length, dtype=jnp.int32)
        key_pos = leading_row - LONGEST_LENGTH + jnp.arange(window, dtype=jnp.int32)
        allowed = (query_seg[:, None] == key_seg[None, :]) & (key_pos[None, :] <= query_pos[:, None])
        scores = lower_backward(jnp.einsum('qhgd,khd->hgqk', query_portion, key_part, precision=highest_precision) * score_scale)
        scores = jnp.where(allowed[None, None], scores, big_negative)
        probs = lower_precision(jax.nn.softmax(scores, axis=-1))
        blended = jnp.einsum('hgqk,khd->qhgd', probs, value_part, precision=highest_precision)
        return blended.reshape(block_length, QUERY_HEADS * HEAD_DIMENSION)
    firsts = (jnp.arange(TOKEN_TOTAL // block_length, dtype=jnp.int32) * block_length).astype(jnp.int32)
    return lax.map(jax.checkpoint(one_block), firsts).reshape(TOKEN_TOTAL, QUERY_HEADS * HEAD_DIMENSION)

def run_expert(expert_args):
    rows_in, gate_up_e, down_e = expert_args
    gate_up_out = lower_backward(jnp.dot(rows_in, gate_up_e, precision=highest_precision))
    hidden = lower_precision(jax.nn.silu(gate_up_out[:, :FF]) * gate_up_out[:, FF:])
    return lower_backward(lower_precision(jnp.dot(hidden, down_e, precision=highest_precision)))

def reference(tokens, norm_gain, w_query, key_weight, value_weight, query_gain, key_gain, w_out, mix_gain, w_router, expert_gate_up, expert_down, lengths, block_deal, routes, cotangent):
    devices_all = N_HEAD * N_BLK
    row_ids = jnp.arange(TOKEN_TOTAL, dtype=jnp.int32)
    device = (row_ids // TOK_DEV).astype(jnp.int32)
    places = (block_deal[device % CYCLE] * BLOCK + device // CYCLE * TOK_DEV + row_ids % TOK_DEV).astype(jnp.int32)
    offsets = sequence_of(places, lengths)[1].astype(jnp.float32)
    stream_segment = sequence_of(row_ids, lengths)[0]
    stream_rows = jnp.zeros((TOKEN_TOTAL,), jnp.int32).at[places].set(row_ids)
    targets = route_targets(routes, devices_all)

    def forward(tokens_f, norm_gain_f, w_query_f, key_weight_float, value_weight_float, query_gain_f, key_gain_f, w_out_f, mix_gain_f, w_router_f, gate_up_f, down_f):
        normed_rows = lower_precision(rms_scale(tokens_f, norm_gain_f))
        query_raw = lower_backward(jnp.dot(normed_rows, w_query_f, precision=highest_precision)).reshape(TOKEN_TOTAL, QUERY_HEADS, HEAD_DIMENSION)
        key_unscaled = lower_backward(jnp.dot(normed_rows, key_weight_float, precision=highest_precision)).reshape(TOKEN_TOTAL, KEY_VALUE_HEADS, HEAD_DIMENSION)
        value_rows = lower_backward(lower_precision(jnp.dot(normed_rows, value_weight_float, precision=highest_precision))).reshape(TOKEN_TOTAL, KEY_VALUE_HEADS, HEAD_DIMENSION)
        query = lower_backward(lower_precision(rope_turn(rms_scale(query_raw, query_gain_f), offsets)))
        key = lower_backward(lower_precision(rope_turn(rms_scale(key_unscaled, key_gain_f), offsets)))
        attended_stream = attend_stream(query[stream_rows], key[stream_rows], value_rows[stream_rows], stream_segment)
        attended = lower_backward(lower_precision(attended_stream[places]))
        attention = lower_backward(jnp.dot(attended, w_out_f, precision=highest_precision))
        residual = tokens_f + attention
        mixed = lower_precision(rms_scale(residual, mix_gain_f))
        logits = lower_backward(jnp.dot(mixed, w_router_f.T, precision=highest_precision))
        gates = jax.nn.softmax(jnp.take_along_axis(logits, routes, axis=1), axis=-1)
        copies = jnp.zeros((EXPERTS * devices_all * CAP, MODEL_DIMENSION), jnp.float32).at[targets].set(jnp.repeat(mixed, TOPK, axis=0))
        copies = lower_backward(copies).reshape(EXPERTS, devices_all * CAP, MODEL_DIMENSION)
        expert_out = lax.map(jax.checkpoint(run_expert), (copies, gate_up_f, down_f))
        picked = expert_out.reshape(-1, MODEL_DIMENSION)[targets].reshape(TOKEN_TOTAL, TOPK, MODEL_DIMENSION)
        return residual + lax.optimization_barrier(jnp.sum(gates[:, :, None] * picked, axis=1))
    floats = (tokens.astype(jnp.float32), norm_gain.astype(jnp.float32), w_query.astype(jnp.float32), key_weight.astype(jnp.float32), value_weight.astype(jnp.float32), query_gain.astype(jnp.float32), key_gain.astype(jnp.float32), w_out.astype(jnp.float32), mix_gain.astype(jnp.float32), w_router.astype(jnp.float32), expert_gate_up.astype(jnp.float32), expert_down.astype(jnp.float32))
    result, pullback = jax.vjp(forward, *floats)
    grads = pullback(cotangent.astype(jnp.float32))
    return (result.astype(jnp.bfloat16), grads[0], grads[1], grads[2], grads[3], grads[4], grads[5], grads[6], grads[7], grads[8], grads[9], grads[10], grads[11])
```

```python
import jax
import jax.numpy as jnp
from jax import lax
from jax.experimental import pallas as pl
from jax.experimental.pallas import tpu as pltpu
from jax.sharding import PartitionSpec as P

MESH = pl.DeviceIdType.MESH
EPS = 1e-06
ROPE_BASE = 1000000.0
LOG2E = 1.4426950408889634
BF = jnp.bfloat16
F32 = jnp.float32
BLOCK = 256
SIZES = {"zc": 4, "c": 2, "x": 4, "y": 4, "zhc": 4, "h": 2, "z": 8, "yx": 16}


def peers_of(kind):
    h = lax.axis_index("head")
    b = lax.axis_index("blk")
    q, r = lax.div(b, 4), lax.rem(b, 4)
    if kind == "zc":
        return lax.div(r, 2) * 2 + h, lambda g: (lax.rem(g, 2), q * 4 + lax.div(g, 2) * 2 + lax.rem(r, 2))
    if kind == "z":
        return lax.rem(r, 2) * 4 + lax.div(r, 2) * 2 + h, lambda g: (
            lax.rem(g, 2),
            q * 4 + lax.rem(lax.div(g, 2), 2) * 2 + lax.div(g, 4),
        )
    if kind == "c":
        return lax.rem(b, 2), lambda g: (h, b - lax.rem(b, 2) + g)
    if kind == "x":
        return lax.rem(q, 4), lambda g: (h, (lax.div(q, 4) * 4 + g) * 4 + r)
    if kind == "y":
        return lax.div(q, 4), lambda g: (h, (g * 4 + lax.rem(q, 4)) * 4 + r)
    if kind == "yx":
        return q, lambda g: (h, g * 4 + r)
    if kind == "zhc":
        return r, lambda g: (h, q * 4 + g)
    return h, lambda g: (g, b)


def exchange(parts, cid):
    count = len(parts)
    sizes = [SIZES[part[1]] for part in parts]
    shapes, chunks = [], []
    for array, kind, gather, axis in parts:
        n = SIZES[kind]
        if gather:
            chunks.append(array.shape)
            shapes.append(array.shape[:axis] + (n,) + array.shape[axis:])
        else:
            chunks.append(array.shape[:axis] + array.shape[axis + 1 :])
            shapes.append((n,) + chunks[-1])

    def entry(ref, axis, index):
        return ref.at[index] if axis == 0 else ref.at[:, index]

    def kernel(*refs):
        ins, outs, rest = refs[:count], refs[count : 2 * count], refs[2 * count :]
        sends, recvs, local = rest[:count], rest[count : 2 * count], rest[2 * count]
        stages = rest[2 * count + 1 :]
        groups = [peers_of(part[1]) for part in parts]
        barrier = pltpu.get_barrier_semaphore()
        seen, total = [], 0
        for i, part in enumerate(parts):
            if part[1] in seen:
                continue
            seen.append(part[1])
            me, member = groups[i]
            for k in range(1, sizes[i]):
                pl.semaphore_signal(barrier, inc=1, device_id=member(lax.rem(me + k, sizes[i])), device_id_type=MESH)
            total += sizes[i] - 1

        def source(i, to):
            return ins[i] if parts[i][2] else entry(ins[i], parts[i][3], to)

        def target(i, sender):
            return entry(outs[i], parts[i][3] if parts[i][2] else 0, sender)

        own = []
        for i in range(count):
            own.append(pltpu.make_async_copy(source(i, groups[i][0]), stages[i], local.at[i]))
            own[i].start()
        pl.semaphore_wait(barrier, total)
        copies = []
        for i in range(count):
            me, member = groups[i]
            for k in range(1, sizes[i]):
                to = lax.rem(me + k, sizes[i])
                copy = pltpu.make_async_remote_copy(
                    src_ref=source(i, to),
                    dst_ref=target(i, me),
                    send_sem=sends[i].at[k],
                    recv_sem=recvs[i].at[k],
                    device_id=member(to),
                    device_id_type=MESH,
                )
                copy.start()
                copies.append(copy)
        backs = []
        for i in range(count):
            own[i].wait()
            backs.append(pltpu.make_async_copy(stages[i], target(i, groups[i][0]), local.at[i]))
            backs[i].start()
        for copy in copies:
            copy.wait()
        for back in backs:
            back.wait()

    return pl.pallas_call(
        kernel,
        out_shape=tuple(jax.ShapeDtypeStruct(s, p[0].dtype) for s, p in zip(shapes, parts)),
        in_specs=[pl.BlockSpec(memory_space=pl.ANY)] * count,
        out_specs=tuple([pl.BlockSpec(memory_space=pl.ANY)] * count),
        scratch_shapes=[pltpu.SemaphoreType.DMA((n,)) for n in sizes] * 2
        + [pltpu.SemaphoreType.DMA((count,))]
        + [pltpu.VMEM(c, p[0].dtype) for c, p in zip(chunks, parts)],
        compiler_params=pltpu.CompilerParams(collective_id=cid, has_side_effects=True, vmem_limit_bytes=32 << 20),
    )(*[part[0] for part in parts])


def add_up(stacked):
    return jnp.sum(stacked.astype(F32), axis=0)


def dot_nn(a, b):
    return lax.dot_general(a, b, (((1,), (0,)), ((), ())), preferred_element_type=F32)


def dot_nt(a, b):
    return lax.dot_general(a, b, (((1,), (1,)), ((), ())), preferred_element_type=F32)


def dot_tn(a, b):
    return lax.dot_general(a, b, (((0,), (0,)), ((), ())), preferred_element_type=F32)


def attend_forward_kernel(scale, lo_ref, full_ref, last_ref, slot_ref, q_ref, k_ref, v_ref, start_ref, o_ref, log_ref, acc, total):
    j = pl.program_id(0)
    heads = q_ref.shape[1]
    last = last_ref[j]
    middle = jnp.minimum(full_ref[j], last)
    acc[...] = jnp.zeros_like(acc)
    total[...] = jnp.zeros_like(total)
    start = start_ref[0]

    def tile(t, masked):
        slot = slot_ref[t]
        keys, values = k_ref[slot], v_ref[slot]
        if masked:
            key_place = t * BLOCK + lax.broadcasted_iota(jnp.int32, (BLOCK, BLOCK), 0)
            query_place = last * BLOCK + lax.broadcasted_iota(jnp.int32, (BLOCK, BLOCK), 1)
            allowed = (key_place >= start) & (key_place <= query_place)
        for n in range(heads):
            weights = jnp.exp2(dot_nt(keys, q_ref[0, n]) * (scale * LOG2E))
            if masked:
                weights = jnp.where(allowed, weights, 0.0)
            total[n] += jnp.sum(weights.reshape(BLOCK // 8, 8, BLOCK), axis=0)
            acc[n] += dot_tn(values, weights.astype(BF))

    pl.loop(lo_ref[j], middle)(lambda t: tile(t, True))
    pl.loop(middle, last)(lambda t: tile(t, False))
    tile(last, True)
    for n in range(heads):
        row = jnp.sum(total[n], axis=0, keepdims=True)
        o_ref[0, n] = (acc[n] / row).T.astype(BF)
        log_ref[0, n] = jnp.log2(row)


def attend_backward_kernel(
    scale, lo_ref, full_ref, last_ref, slot_ref, q_ref, k_ref, v_ref, start_ref, g_ref, log_ref, delta_ref, dq_ref, dk_ref, dv_ref, acc, dk, dv
):
    j = pl.program_id(0)
    heads = q_ref.shape[1]
    last = last_ref[j]
    middle = jnp.minimum(full_ref[j], last)
    slots = k_ref.shape[0]

    @pl.when(j == 0)
    def _():
        @pl.loop(0, slots)
        def _(s):
            dk[s] = jnp.zeros(dk.shape[1:], F32)
            dv[s] = jnp.zeros(dv.shape[1:], F32)

    acc[...] = jnp.zeros_like(acc)
    start = start_ref[0]

    def tile(t, masked):
        slot = slot_ref[t]
        keys, values = k_ref[slot], v_ref[slot]
        if masked:
            key_place = t * BLOCK + lax.broadcasted_iota(jnp.int32, (BLOCK, BLOCK), 0)
            query_place = last * BLOCK + lax.broadcasted_iota(jnp.int32, (BLOCK, BLOCK), 1)
            allowed = (key_place >= start) & (key_place <= query_place)
        dk_now, dv_now = dk[slot], dv[slot]
        for n in range(heads):
            probs = jnp.exp2(dot_nt(keys, q_ref[0, n]) * (scale * LOG2E) - log_ref[0, n])
            if masked:
                probs = jnp.where(allowed, probs, 0.0)
            grad_scores = (probs * (dot_nt(values, g_ref[0, n]) - delta_ref[0, n])).astype(BF)
            dv_now += dot_nn(probs.astype(BF), g_ref[0, n])
            dk_now += dot_nn(grad_scores, q_ref[0, n])
            acc[n] += dot_tn(keys, grad_scores)
        dk[slot], dv[slot] = dk_now, dv_now

    pl.loop(lo_ref[j], middle)(lambda t: tile(t, True))
    pl.loop(middle, last)(lambda t: tile(t, False))
    tile(last, True)
    for n in range(heads):
        dq_ref[0, n] = (acc[n] * scale).T.astype(BF)

    @pl.when(j == pl.num_programs(0) - 1)
    def _():
        @pl.loop(0, slots)
        def _(s):
            dk_ref[s] = (dk[s] * scale).astype(BF)
            dv_ref[s] = dv[s].astype(BF)


def per_block(shape):
    return pl.BlockSpec((1,) + shape[1:], lambda j, *_: (j,) + (0,) * (len(shape) - 1))


def resident(shape):
    return pl.BlockSpec(shape, lambda j, *_: (0,) * len(shape), pipeline_mode=pl.Buffered(1))


def attend_forward(meta, queries, keys, values, start, scale):
    blocks, heads, rows, size = queries.shape
    log_shape = (blocks, heads, 1, rows)
    return pl.pallas_call(
        lambda *refs: attend_forward_kernel(scale, *refs),
        out_shape=(jax.ShapeDtypeStruct(queries.shape, BF), jax.ShapeDtypeStruct(log_shape, F32)),
        grid_spec=pltpu.PrefetchScalarGridSpec(
            num_scalar_prefetch=4,
            grid=(blocks,),
            in_specs=[per_block(queries.shape), resident(keys.shape), resident(values.shape), per_block(start.shape)],
            out_specs=(per_block(queries.shape), per_block(log_shape)),
            scratch_shapes=[pltpu.VMEM((heads, size, rows), F32), pltpu.VMEM((heads, 8, rows), F32)],
        ),
        compiler_params=pltpu.CompilerParams(vmem_limit_bytes=48 << 20),
    )(*meta, queries, keys, values, start)


def attend_backward(meta, queries, keys, values, start, grads, logs, delta, scale):
    blocks, heads, rows, size = queries.shape
    return pl.pallas_call(
        lambda *refs: attend_backward_kernel(scale, *refs),
        out_shape=(
            jax.ShapeDtypeStruct(queries.shape, BF),
            jax.ShapeDtypeStruct(keys.shape, BF),
            jax.ShapeDtypeStruct(values.shape, BF),
        ),
        grid_spec=pltpu.PrefetchScalarGridSpec(
            num_scalar_prefetch=4,
            grid=(blocks,),
            in_specs=[
                per_block(queries.shape),
                resident(keys.shape),
                resident(values.shape),
                per_block(start.shape),
                per_block(queries.shape),
                per_block(logs.shape),
                per_block(delta.shape),
            ],
            out_specs=(per_block(queries.shape), resident(keys.shape), resident(values.shape)),
            scratch_shapes=[
                pltpu.VMEM((heads, size, rows), F32),
                pltpu.VMEM(keys.shape, F32),
                pltpu.VMEM(values.shape, F32),
            ],
        ),
        compiler_params=pltpu.CompilerParams(vmem_limit_bytes=56 << 20),
    )(*meta, queries, keys, values, start, grads, logs, delta)


def rms_scale(values, gain_vec):
    return values * lax.rsqrt(jnp.mean(values * values, axis=-1, keepdims=True) + EPS) * gain_vec


def rope_table(offsets, size):
    half = size // 2
    spacing = ROPE_BASE ** (-2.0 * jnp.arange(half, dtype=F32) / size)
    angles = offsets.astype(F32)[:, None] * spacing[None, :]
    return jnp.cos(angles), jnp.sin(angles)


def rope_turn(values, cosine, sine):
    half = values.shape[-1] // 2
    front, back = values[..., :half], values[..., half:]
    return jnp.concatenate([front * cosine - back * sine, back * cosine + front * sine], axis=-1)


def swiglu(gate_part, up_part):
    return jax.nn.silu(gate_part) * up_part


def two_parts(wide):
    high = wide.astype(BF)
    return high, (wide - high.astype(F32)).astype(BF)


def all_to_all(stacked):
    return lax.all_to_all(stacked, ("head", "blk"), split_axis=0, concat_axis=0, tiled=True)


def body(
    tokens,
    norm_gain,
    w_query,
    key_weight,
    value_weight,
    query_gain,
    key_gain,
    w_out,
    mix_gain,
    w_router,
    expert_gate_up,
    expert_down,
    lengths,
    block_deal,
    routes,
    cotangent,
):
    own, width = tokens.shape
    size = query_gain.shape[0]
    scale = size ** (-0.5)
    blk = lax.axis_index("blk")
    plane, core = blk // 4, blk % 2
    devices = lax.axis_size("head") * lax.axis_size("blk")
    experts = w_router.shape[0] * 2
    cap = own * routes.shape[1] // experts
    gate_up, down = expert_gate_up[0], expert_down[0]
    ff = down.shape[0]
    group_rows = 8 * own
    q_cols = w_query.shape[1] // 4
    heads = q_cols // size

    chosen = jnp.sum((routes[:, :, None] == jnp.arange(experts, dtype=jnp.int32)).astype(jnp.int32), axis=1)
    order = jnp.arange(own)
    earlier = dot_nn((order[:, None] > order[None, :]).astype(BF), chosen.astype(BF)).astype(jnp.int32)
    assign = (chosen[:, :, None] > 0) & (earlier[:, :, None] == jnp.arange(cap, dtype=jnp.int32))
    assign_wide = assign.astype(F32)
    assign_low = assign.astype(BF).reshape(own, experts * cap)
    grad_rows = all_to_all(dot_tn(assign_low, cotangent).astype(BF).reshape(devices, cap, width)).reshape(-1, width)

    wide = tokens.astype(F32)
    normed, norm_back = jax.vjp(rms_scale, wide, norm_gain)
    normed_low = normed.astype(BF)
    depth = w_query.shape[0]
    kv = jnp.concatenate([key_weight.reshape(depth, 2, 1, size), value_weight.reshape(depth, 2, 1, size)], axis=2)
    kv = jnp.repeat(kv.reshape(depth, 2, 2 * size), 2, axis=1)
    qkv_pack = jnp.concatenate([w_query.reshape(depth, 4, q_cols), kv], axis=2).transpose(1, 0, 2)
    out_pack = w_out.reshape(4, q_cols, depth).transpose(0, 2, 1)
    ring_tokens, w_qkv, out_pack, router_pack = exchange(
        [(normed_low, "zc", True, 0), (qkv_pack, "zhc", False, 0), (out_pack, "zhc", False, 0), (w_router.T, "z", True, 0)], 0
    )
    router_pack = router_pack.reshape(2, 2, 2, depth, -1).transpose(1, 0, 3, 2, 4).reshape(4 * depth, experts)
    w_qkv = w_qkv.reshape(4 * depth, -1)
    w_rest = jnp.concatenate([out_pack.reshape(4 * depth, q_cols), router_pack], axis=1)
    group_tokens, w_qkv, w_rest = exchange([(ring_tokens, "c", True, 0), (w_qkv, "x", True, 0), (w_rest, "y", True, 0)], 1)
    w_qkv, w_rest = exchange([(w_qkv, "y", True, 0), (w_rest, "x", True, 1)], 2)
    normed_group = group_tokens.reshape(group_rows, width)
    w_qkv = w_qkv.reshape(width, -1)
    w_rest = w_rest.reshape(width, -1)
    w_out_t, w_router_t = w_rest[:, :q_cols], w_rest[:, q_cols:]

    group_blocks = plane * 4 + jnp.array([0, 2, 1, 3], jnp.int32)
    ids = jnp.arange(block_deal.shape[0], dtype=jnp.int32)
    last = jnp.sum(jnp.where(group_blocks[:, None] == ids[None, :], block_deal[None, :], 0), axis=1)
    slots = (ids % 2) * (ids.shape[0] // 2) + (ids // 4) * 2 + (ids % 4) // 2
    slot_of = jnp.sum(jnp.where(block_deal[None, :] == ids[:, None], slots[None, :], 0), axis=1)
    place = (last[:, None] * BLOCK + jnp.arange(BLOCK, dtype=jnp.int32)[None, :]).reshape(-1)
    passed = place[:, None] >= jnp.cumsum(lengths)[None, :]
    start = jnp.sum(jnp.where(passed, lengths[None, :], 0), axis=1)
    start_rows = start.reshape(-1, 1, BLOCK)
    meta = (start_rows[:, 0, 0] // BLOCK, (start_rows[:, 0, BLOCK - 1] + BLOCK - 1) // BLOCK, last, slot_of)
    cosine, sine = rope_table(place - start, size)

    half_rows = group_rows // 2
    half = core * half_rows

    def own_half(array):
        return lax.dynamic_slice_in_dim(array, half, half_rows, 0)

    qkv = dot_nn(normed_group, w_qkv)
    q_raw = qkv[:, :q_cols].reshape(group_rows, heads, size).transpose(1, 0, 2)
    kv_raw = own_half(qkv[:, q_cols:])
    query, query_back = jax.vjp(lambda raw, gain: rope_turn(rms_scale(raw, gain), cosine, sine), q_raw, query_gain)
    key, key_back = jax.vjp(
        lambda raw, gain: rope_turn(rms_scale(raw, gain), own_half(cosine), own_half(sine)), kv_raw[:, :size], key_gain
    )

    def by_block(array):
        return array.reshape(heads, -1, BLOCK, size).transpose(1, 0, 2, 3)

    queries = by_block(query.astype(BF))
    keys, values = exchange([(key.astype(BF), "x", True, 0), (kv_raw[:, size:].astype(BF), "y", True, 0)], 3)
    keys, values = exchange([(keys, "y", True, 0), (values, "x", True, 1)], 4)
    keys, values = exchange([(keys, "c", True, 0), (values, "c", True, 0)], 5)
    keys, values = keys.reshape(-1, BLOCK, size), values.reshape(-1, BLOCK, size)
    attended, logs = attend_forward(meta, queries, keys, values, start_rows, scale)
    attended_group = attended.transpose(0, 2, 1, 3).reshape(group_rows, q_cols)

    def group_sum(partial, cid):
        halves = exchange([(partial.astype(BF).reshape(2, 4, own, width), "c", False, 0)], cid)[0]
        return add_up(exchange([(add_up(halves).astype(BF), "zc", False, 0)], cid + 1)[0])

    residual = wide + group_sum(dot_nt(attended_group, w_out_t), 6)
    mixed, mix_back = jax.vjp(rms_scale, residual, mix_gain)
    mixed_low = mixed.astype(BF)
    logits = dot_nn(mixed_low, w_router_t)
    gates = jax.nn.softmax(jnp.where(chosen > 0, logits, -1e30), axis=-1)
    gate_slots = gates[:, :, None] * assign_wide
    high, low = two_parts(jnp.sum(gate_slots, axis=0).reshape(-1, 1))
    pad = jnp.zeros((experts * cap, 126), BF)
    outgoing = jnp.concatenate([dot_tn(assign_low, mixed_low).astype(BF), high, low, pad], axis=1)
    arrived = all_to_all(outgoing.reshape(devices, cap, -1)).reshape(experts * cap, -1)

    rows, gate = arrived[:, :width], jnp.sum(arrived[:, width : width + 2].astype(F32), axis=1, keepdims=True)
    gate_up_out = dot_nn(rows, gate_up)
    hidden, swiglu_back = jax.vjp(swiglu, gate_up_out[:, :ff], gate_up_out[:, ff:])
    hidden_low = hidden.astype(BF)
    plain_grad = dot_nt(grad_rows, down)
    gate_grad = jnp.sum(hidden_low.astype(F32) * plain_grad, axis=1, keepdims=True)
    grad_both = jnp.concatenate(swiglu_back(plain_grad * gate), axis=1).astype(BF)
    high, low = two_parts(gate_grad)
    back = jnp.concatenate([dot_nt(grad_both, gate_up).astype(BF), high, low, pad], axis=1)
    back = all_to_all(back.reshape(devices, cap, -1)).reshape(experts * cap, -1)
    expert_out = all_to_all(dot_nn(hidden_low, down).astype(BF).reshape(devices, cap, width)).reshape(-1, width)
    grad_down = dot_tn((hidden * gate).astype(BF), grad_rows)
    grad_gate_up = dot_tn(rows, grad_both)

    high, low = two_parts(gate_slots.reshape(own, -1))
    output = (residual + dot_nn(high, expert_out) + dot_nn(low, expert_out)).astype(BF)
    gate_grads = jnp.sum(back[:, width : width + 2].astype(F32), axis=1).reshape(experts, cap)
    gate_grads = jnp.sum(assign_wide * gate_grads[None], axis=2)
    grad_logits = (gates * (gate_grads - jnp.sum(gates * gate_grads, axis=1, keepdims=True))).astype(BF)
    grad_mixed = dot_nn(assign_low, back[:, :width]) + dot_nt(grad_logits, w_router_t)
    grad_router_t = dot_tn(mixed_low, grad_logits)
    grad_from_mix, grad_mix_gain = mix_back(grad_mixed)
    grad_residual = cotangent.astype(F32) + grad_from_mix
    ring_grads = exchange([(grad_residual.astype(BF), "zc", True, 0)], 8)[0]
    grad_group = exchange([(ring_grads, "c", True, 0)], 9)[0].reshape(group_rows, width)
    grad_attended = dot_nn(grad_group, w_out_t).astype(BF)
    grad_out_t = dot_tn(grad_group, attended_group)
    grads = grad_attended.reshape(-1, BLOCK, heads, size).transpose(0, 2, 1, 3)
    delta = jnp.sum(grads.astype(F32) * attended.astype(F32), axis=-1)[:, :, None, :]
    grad_query, grad_keys, grad_values = attend_backward(meta, queries, keys, values, start_rows, grads, logs, delta, scale)

    split = (2, 4, 4, half_rows, size)
    grad_keys, grad_values = exchange([(grad_keys.reshape(split), "c", False, 0), (grad_values.reshape(split), "c", False, 0)], 10)
    grad_keys, grad_values = add_up(grad_keys).astype(BF), add_up(grad_values).astype(BF)
    grad_keys, grad_values = exchange([(grad_keys, "y", False, 0), (grad_values, "x", False, 1)], 11)
    grad_keys, grad_values = add_up(grad_keys).astype(BF), add_up(grad_values).astype(BF)
    grad_keys, grad_values = exchange([(grad_keys, "x", False, 0), (grad_values, "y", False, 0)], 12)
    grad_key, grad_value = add_up(grad_keys).astype(BF), add_up(grad_values).astype(BF)
    grad_query = grad_query.transpose(1, 0, 2, 3).reshape(heads, group_rows, size).astype(F32)
    grad_q_raw, grad_query_gain = query_back(grad_query)
    grad_k_raw, grad_key_gain = key_back(grad_key.astype(F32))
    grad_kv = jnp.concatenate([grad_k_raw.astype(BF), grad_value], axis=1)
    grad_kv = lax.dynamic_update_slice_in_dim(jnp.zeros((group_rows, 2 * size), BF), grad_kv, half, 0)
    grad_q_flat = grad_q_raw.astype(BF).transpose(1, 0, 2).reshape(group_rows, q_cols)
    grad_qkv = jnp.concatenate([grad_q_flat, grad_kv], axis=1)
    grad_normed = group_sum(dot_nt(grad_qkv, w_qkv), 13)
    grad_from_norm, grad_norm_gain = norm_back(grad_normed)
    grad_tokens = grad_residual + grad_from_norm

    plane_split = (4, 4, 4 * depth, -1)
    grad_w = dot_tn(normed_group, grad_qkv).astype(BF).reshape(plane_split)
    grad_rest = jnp.concatenate([grad_out_t, grad_router_t], axis=1).astype(BF).reshape(plane_split)
    gains = jnp.concatenate([grad_norm_gain, grad_mix_gain, grad_query_gain, grad_key_gain, jnp.zeros((768,), F32)]).reshape(-1, size)
    grad_w, grad_rest, gains = exchange([(grad_w, "y", False, 0), (grad_rest, "x", False, 1), (gains, "x", True, 0)], 15)
    grad_w, grad_rest, gains = add_up(grad_w).astype(BF), add_up(grad_rest).astype(BF), add_up(gains)
    grad_w, grad_rest, gains = exchange([(grad_w, "x", False, 0), (grad_rest, "y", False, 0), (gains, "y", True, 0)], 16)
    grad_w, grad_rest, gains = add_up(grad_w).astype(BF), add_up(grad_rest).astype(BF), add_up(gains)
    grad_out_part = grad_rest[:, :q_cols].reshape(4, depth, q_cols)
    router_part = grad_rest[:, q_cols:].reshape(2, 2, depth, 2, experts // 2).transpose(1, 0, 3, 2, 4).reshape(8, depth, -1)
    grad_w, grad_out_part, router_part, gains = exchange(
        [(grad_w.reshape(4, depth, -1), "zhc", False, 0), (grad_out_part, "zhc", False, 0), (router_part, "z", False, 0), (gains, "z", True, 0)],
        17,
    )
    grad_w = grad_w.astype(F32)
    gains = add_up(gains).reshape(-1)
    grad_w_query = grad_w[:, :, :q_cols].transpose(1, 0, 2).reshape(depth, -1)
    grad_kv_w = jnp.sum(grad_w[:, :, q_cols:].reshape(2, 2, depth, 2, size), axis=1)
    grad_w_key = grad_kv_w[:, :, 0].transpose(1, 0, 2).reshape(depth, -1)
    grad_w_value = grad_kv_w[:, :, 1].transpose(1, 0, 2).reshape(depth, -1)
    grad_w_out = grad_out_part.astype(F32).transpose(0, 2, 1).reshape(-1, depth)
    grad_w_router = add_up(router_part).T
    return (
        output,
        grad_tokens,
        gains[:width],
        grad_w_query,
        grad_w_key,
        grad_w_value,
        gains[2 * width : 2 * width + size],
        gains[2 * width + size : 2 * width + 2 * size],
        grad_w_out,
        gains[width : 2 * width],
        grad_w_router,
        grad_gate_up[None],
        grad_down[None],
    )


def solution(mesh):
    rows, both = P(("head", "blk"), None), P("blk", "head")
    expert, turned = P(("head", "blk"), None, None), P("head", "blk")
    in_specs = (rows, P(), both, both, both, P(), P(), turned, P(), turned, expert, expert, P(), P(), rows, rows)
    out_specs = (rows, rows, P(), both, both, both, P(), P(), turned, P(), turned, expert, expert)
    return jax.shard_map(body, mesh=mesh, in_specs=in_specs, out_specs=out_specs, check_vma=False)
```

```python
import jax
import jax.numpy as jnp
from jax import lax
from jax.experimental import pallas as pl
from jax.experimental.pallas import tpu as pltpu
from jax.sharding import PartitionSpec as P

MESH = pl.DeviceIdType.MESH
EPS = 1e-06
ROPE_BASE = 1000000.0
LOG2E = 1.4426950408889634
BF = jnp.bfloat16
F32 = jnp.float32
BLOCK = 256
SIZES = {"zc": 4, "c": 2, "x": 4, "y": 4, "zhc": 4, "h": 2, "z": 8, "yx": 16}


def peers_of(kind):
    h = lax.axis_index("head")
    b = lax.axis_index("blk")
    q, r = lax.div(b, 4), lax.rem(b, 4)
    if kind == "zc":
        return lax.div(r, 2) * 2 + h, lambda g: (lax.rem(g, 2), q * 4 + lax.div(g, 2) * 2 + lax.rem(r, 2))
    if kind == "z":
        return lax.rem(r, 2) * 4 + lax.div(r, 2) * 2 + h, lambda g: (
            lax.rem(g, 2),
            q * 4 + lax.rem(lax.div(g, 2), 2) * 2 + lax.div(g, 4),
        )
    if kind == "c":
        return lax.rem(b, 2), lambda g: (h, b - lax.rem(b, 2) + g)
    if kind == "x":
        return lax.rem(q, 4), lambda g: (h, (lax.div(q, 4) * 4 + g) * 4 + r)
    if kind == "y":
        return lax.div(q, 4), lambda g: (h, (g * 4 + lax.rem(q, 4)) * 4 + r)
    if kind == "yx":
        return q, lambda g: (h, g * 4 + r)
    if kind == "zhc":
        return r, lambda g: (h, q * 4 + g)
    return h, lambda g: (g, b)


def cost_of(microseconds):
    return pl.CostEstimate(flops=microseconds * 10**9, bytes_accessed=microseconds * 3 * 10**6, transcendentals=0)


class Flow:
    def __init__(self, inputs, outputs, scratch, partners, steps):
        self.inputs, self.outputs, self.scratch = inputs, outputs, scratch
        self.partners, self.steps = partners, steps


def launch(flows, cid, cost, vmem=40):
    partners = sorted({p for flow in flows for p in flow.partners})

    def kernel(*refs):
        n_in, n_out = sum(len(f.inputs) for f in flows), sum(len(f.outputs) for f in flows)
        ins, outs, rest = list(refs[:n_in]), list(refs[n_in : n_in + n_out]), list(refs[n_in + n_out :])
        barrier = pltpu.get_barrier_semaphore()
        for kind, distance in partners:
            me, member = peers_of(kind)
            to = member(lax.rem(me + distance, SIZES[kind]))
            pl.semaphore_signal(barrier, inc=1, device_id=to, device_id_type=MESH)
        pl.semaphore_wait(barrier, len(partners))
        running = []
        for flow in flows:
            own = [[group.pop(0) for _ in part] for group, part in ((ins, flow.inputs), (outs, flow.outputs), (rest, flow.scratch))]
            running.append(flow.steps(*own))
        while running:
            running = [steps for steps in running if next(steps, running) is not running]

    return pl.pallas_call(
        kernel,
        out_shape=tuple(jax.ShapeDtypeStruct(s, d) for f in flows for s, d, _ in f.outputs),
        in_specs=[pl.BlockSpec(memory_space=space) for f in flows for _, space in f.inputs],
        out_specs=tuple(pl.BlockSpec(memory_space=space) for f in flows for _, _, space in f.outputs),
        scratch_shapes=[x for f in flows for x in f.scratch],
        compiler_params=pltpu.CompilerParams(collective_id=cid, has_side_effects=True, vmem_limit_bytes=vmem << 20),
        cost_estimate=cost_of(cost),
        name=f"links_{cid}",
    )(*[x for f in flows for x, _ in f.inputs])


def remote(src, dst, send, recv, device):
    return pltpu.make_async_remote_copy(
        src_ref=src, dst_ref=dst, send_sem=send, recv_sem=recv, device_id=device, device_id_type=MESH
    )


def piece(ref, which):
    rows = ref.shape[0] // 2
    return ref.at[pl.ds(which * rows, rows)]


def ring_partners(kind):
    return [(kind, 1), (kind, 3)]


class RingGather:
    def __init__(self, kind, slot, src, send, recv):
        me, member = peers_of(kind)
        up, down = lax.rem(me + 1, 4), lax.rem(me + 3, 4)

        def copy(source, target, i, to):
            return remote(source, target, send.at[i], recv.at[i], member(to))

        mine = slot(me)
        self.copies = [
            copy(piece(src, 0), piece(mine, 0), 0, up),
            copy(piece(src, 1), piece(mine, 1), 1, up),
            copy(piece(src, 1), piece(mine, 1), 2, down),
            copy(piece(src, 0), piece(mine, 0), 3, down),
            copy(piece(slot(down), 0), piece(slot(down), 0), 4, up),
            copy(piece(slot(up), 1), piece(slot(up), 1), 5, down),
        ]

    def start(self):
        for i in (0, 2, 1, 3):
            self.copies[i].start()

    def forward(self):
        self.copies[0].wait_recv()
        self.copies[4].start()
        self.copies[2].wait_recv()
        self.copies[5].start()

    def near(self):
        self.copies[1].wait_recv()
        self.copies[3].wait_recv()

    def far(self):
        self.copies[4].wait_recv()
        self.copies[5].wait_recv()

    def sent(self):
        for copy in self.copies:
            copy.wait_send()


class RingScatter:
    def __init__(self, kind, chunk, bufs, send, recv):
        self.me, member = peers_of(kind)
        self.up, self.down, self.far = (lax.rem(self.me + k, 4) for k in (1, 3, 2))
        self.chunk, self.bufs = chunk, bufs

        def copy(source, target, i, to):
            return remote(source, bufs.at[target], send.at[i], recv.at[i], member(to))

        self.copies = [
            copy(piece(chunk(self.far), 0), 0, 0, self.up),
            copy(piece(chunk(self.far), 1), 1, 1, self.down),
            copy(piece(chunk(self.up), 1), 2, 2, self.up),
            copy(piece(chunk(self.down), 0), 3, 3, self.down),
            copy(bufs.at[6], 4, 4, self.up),
            copy(bufs.at[7], 5, 5, self.down),
        ]

    def start_far(self):
        self.copies[0].start()
        self.copies[1].start()

    def start_up(self):
        self.copies[2].start()

    def start_down(self):
        self.copies[3].start()

    def add(self):
        self.copies[0].wait_recv()
        self.bufs[6] = (piece(self.chunk(self.up), 0)[...].astype(F32) + self.bufs[0].astype(F32)).astype(BF)
        self.copies[4].start()
        self.copies[1].wait_recv()
        self.bufs[7] = (piece(self.chunk(self.down), 1)[...].astype(F32) + self.bufs[1].astype(F32)).astype(BF)
        self.copies[5].start()

    def total(self, which):
        first, second = ((4, 3), (2, 5))[which]
        self.copies[first].wait_recv()
        self.copies[second].wait_recv()
        return self.bufs[first].astype(F32) + self.bufs[second].astype(F32)

    def sent(self):
        for copy in self.copies:
            copy.wait_send()


def dma(*shape):
    return pltpu.SemaphoreType.DMA(shape)


def ring_gather_flow(array):
    shape = (2, 4) + array.shape

    def steps(ins, outs, scratch):
        (src,), (out,) = ins, outs
        stage, send, recv, pass_send, pass_recv, local = scratch
        me, _ = peers_of("zc")
        core, member = peers_of("c")
        own = pltpu.make_async_copy(src, stage, local.at[0])
        own.start()
        ring = RingGather("zc", lambda g: out.at[core, g], src, send, recv)

        def passing(k):
            g = lax.rem(me + k, 4)
            return remote(src if k == 0 else out.at[core, g], out.at[core, g], pass_send.at[k], pass_recv.at[k], member(1 - core))

        passes = [passing(k) for k in range(4)]
        ring.start()
        passes[0].start()
        yield
        ring.forward()
        own.wait()
        back = pltpu.make_async_copy(stage, out.at[core, me], local.at[0])
        back.start()
        yield
        ring.near()
        passes[1].start()
        passes[3].start()
        yield
        ring.far()
        passes[2].start()
        yield
        back.wait()
        ring.sent()
        for copy in passes:
            copy.wait()

    return Flow(
        [(array, pl.ANY)],
        [(shape, array.dtype, pl.ANY)],
        [pltpu.VMEM(array.shape, array.dtype), dma(6), dma(6), dma(4), dma(4), dma(1)],
        ring_partners("zc") + [("c", 1)],
        steps,
    )


def plane_gather_flow(array, first, second, to_core=False, ahead=None, half=False):
    shard = (array.shape[0] // 2,) + array.shape[1:] if half else ((8,) if ahead == "z" else ()) + array.shape
    shape = ((2,) if to_core else ()) + (4, 4) + shard
    others = range(1, SIZES[ahead]) if ahead else ()

    def steps(ins, outs, scratch):
        (src,), (out,) = ins, outs
        stage, send, recv, pass_send, pass_recv, local, ahead_send, ahead_recv = scratch
        core, member = peers_of("c")
        here, _ = peers_of(first)
        there, _ = peers_of(second)
        view = out.at[core] if to_core else out

        def slot(a, b):
            return view.at[b, a] if first == "x" else view.at[a, b]

        if half:
            src = src.at[pl.ds(pl.multiple_of(core * shard[0], shard[0]), shard[0])]
        if ahead:
            mine, at = peers_of(ahead)
            own = pltpu.make_async_copy(src.at[mine] if ahead == "zhc" else src, stage.at[mine], local.at[0])
            own.start()
            early = []
            for k in others:
                to = lax.rem(mine + k, SIZES[ahead])
                early.append(remote(src.at[to] if ahead == "zhc" else src, stage.at[mine], ahead_send.at[k], ahead_recv.at[k], at(to)))
                early[-1].start()
            yield
            own.wait()
            for copy in early:
                copy.wait()
            src = stage
        else:
            own = pltpu.make_async_copy(src, stage, local.at[0])
            own.start()
        ring = RingGather(first, lambda g: slot(g, there), src, send.at[4], recv.at[4])
        columns = [lax.rem(here + k, 4) for k in range(4)]
        rings = [
            RingGather(second, lambda g, a=a: slot(a, g), src if k == 0 else slot(a, there), send.at[k], recv.at[k])
            for k, a in enumerate(columns)
        ]

        def passing(k, m):
            ref = slot(columns[k], lax.rem(there + m, 4))
            return remote(src if k == m == 0 else ref, ref, pass_send.at[k * 4 + m], pass_recv.at[k * 4 + m], member(1 - core))

        passes = {}

        def hand_over(k, m):
            if to_core:
                passes[k, m] = passing(k, m)
                passes[k, m].start()

        ring.start()
        rings[0].start()
        hand_over(0, 0)
        yield
        ring.forward()
        if not ahead:
            own.wait()
        back = pltpu.make_async_copy(stage, slot(here, there), local.at[0])
        back.start()
        yield
        rings[0].forward()
        yield
        ring.near()
        for k in (1, 3):
            rings[k].start()
            hand_over(k, 0)
        yield
        ring.far()
        rings[2].start()
        hand_over(2, 0)
        yield
        for k in (0, 1, 3, 2):
            if k > 0:
                rings[k].forward()
            rings[k].near()
            hand_over(k, 1)
            hand_over(k, 3)
            yield
            rings[k].far()
            hand_over(k, 2)
            yield
        back.wait()
        ring.sent()
        for one in rings:
            one.sent()
        for copy in passes.values():
            copy.wait()

    return Flow(
        [(array, pl.ANY)],
        [(shape, array.dtype, pl.ANY)],
        [pltpu.VMEM(shard, array.dtype), dma(5, 6), dma(5, 6), dma(16), dma(16), dma(1), dma(8), dma(8)],
        ring_partners("x") + ring_partners("y") + ([("c", 1)] if to_core else []) + [(ahead, k) for k in others],
        steps,
    )


def product_scatter_flow(lefts, right):
    own, wide = lefts[0].shape[0] // 8, right.shape[0]
    spans = [0]
    for left in lefts:
        spans.append(spans[-1] + left.shape[1])

    def steps(ins, outs, scratch):
        (*left_refs, right_ref), (out,) = ins, outs
        theirs, came, chunks, bufs, send, recv, pass_send, pass_recv = scratch
        core, member = peers_of("c")
        me, _ = peers_of("zc")
        ring = RingScatter("zc", lambda g: chunks.at[g], bufs, send, recv)

        def product(c, k, column):
            row = pl.multiple_of((c * 4 + lax.rem(me + k, 4)) * own, own)
            return sum(
                dot_nt(left_ref[pl.ds(row, own), :], right_ref[column : column + 512, spans[i] : spans[i + 1]])
                for i, left_ref in enumerate(left_refs)
            )

        passes = [
            remote(theirs.at[k], came.at[k], pass_send.at[k], pass_recv.at[k], member(1 - core)) for k in range(4)
        ]
        for k in (2, 1, 3, 0):
            for column in range(0, wide, 512):
                theirs[k, :, column : column + 512] = product(1 - core, k, column).astype(BF)
            passes[k].start()
            yield
        for k in (2, 1, 3, 0):
            passes[k].wait_recv()
            g = lax.rem(me + k, 4)
            for column in range(0, wide, 512):
                span = slice(column, column + 512)
                value = product(core, k, column) + came[k, :, span].astype(F32)
                if k == 0:
                    out[:, span] = value
                else:
                    chunks[g, :, span] = value.astype(BF)
            if k == 2:
                ring.start_far()
            elif k == 1:
                ring.start_up()
            elif k == 3:
                ring.start_down()
            yield
        ring.add()
        yield
        for h in range(2):
            rows = slice(h * own // 2, (h + 1) * own // 2)
            out[rows, :] += ring.total(h)
        yield
        ring.sent()
        for copy in passes:
            copy.wait_send()

    return Flow(
        [(x, pltpu.VMEM) for x in (*lefts, right)],
        [((own, wide), F32, pltpu.VMEM)],
        [
            pltpu.VMEM((4, own, wide), BF),
            pltpu.VMEM((4, own, wide), BF),
            pltpu.VMEM((4, own, wide), BF),
            pltpu.VMEM((8, own // 2, wide), BF),
            dma(6),
            dma(6),
            dma(4),
            dma(4),
        ],
        ring_partners("zc") + [("c", 1)],
        steps,
    )


def plane_scatter_flow(array, first, second, from_core):
    rows, columns = array.shape[-2:]

    def steps(ins, outs, scratch):
        (src,), (out,) = ins, outs
        came, sums, middle, bufs, late_bufs, send, recv, late_send, late_recv, pass_send, pass_recv = scratch
        core, member = peers_of("c")
        me, _ = peers_of(first)

        def along(ref, g):
            return ref.at[g] if first == "y" else ref.at[:, g]

        mine = src.at[core] if from_core else src
        ready = sums if from_core else src
        ring = RingScatter(first, lambda g: along(ready, g), bufs, send, recv)
        order = [lax.rem(me + k, 4) for k in (2, 1, 3, 0)]
        starts = [ring.start_far, ring.start_up, ring.start_down, lambda: None]
        passes = []
        if from_core:
            for i, g in enumerate(order):
                passes.append(
                    remote(along(src.at[1 - core], g), along(came, g), pass_send.at[i], pass_recv.at[i], member(1 - core))
                )
                passes[i].start()
            yield
        for i, g in enumerate(order):
            if from_core:
                passes[i].wait_recv()
                for k in range(4):
                    total = along(mine, g)[k].astype(F32) + along(came, g)[k].astype(F32)
                    along(sums, g)[k] = total.astype(BF)
            starts[i]()
            yield
        ring.add()
        yield
        own = along(ready, me)
        for h in range(2):
            came_half = ring.total(h)
            for k in range(2):
                middle[h * 2 + k] = (own[h * 2 + k].astype(F32) + came_half[k]).astype(BF)
        yield
        last = RingScatter(second, lambda g: middle.at[g], late_bufs, late_send, late_recv)
        last.start_far()
        last.start_up()
        last.start_down()
        yield
        last.add()
        yield
        for h in range(2):
            half = slice(h * rows // 2, (h + 1) * rows // 2)
            out[half, :] = piece(middle.at[last.me], h)[...].astype(F32) + last.total(h)
        yield
        ring.sent()
        last.sent()
        for copy in passes:
            copy.wait_send()

    block = (4, 4, rows, columns) if from_core else (8, 128)
    return Flow(
        [(array, pltpu.VMEM)],
        [((rows, columns), F32, pltpu.VMEM)],
        [
            pltpu.VMEM(block, BF),
            pltpu.VMEM(block, BF),
            pltpu.VMEM((4, rows, columns), BF),
            pltpu.VMEM((8, 2, rows, columns), BF),
            pltpu.VMEM((8, rows // 2, columns), BF),
            dma(6),
            dma(6),
            dma(6),
            dma(6),
            dma(4),
            dma(4),
        ],
        ring_partners("x") + ring_partners("y") + ([("c", 1)] if from_core else []),
        steps,
    )


def exchange_flow(array, kind):
    n = SIZES[kind]

    def steps(ins, outs, scratch):
        (src,), (out,) = ins, outs
        stage, send, recv, local = scratch
        me, member = peers_of(kind)
        own = pltpu.make_async_copy(src.at[me], stage, local.at[0])
        own.start()
        copies = []
        for k in range(1, n):
            to = lax.rem(me + k, n)
            copies.append(remote(src.at[to], out.at[me], send.at[k], recv.at[k], member(to)))
            copies[-1].start()
        yield
        own.wait()
        back = pltpu.make_async_copy(stage, out.at[me], local.at[0])
        back.start()
        yield
        for copy in copies:
            copy.wait()
        back.wait()

    return Flow(
        [(array, pl.ANY)],
        [(array.shape, array.dtype, pl.ANY)],
        [pltpu.VMEM(array.shape[1:], array.dtype), dma(n), dma(n), dma(1)],
        [(kind, k) for k in range(1, n)],
        steps,
    )


def sum_flow(array):
    def steps(ins, outs, scratch):
        (src,), (out,) = ins, outs
        wide, far, middle, sends, recvs, far_sends, far_recvs = scratch
        me, member = peers_of("yx")
        copies = []
        for k in range(1, 16):
            copies.append(remote(src, wide.at[me], sends.at[k], recvs.at[k], member(lax.rem(me + k, 16))))
            copies[-1].start()
        yield
        wide[me] = src[...]
        for copy in copies:
            copy.wait()
        middle[...] = jnp.sum(wide[...], axis=0)
        ring, ring_member = peers_of("z")
        late = []
        for k in range(1, 8):
            late.append(remote(middle, far.at[ring], far_sends.at[k], far_recvs.at[k], ring_member(lax.rem(ring + k, 8))))
            late[-1].start()
        yield
        far[ring] = middle[...]
        for copy in late:
            copy.wait()
        out[...] = jnp.sum(far[...], axis=0)

    return Flow(
        [(array, pltpu.VMEM)],
        [(array.shape, F32, pltpu.VMEM)],
        [
            pltpu.VMEM((16,) + array.shape, F32),
            pltpu.VMEM((8,) + array.shape, F32),
            pltpu.VMEM(array.shape, F32),
            dma(16),
            dma(16),
            dma(8),
            dma(8),
        ],
        [("yx", k) for k in range(1, 16)] + [("z", k) for k in range(1, 8)],
        steps,
    )


def add_up(stacked):
    return jnp.sum(stacked.astype(F32), axis=0)


def dot_nn(a, b):
    return lax.dot_general(a, b, (((1,), (0,)), ((), ())), preferred_element_type=F32)


def dot_nt(a, b):
    return lax.dot_general(a, b, (((1,), (1,)), ((), ())), preferred_element_type=F32)


def dot_tn(a, b):
    return lax.dot_general(a, b, (((0,), (0,)), ((), ())), preferred_element_type=F32)


def norm_rope(raw, gain, cosine, sine):
    unit = raw * lax.rsqrt(jnp.mean(raw * raw, axis=-1, keepdims=True) + EPS)
    scaled = unit * gain
    return scaled * cosine + pltpu.roll(scaled, 64, 1) * sine


def norm_rope_back(grad, raw, gain, cosine, sine):
    inverse = lax.rsqrt(jnp.mean(raw * raw, axis=-1, keepdims=True) + EPS)
    unit = raw * inverse
    turned = grad * cosine + pltpu.roll(grad * sine, 64, 1)
    scaled = turned * gain
    return inverse * (scaled - unit * jnp.mean(scaled * unit, axis=-1, keepdims=True)), turned * unit


def project_kernel(rows_ref, w_ref, gain_ref, cos_ref, sin_ref, q_ref, raw_ref, k_ref, v_ref):
    wide, size = q_ref.shape[1], k_ref.shape[1]
    product = dot_nn(rows_ref[...], w_ref[...])
    q_ref[...] = product[:, :wide]
    raw = product[:, wide : wide + size]
    raw_ref[...] = raw
    k_ref[...] = norm_rope(raw, gain_ref[...], cos_ref[...], sin_ref[...]).astype(BF)
    v_ref[...] = product[:, wide + size :].astype(BF)


def key_back_kernel(dk_ref, dv_ref, raw_ref, gain_ref, cos_ref, sin_ref, out_ref, sum_ref):
    half, size = dk_ref.shape
    core, _ = peers_of("c")
    rows = pl.ds(pl.multiple_of(core * half, half), half)
    grad = dk_ref[...].astype(BF).astype(F32)
    grad_raw, grad_gain = norm_rope_back(grad, raw_ref[rows, :], gain_ref[...], cos_ref[rows, :], sin_ref[rows, :])
    out_ref[...] = jnp.zeros_like(out_ref)
    out_ref[rows, :size] = grad_raw.astype(BF)
    out_ref[rows, size:] = dv_ref[...].astype(BF)
    sum_ref[...] = jnp.sum(grad_gain, axis=0, keepdims=True)


def key_tiles(lo, full, last, tile):
    middle = jnp.minimum(full, last)
    pl.loop(lo, middle)(lambda t: tile(t, True))
    pl.loop(middle, last)(lambda t: tile(t, False))
    tile(last, True)


def allowed_pairs(t, last, start, shape):
    key_place = t * BLOCK + lax.broadcasted_iota(jnp.int32, shape, 0)
    query_place = last * BLOCK + lax.rem(lax.broadcasted_iota(jnp.int32, shape, 1), BLOCK)
    return (key_place >= start) & (key_place <= query_place)


def attend_forward_kernel(
    lo_ref, full_ref, last_ref, slot_ref, raw_ref, gain_ref, cos_ref, sin_ref, k_ref, v_ref, start_ref, q_ref, o_ref, log_ref, q_t, acc, total
):
    j = pl.program_id(0)
    size = k_ref.shape[2]
    heads = raw_ref.shape[1] // size
    scale = size**-0.5 * LOG2E
    last = last_ref[j]
    for n in range(heads):
        span = slice(n * size, (n + 1) * size)
        query = norm_rope(raw_ref[:, span], gain_ref[...], cos_ref[...], sin_ref[...])
        q_ref[:, span] = query.astype(BF)
        q_t[:, n * BLOCK : (n + 1) * BLOCK] = query.T.astype(BF)
    acc[...] = jnp.zeros_like(acc)
    total[...] = jnp.zeros_like(total)
    start = start_ref[0]

    def tile(t, masked):
        slot = slot_ref[t]
        weights = jnp.exp2(dot_nn(k_ref[slot], q_t[...]) * scale)
        if masked:
            weights = jnp.where(allowed_pairs(t, last, start, weights.shape), weights, 0.0)
        total[...] += jnp.sum(weights.reshape(BLOCK // 8, 8, heads * BLOCK), axis=0)
        acc[...] += dot_nn(v_ref[slot].T, weights.astype(BF))

    key_tiles(lo_ref[j], full_ref[j], last, tile)
    row = jnp.sum(total[...], axis=0, keepdims=True)
    log_ref[0] = jnp.log2(row)
    out = acc[...] / row
    for n in range(heads):
        o_ref[:, n * size : (n + 1) * size] = out[:, n * BLOCK : (n + 1) * BLOCK].T.astype(BF)


def attend_backward_kernel(
    lo_ref,
    full_ref,
    last_ref,
    slot_ref,
    raw_ref,
    gain_ref,
    cos_ref,
    sin_ref,
    k_ref,
    v_ref,
    start_ref,
    q_ref,
    o_ref,
    g_ref,
    log_ref,
    dq_ref,
    sum_ref,
    dk_ref,
    dv_ref,
    queries,
    q_t,
    grads,
    g_t,
    delta,
    acc,
    dk,
    dv,
):
    j = pl.program_id(0)
    slots, _, size = k_ref.shape
    heads = raw_ref.shape[1] // size
    scale = size**-0.5
    last = last_ref[j]

    @pl.when(j == 0)
    def _():
        sum_ref[...] = jnp.zeros_like(sum_ref)

        @pl.loop(0, slots)
        def _(s):
            dk[s] = jnp.zeros(dk.shape[1:], F32)
            dv[s] = jnp.zeros(dv.shape[1:], F32)

    for n in range(heads):
        span, rows = slice(n * size, (n + 1) * size), slice(n * BLOCK, (n + 1) * BLOCK)
        queries[rows, :] = q_ref[:, span]
        q_t[:, rows] = q_ref[:, span].T
        grads[rows, :] = g_ref[:, span]
        grad_t = g_ref[:, span].T
        g_t[:, rows] = grad_t
        delta[:, rows] = jnp.sum(grad_t.astype(F32) * o_ref[:, span].T.astype(F32), axis=0, keepdims=True)
    acc[...] = jnp.zeros_like(acc)
    start = start_ref[0]
    logs = log_ref[0]

    def tile(t, masked):
        slot = slot_ref[t]
        keys = k_ref[slot]
        probs = jnp.exp2(dot_nn(keys, q_t[...]) * (scale * LOG2E) - logs)
        if masked:
            probs = jnp.where(allowed_pairs(t, last, start, probs.shape), probs, 0.0)
        grad_scores = (probs * (dot_nn(v_ref[slot], g_t[...]) - delta[...])).astype(BF)
        dv[slot] += dot_nn(probs.astype(BF), grads[...])
        dk[slot] += dot_nn(grad_scores, queries[...])
        acc[...] += dot_nn(keys.T, grad_scores)

    key_tiles(lo_ref[j], full_ref[j], last, tile)
    for n in range(heads):
        span = slice(n * size, (n + 1) * size)
        grad = (acc[:, n * BLOCK : (n + 1) * BLOCK] * scale).T.astype(BF).astype(F32)
        grad_raw, grad_gain = norm_rope_back(grad, raw_ref[:, span], gain_ref[...], cos_ref[...], sin_ref[...])
        dq_ref[:, span] = grad_raw.astype(BF)
        sum_ref[...] += jnp.sum(grad_gain, axis=0, keepdims=True)

    @pl.when(j == pl.num_programs(0) - 1)
    def _():
        @pl.loop(0, slots)
        def _(s):
            dk_ref[s] = (dk[s] * scale).astype(BF)
            dv_ref[s] = dv[s].astype(BF)


def by_rows(array, rows=BLOCK):
    return pl.BlockSpec((rows,) + array.shape[1:], lambda j, *_: (j,) + (0,) * (array.ndim - 1))


def resident(array):
    return pl.BlockSpec(array.shape, lambda j, *_: (0,) * array.ndim, pipeline_mode=pl.Buffered(1))


def shaped(shape, dtype):
    return jax.ShapeDtypeStruct(shape, dtype)


def project(rows, weights, gain, cosine, sine, q_cols):
    size = gain.shape[1]
    outs = (shaped((rows.shape[0], q_cols), F32), shaped((rows.shape[0], size), F32)) + (shaped((rows.shape[0], size), BF),) * 2
    return pl.pallas_call(
        project_kernel,
        out_shape=outs,
        grid=(rows.shape[0] // BLOCK,),
        in_specs=[by_rows(rows), resident(weights), resident(gain), by_rows(cosine), by_rows(sine)],
        out_specs=tuple(by_rows(x) for x in outs),
        compiler_params=pltpu.CompilerParams(vmem_limit_bytes=32 << 20),
        cost_estimate=cost_of(6),
        name="project",
    )(rows, weights, gain, cosine, sine)


def key_back(grad_key, grad_value, raw, gain, cosine, sine):
    rows, size = raw.shape
    return pl.pallas_call(
        key_back_kernel,
        out_shape=(shaped((rows, 2 * size), BF), shaped((1, size), F32)),
        compiler_params=pltpu.CompilerParams(vmem_limit_bytes=32 << 20),
        cost_estimate=cost_of(2),
        name="key_back",
    )(grad_key, grad_value, raw, gain, cosine, sine)


def attend_forward(meta, raw, gain, cosine, sine, keys, values, start):
    rows, wide = raw.shape
    blocks, size = rows // BLOCK, keys.shape[2]
    lanes = wide // size * BLOCK
    outs = (shaped((rows, wide), BF), shaped((rows, wide), BF), shaped((blocks, 1, lanes), F32))
    return pl.pallas_call(
        attend_forward_kernel,
        out_shape=outs,
        grid_spec=pltpu.PrefetchScalarGridSpec(
            num_scalar_prefetch=4,
            grid=(blocks,),
            in_specs=[
                by_rows(raw),
                resident(gain),
                by_rows(cosine),
                by_rows(sine),
                resident(keys),
                resident(values),
                by_rows(start, 1),
            ],
            out_specs=(by_rows(outs[0]), by_rows(outs[1]), by_rows(outs[2], 1)),
            scratch_shapes=[pltpu.VMEM((size, lanes), BF), pltpu.VMEM((size, lanes), F32), pltpu.VMEM((8, lanes), F32)],
        ),
        compiler_params=pltpu.CompilerParams(vmem_limit_bytes=48 << 20),
        cost_estimate=cost_of(30),
        name="attend",
    )(*meta, raw, gain, cosine, sine, keys, values, start)


def attend_backward(meta, raw, gain, cosine, sine, keys, values, start, queries, attended, grads, logs):
    rows, wide = raw.shape
    blocks, size = rows // BLOCK, keys.shape[2]
    lanes = wide // size * BLOCK
    outs = (shaped((rows, wide), BF), shaped((1, size), F32), shaped(keys.shape, BF), shaped(values.shape, BF))
    return pl.pallas_call(
        attend_backward_kernel,
        out_shape=outs,
        grid_spec=pltpu.PrefetchScalarGridSpec(
            num_scalar_prefetch=4,
            grid=(blocks,),
            in_specs=[
                by_rows(raw),
                resident(gain),
                by_rows(cosine),
                by_rows(sine),
                resident(keys),
                resident(values),
                by_rows(start, 1),
                by_rows(queries),
                by_rows(attended),
                by_rows(grads),
                by_rows(logs, 1),
            ],
            out_specs=(by_rows(outs[0]),) + tuple(resident(x) for x in outs[1:]),
            scratch_shapes=[
                pltpu.VMEM((lanes, size), BF),
                pltpu.VMEM((size, lanes), BF),
                pltpu.VMEM((lanes, size), BF),
                pltpu.VMEM((size, lanes), BF),
                pltpu.VMEM((1, lanes), F32),
                pltpu.VMEM((size, lanes), F32),
                pltpu.VMEM(keys.shape, F32),
                pltpu.VMEM(values.shape, F32),
            ],
        ),
        compiler_params=pltpu.CompilerParams(vmem_limit_bytes=58 << 20),
        cost_estimate=cost_of(40),
        name="attend_back",
    )(*meta, raw, gain, cosine, sine, keys, values, start, queries, attended, grads, logs)


def rms_scale(values, gain_vec):
    return values * lax.rsqrt(jnp.mean(values * values, axis=-1, keepdims=True) + EPS) * gain_vec


def rope_table(offsets, size):
    half = size // 2
    spacing = ROPE_BASE ** (-2.0 * jnp.arange(half, dtype=F32) / size)
    angles = offsets.astype(F32)[:, None] * spacing[None, :]
    cosine, sine = jnp.cos(angles), jnp.sin(angles)
    return jnp.concatenate([cosine, cosine], axis=1), jnp.concatenate([-sine, sine], axis=1)


def swiglu(gate_part, up_part):
    return jax.nn.silu(gate_part) * up_part


def two_parts(wide):
    high = wide.astype(BF)
    return high, (wide - high.astype(F32)).astype(BF)


def all_to_all(stacked):
    return lax.all_to_all(stacked, ("head", "blk"), split_axis=0, concat_axis=0, tiled=True)


def body(
    tokens,
    norm_gain,
    w_query,
    key_weight,
    value_weight,
    query_gain,
    key_gain,
    w_out,
    mix_gain,
    w_router,
    expert_gate_up,
    expert_down,
    lengths,
    block_deal,
    routes,
    cotangent,
):
    own, width = tokens.shape
    size = query_gain.shape[0]
    scale = size ** (-0.5)
    blk = lax.axis_index("blk")
    plane, core = blk // 4, blk % 2
    devices = lax.axis_size("head") * lax.axis_size("blk")
    experts = w_router.shape[0] * 2
    cap = own * routes.shape[1] // experts
    gate_up, down = expert_gate_up[0], expert_down[0]
    ff = down.shape[0]
    group_rows = 8 * own
    q_cols = w_query.shape[1] // 4
    heads = q_cols // size

    chosen = jnp.sum((routes[:, :, None] == jnp.arange(experts, dtype=jnp.int32)).astype(jnp.int32), axis=1)
    order = jnp.arange(own)
    earlier = dot_nn((order[:, None] > order[None, :]).astype(BF), chosen.astype(BF)).astype(jnp.int32)
    assign = (chosen[:, :, None] > 0) & (earlier[:, :, None] == jnp.arange(cap, dtype=jnp.int32))
    assign_wide = assign.astype(F32)
    assign_low = assign.astype(BF).reshape(own, experts * cap)
    grad_rows = dot_tn(assign_low, cotangent).astype(BF)

    wide = tokens.astype(F32)
    normed, norm_back = jax.vjp(rms_scale, wide, norm_gain)
    normed_low = normed.astype(BF)
    depth = w_query.shape[0]
    kv = jnp.concatenate([key_weight.reshape(depth, 2, 1, size), value_weight.reshape(depth, 2, 1, size)], axis=2)
    kv = jnp.repeat(kv.reshape(depth, 2, 2 * size), 2, axis=1)
    qkv_pack = jnp.concatenate([w_query.reshape(depth, 4, q_cols), kv], axis=2).transpose(1, 0, 2)
    out_pack = w_out.reshape(4, q_cols, depth).transpose(0, 2, 1)
    w_qkv, w_out_t, w_router_t, group_tokens = launch(
        [
            plane_gather_flow(qkv_pack, "x", "y", ahead="zhc"),
            plane_gather_flow(out_pack, "y", "x", ahead="zhc"),
            plane_gather_flow(w_router.T, "y", "x", ahead="z"),
            ring_gather_flow(normed_low),
        ],
        0,
        45,
    )
    normed_group = group_tokens.reshape(group_rows, width)
    w_qkv, w_out_t = w_qkv.reshape(width, -1), w_out_t.reshape(width, -1)
    w_router_t = w_router_t.reshape(16, 2, 2, 2, depth, -1).transpose(0, 2, 1, 4, 3, 5).reshape(width, experts)

    group_blocks = plane * 4 + jnp.array([0, 2, 1, 3], jnp.int32)
    ids = jnp.arange(block_deal.shape[0], dtype=jnp.int32)
    last = jnp.sum(jnp.where(group_blocks[:, None] == ids[None, :], block_deal[None, :], 0), axis=1)
    slots = (ids % 2) * (ids.shape[0] // 2) + (ids // 4) * 2 + (ids % 4) // 2
    slot_of = jnp.sum(jnp.where(block_deal[None, :] == ids[:, None], slots[None, :], 0), axis=1)
    place = (last[:, None] * BLOCK + jnp.arange(BLOCK, dtype=jnp.int32)[None, :]).reshape(-1)
    passed = place[:, None] >= jnp.cumsum(lengths)[None, :]
    start = jnp.sum(jnp.where(passed, lengths[None, :], 0), axis=1)
    start_rows = start.reshape(-1, 1, BLOCK)
    meta = (start_rows[:, 0, 0] // BLOCK, (start_rows[:, 0, BLOCK - 1] + BLOCK - 1) // BLOCK, last, slot_of)
    start_rows = jnp.tile(start_rows, (1, 1, heads))
    cosine, sine = rope_table(place - start, size)

    q_gain, k_gain = query_gain[None], key_gain[None]
    q_raw, k_raw, keys, values = project(normed_group, w_qkv, k_gain, cosine, sine, q_cols)
    keys, values = launch(
        [plane_gather_flow(keys, "x", "y", to_core=True, half=True), plane_gather_flow(values, "y", "x", to_core=True, half=True)], 1, 30
    )
    keys, values, grad_rows = lax.optimization_barrier((keys, values, grad_rows))
    grad_rows = all_to_all(grad_rows.reshape(devices, cap, width)).reshape(-1, width)
    keys, values = keys.reshape(-1, BLOCK, size), values.reshape(-1, BLOCK, size)
    queries, attended, logs = attend_forward(meta, q_raw, q_gain, cosine, sine, keys, values, start_rows)

    residual = wide + launch([product_scatter_flow([attended], w_out_t)], 2, 25)[0]
    mixed, mix_back = jax.vjp(rms_scale, residual, mix_gain)
    mixed_low, grad_rows = lax.optimization_barrier((mixed.astype(BF), grad_rows))
    logits = dot_nn(mixed_low, w_router_t)
    gates = jax.nn.softmax(jnp.where(chosen > 0, logits, -1e30), axis=-1)
    gate_slots = gates[:, :, None] * assign_wide
    outgoing = dot_tn(assign_low, jnp.concatenate([mixed_low, gates.astype(BF)], axis=1)).astype(BF)
    arrived = all_to_all(outgoing.reshape(devices, cap, -1)).reshape(experts * cap, -1)

    rows = arrived[:, :width]
    here = jnp.arange(experts, dtype=jnp.int32) == lax.axis_index("head") * lax.axis_size("blk") + blk
    gate = jnp.sum(jnp.where(here[None, :], arrived[:, width:].astype(F32), 0.0), axis=1, keepdims=True)
    gate_up_out = dot_nn(rows, gate_up)
    hidden, swiglu_back = jax.vjp(swiglu, gate_up_out[:, :ff], gate_up_out[:, ff:])
    hidden_low = hidden.astype(BF)
    plain_grad = dot_nt(grad_rows, down)
    gate_grad = jnp.sum(hidden_low.astype(F32) * plain_grad, axis=1, keepdims=True)
    grad_both = jnp.concatenate(swiglu_back(plain_grad * gate), axis=1).astype(BF)
    high, low = two_parts(gate_grad)
    pad = jnp.zeros((experts * cap, 126), BF)
    back = jnp.concatenate([dot_nt(grad_both, gate_up).astype(BF), high, low, pad], axis=1)
    back = all_to_all(back.reshape(devices, cap, -1)).reshape(experts * cap, -1)
    back, expert_out = lax.optimization_barrier((back, dot_nn(hidden_low, down).astype(BF)))
    grad_down = dot_tn((hidden * gate).astype(BF), grad_rows)
    grad_gate_up = dot_tn(rows, grad_both)

    gate_grads = jnp.sum(back[:, width : width + 2].astype(F32), axis=1).reshape(experts, cap)
    gate_grads = jnp.sum(assign_wide * gate_grads[None], axis=2)
    grad_logits = (gates * (gate_grads - jnp.sum(gates * gate_grads, axis=1, keepdims=True))).astype(BF)
    grad_mixed = dot_nn(assign_low, back[:, :width]) + dot_nt(grad_logits, w_router_t)
    grad_router_t = dot_tn(mixed_low, grad_logits)
    grad_from_mix, grad_mix_gain = mix_back(grad_mixed)
    grad_residual = cotangent.astype(F32) + grad_from_mix
    grad_group = launch([ring_gather_flow(grad_residual.astype(BF))], 3, 20)[0].reshape(group_rows, width)
    grad_group, expert_out = lax.optimization_barrier((grad_group, expert_out))
    expert_out = all_to_all(expert_out.reshape(devices, cap, width)).reshape(-1, width)
    grad_attended = dot_nn(grad_group, w_out_t).astype(BF)
    grad_out_t = dot_tn(grad_group, attended)
    grad_q, grad_query_gain, grad_keys, grad_values = attend_backward(
        meta, q_raw, q_gain, cosine, sine, keys, values, start_rows, queries, attended, grad_attended, logs
    )

    split = (2, 4, 4, group_rows // 2, size)
    grad_key, grad_value = launch(
        [plane_scatter_flow(grad_keys.reshape(split), "y", "x", True), plane_scatter_flow(grad_values.reshape(split), "x", "y", True)], 4, 35
    )
    grad_kv, grad_key_gain = key_back(grad_key, grad_value, k_raw, k_gain, cosine, sine)

    grad_q, grad_kv, expert_out = lax.optimization_barrier((grad_q, grad_kv, expert_out))
    high, low = two_parts(gate_slots.reshape(own, -1))
    output = (residual + dot_nn(high, expert_out) + dot_nn(low, expert_out)).astype(BF)
    plane_split = (4, 4, 4 * depth, -1)
    grad_normed, grad_wq, grad_wkv, grad_wo, grad_wr = launch(
        [
            product_scatter_flow([grad_q, grad_kv], w_qkv),
            plane_scatter_flow(dot_tn(normed_group, grad_q).astype(BF).reshape(plane_split), "y", "x", False),
            plane_scatter_flow(dot_tn(normed_group, grad_kv).astype(BF).reshape(plane_split), "y", "x", False),
            plane_scatter_flow(grad_out_t.astype(BF).reshape(plane_split), "x", "y", False),
            plane_scatter_flow(grad_router_t.astype(BF).reshape(plane_split), "x", "y", False),
        ],
        5,
        40,
        60,
    )
    grad_from_norm, grad_norm_gain = norm_back(grad_normed)
    grad_tokens = grad_residual + grad_from_norm

    gains = jnp.concatenate([grad_norm_gain, grad_mix_gain, grad_query_gain[0], grad_key_gain[0], jnp.zeros((768,), F32)]).reshape(-1, size)
    router_part = grad_wr.astype(BF).reshape(2, 2, depth, 2, experts // 2).transpose(1, 0, 3, 2, 4).reshape(8, depth, -1)
    grad_wq, grad_wkv, grad_wo, router_part, gains = launch(
        [
            exchange_flow(grad_wq.astype(BF).reshape(4, depth, -1), "zhc"),
            exchange_flow(grad_wkv.astype(BF).reshape(4, depth, -1), "zhc"),
            exchange_flow(grad_wo.astype(BF).reshape(4, depth, -1), "zhc"),
            exchange_flow(router_part, "z"),
            sum_flow(gains),
        ],
        6,
        15,
    )
    gains = gains.reshape(-1)
    grad_w_query = grad_wq.astype(F32).transpose(1, 0, 2).reshape(depth, -1)
    grad_kv_w = jnp.sum(grad_wkv.astype(F32).reshape(2, 2, depth, 2, size), axis=1)
    grad_w_key = grad_kv_w[:, :, 0].transpose(1, 0, 2).reshape(depth, -1)
    grad_w_value = grad_kv_w[:, :, 1].transpose(1, 0, 2).reshape(depth, -1)
    grad_w_out = grad_wo.astype(F32).transpose(0, 2, 1).reshape(-1, depth)
    grad_w_router = add_up(router_part).T
    return (
        output,
        grad_tokens,
        gains[:width],
        grad_w_query,
        grad_w_key,
        grad_w_value,
        gains[2 * width : 2 * width + size],
        gains[2 * width + size : 2 * width + 2 * size],
        grad_w_out,
        gains[width : 2 * width],
        grad_w_router,
        grad_gate_up[None],
        grad_down[None],
    )


def solution(mesh):
    rows, both = P(("head", "blk"), None), P("blk", "head")
    expert, turned = P(("head", "blk"), None, None), P("head", "blk")
    in_specs = (rows, P(), both, both, both, P(), P(), turned, P(), turned, expert, expert, P(), P(), rows, rows)
    out_specs = (rows, rows, P(), both, both, both, P(), P(), turned, P(), turned, expert, expert)
    return jax.shard_map(body, mesh=mesh, in_specs=in_specs, out_specs=out_specs, check_vma=False)
```

```python
import jax
import jax.numpy as jnp
from jax import lax
from jax.experimental import pallas as pl
from jax.experimental.pallas import tpu as pltpu
from jax.sharding import PartitionSpec as P

MESH = pl.DeviceIdType.MESH
EPS = 1e-06
ROPE_BASE = 1000000.0
LOG2E = 1.4426950408889634
BF = jnp.bfloat16
F32 = jnp.float32
BLOCK = 256
VMEM_LIMIT = 60 << 20
SIZES = {"zc": 4, "c": 2, "x": 4, "y": 4, "zhc": 4, "z": 8, "yx": 16}


def peers_of(kind):
    h = lax.axis_index("head")
    b = lax.axis_index("blk")
    q, r = lax.div(b, 4), lax.rem(b, 4)
    if kind == "zc":
        return lax.div(r, 2) * 2 + h, lambda g: (lax.rem(g, 2), q * 4 + lax.div(g, 2) * 2 + lax.rem(r, 2))
    if kind == "z":
        return r * 2 + h, lambda g: (lax.rem(g, 2), q * 4 + lax.div(g, 2))
    if kind == "c":
        return lax.rem(b, 2), lambda g: (h, b - lax.rem(b, 2) + g)
    if kind == "x":
        return lax.rem(q, 4), lambda g: (h, (lax.div(q, 4) * 4 + g) * 4 + r)
    if kind == "y":
        return lax.div(q, 4), lambda g: (h, (g * 4 + lax.rem(q, 4)) * 4 + r)
    if kind == "yx":
        return q, lambda g: (h, g * 4 + r)
    return r, lambda g: (h, q * 4 + g)


def cost_of(microseconds):
    return pl.CostEstimate(flops=microseconds * 10**9, bytes_accessed=microseconds * 3 * 10**6, transcendentals=0)


class Flow:
    def __init__(self, inputs, outputs, scratch, partners, steps):
        self.inputs, self.outputs, self.scratch = inputs, outputs, scratch
        self.partners, self.steps = partners, steps


def launch(flows, cid, cost):
    partners = sorted({p for flow in flows for p in flow.partners})

    def kernel(*refs):
        n_in, n_out = sum(len(f.inputs) for f in flows), sum(len(f.outputs) for f in flows)
        ins, outs, rest = list(refs[:n_in]), list(refs[n_in : n_in + n_out]), list(refs[n_in + n_out :])
        barrier = pltpu.get_barrier_semaphore()
        for kind, distance in partners:
            me, member = peers_of(kind)
            to = member(lax.rem(me + distance, SIZES[kind]))
            pl.semaphore_signal(barrier, inc=1, device_id=to, device_id_type=MESH)
        pl.semaphore_wait(barrier, len(partners))
        running = []
        for flow in flows:
            own = [[group.pop(0) for _ in part] for group, part in ((ins, flow.inputs), (outs, flow.outputs), (rest, flow.scratch))]
            running.append(flow.steps(*own))
        while running:
            running = [steps for steps in running if next(steps, running) is not running]

    return pl.pallas_call(
        kernel,
        out_shape=tuple(jax.ShapeDtypeStruct(s, d) for f in flows for s, d, _ in f.outputs),
        in_specs=[pl.BlockSpec(memory_space=space) for f in flows for _, space in f.inputs],
        out_specs=tuple(pl.BlockSpec(memory_space=space) for f in flows for _, _, space in f.outputs),
        scratch_shapes=[x for f in flows for x in f.scratch],
        compiler_params=pltpu.CompilerParams(collective_id=cid, has_side_effects=True, vmem_limit_bytes=VMEM_LIMIT),
        cost_estimate=cost_of(cost),
        name=f"links_{cid}",
    )(*[x for f in flows for x, _ in f.inputs])


def remote(src, dst, send, recv, device):
    return pltpu.make_async_remote_copy(
        src_ref=src, dst_ref=dst, send_sem=send, recv_sem=recv, device_id=device, device_id_type=MESH
    )


def piece(ref, which):
    rows = ref.shape[0] // 2
    return ref.at[pl.ds(which * rows, rows)]


def ring_partners(kind):
    return [(kind, 1), (kind, 3)]


class RingGather:
    def __init__(self, kind, slot, src, send, recv):
        me, member = peers_of(kind)
        up, down = lax.rem(me + 1, 4), lax.rem(me + 3, 4)

        def copy(source, target, i, to):
            return remote(source, target, send.at[i], recv.at[i], member(to))

        mine = slot(me)
        self.copies = [
            copy(piece(src, 0), piece(mine, 0), 0, up),
            copy(piece(src, 1), piece(mine, 1), 1, up),
            copy(piece(src, 1), piece(mine, 1), 2, down),
            copy(piece(src, 0), piece(mine, 0), 3, down),
            copy(piece(slot(down), 0), piece(slot(down), 0), 4, up),
            copy(piece(slot(up), 1), piece(slot(up), 1), 5, down),
        ]

    def start(self):
        for i in (0, 2, 1, 3):
            self.copies[i].start()

    def forward(self):
        self.copies[0].wait_recv()
        self.copies[4].start()
        self.copies[2].wait_recv()
        self.copies[5].start()

    def near(self):
        self.copies[1].wait_recv()
        self.copies[3].wait_recv()

    def far(self):
        self.copies[4].wait_recv()
        self.copies[5].wait_recv()

    def sent(self):
        for copy in self.copies:
            copy.wait_send()


class RingScatter:
    def __init__(self, kind, chunk, bufs, send, recv):
        self.me, member = peers_of(kind)
        self.up, self.down, self.far = (lax.rem(self.me + k, 4) for k in (1, 3, 2))
        self.chunk, self.bufs = chunk, bufs

        def copy(source, target, i, to):
            return remote(source, bufs.at[target], send.at[i], recv.at[i], member(to))

        self.copies = [
            copy(piece(chunk(self.far), 0), 0, 0, self.up),
            copy(piece(chunk(self.far), 1), 1, 1, self.down),
            copy(piece(chunk(self.up), 1), 2, 2, self.up),
            copy(piece(chunk(self.down), 0), 3, 3, self.down),
            copy(bufs.at[6], 4, 4, self.up),
            copy(bufs.at[7], 5, 5, self.down),
        ]

    def start_far(self):
        self.copies[0].start()
        self.copies[1].start()

    def start_up(self):
        self.copies[2].start()

    def start_down(self):
        self.copies[3].start()

    def add(self):
        self.copies[0].wait_recv()
        self.bufs[6] = (piece(self.chunk(self.up), 0)[...].astype(F32) + self.bufs[0].astype(F32)).astype(BF)
        self.copies[4].start()
        self.copies[1].wait_recv()
        self.bufs[7] = (piece(self.chunk(self.down), 1)[...].astype(F32) + self.bufs[1].astype(F32)).astype(BF)
        self.copies[5].start()

    def total(self, which):
        first, second = ((4, 3), (2, 5))[which]
        self.copies[first].wait_recv()
        self.copies[second].wait_recv()
        return self.bufs[first].astype(F32) + self.bufs[second].astype(F32)

    def sent(self):
        for copy in self.copies:
            copy.wait_send()


def dma(*shape):
    return pltpu.SemaphoreType.DMA(shape)


def ring_gather_flow(array):
    shape = (2, 4) + array.shape

    def steps(ins, outs, scratch):
        (src,), (out,) = ins, outs
        stage, send, recv, pass_send, pass_recv, local = scratch
        me, _ = peers_of("zc")
        core, member = peers_of("c")
        own = pltpu.make_async_copy(src, stage, local.at[0])
        own.start()
        ring = RingGather("zc", lambda g: out.at[core, g], src, send, recv)

        def passing(k):
            g = lax.rem(me + k, 4)
            return remote(src if k == 0 else out.at[core, g], out.at[core, g], pass_send.at[k], pass_recv.at[k], member(1 - core))

        passes = [passing(k) for k in range(4)]
        ring.start()
        passes[0].start()
        yield
        ring.forward()
        own.wait()
        back = pltpu.make_async_copy(stage, out.at[core, me], local.at[0])
        back.start()
        yield
        ring.near()
        passes[1].start()
        passes[3].start()
        yield
        ring.far()
        passes[2].start()
        yield
        back.wait()
        ring.sent()
        for copy in passes:
            copy.wait()

    return Flow(
        [(array, pl.ANY)],
        [(shape, array.dtype, pl.ANY)],
        [pltpu.VMEM(array.shape, array.dtype), dma(6), dma(6), dma(4), dma(4), dma(1)],
        ring_partners("zc") + [("c", 1)],
        steps,
    )


def plane_gather_flow(arrays, first, second, to_core=False, ahead=None):
    dtype = arrays[0][0].dtype
    if ahead == "zhc":
        shard = (4, arrays[0][0].shape[0], sum(columns for _, columns, _ in arrays))
    elif ahead == "z":
        shard = (8,) + arrays[0][0].shape
    else:
        shard = (arrays[0][0].shape[0] // 2,) + arrays[0][0].shape[1:]
    shape = ((2,) if to_core else ()) + (4, 4) + shard
    n_ahead = SIZES[ahead] if ahead else 1

    def steps(ins, outs, scratch):
        (out,) = outs
        stage, send, recv, pass_send, pass_recv, local, ahead_send, ahead_recv = scratch
        core, member = peers_of("c")
        here, _ = peers_of(first)
        there, _ = peers_of(second)
        view = out.at[core] if to_core else out

        def slot(a, b):
            return view.at[b, a] if first == "x" else view.at[a, b]

        if ahead:
            mine, at = peers_of(ahead)

            def parts(to):
                if ahead == "z":
                    return [(ins[0], stage.at[mine])]
                found, begin = [], 0
                for ref, (_, columns, share) in zip(ins, arrays):
                    source = ref.at[:, pl.ds(pl.multiple_of(lax.div(to, share) * columns, columns), columns)]
                    found.append((source, stage.at[mine, :, pl.ds(begin, columns)]))
                    begin += columns
                return found

            early = [pltpu.make_async_copy(source, target, local.at[i]) for i, (source, target) in enumerate(parts(mine))]
            for k in range(1, n_ahead):
                to = lax.rem(mine + k, n_ahead)
                for i, (source, target) in enumerate(parts(to)):
                    early.append(remote(source, target, ahead_send.at[i, k], ahead_recv.at[i, k], at(to)))
            for copy in early:
                copy.start()
            yield
            for copy in early:
                copy.wait()
            src = stage
        else:
            src = ins[0].at[pl.ds(pl.multiple_of(core * shard[0], shard[0]), shard[0])]
            own = pltpu.make_async_copy(src, stage, local.at[0])
            own.start()
        ring = RingGather(first, lambda g: slot(g, there), src, send.at[4], recv.at[4])
        columns = [lax.rem(here + k, 4) for k in range(4)]
        rings = [
            RingGather(second, lambda g, a=a: slot(a, g), src if k == 0 else slot(a, there), send.at[k], recv.at[k])
            for k, a in enumerate(columns)
        ]

        def passing(k, m):
            ref = slot(columns[k], lax.rem(there + m, 4))
            return remote(src if k == m == 0 else ref, ref, pass_send.at[k * 4 + m], pass_recv.at[k * 4 + m], member(1 - core))

        passes = {}

        def hand_over(k, m):
            if to_core:
                passes[k, m] = passing(k, m)
                passes[k, m].start()

        ring.start()
        rings[0].start()
        hand_over(0, 0)
        yield
        ring.forward()
        if not ahead:
            own.wait()
        back = pltpu.make_async_copy(stage, slot(here, there), local.at[0])
        back.start()
        yield
        rings[0].forward()
        yield
        ring.near()
        for k in (1, 3):
            rings[k].start()
            hand_over(k, 0)
        yield
        ring.far()
        rings[2].start()
        hand_over(2, 0)
        yield
        for k in (0, 1, 3, 2):
            if k > 0:
                rings[k].forward()
            rings[k].near()
            hand_over(k, 1)
            hand_over(k, 3)
            yield
            rings[k].far()
            hand_over(k, 2)
            yield
        back.wait()
        ring.sent()
        for one in rings:
            one.sent()
        for copy in passes.values():
            copy.wait()

    return Flow(
        [(array, pl.ANY) for array, *_ in arrays],
        [(shape, dtype, pl.ANY)],
        [pltpu.VMEM(shard, dtype), dma(5, 6), dma(5, 6), dma(16), dma(16), dma(3), dma(3, 8), dma(3, 8)],
        ring_partners("x") + ring_partners("y") + ([("c", 1)] if to_core else []) + [(ahead, k) for k in range(1, n_ahead)],
        steps,
    )


def product_flow(left, right):
    columns, width = left.shape[1], right.shape[1]

    def steps(ins, outs, scratch):
        (out,) = outs
        left_ref, right_ref, local = scratch
        copies = [pltpu.make_async_copy(source, target, local.at[i]) for i, (source, target) in enumerate(zip(ins, (left_ref, right_ref)))]
        for copy in copies:
            copy.start()
        yield
        for copy in copies:
            copy.wait()
        for column in range(0, columns, 256):
            span = slice(column, column + 256)
            out[span, :] = dot_tn(left_ref[:, span], right_ref[...]).astype(BF)
            yield

    return Flow(
        [(left, pl.ANY), (right, pl.ANY)],
        [((columns, width), BF, pltpu.VMEM)],
        [pltpu.VMEM(left.shape, BF), pltpu.VMEM(right.shape, BF), dma(2)],
        [],
        steps,
    )


def output_flow(residual, high, low, expert_out):
    width = residual.shape[1]

    def steps(ins, outs, scratch):
        residual_ref, high_ref, low_ref, expert_hbm = ins
        (out,) = outs
        expert_ref, local = scratch
        copy = pltpu.make_async_copy(expert_hbm, expert_ref, local.at[0])
        copy.start()
        yield
        copy.wait()
        for column in range(0, width, 512):
            span = slice(column, column + 512)
            experts = expert_ref[:, span]
            out[:, span] = (residual_ref[:, span] + dot_nn(high_ref[...], experts) + dot_nn(low_ref[...], experts)).astype(BF)
            yield

    return Flow(
        [(residual, pltpu.VMEM), (high, pltpu.VMEM), (low, pltpu.VMEM), (expert_out, pl.ANY)],
        [(residual.shape, BF, pltpu.VMEM)],
        [pltpu.VMEM(expert_out.shape, BF), dma(1)],
        [],
        steps,
    )


def product_scatter_flow(lefts, right):
    own, wide = lefts[0].shape[0] // 8, right.shape[0]
    spans = [0]
    for left in lefts:
        spans.append(spans[-1] + left.shape[1])

    def steps(ins, outs, scratch):
        (*left_refs, right_ref), (out,) = ins, outs
        theirs, came, chunks, bufs, send, recv, pass_send, pass_recv = scratch
        core, member = peers_of("c")
        me, _ = peers_of("zc")
        ring = RingScatter("zc", lambda g: chunks.at[g], bufs, send, recv)

        def product(c, k, column):
            row = pl.multiple_of((c * 4 + lax.rem(me + k, 4)) * own, own)
            return sum(
                dot_nt(left_ref[pl.ds(row, own), :], right_ref[column : column + 512, spans[i] : spans[i + 1]])
                for i, left_ref in enumerate(left_refs)
            )

        passes = [
            remote(theirs.at[k], came.at[k], pass_send.at[k], pass_recv.at[k], member(1 - core)) for k in range(4)
        ]
        for k in (2, 1, 3, 0):
            for column in range(0, wide, 512):
                theirs[k, :, column : column + 512] = product(1 - core, k, column).astype(BF)
            passes[k].start()
            yield
        for k in (2, 1, 3, 0):
            passes[k].wait_recv()
            g = lax.rem(me + k, 4)
            for column in range(0, wide, 512):
                span = slice(column, column + 512)
                value = product(core, k, column) + came[k, :, span].astype(F32)
                if k == 0:
                    out[:, span] = value
                else:
                    chunks[g, :, span] = value.astype(BF)
            if k == 2:
                ring.start_far()
            elif k == 1:
                ring.start_up()
            elif k == 3:
                ring.start_down()
            yield
        ring.add()
        yield
        for h in range(2):
            rows = slice(h * own // 2, (h + 1) * own // 2)
            out[rows, :] += ring.total(h)
        yield
        ring.sent()
        for copy in passes:
            copy.wait_send()

    return Flow(
        [(x, pltpu.VMEM) for x in (*lefts, right)],
        [((own, wide), F32, pltpu.VMEM)],
        [
            pltpu.VMEM((4, own, wide), BF),
            pltpu.VMEM((4, own, wide), BF),
            pltpu.VMEM((4, own, wide), BF),
            pltpu.VMEM((8, own // 2, wide), BF),
            dma(6),
            dma(6),
            dma(4),
            dma(4),
        ],
        ring_partners("zc") + [("c", 1)],
        steps,
    )


def plane_scatter_flow(array, first, second, from_core, dtype):
    rows, columns = array.shape[-2:]

    def steps(ins, outs, scratch):
        (src,), (out,) = ins, outs
        came, sums, middle, bufs, late_bufs, send, recv, late_send, late_recv, pass_send, pass_recv, local = scratch
        core, member = peers_of("c")
        me, _ = peers_of(first)

        def along(ref, g):
            return ref.at[g] if first == "y" else ref.at[:, g]

        ring = RingScatter(first, lambda g: along(sums, g), bufs, send, recv)
        order = [lax.rem(me + k, 4) for k in (2, 1, 3, 0)]
        starts = [ring.start_far, ring.start_up, ring.start_down, lambda: None]
        passes, loads = [], []
        for i, g in enumerate(order):
            if from_core:
                passes.append(
                    remote(along(src.at[1 - core], g), along(came, g), pass_send.at[i], pass_recv.at[i], member(1 - core))
                )
                passes[i].start()
            loads.append(pltpu.make_async_copy(along(src.at[core] if from_core else src, g), along(sums, g), local.at[i]))
            loads[i].start()
        yield
        for i, g in enumerate(order):
            loads[i].wait()
            if from_core:
                passes[i].wait_recv()
                for k in range(4):
                    total = along(sums, g)[k].astype(F32) + along(came, g)[k].astype(F32)
                    along(sums, g)[k] = total.astype(BF)
            starts[i]()
            yield
        ring.add()
        yield
        own = along(sums, me)
        for h in range(2):
            came_half = ring.total(h)
            for k in range(2):
                middle[h * 2 + k] = (own[h * 2 + k].astype(F32) + came_half[k]).astype(BF)
        yield
        last = RingScatter(second, lambda g: middle.at[g], late_bufs, late_send, late_recv)
        last.start_far()
        last.start_up()
        last.start_down()
        yield
        last.add()
        yield
        for h in range(2):
            half = slice(h * rows // 2, (h + 1) * rows // 2)
            out[half, :] = (piece(middle.at[last.me], h)[...].astype(F32) + last.total(h)).astype(dtype)
        yield
        ring.sent()
        last.sent()
        for copy in passes:
            copy.wait_send()

    block = (4, 4, rows, columns)
    return Flow(
        [(array, pl.ANY)],
        [((rows, columns), dtype, pltpu.VMEM)],
        [
            pltpu.VMEM(block if from_core else (8, 128), BF),
            pltpu.VMEM(block, BF),
            pltpu.VMEM((4, rows, columns), BF),
            pltpu.VMEM((8, 2, rows, columns), BF),
            pltpu.VMEM((8, rows // 2, columns), BF),
            dma(6),
            dma(6),
            dma(6),
            dma(6),
            dma(4),
            dma(4),
            dma(4),
        ],
        ring_partners("x") + ring_partners("y") + ([("c", 1)] if from_core else []),
        steps,
    )


def exchange_flow(array, kind):
    n = SIZES[kind]

    def steps(ins, outs, scratch):
        (src,), (out,) = ins, outs
        stage, send, recv, local = scratch
        me, member = peers_of(kind)
        own = pltpu.make_async_copy(src.at[me], stage, local.at[0])
        own.start()
        copies = []
        for k in range(1, n):
            to = lax.rem(me + k, n)
            copies.append(remote(src.at[to], out.at[me], send.at[k], recv.at[k], member(to)))
            copies[-1].start()
        yield
        own.wait()
        back = pltpu.make_async_copy(stage, out.at[me], local.at[0])
        back.start()
        yield
        for copy in copies:
            copy.wait()
        back.wait()

    return Flow(
        [(array, pl.ANY)],
        [(array.shape, array.dtype, pl.ANY)],
        [pltpu.VMEM(array.shape[1:], array.dtype), dma(n), dma(n), dma(1)],
        [(kind, k) for k in range(1, n)],
        steps,
    )


def sum_flow(array):
    def steps(ins, outs, scratch):
        (src,), (out,) = ins, outs
        wide, far, middle, sends, recvs, far_sends, far_recvs = scratch
        me, member = peers_of("yx")
        copies = []
        for k in range(1, 16):
            copies.append(remote(src, wide.at[me], sends.at[k], recvs.at[k], member(lax.rem(me + k, 16))))
            copies[-1].start()
        yield
        wide[me] = src[...]
        for copy in copies:
            copy.wait()
        middle[...] = jnp.sum(wide[...], axis=0)
        ring, ring_member = peers_of("z")
        late = []
        for k in range(1, 8):
            late.append(remote(middle, far.at[ring], far_sends.at[k], far_recvs.at[k], ring_member(lax.rem(ring + k, 8))))
            late[-1].start()
        yield
        far[ring] = middle[...]
        for copy in late:
            copy.wait()
        out[...] = jnp.sum(far[...], axis=0)

    return Flow(
        [(array, pltpu.VMEM)],
        [(array.shape, F32, pltpu.VMEM)],
        [
            pltpu.VMEM((16,) + array.shape, F32),
            pltpu.VMEM((8,) + array.shape, F32),
            pltpu.VMEM(array.shape, F32),
            dma(16),
            dma(16),
            dma(8),
            dma(8),
        ],
        [("yx", k) for k in range(1, 16)] + [("z", k) for k in range(1, 8)],
        steps,
    )


def add_up(stacked):
    return jnp.sum(stacked.astype(F32), axis=0)


def dot_nn(a, b):
    return lax.dot_general(a, b, (((1,), (0,)), ((), ())), preferred_element_type=F32)


def dot_nt(a, b):
    return lax.dot_general(a, b, (((1,), (1,)), ((), ())), preferred_element_type=F32)


def dot_tn(a, b):
    return lax.dot_general(a, b, (((0,), (0,)), ((), ())), preferred_element_type=F32)


def norm_rope(raw, gain, cosine, sine):
    unit = raw * lax.rsqrt(jnp.mean(raw * raw, axis=-1, keepdims=True) + EPS)
    scaled = unit * gain
    return scaled * cosine + pltpu.roll(scaled, 64, 1) * sine


def norm_rope_back(grad, raw, gain, cosine, sine):
    inverse = lax.rsqrt(jnp.mean(raw * raw, axis=-1, keepdims=True) + EPS)
    unit = raw * inverse
    turned = grad * cosine + pltpu.roll(grad * sine, 64, 1)
    scaled = turned * gain
    return inverse * (scaled - unit * jnp.mean(scaled * unit, axis=-1, keepdims=True)), turned * unit


def project_kernel(rows_ref, w_ref, gain_ref, cos_ref, sin_ref, q_ref, raw_ref, k_ref, v_ref):
    wide, size = q_ref.shape[1], k_ref.shape[1]
    product = dot_nn(rows_ref[...], w_ref[...])
    q_ref[...] = product[:, :wide]
    raw = product[:, wide : wide + size]
    raw_ref[...] = raw
    k_ref[...] = norm_rope(raw, gain_ref[...], cos_ref[...], sin_ref[...]).astype(BF)
    v_ref[...] = product[:, wide + size :].astype(BF)


def key_back_kernel(dk_ref, dv_ref, raw_ref, gain_ref, cos_ref, sin_ref, rows_hbm, out_ref, w_ref, sum_ref, rows_ref, local):
    half, size = dk_ref.shape
    core, _ = peers_of("c")
    rows = pl.ds(pl.multiple_of(core * half, half), half)
    copy = pltpu.make_async_copy(rows_hbm.at[rows], rows_ref, local.at[0])
    copy.start()
    grad = dk_ref[...].astype(F32)
    grad_raw, grad_gain = norm_rope_back(grad, raw_ref[rows, :], gain_ref[...], cos_ref[rows, :], sin_ref[rows, :])
    out_ref[...] = jnp.zeros_like(out_ref)
    out_ref[rows, :size] = grad_raw.astype(BF)
    out_ref[rows, size:] = dv_ref[...]
    sum_ref[...] = jnp.sum(grad_gain, axis=0, keepdims=True)
    copy.wait()
    for column in range(0, rows_ref.shape[1], 256):
        span = slice(column, column + 256)
        w_ref[span, :] = dot_tn(rows_ref[:, span], out_ref[rows, :]).astype(BF)


def expert_kernel(rows_ref, plain_ref, w_ref, back_ref, hidden_ref, gated_ref, both_ref):
    width, ff = w_ref.shape[0], plain_ref.shape[1]
    own = lax.axis_index("head") * lax.axis_size("blk") + lax.axis_index("blk")
    gates = rows_ref[:, width:].astype(F32)
    lane = lax.broadcasted_iota(jnp.int32, gates.shape, 1)
    gate = jnp.sum(jnp.where(lane == own, gates, 0.0), axis=1, keepdims=True)
    gate_up = dot_nn(rows_ref[:, :width], w_ref[...])
    first, up = gate_up[:, :ff], gate_up[:, ff:]
    sigma = 1.0 / (1.0 + jnp.exp(-first))
    silu = first * sigma
    hidden = silu * up
    hidden_ref[...] = hidden.astype(BF)
    gated_ref[...] = (hidden * gate).astype(BF)
    plain = plain_ref[...]
    gate_grad = jnp.sum(hidden * plain, axis=1, keepdims=True)
    grad = plain * gate
    both_ref[:, :ff] = (grad * up * (sigma * (1.0 + first * (1.0 - sigma)))).astype(BF)
    both_ref[:, ff:] = (grad * silu).astype(BF)
    back_ref[:, :width] = dot_nt(both_ref[...], w_ref[...]).astype(BF)
    high = gate_grad.astype(BF).astype(F32)
    back_ref[:, width:] = jnp.where(lane == 0, high, jnp.where(lane == 1, gate_grad - high, 0.0)).astype(BF)


def key_tiles(lo, full, last, tile):
    middle = jnp.minimum(full, last)
    pl.loop(lo, middle)(lambda t: tile(t, True))
    pl.loop(middle, last)(lambda t: tile(t, False))
    tile(last, True)


def allowed_pairs(t, last, start, shape):
    key_place = t * BLOCK + lax.broadcasted_iota(jnp.int32, shape, 0)
    query_place = last * BLOCK + lax.rem(lax.broadcasted_iota(jnp.int32, shape, 1), BLOCK)
    return (key_place >= start) & (key_place <= query_place)


def attend_forward_kernel(
    lo_ref, full_ref, last_ref, slot_ref, raw_ref, gain_ref, cos_ref, sin_ref, k_ref, v_ref, start_ref, q_ref, o_ref, log_ref, q_t, acc, total
):
    j = pl.program_id(0)
    size = k_ref.shape[2]
    heads = raw_ref.shape[1] // size
    scale = size**-0.5 * LOG2E
    last = last_ref[j]
    for n in range(heads):
        span = slice(n * size, (n + 1) * size)
        query = norm_rope(raw_ref[:, span], gain_ref[...], cos_ref[...], sin_ref[...])
        q_ref[:, span] = query.astype(BF)
        q_t[:, n * BLOCK : (n + 1) * BLOCK] = query.T.astype(BF)
    acc[...] = jnp.zeros_like(acc)
    total[...] = jnp.zeros_like(total)
    start = start_ref[0]

    def tile(t, masked):
        slot = slot_ref[t]
        weights = jnp.exp2(dot_nn(k_ref[slot], q_t[...]) * scale)
        if masked:
            weights = jnp.where(allowed_pairs(t, last, start, weights.shape), weights, 0.0)
        total[...] += jnp.sum(weights.reshape(BLOCK // 8, 8, heads * BLOCK), axis=0)
        acc[...] += dot_nn(v_ref[slot].T, weights.astype(BF))

    key_tiles(lo_ref[j], full_ref[j], last, tile)
    row = jnp.sum(total[...], axis=0, keepdims=True)
    log_ref[0] = jnp.log2(row)
    out = acc[...] / row
    for n in range(heads):
        o_ref[:, n * size : (n + 1) * size] = out[:, n * BLOCK : (n + 1) * BLOCK].T.astype(BF)


def attend_backward_kernel(
    lo_ref,
    full_ref,
    last_ref,
    slot_ref,
    raw_ref,
    gain_ref,
    cos_ref,
    sin_ref,
    k_ref,
    v_ref,
    start_ref,
    q_ref,
    o_ref,
    g_ref,
    log_ref,
    dq_ref,
    sum_ref,
    dk_ref,
    dv_ref,
    queries,
    q_t,
    grads,
    g_t,
    delta,
    acc,
    dk,
    dv,
):
    j = pl.program_id(0)
    slots, _, size = k_ref.shape
    heads = raw_ref.shape[1] // size
    scale = size**-0.5
    last = last_ref[j]

    @pl.when(j == 0)
    def _():
        sum_ref[...] = jnp.zeros_like(sum_ref)

        @pl.loop(0, slots)
        def _(s):
            dk[s] = jnp.zeros(dk.shape[1:], F32)
            dv[s] = jnp.zeros(dv.shape[1:], F32)

    for n in range(heads):
        span, rows = slice(n * size, (n + 1) * size), slice(n * BLOCK, (n + 1) * BLOCK)
        queries[rows, :] = q_ref[:, span]
        q_t[:, rows] = q_ref[:, span].T
        grads[rows, :] = g_ref[:, span]
        grad_t = g_ref[:, span].T
        g_t[:, rows] = grad_t
        delta[:, rows] = jnp.sum(grad_t.astype(F32) * o_ref[:, span].T.astype(F32), axis=0, keepdims=True)
    acc[...] = jnp.zeros_like(acc)
    start = start_ref[0]
    logs = log_ref[0]

    def tile(t, masked):
        slot = slot_ref[t]
        keys = k_ref[slot]
        probs = jnp.exp2(dot_nn(keys, q_t[...]) * (scale * LOG2E) - logs)
        if masked:
            probs = jnp.where(allowed_pairs(t, last, start, probs.shape), probs, 0.0)
        grad_scores = (probs * (dot_nn(v_ref[slot], g_t[...]) - delta[...])).astype(BF)
        dv[slot] += dot_nn(probs.astype(BF), grads[...])
        dk[slot] += dot_nn(grad_scores, queries[...])
        acc[...] += dot_nn(keys.T, grad_scores)

    key_tiles(lo_ref[j], full_ref[j], last, tile)
    for n in range(heads):
        span = slice(n * size, (n + 1) * size)
        grad = (acc[:, n * BLOCK : (n + 1) * BLOCK] * scale).T.astype(BF).astype(F32)
        grad_raw, grad_gain = norm_rope_back(grad, raw_ref[:, span], gain_ref[...], cos_ref[...], sin_ref[...])
        dq_ref[:, span] = grad_raw.astype(BF)
        sum_ref[...] += jnp.sum(grad_gain, axis=0, keepdims=True)

    @pl.when(j == pl.num_programs(0) - 1)
    def _():
        @pl.loop(0, slots)
        def _(s):
            dk_ref[s] = (dk[s] * scale).astype(BF)
            dv_ref[s] = dv[s].astype(BF)


def by_rows(array, rows=BLOCK):
    return pl.BlockSpec((rows,) + array.shape[1:], lambda j, *_: (j,) + (0,) * (array.ndim - 1))


def resident(array):
    return pl.BlockSpec(array.shape, lambda j, *_: (0,) * array.ndim, pipeline_mode=pl.Buffered(1))


def shaped(shape, dtype):
    return jax.ShapeDtypeStruct(shape, dtype)


def project(rows, weights, gain, cosine, sine, q_cols):
    size = gain.shape[1]
    outs = (shaped((rows.shape[0], q_cols), F32), shaped((rows.shape[0], size), F32)) + (shaped((rows.shape[0], size), BF),) * 2
    return pl.pallas_call(
        project_kernel,
        out_shape=outs,
        grid=(rows.shape[0] // BLOCK,),
        in_specs=[by_rows(rows), resident(weights), resident(gain), by_rows(cosine), by_rows(sine)],
        out_specs=tuple(by_rows(x) for x in outs),
        compiler_params=pltpu.CompilerParams(vmem_limit_bytes=VMEM_LIMIT),
        cost_estimate=cost_of(6),
        name="project",
    )(rows, weights, gain, cosine, sine)


def key_back(grad_key, grad_value, raw, gain, cosine, sine, group):
    rows, size = raw.shape
    width = group.shape[1]
    whole = pl.BlockSpec(memory_space=pltpu.VMEM)
    return pl.pallas_call(
        key_back_kernel,
        out_shape=(shaped((rows, 2 * size), BF), shaped((width, 2 * size), BF), shaped((1, size), F32)),
        in_specs=[whole] * 6 + [pl.BlockSpec(memory_space=pl.ANY)],
        out_specs=(whole,) * 3,
        scratch_shapes=[pltpu.VMEM((rows // 2, width), BF), dma(1)],
        compiler_params=pltpu.CompilerParams(vmem_limit_bytes=VMEM_LIMIT),
        cost_estimate=cost_of(4),
        name="key_back",
    )(grad_key, grad_value, raw, gain, cosine, sine, group)


def expert(rows, plain, weights, block=512):
    count, ff = plain.shape
    outs = (shaped(rows.shape, BF), shaped((count, ff), BF), shaped((count, ff), BF), shaped((count, 2 * ff), BF))
    return pl.pallas_call(
        expert_kernel,
        out_shape=outs,
        grid=(count // block,),
        in_specs=[by_rows(rows, block), by_rows(plain, block), resident(weights)],
        out_specs=tuple(by_rows(x, block) for x in outs),
        compiler_params=pltpu.CompilerParams(vmem_limit_bytes=VMEM_LIMIT),
        cost_estimate=cost_of(20),
        name="expert",
    )(rows, plain, weights)


def attend_forward(meta, raw, gain, cosine, sine, keys, values, start):
    rows, wide = raw.shape
    blocks, size = rows // BLOCK, keys.shape[2]
    lanes = wide // size * BLOCK
    outs = (shaped((rows, wide), BF), shaped((rows, wide), BF), shaped((blocks, 1, lanes), F32))
    return pl.pallas_call(
        attend_forward_kernel,
        out_shape=outs,
        grid_spec=pltpu.PrefetchScalarGridSpec(
            num_scalar_prefetch=4,
            grid=(blocks,),
            in_specs=[
                by_rows(raw),
                resident(gain),
                by_rows(cosine),
                by_rows(sine),
                resident(keys),
                resident(values),
                by_rows(start, 1),
            ],
            out_specs=(by_rows(outs[0]), by_rows(outs[1]), by_rows(outs[2], 1)),
            scratch_shapes=[pltpu.VMEM((size, lanes), BF), pltpu.VMEM((size, lanes), F32), pltpu.VMEM((8, lanes), F32)],
        ),
        compiler_params=pltpu.CompilerParams(vmem_limit_bytes=VMEM_LIMIT),
        cost_estimate=cost_of(30),
        name="attend",
    )(*meta, raw, gain, cosine, sine, keys, values, start)


def attend_backward(meta, raw, gain, cosine, sine, keys, values, start, queries, attended, grads, logs):
    rows, wide = raw.shape
    blocks, size = rows // BLOCK, keys.shape[2]
    lanes = wide // size * BLOCK
    outs = (shaped((rows, wide), BF), shaped((1, size), F32), shaped(keys.shape, BF), shaped(values.shape, BF))
    return pl.pallas_call(
        attend_backward_kernel,
        out_shape=outs,
        grid_spec=pltpu.PrefetchScalarGridSpec(
            num_scalar_prefetch=4,
            grid=(blocks,),
            in_specs=[
                by_rows(raw),
                resident(gain),
                by_rows(cosine),
                by_rows(sine),
                resident(keys),
                resident(values),
                by_rows(start, 1),
                by_rows(queries),
                by_rows(attended),
                by_rows(grads),
                by_rows(logs, 1),
            ],
            out_specs=(by_rows(outs[0]),) + tuple(resident(x) for x in outs[1:]),
            scratch_shapes=[
                pltpu.VMEM((lanes, size), BF),
                pltpu.VMEM((size, lanes), BF),
                pltpu.VMEM((lanes, size), BF),
                pltpu.VMEM((size, lanes), BF),
                pltpu.VMEM((1, lanes), F32),
                pltpu.VMEM((size, lanes), F32),
                pltpu.VMEM(keys.shape, F32),
                pltpu.VMEM(values.shape, F32),
            ],
        ),
        compiler_params=pltpu.CompilerParams(vmem_limit_bytes=VMEM_LIMIT),
        cost_estimate=cost_of(40),
        name="attend_back",
    )(*meta, raw, gain, cosine, sine, keys, values, start, queries, attended, grads, logs)


def rms_scale(values, gain_vec):
    return values * lax.rsqrt(jnp.mean(values * values, axis=-1, keepdims=True) + EPS) * gain_vec


def rope_table(offsets, size):
    half = size // 2
    spacing = ROPE_BASE ** (-2.0 * jnp.arange(half, dtype=F32) / size)
    angles = offsets.astype(F32)[:, None] * spacing[None, :]
    cosine, sine = jnp.cos(angles), jnp.sin(angles)
    return jnp.concatenate([cosine, cosine], axis=1), jnp.concatenate([-sine, sine], axis=1)


def two_parts(wide):
    high = wide.astype(BF)
    return high, (wide - high.astype(F32)).astype(BF)


def all_to_all(stacked):
    return lax.all_to_all(stacked, ("head", "blk"), split_axis=0, concat_axis=0, tiled=True)


def body(
    tokens,
    norm_gain,
    w_query,
    key_weight,
    value_weight,
    query_gain,
    key_gain,
    w_out,
    mix_gain,
    w_router,
    expert_gate_up,
    expert_down,
    lengths,
    block_deal,
    routes,
    cotangent,
):
    own, width = tokens.shape
    size = query_gain.shape[0]
    scale = size ** (-0.5)
    blk = lax.axis_index("blk")
    plane, core = blk // 4, blk % 2
    devices = lax.axis_size("head") * lax.axis_size("blk")
    experts = w_router.shape[0] * 2
    cap = own * routes.shape[1] // experts
    gate_up, down = expert_gate_up[0], expert_down[0]
    ff = down.shape[0]
    group_rows = 8 * own
    q_cols = w_query.shape[1] // 4
    heads = q_cols // size

    chosen = jnp.sum((routes[:, :, None] == jnp.arange(experts, dtype=jnp.int32)).astype(jnp.int32), axis=1)
    order = jnp.arange(own)
    earlier = dot_nn((order[:, None] > order[None, :]).astype(BF), chosen.astype(BF)).astype(jnp.int32)
    assign = (chosen[:, :, None] > 0) & (earlier[:, :, None] == jnp.arange(cap, dtype=jnp.int32))
    assign_wide = assign.astype(F32)
    assign_low = assign.astype(BF).reshape(own, experts * cap)

    wide = tokens.astype(F32)
    normed, norm_back = jax.vjp(rms_scale, wide, norm_gain)
    normed_low = normed.astype(BF)
    depth = w_query.shape[0]
    out_pack = w_out.reshape(4, q_cols, depth).transpose(2, 0, 1).reshape(depth, -1)
    side = lax.axis_index("head") == jnp.arange(2, dtype=jnp.int32)
    router_pack = jnp.where(side[None, :, None], w_router.T[:, None, :], 0).astype(BF).reshape(depth, experts)
    w_qkv, w_out_t, w_router_t, group_tokens = launch(
        [
            plane_gather_flow([(w_query, q_cols, 1), (key_weight, size, 2), (value_weight, size, 2)], "x", "y", ahead="zhc"),
            plane_gather_flow([(out_pack, q_cols, 1)], "y", "x", ahead="zhc"),
            plane_gather_flow([(router_pack, experts, 1)], "y", "x", ahead="z"),
            ring_gather_flow(normed_low),
        ],
        0,
        45,
    )
    normed_group = group_tokens.reshape(group_rows, width)
    w_qkv, w_out_t = w_qkv.reshape(width, -1), w_out_t.reshape(width, -1)
    w_router_t = jnp.sum(w_router_t.reshape(-1, 2, depth, experts), axis=1).reshape(width, experts)

    group_blocks = plane * 4 + jnp.array([0, 2, 1, 3], jnp.int32)
    ids = jnp.arange(block_deal.shape[0], dtype=jnp.int32)
    last = jnp.sum(jnp.where(group_blocks[:, None] == ids[None, :], block_deal[None, :], 0), axis=1)
    slots = (ids % 2) * (ids.shape[0] // 2) + (ids // 4) * 2 + (ids % 4) // 2
    slot_of = jnp.sum(jnp.where(block_deal[None, :] == ids[:, None], slots[None, :], 0), axis=1)
    place = (last[:, None] * BLOCK + jnp.arange(BLOCK, dtype=jnp.int32)[None, :]).reshape(-1)
    passed = place[:, None] >= jnp.cumsum(lengths)[None, :]
    start = jnp.sum(jnp.where(passed, lengths[None, :], 0), axis=1)
    start_rows = start.reshape(-1, 1, BLOCK)
    meta = (start_rows[:, 0, 0] // BLOCK, (start_rows[:, 0, BLOCK - 1] + BLOCK - 1) // BLOCK, last, slot_of)
    start_rows = jnp.tile(start_rows, (1, 1, heads))
    cosine, sine = rope_table(place - start, size)

    q_gain, k_gain = query_gain[None], key_gain[None]
    q_raw, k_raw, keys, values = project(normed_group, w_qkv, k_gain, cosine, sine, q_cols)
    keys, values, grad_rows = launch(
        [
            plane_gather_flow([(keys, size, 1)], "x", "y", to_core=True),
            plane_gather_flow([(values, size, 1)], "y", "x", to_core=True),
            product_flow(assign_low, cotangent),
        ],
        1,
        30,
    )
    grad_rows = all_to_all(grad_rows.reshape(devices, cap, width)).reshape(-1, width)
    keys, values = keys.reshape(-1, BLOCK, size), values.reshape(-1, BLOCK, size)
    queries, attended, logs = attend_forward(meta, q_raw, q_gain, cosine, sine, keys, values, start_rows)

    residual = wide + launch([product_scatter_flow([attended], w_out_t)], 2, 25)[0]
    mixed, mix_back = jax.vjp(rms_scale, residual, mix_gain)
    mixed_low, grad_rows = lax.optimization_barrier((mixed.astype(BF), grad_rows))
    logits = dot_nn(mixed_low, w_router_t)
    gates = jax.nn.softmax(jnp.where(chosen > 0, logits, -1e30), axis=-1)
    gate_slots = gates[:, :, None] * assign_wide
    outgoing = dot_tn(assign_low, jnp.concatenate([mixed_low, gates.astype(BF)], axis=1)).astype(BF)
    arrived = all_to_all(outgoing.reshape(devices, cap, -1)).reshape(experts * cap, -1)

    plain_grad = lax.optimization_barrier(dot_nt(grad_rows, down))
    rows, plain_grad = lax.optimization_barrier((arrived, plain_grad))
    back, hidden, gated, grad_both = expert(rows, plain_grad, gate_up)
    back = all_to_all(back.reshape(devices, cap, -1)).reshape(experts * cap, -1)
    back, expert_out = lax.optimization_barrier((back, dot_nn(hidden, down).astype(BF)))
    grad_down = dot_tn(gated, grad_rows)
    grad_gate_up = dot_tn(rows[:, :width], grad_both)

    gate_grads = jnp.sum(back[:, width : width + 2].astype(F32), axis=1).reshape(experts, cap)
    gate_grads = jnp.sum(assign_wide * gate_grads[None], axis=2)
    grad_logits = (gates * (gate_grads - jnp.sum(gates * gate_grads, axis=1, keepdims=True))).astype(BF)
    grad_mixed = dot_nn(assign_low, back[:, :width]) + dot_nt(grad_logits, w_router_t)
    grad_router_t = dot_tn(mixed_low, grad_logits)
    grad_from_mix, grad_mix_gain = mix_back(grad_mixed)
    grad_residual = cotangent.astype(F32) + grad_from_mix
    grad_group = launch([ring_gather_flow(grad_residual.astype(BF))], 3, 20)[0].reshape(group_rows, width)
    grad_group, expert_out = lax.optimization_barrier((grad_group, expert_out))
    expert_out = all_to_all(expert_out.reshape(devices, cap, width)).reshape(-1, width)
    grad_attended = dot_nn(grad_group, w_out_t).astype(BF)
    grad_q, grad_query_gain, grad_keys, grad_values = attend_backward(
        meta, q_raw, q_gain, cosine, sine, keys, values, start_rows, queries, attended, grad_attended, logs
    )

    split = (2, 4, 4, group_rows // 2, size)
    grad_key, grad_value, grad_wq, grad_wo = launch(
        [
            plane_scatter_flow(grad_keys.reshape(split), "y", "x", True, BF),
            plane_scatter_flow(grad_values.reshape(split), "x", "y", True, BF),
            product_flow(normed_group, grad_q),
            product_flow(grad_group, attended),
        ],
        4,
        35,
    )
    grad_kv, grad_wkv, grad_key_gain = key_back(grad_key, grad_value, k_raw, k_gain, cosine, sine, normed_group)

    grad_kv, expert_out = lax.optimization_barrier((grad_kv, expert_out))
    plane_split = (4, 4, 4 * depth, -1)
    grad_normed, grad_wq, grad_wkv, grad_wo, grad_wr, output = launch(
        [
            product_scatter_flow([grad_q, grad_kv], w_qkv),
            plane_scatter_flow(grad_wq.reshape(plane_split), "y", "x", False, BF),
            plane_scatter_flow(grad_wkv.reshape(plane_split), "y", "x", False, BF),
            plane_scatter_flow(grad_wo.reshape(plane_split), "x", "y", False, BF),
            plane_scatter_flow(grad_router_t.astype(BF).reshape(plane_split), "x", "y", False, BF),
            output_flow(residual, *two_parts(gate_slots.reshape(own, -1)), expert_out),
        ],
        5,
        40,
    )
    grad_from_norm, grad_norm_gain = norm_back(grad_normed)
    grad_tokens = grad_residual + grad_from_norm

    gains = jnp.concatenate([grad_norm_gain, grad_mix_gain, grad_query_gain[0], grad_key_gain[0], jnp.zeros((768,), F32)]).reshape(-1, size)
    router_part = grad_wr.reshape(4, depth, 2, experts // 2).transpose(0, 2, 1, 3).reshape(8, depth, -1)
    grad_wq, grad_wkv, grad_wo, router_part, gains = launch(
        [
            exchange_flow(grad_wq.reshape(4, depth, -1), "zhc"),
            exchange_flow(grad_wkv.reshape(4, depth, -1), "zhc"),
            exchange_flow(grad_wo.reshape(4, depth, -1), "zhc"),
            exchange_flow(router_part, "z"),
            sum_flow(gains),
        ],
        6,
        15,
    )
    gains = gains.reshape(-1)
    grad_w_query = grad_wq.astype(F32).transpose(1, 0, 2).reshape(depth, -1)
    grad_kv_w = jnp.sum(grad_wkv.astype(F32).reshape(2, 2, depth, 2, size), axis=1)
    grad_w_key = grad_kv_w[:, :, 0].transpose(1, 0, 2).reshape(depth, -1)
    grad_w_value = grad_kv_w[:, :, 1].transpose(1, 0, 2).reshape(depth, -1)
    grad_w_out = grad_wo.astype(F32).transpose(0, 2, 1).reshape(-1, depth)
    grad_w_router = add_up(router_part).T
    return (
        output,
        grad_tokens,
        gains[:width],
        grad_w_query,
        grad_w_key,
        grad_w_value,
        gains[2 * width : 2 * width + size],
        gains[2 * width + size : 2 * width + 2 * size],
        grad_w_out,
        gains[width : 2 * width],
        grad_w_router,
        grad_gate_up[None],
        grad_down[None],
    )


def solution(mesh):
    rows, both = P(("head", "blk"), None), P("blk", "head")
    expert, turned = P(("head", "blk"), None, None), P("head", "blk")
    in_specs = (rows, P(), both, both, both, P(), P(), turned, P(), turned, expert, expert, P(), P(), rows, rows)
    out_specs = (rows, rows, P(), both, both, both, P(), P(), turned, P(), turned, expert, expert)
    return jax.shard_map(body, mesh=mesh, in_specs=in_specs, out_specs=out_specs, check_vma=False)
```

```python
import jax
import jax.numpy as jnp
from jax import lax
from jax.experimental import pallas as pl
from jax.experimental.pallas import tpu as pltpu
from jax.sharding import PartitionSpec as P

MESH = pl.DeviceIdType.MESH
EPS = 1e-06
ROPE_BASE = 1000000.0
LOG2E = 1.4426950408889634
BF = jnp.bfloat16
F32 = jnp.float32
BLOCK = 256
VMEM_LIMIT = 60 << 20
SIZES = {"zc": 4, "c": 2, "x": 4, "y": 4, "zhc": 4, "z": 8, "yx": 16}


def peers_of(kind):
    h = lax.axis_index("head")
    b = lax.axis_index("blk")
    q, r = lax.div(b, 4), lax.rem(b, 4)
    if kind == "zc":
        return lax.div(r, 2) * 2 + h, lambda g: (lax.rem(g, 2), q * 4 + lax.div(g, 2) * 2 + lax.rem(r, 2))
    if kind == "z":
        return r * 2 + h, lambda g: (lax.rem(g, 2), q * 4 + lax.div(g, 2))
    if kind == "c":
        return lax.rem(b, 2), lambda g: (h, b - lax.rem(b, 2) + g)
    if kind == "x":
        return lax.rem(q, 4), lambda g: (h, (lax.div(q, 4) * 4 + g) * 4 + r)
    if kind == "y":
        return lax.div(q, 4), lambda g: (h, (g * 4 + lax.rem(q, 4)) * 4 + r)
    if kind == "yx":
        return q, lambda g: (h, g * 4 + r)
    return r, lambda g: (h, q * 4 + g)


def cost_of(microseconds):
    return pl.CostEstimate(flops=microseconds * 10**9, bytes_accessed=microseconds * 3 * 10**6, transcendentals=0)


class Flow:
    def __init__(self, inputs, outputs, scratch, partners, steps):
        self.inputs, self.outputs, self.scratch = inputs, outputs, scratch
        self.partners, self.steps = partners, steps


def launch(flows, cid, cost):
    partners = sorted({p for flow in flows for p in flow.partners})

    def kernel(*refs):
        n_in, n_out = sum(len(f.inputs) for f in flows), sum(len(f.outputs) for f in flows)
        ins, outs, rest = list(refs[:n_in]), list(refs[n_in : n_in + n_out]), list(refs[n_in + n_out :])
        barrier = pltpu.get_barrier_semaphore()
        for kind, distance in partners:
            me, member = peers_of(kind)
            to = member(lax.rem(me + distance, SIZES[kind]))
            pl.semaphore_signal(barrier, inc=1, device_id=to, device_id_type=MESH)
        pl.semaphore_wait(barrier, len(partners))
        running = []
        for flow in flows:
            own = [[group.pop(0) for _ in part] for group, part in ((ins, flow.inputs), (outs, flow.outputs), (rest, flow.scratch))]
            running.append(flow.steps(*own))
        while running:
            going = []
            for steps in running:
                more = next(steps, running)
                if more is not running:
                    going += [steps] if more is None else [steps, more]
            running = going

    return pl.pallas_call(
        kernel,
        out_shape=tuple(jax.ShapeDtypeStruct(s, d) for f in flows for s, d, _ in f.outputs),
        in_specs=[pl.BlockSpec(memory_space=space) for f in flows for _, space in f.inputs],
        out_specs=tuple(pl.BlockSpec(memory_space=space) for f in flows for _, _, space in f.outputs),
        scratch_shapes=[x for f in flows for x in f.scratch],
        compiler_params=pltpu.CompilerParams(collective_id=cid, has_side_effects=True, vmem_limit_bytes=VMEM_LIMIT),
        cost_estimate=cost_of(cost),
        name=f"links_{cid}",
    )(*[x for f in flows for x, _ in f.inputs])


def remote(src, dst, send, recv, device):
    return pltpu.make_async_remote_copy(
        src_ref=src, dst_ref=dst, send_sem=send, recv_sem=recv, device_id=device, device_id_type=MESH
    )


def piece(ref, which):
    rows = ref.shape[0] // 2
    return ref.at[pl.ds(which * rows, rows)]


def ring_partners(kind):
    return [(kind, 1), (kind, 3)]


class RingGather:
    def __init__(self, kind, slot, src, send, recv):
        me, member = peers_of(kind)
        up, down = lax.rem(me + 1, 4), lax.rem(me + 3, 4)

        def copy(source, target, i, to):
            return remote(source, target, send.at[i], recv.at[i], member(to))

        mine = slot(me)
        self.copies = [
            copy(piece(src, 0), piece(mine, 0), 0, up),
            copy(piece(src, 1), piece(mine, 1), 1, up),
            copy(piece(src, 1), piece(mine, 1), 2, down),
            copy(piece(src, 0), piece(mine, 0), 3, down),
            copy(piece(slot(down), 0), piece(slot(down), 0), 4, up),
            copy(piece(slot(up), 1), piece(slot(up), 1), 5, down),
        ]

    def start(self):
        for i in (0, 2, 1, 3):
            self.copies[i].start()

    def forward(self):
        self.copies[0].wait_recv()
        self.copies[4].start()
        self.copies[2].wait_recv()
        self.copies[5].start()

    def near(self):
        self.copies[1].wait_recv()
        self.copies[3].wait_recv()

    def far(self):
        self.copies[4].wait_recv()
        self.copies[5].wait_recv()

    def sent(self):
        for copy in self.copies:
            copy.wait_send()


class RingScatter:
    def __init__(self, kind, chunk, bufs, send, recv):
        self.me, member = peers_of(kind)
        self.up, self.down, self.far = (lax.rem(self.me + k, 4) for k in (1, 3, 2))
        self.chunk, self.bufs = chunk, bufs

        def copy(source, target, i, to):
            return remote(source, bufs.at[target], send.at[i], recv.at[i], member(to))

        self.copies = [
            copy(piece(chunk(self.far), 0), 0, 0, self.up),
            copy(piece(chunk(self.far), 1), 1, 1, self.down),
            copy(piece(chunk(self.up), 1), 2, 2, self.up),
            copy(piece(chunk(self.down), 0), 3, 3, self.down),
            copy(bufs.at[6], 4, 4, self.up),
            copy(bufs.at[7], 5, 5, self.down),
        ]

    def start_far(self):
        self.copies[0].start()
        self.copies[1].start()

    def start_up(self):
        self.copies[2].start()

    def start_down(self):
        self.copies[3].start()

    def add(self):
        self.copies[0].wait_recv()
        self.bufs[6] = (piece(self.chunk(self.up), 0)[...].astype(F32) + self.bufs[0].astype(F32)).astype(BF)
        self.copies[4].start()
        self.copies[1].wait_recv()
        self.bufs[7] = (piece(self.chunk(self.down), 1)[...].astype(F32) + self.bufs[1].astype(F32)).astype(BF)
        self.copies[5].start()

    def total(self, which):
        first, second = ((4, 3), (2, 5))[which]
        self.copies[first].wait_recv()
        self.copies[second].wait_recv()
        return self.bufs[first].astype(F32) + self.bufs[second].astype(F32)

    def sent(self):
        for copy in self.copies:
            copy.wait_send()


def dma(*shape):
    return pltpu.SemaphoreType.DMA(shape)


def ring_gather_flow(array):
    shape = (2, 4) + array.shape

    def steps(ins, outs, scratch):
        (src,), (out,) = ins, outs
        stage, send, recv, pass_send, pass_recv, local = scratch
        me, _ = peers_of("zc")
        core, member = peers_of("c")
        own = pltpu.make_async_copy(src, stage, local.at[0])
        own.start()
        ring = RingGather("zc", lambda g: out.at[core, g], src, send, recv)

        def passing(k):
            g = lax.rem(me + k, 4)
            return remote(src if k == 0 else out.at[core, g], out.at[core, g], pass_send.at[k], pass_recv.at[k], member(1 - core))

        passes = [passing(k) for k in range(4)]
        ring.start()
        passes[0].start()
        yield
        ring.forward()
        own.wait()
        back = pltpu.make_async_copy(stage, out.at[core, me], local.at[0])
        back.start()
        yield
        ring.near()
        passes[1].start()
        passes[3].start()
        yield
        ring.far()
        passes[2].start()
        yield
        back.wait()
        ring.sent()
        for copy in passes:
            copy.wait()

    return Flow(
        [(array, pl.ANY)],
        [(shape, array.dtype, pl.ANY)],
        [pltpu.VMEM(array.shape, array.dtype), dma(6), dma(6), dma(4), dma(4), dma(1)],
        ring_partners("zc") + [("c", 1)],
        steps,
    )


def plane_gather_flow(arrays, first, second, to_core=False, ahead=None):
    dtype = arrays[0][0].dtype
    if ahead == "zhc":
        shard = (4, arrays[0][0].shape[0], sum(columns for _, columns, _ in arrays))
    elif ahead == "z":
        shard = (8,) + arrays[0][0].shape
    else:
        shard = (arrays[0][0].shape[0] // 2,) + arrays[0][0].shape[1:]
    shape = ((2,) if to_core else ()) + (4, 4) + shard
    n_ahead = SIZES[ahead] if ahead else 1

    def steps(ins, outs, scratch):
        (out,) = outs
        stage, send, recv, pass_send, pass_recv, local, ahead_send, ahead_recv = scratch
        core, member = peers_of("c")
        here, _ = peers_of(first)
        there, _ = peers_of(second)
        view = out.at[core] if to_core else out

        def slot(a, b):
            return view.at[b, a] if first == "x" else view.at[a, b]

        if ahead:
            mine, at = peers_of(ahead)

            def parts(to):
                if ahead == "z":
                    return [(ins[0], stage.at[mine])]
                found, begin = [], 0
                for ref, (_, columns, share) in zip(ins, arrays):
                    source = ref.at[:, pl.ds(pl.multiple_of(lax.div(to, share) * columns, columns), columns)]
                    found.append((source, stage.at[mine, :, pl.ds(begin, columns)]))
                    begin += columns
                return found

            early = [pltpu.make_async_copy(source, target, local.at[i]) for i, (source, target) in enumerate(parts(mine))]
            for k in range(1, n_ahead):
                to = lax.rem(mine + k, n_ahead)
                for i, (source, target) in enumerate(parts(to)):
                    early.append(remote(source, target, ahead_send.at[i, k], ahead_recv.at[i, k], at(to)))
            for copy in early:
                copy.start()
            yield
            for copy in early:
                copy.wait()
            src = stage
        else:
            src = ins[0].at[pl.ds(pl.multiple_of(core * shard[0], shard[0]), shard[0])]
            own = pltpu.make_async_copy(src, stage, local.at[0])
            own.start()
        ring = RingGather(first, lambda g: slot(g, there), src, send.at[4], recv.at[4])
        columns = [lax.rem(here + k, 4) for k in range(4)]
        rings = [
            RingGather(second, lambda g, a=a: slot(a, g), src if k == 0 else slot(a, there), send.at[k], recv.at[k])
            for k, a in enumerate(columns)
        ]

        def passing(k, m):
            ref = slot(columns[k], lax.rem(there + m, 4))
            return remote(src if k == m == 0 else ref, ref, pass_send.at[k * 4 + m], pass_recv.at[k * 4 + m], member(1 - core))

        passes = {}

        def hand_over(k, m):
            if to_core:
                passes[k, m] = passing(k, m)
                passes[k, m].start()

        ring.start()
        rings[0].start()
        hand_over(0, 0)
        yield
        ring.forward()
        if not ahead:
            own.wait()
        back = pltpu.make_async_copy(stage, slot(here, there), local.at[0])
        back.start()
        yield
        rings[0].forward()
        yield
        ring.near()
        for k in (1, 3):
            rings[k].start()
            hand_over(k, 0)
        yield
        ring.far()
        rings[2].start()
        hand_over(2, 0)
        yield
        for k in (0, 1, 3, 2):
            if k > 0:
                rings[k].forward()
            rings[k].near()
            hand_over(k, 1)
            hand_over(k, 3)
            yield
            rings[k].far()
            hand_over(k, 2)
            yield
        back.wait()
        ring.sent()
        for one in rings:
            one.sent()
        for copy in passes.values():
            copy.wait()

    return Flow(
        [(array, pl.ANY) for array, *_ in arrays],
        [(shape, dtype, pl.ANY)],
        [pltpu.VMEM(shard, dtype), dma(5, 6), dma(5, 6), dma(16), dma(16), dma(3), dma(3, 8), dma(3, 8)],
        ring_partners("x") + ring_partners("y") + ([("c", 1)] if to_core else []) + [(ahead, k) for k in range(1, n_ahead)],
        steps,
    )


def product_flow(left, right):
    columns, width = left.shape[1], right.shape[1]

    def steps(ins, outs, scratch):
        (out,) = outs
        left_ref, right_ref, local = scratch
        copies = [pltpu.make_async_copy(source, target, local.at[i]) for i, (source, target) in enumerate(zip(ins, (left_ref, right_ref)))]
        for copy in copies:
            copy.start()
        yield
        for copy in copies:
            copy.wait()
        for column in range(0, columns, 256):
            span = slice(column, column + 256)
            out[span, :] = dot_tn(left_ref[:, span], right_ref[...]).astype(BF)
            yield

    return Flow(
        [(left, pl.ANY), (right, pl.ANY)],
        [((columns, width), BF, pltpu.VMEM)],
        [pltpu.VMEM(left.shape, BF), pltpu.VMEM(right.shape, BF), dma(2)],
        [],
        steps,
    )


def output_flow(residual, gates, assign, expert_out):
    own, width = residual.shape
    experts = gates.shape[1]
    count = expert_out.shape[0]

    def steps(ins, outs, scratch):
        residual_ref, gates_ref, assign_ref, expert_hbm = ins
        (out,) = outs
        expert_ref, mixing, local = scratch
        copy = pltpu.make_async_copy(expert_hbm, expert_ref, local.at[0])
        copy.start()
        wide = (experts, count)
        cap = count // experts
        spread = (lax.broadcasted_iota(jnp.int32, wide, 1) // cap == lax.broadcasted_iota(jnp.int32, wide, 0)).astype(F32).astype(BF)
        taken = assign_ref[...].astype(F32)
        high = gates_ref[...].astype(BF)
        low = (gates_ref[...] - high.astype(F32)).astype(BF)
        mixing[0] = (dot_nn(high, spread) * taken).astype(BF)
        mixing[1] = (dot_nn(low, spread) * taken).astype(BF)
        yield
        copy.wait()
        for column in range(0, width, 512):
            span = slice(column, column + 512)
            rows = expert_ref[:, span]
            out[:, span] = (residual_ref[:, span] + dot_nn(mixing[0], rows) + dot_nn(mixing[1], rows)).astype(BF)
            yield

    return Flow(
        [(residual, pltpu.VMEM), (gates, pltpu.VMEM), (assign, pltpu.VMEM), (expert_out, pl.ANY)],
        [(residual.shape, BF, pltpu.VMEM)],
        [pltpu.VMEM(expert_out.shape, BF), pltpu.VMEM((2, own, count), BF), dma(1)],
        [],
        steps,
    )


sum_partners = [("yx", k) for k in range(1, 16)] + [("z", k) for k in range(1, 8)]


def sum_room(shape):
    return [pltpu.VMEM((16,) + shape, F32), pltpu.VMEM((8,) + shape, F32), pltpu.VMEM(shape, F32), dma(16), dma(16), dma(8), dma(8)]


def sum_steps(src, out, scratch):
    wide, far, middle, sends, recvs, far_sends, far_recvs = scratch
    me, member = peers_of("yx")
    copies = []
    for k in range(1, 16):
        copies.append(remote(src, wide.at[me], sends.at[k], recvs.at[k], member(lax.rem(me + k, 16))))
        copies[-1].start()
    wide[me] = src[...]
    yield
    for copy in copies:
        copy.wait()
    middle[...] = jnp.sum(wide[...], axis=0)
    ring, ring_member = peers_of("z")
    late = []
    for k in range(1, 8):
        late.append(remote(middle, far.at[ring], far_sends.at[k], far_recvs.at[k], ring_member(lax.rem(ring + k, 8))))
        late[-1].start()
    far[ring] = middle[...]
    yield
    for copy in late:
        copy.wait()
    out[...] = jnp.sum(far[...], axis=0)


def product_scatter_flow(lefts, right, units=None, gains=None):
    own, wide = lefts[0].shape[0] // 8, right.shape[0]
    spans = [0]
    for left in lefts:
        spans.append(spans[-1] + left.shape[1])

    def steps(ins, outs, scratch):
        left_refs, right_ref, out = ins[: len(lefts)], ins[len(lefts)], outs[0]
        theirs, came, chunks, bufs, send, recv, pass_send, pass_recv, *rest = scratch
        core, member = peers_of("c")
        me, _ = peers_of("zc")
        ring = RingScatter("zc", lambda g: chunks.at[g], bufs, send, recv)

        if units is not None:
            unit_hbm, gains_ref = ins[len(lefts) + 1 :]
            unit_ref, sums, unit_local, *sum_scratch = rest
            unit_copy = pltpu.make_async_copy(unit_hbm, unit_ref, unit_local.at[0])
            unit_copy.start()
            unit_copy.wait()
            sums[...] = gains_ref[...]

        def product(c, k, column):
            row = pl.multiple_of((c * 4 + lax.rem(me + k, 4)) * own, own)
            value = sum(
                dot_nt(left_ref[pl.ds(row, own), :], right_ref[column : column + 512, spans[i] : spans[i + 1]])
                for i, left_ref in enumerate(left_refs)
            )
            if units is not None:
                row_sum = jnp.sum(value * unit_ref[pl.ds(row, own), column : column + 512].astype(F32), axis=0, keepdims=True)
                for lane in range(0, 512, 128):
                    at = (column + lane) // 128
                    sums[at : at + 1, :] += row_sum[:, lane : lane + 128]
            return value

        passes = [
            remote(theirs.at[k], came.at[k], pass_send.at[k], pass_recv.at[k], member(1 - core)) for k in range(4)
        ]
        for k in (2, 1, 3, 0):
            for column in range(0, wide, 512):
                theirs[k, :, column : column + 512] = product(1 - core, k, column).astype(BF)
            passes[k].start()
            yield
        for k in (2, 1, 3, 0):
            passes[k].wait_recv()
            g = lax.rem(me + k, 4)
            for column in range(0, wide, 512):
                span = slice(column, column + 512)
                value = product(core, k, column) + came[k, :, span].astype(F32)
                if k == 0:
                    out[:, span] = value
                else:
                    chunks[g, :, span] = value.astype(BF)
            if k == 2:
                ring.start_far()
            elif k == 1:
                ring.start_up()
            elif k == 3:
                ring.start_down()
            yield
        if units is not None:
            yield sum_steps(sums, outs[1], sum_scratch)
        ring.add()
        yield
        for h in range(2):
            rows = slice(h * own // 2, (h + 1) * own // 2)
            out[rows, :] += ring.total(h)
        yield
        ring.sent()
        for copy in passes:
            copy.wait_send()

    return Flow(
        [(x, pltpu.VMEM) for x in (*lefts, right)] + ([] if units is None else [(units, pl.ANY), (gains, pltpu.VMEM)]),
        [((own, wide), F32, pltpu.VMEM)] + ([] if units is None else [(gains.shape, F32, pltpu.VMEM)]),
        [
            pltpu.VMEM((4, own, wide), BF),
            pltpu.VMEM((4, own, wide), BF),
            pltpu.VMEM((4, own, wide), BF),
            pltpu.VMEM((8, own // 2, wide), BF),
            dma(6),
            dma(6),
            dma(4),
            dma(4),
        ]
        + ([] if units is None else [pltpu.VMEM(units.shape, BF), pltpu.VMEM(gains.shape, F32), dma(1)] + sum_room(gains.shape)),
        ring_partners("zc") + [("c", 1)] + ([] if units is None else sum_partners),
        steps,
    )


def plane_scatter_flow(array, first, second, from_core=False, last_in=None):
    rows, columns = array.shape[-2:]
    n_last = SIZES[last_in] if last_in else 1
    result = (n_last, rows // 4, columns) if last_in else (rows, columns)

    def steps(ins, outs, scratch):
        (src,), (out,) = ins, outs
        came, sums, middle, bufs, late_bufs, send, recv, late_send, late_recv, pass_send, pass_recv, local, cut, cut_send, cut_recv = scratch
        core, member = peers_of("c")
        me, _ = peers_of(first)

        def along(ref, g):
            return ref.at[g] if first == "y" else ref.at[:, g]

        ring = RingScatter(first, lambda g: along(sums, g), bufs, send, recv)
        order = [lax.rem(me + k, 4) for k in (2, 1, 3, 0)]
        starts = [ring.start_far, ring.start_up, ring.start_down, lambda: None]
        passes, loads = [], []
        for i, g in enumerate(order):
            if from_core:
                passes.append(
                    remote(along(src.at[1 - core], g), along(came, g), pass_send.at[i], pass_recv.at[i], member(1 - core))
                )
                passes[i].start()
            loads.append(pltpu.make_async_copy(along(src.at[core] if from_core else src, g), along(sums, g), local.at[i]))
            loads[i].start()
        yield
        for i, g in enumerate(order):
            loads[i].wait()
            if from_core:
                passes[i].wait_recv()
                for k in range(4):
                    total = along(sums, g)[k].astype(F32) + along(came, g)[k].astype(F32)
                    along(sums, g)[k] = total.astype(BF)
            starts[i]()
            yield
        ring.add()
        yield
        own = along(sums, me)
        for h in range(2):
            came_half = ring.total(h)
            for k in range(2):
                middle[h * 2 + k] = (own[h * 2 + k].astype(F32) + came_half[k]).astype(BF)
        yield
        last = RingScatter(second, lambda g: middle.at[g], late_bufs, late_send, late_recv)
        last.start_far()
        last.start_up()
        last.start_down()
        yield
        last.add()
        yield
        for h in range(2):
            total = (piece(middle.at[last.me], h)[...].astype(F32) + last.total(h)).astype(BF)
            if last_in:
                cut[2 * h] = total[: rows // 4]
                cut[2 * h + 1] = total[rows // 4 :]
            else:
                out[h * rows // 2 : (h + 1) * rows // 2, :] = total
        cuts = []
        if last_in:
            mine, at = peers_of(last_in)
            share = n_last // 4
            for k in range(1, n_last):
                to = lax.rem(mine + k, n_last)
                cuts.append(remote(cut.at[lax.div(to, share)], out.at[mine], cut_send.at[k], cut_recv.at[k], at(to)))
                cuts[-1].start()
            out[mine] = cut[lax.div(mine, share)]
        yield
        ring.sent()
        last.sent()
        for copy in passes:
            copy.wait_send()
        for copy in cuts:
            copy.wait()

    block = (4, 4, rows, columns)
    return Flow(
        [(array, pl.ANY)],
        [(result, BF, pltpu.VMEM)],
        [
            pltpu.VMEM(block if from_core else (8, 128), BF),
            pltpu.VMEM(block, BF),
            pltpu.VMEM((4, rows, columns), BF),
            pltpu.VMEM((8, 2, rows, columns), BF),
            pltpu.VMEM((8, rows // 2, columns), BF),
            dma(6),
            dma(6),
            dma(6),
            dma(6),
            dma(4),
            dma(4),
            dma(4),
            pltpu.VMEM((4, rows // 4, columns), BF),
            dma(8),
            dma(8),
        ],
        ring_partners("x")
        + ring_partners("y")
        + ([("c", 1)] if from_core else [])
        + [(last_in, k) for k in range(1, n_last)],
        steps,
    )


def tables_flow(routes, offsets, spacing, experts, cap):
    own, top = routes.shape
    rows, size = offsets.shape[0], spacing.shape[1]

    def steps(ins, outs, scratch):
        routes_ref, offsets_ref, spacing_ref = ins
        assign, chosen_ref, cosine, sine = outs
        lane = lax.broadcasted_iota(jnp.int32, (own, experts), 1)
        chosen = jnp.zeros((own, experts), F32)
        for k in range(top):
            chosen += (routes_ref[:, k : k + 1] == lane).astype(F32)
        chosen_ref[...] = chosen
        before = lax.broadcasted_iota(jnp.int32, (own, own), 0) > lax.broadcasted_iota(jnp.int32, (own, own), 1)
        earlier = dot_nn(before.astype(F32).astype(BF), chosen.astype(BF))
        wide = (experts, experts * cap)
        spread = (lax.broadcasted_iota(jnp.int32, wide, 1) // cap == lax.broadcasted_iota(jnp.int32, wide, 0)).astype(F32).astype(BF)
        slot = lax.rem(lax.broadcasted_iota(jnp.int32, (own, experts * cap), 1), cap).astype(F32)
        taken = (dot_nn(chosen.astype(BF), spread) > 0.5) & (dot_nn(earlier.astype(BF), spread) == slot)
        assign[...] = taken.astype(F32).astype(BF)
        yield
        sign = jnp.where(lax.broadcasted_iota(jnp.int32, (1, size), 1) < size // 2, -1.0, 1.0)
        for row in range(0, rows, BLOCK):
            span = slice(row, row + BLOCK)
            angles = offsets_ref[span, :] * spacing_ref[...]
            cosine[span, :] = jnp.cos(angles)
            sine[span, :] = jnp.sin(angles) * sign
            yield

    return Flow(
        [(routes, pltpu.VMEM), (offsets, pltpu.VMEM), (spacing, pltpu.VMEM)],
        [
            ((own, experts * cap), BF, pltpu.VMEM),
            ((own, experts), F32, pltpu.VMEM),
            ((rows, size), F32, pltpu.VMEM),
            ((rows, size), F32, pltpu.VMEM),
        ],
        [],
        [],
        steps,
    )


def add_up(stacked):
    return jnp.sum(stacked.astype(F32), axis=0)


def dot_nn(a, b):
    return lax.dot_general(a, b, (((1,), (0,)), ((), ())), preferred_element_type=F32)


def dot_nt(a, b):
    return lax.dot_general(a, b, (((1,), (1,)), ((), ())), preferred_element_type=F32)


def dot_tn(a, b):
    return lax.dot_general(a, b, (((0,), (0,)), ((), ())), preferred_element_type=F32)


def norm_rope(raw, gain, cosine, sine):
    unit = raw * lax.rsqrt(jnp.mean(raw * raw, axis=-1, keepdims=True) + EPS)
    scaled = unit * gain
    return scaled * cosine + pltpu.roll(scaled, 64, 1) * sine


def norm_rope_back(grad, raw, gain, cosine, sine):
    inverse = lax.rsqrt(jnp.mean(raw * raw, axis=-1, keepdims=True) + EPS)
    unit = raw * inverse
    turned = grad * cosine + pltpu.roll(grad * sine, 64, 1)
    scaled = turned * gain
    return inverse * (scaled - unit * jnp.mean(scaled * unit, axis=-1, keepdims=True)), turned * unit


def project_kernel(rows_ref, w_ref, gain_ref, cos_ref, sin_ref, q_ref, raw_ref, k_ref, v_ref):
    wide, size = q_ref.shape[1], k_ref.shape[1]
    product = dot_nn(rows_ref[...], w_ref[...])
    q_ref[...] = product[:, :wide]
    raw = product[:, wide : wide + size]
    raw_ref[...] = raw
    k_ref[...] = norm_rope(raw, gain_ref[...], cos_ref[...], sin_ref[...]).astype(BF)
    v_ref[...] = product[:, wide + size :].astype(BF)


def key_back_kernel(dk_ref, dv_ref, raw_ref, gain_ref, cos_ref, sin_ref, rows_hbm, out_ref, w_ref, sum_ref, rows_ref, local):
    half, size = dk_ref.shape
    core, _ = peers_of("c")
    rows = pl.ds(pl.multiple_of(core * half, half), half)
    copy = pltpu.make_async_copy(rows_hbm.at[rows], rows_ref, local.at[0])
    copy.start()
    grad = dk_ref[...].astype(F32)
    grad_raw, grad_gain = norm_rope_back(grad, raw_ref[rows, :], gain_ref[...], cos_ref[rows, :], sin_ref[rows, :])
    out_ref[...] = jnp.zeros_like(out_ref)
    out_ref[rows, :size] = grad_raw.astype(BF)
    out_ref[rows, size:] = dv_ref[...]
    sum_ref[...] = jnp.sum(grad_gain, axis=0, keepdims=True)
    copy.wait()
    for column in range(0, rows_ref.shape[1], 256):
        span = slice(column, column + 256)
        w_ref[span, :] = dot_tn(rows_ref[:, span], out_ref[rows, :]).astype(BF)


def expert_kernel(rows_ref, plain_ref, w_ref, back_ref, hidden_ref, gated_ref, both_ref):
    width, ff = w_ref.shape[0], plain_ref.shape[1]
    own = lax.axis_index("head") * lax.axis_size("blk") + lax.axis_index("blk")
    gates = rows_ref[:, width:].astype(F32)
    lane = lax.broadcasted_iota(jnp.int32, gates.shape, 1)
    gate = jnp.sum(jnp.where(lane == own, gates, 0.0), axis=1, keepdims=True)
    gate_up = dot_nn(rows_ref[:, :width], w_ref[...])
    first, up = gate_up[:, :ff], gate_up[:, ff:]
    sigma = 1.0 / (1.0 + jnp.exp(-first))
    silu = first * sigma
    hidden = silu * up
    hidden_ref[...] = hidden.astype(BF)
    gated_ref[...] = (hidden * gate).astype(BF)
    plain = plain_ref[...]
    gate_grad = jnp.sum(hidden * plain, axis=1, keepdims=True)
    grad = plain * gate
    both_ref[:, :ff] = (grad * up * (sigma * (1.0 + first * (1.0 - sigma)))).astype(BF)
    both_ref[:, ff:] = (grad * silu).astype(BF)
    back_ref[:, :width] = dot_nt(both_ref[...], w_ref[...]).astype(BF)
    high = gate_grad.astype(BF).astype(F32)
    back_ref[:, width:] = jnp.where(lane == 0, high, jnp.where(lane == 1, gate_grad - high, 0.0)).astype(BF)


def key_tiles(lo, full, last, tile):
    middle = jnp.minimum(full, last)
    pl.loop(lo, middle)(lambda t: tile(t, True))
    pl.loop(middle, last)(lambda t: tile(t, False))
    tile(last, True)


def allowed_pairs(t, last, start, shape):
    key_place = t * BLOCK + lax.broadcasted_iota(jnp.int32, shape, 0)
    query_place = last * BLOCK + lax.rem(lax.broadcasted_iota(jnp.int32, shape, 1), BLOCK)
    return (key_place >= start) & (key_place <= query_place)


def attend_forward_kernel(
    lo_ref, full_ref, last_ref, slot_ref, raw_ref, gain_ref, cos_ref, sin_ref, k_ref, v_ref, start_ref, q_ref, o_ref, log_ref, q_t, acc, total
):
    j = pl.program_id(0)
    size = k_ref.shape[2]
    heads = raw_ref.shape[1] // size
    scale = size**-0.5 * LOG2E
    last = last_ref[j]
    for n in range(heads):
        span = slice(n * size, (n + 1) * size)
        query = norm_rope(raw_ref[:, span], gain_ref[...], cos_ref[...], sin_ref[...])
        q_ref[:, span] = query.astype(BF)
        q_t[:, n * BLOCK : (n + 1) * BLOCK] = query.T.astype(BF)
    acc[...] = jnp.zeros_like(acc)
    total[...] = jnp.zeros_like(total)
    start = start_ref[0]

    def tile(t, masked):
        slot = slot_ref[t]
        weights = jnp.exp2(dot_nn(k_ref[slot], q_t[...]) * scale)
        if masked:
            weights = jnp.where(allowed_pairs(t, last, start, weights.shape), weights, 0.0)
        total[...] += jnp.sum(weights.reshape(BLOCK // 8, 8, heads * BLOCK), axis=0)
        acc[...] += dot_nn(v_ref[slot].T, weights.astype(BF))

    key_tiles(lo_ref[j], full_ref[j], last, tile)
    row = jnp.sum(total[...], axis=0, keepdims=True)
    log_ref[0] = jnp.log2(row)
    out = acc[...] / row
    for n in range(heads):
        o_ref[:, n * size : (n + 1) * size] = out[:, n * BLOCK : (n + 1) * BLOCK].T.astype(BF)


def attend_backward_kernel(
    lo_ref,
    full_ref,
    last_ref,
    slot_ref,
    raw_ref,
    gain_ref,
    cos_ref,
    sin_ref,
    k_ref,
    v_ref,
    start_ref,
    q_ref,
    o_ref,
    g_ref,
    w_ref,
    log_ref,
    dq_ref,
    sum_ref,
    dk_ref,
    dv_ref,
    queries,
    q_t,
    grads,
    g_t,
    delta,
    acc,
    dk,
    dv,
    keys_ref,
    values_ref,
    local,
):
    j = pl.program_id(0)
    slots, _, size = keys_ref.shape
    takes = [pltpu.make_async_copy(k_ref, keys_ref, local.at[0]), pltpu.make_async_copy(v_ref, values_ref, local.at[1])]
    heads = raw_ref.shape[1] // size
    scale = size**-0.5
    last = last_ref[j]

    @pl.when(j == 0)
    def _():
        for copy in takes:
            copy.start()
        sum_ref[...] = jnp.zeros_like(sum_ref)

        @pl.loop(0, slots)
        def _(s):
            dk[s] = jnp.zeros(dk.shape[1:], F32)
            dv[s] = jnp.zeros(dv.shape[1:], F32)

    attended_grad = dot_nn(g_ref[...], w_ref[...]).astype(BF)
    for n in range(heads):
        span, rows = slice(n * size, (n + 1) * size), slice(n * BLOCK, (n + 1) * BLOCK)
        queries[rows, :] = q_ref[:, span]
        q_t[:, rows] = q_ref[:, span].T
        grads[rows, :] = attended_grad[:, span]
        grad_t = attended_grad[:, span].T
        g_t[:, rows] = grad_t
        delta[:, rows] = jnp.sum(grad_t.astype(F32) * o_ref[:, span].T.astype(F32), axis=0, keepdims=True)
    acc[...] = jnp.zeros_like(acc)
    start = start_ref[0]
    logs = log_ref[0]

    @pl.when(j == 0)
    def _():
        for copy in takes:
            copy.wait()

    def tile(t, masked):
        slot = slot_ref[t]
        keys = keys_ref[slot]
        probs = jnp.exp2(dot_nn(keys, q_t[...]) * (scale * LOG2E) - logs)
        if masked:
            probs = jnp.where(allowed_pairs(t, last, start, probs.shape), probs, 0.0)
        grad_scores = (probs * (dot_nn(values_ref[slot], g_t[...]) - delta[...])).astype(BF)
        dv[slot] += dot_nn(probs.astype(BF), grads[...])
        dk[slot] += dot_nn(grad_scores, queries[...])
        acc[...] += dot_nn(keys.T, grad_scores)

    key_tiles(lo_ref[j], full_ref[j], last, tile)
    for n in range(heads):
        span = slice(n * size, (n + 1) * size)
        grad = (acc[:, n * BLOCK : (n + 1) * BLOCK] * scale).T.astype(BF).astype(F32)
        grad_raw, grad_gain = norm_rope_back(grad, raw_ref[:, span], gain_ref[...], cos_ref[...], sin_ref[...])
        dq_ref[:, span] = grad_raw.astype(BF)
        sum_ref[...] += jnp.sum(grad_gain, axis=0, keepdims=True)

    @pl.when(j == pl.num_programs(0) - 1)
    def _():
        def out(s, n):
            span = pl.ds(s, n)
            return (
                pltpu.make_async_copy(keys_ref.at[span], dk_ref.at[span], local.at[0]),
                pltpu.make_async_copy(values_ref.at[span], dv_ref.at[span], local.at[1]),
            )

        @pl.loop(0, slots, step=8)
        def _(s):
            for i in range(8):
                keys_ref[s + i] = (dk[s + i] * scale).astype(BF)
                values_ref[s + i] = dv[s + i].astype(BF)
            for copy in out(s, 8):
                copy.start()

        for copy in out(0, slots):
            copy.wait()


def by_rows(array, rows=BLOCK):
    return pl.BlockSpec((rows,) + array.shape[1:], lambda j, *_: (j,) + (0,) * (array.ndim - 1))


def resident(array):
    return pl.BlockSpec(array.shape, lambda j, *_: (0,) * array.ndim, pipeline_mode=pl.Buffered(1))


def shaped(shape, dtype):
    return jax.ShapeDtypeStruct(shape, dtype)


def project(rows, weights, gain, cosine, sine, q_cols):
    size = gain.shape[1]
    outs = (shaped((rows.shape[0], q_cols), F32), shaped((rows.shape[0], size), F32)) + (shaped((rows.shape[0], size), BF),) * 2
    return pl.pallas_call(
        project_kernel,
        out_shape=outs,
        grid=(rows.shape[0] // BLOCK,),
        in_specs=[by_rows(rows), resident(weights), resident(gain), by_rows(cosine), by_rows(sine)],
        out_specs=tuple(by_rows(x) for x in outs),
        compiler_params=pltpu.CompilerParams(vmem_limit_bytes=VMEM_LIMIT),
        cost_estimate=cost_of(6),
        name="project",
    )(rows, weights, gain, cosine, sine)


def key_back(grad_key, grad_value, raw, gain, cosine, sine, group):
    rows, size = raw.shape
    width = group.shape[1]
    whole = pl.BlockSpec(memory_space=pltpu.VMEM)
    return pl.pallas_call(
        key_back_kernel,
        out_shape=(shaped((rows, 2 * size), BF), shaped((width, 2 * size), BF), shaped((1, size), F32)),
        in_specs=[whole] * 6 + [pl.BlockSpec(memory_space=pl.ANY)],
        out_specs=(whole,) * 3,
        scratch_shapes=[pltpu.VMEM((rows // 2, width), BF), dma(1)],
        compiler_params=pltpu.CompilerParams(vmem_limit_bytes=VMEM_LIMIT),
        cost_estimate=cost_of(4),
        name="key_back",
    )(grad_key, grad_value, raw, gain, cosine, sine, group)


def expert(rows, plain, weights, block=512):
    count, ff = plain.shape
    outs = (shaped(rows.shape, BF), shaped((count, ff), BF), shaped((count, ff), BF), shaped((count, 2 * ff), BF))
    return pl.pallas_call(
        expert_kernel,
        out_shape=outs,
        grid=(count // block,),
        in_specs=[by_rows(rows, block), by_rows(plain, block), resident(weights)],
        out_specs=tuple(by_rows(x, block) for x in outs),
        compiler_params=pltpu.CompilerParams(vmem_limit_bytes=VMEM_LIMIT),
        cost_estimate=cost_of(20),
        name="expert",
    )(rows, plain, weights)


def attend_forward(meta, raw, gain, cosine, sine, keys, values, start):
    rows, wide = raw.shape
    blocks, size = rows // BLOCK, keys.shape[2]
    lanes = wide // size * BLOCK
    outs = (shaped((rows, wide), BF), shaped((rows, wide), BF), shaped((blocks, 1, lanes), F32))
    return pl.pallas_call(
        attend_forward_kernel,
        out_shape=outs,
        grid_spec=pltpu.PrefetchScalarGridSpec(
            num_scalar_prefetch=4,
            grid=(blocks,),
            in_specs=[
                by_rows(raw),
                resident(gain),
                by_rows(cosine),
                by_rows(sine),
                resident(keys),
                resident(values),
                by_rows(start, 1),
            ],
            out_specs=(by_rows(outs[0]), by_rows(outs[1]), by_rows(outs[2], 1)),
            scratch_shapes=[pltpu.VMEM((size, lanes), BF), pltpu.VMEM((size, lanes), F32), pltpu.VMEM((8, lanes), F32)],
        ),
        compiler_params=pltpu.CompilerParams(vmem_limit_bytes=VMEM_LIMIT),
        cost_estimate=cost_of(30),
        name="attend",
    )(*meta, raw, gain, cosine, sine, keys, values, start)


def attend_backward(meta, raw, gain, cosine, sine, keys, values, start, queries, attended, grads, w_out_t, logs):
    rows, wide = raw.shape
    blocks, size = rows // BLOCK, keys.shape[2]
    lanes = wide // size * BLOCK
    outs = (shaped((rows, wide), BF), shaped((1, size), F32), shaped(keys.shape, BF), shaped(values.shape, BF))
    return pl.pallas_call(
        attend_backward_kernel,
        out_shape=outs,
        grid_spec=pltpu.PrefetchScalarGridSpec(
            num_scalar_prefetch=4,
            grid=(blocks,),
            in_specs=[
                by_rows(raw),
                resident(gain),
                by_rows(cosine),
                by_rows(sine),
                pl.BlockSpec(memory_space=pl.ANY),
                pl.BlockSpec(memory_space=pl.ANY),
                by_rows(start, 1),
                by_rows(queries),
                by_rows(attended),
                by_rows(grads),
                resident(w_out_t),
                by_rows(logs, 1),
            ],
            out_specs=(by_rows(outs[0]), resident(outs[1])) + (pl.BlockSpec(memory_space=pl.ANY),) * 2,
            scratch_shapes=[
                pltpu.VMEM((lanes, size), BF),
                pltpu.VMEM((size, lanes), BF),
                pltpu.VMEM((lanes, size), BF),
                pltpu.VMEM((size, lanes), BF),
                pltpu.VMEM((1, lanes), F32),
                pltpu.VMEM((size, lanes), F32),
                pltpu.VMEM(keys.shape, F32),
                pltpu.VMEM(values.shape, F32),
                pltpu.VMEM(keys.shape, BF),
                pltpu.VMEM(values.shape, BF),
                dma(2),
            ],
        ),
        compiler_params=pltpu.CompilerParams(vmem_limit_bytes=VMEM_LIMIT),
        cost_estimate=cost_of(40),
        name="attend_back",
    )(*meta, raw, gain, cosine, sine, keys, values, start, queries, attended, grads, w_out_t, logs)


def rms_scale(values, gain_vec):
    return values * lax.rsqrt(jnp.mean(values * values, axis=-1, keepdims=True) + EPS) * gain_vec


def two_parts(wide):
    high = wide.astype(BF)
    return high, (wide - high.astype(F32)).astype(BF)


def all_to_all(stacked):
    return lax.all_to_all(stacked, ("head", "blk"), split_axis=0, concat_axis=0, tiled=True)


def body(
    tokens,
    norm_gain,
    w_query,
    key_weight,
    value_weight,
    query_gain,
    key_gain,
    w_out,
    mix_gain,
    w_router,
    expert_gate_up,
    expert_down,
    lengths,
    block_deal,
    routes,
    cotangent,
):
    own, width = tokens.shape
    size = query_gain.shape[0]
    scale = size ** (-0.5)
    blk = lax.axis_index("blk")
    plane, core = blk // 4, blk % 2
    devices = lax.axis_size("head") * lax.axis_size("blk")
    experts = w_router.shape[0] * 2
    cap = own * routes.shape[1] // experts
    gate_up, down = expert_gate_up[0], expert_down[0]
    ff = down.shape[0]
    group_rows = 8 * own
    q_cols = w_query.shape[1] // 4
    heads = q_cols // size

    group_blocks = plane * 4 + jnp.array([0, 2, 1, 3], jnp.int32)
    ids = jnp.arange(block_deal.shape[0], dtype=jnp.int32)
    last = jnp.sum(jnp.where(group_blocks[:, None] == ids[None, :], block_deal[None, :], 0), axis=1)
    slots = (ids % 2) * (ids.shape[0] // 2) + (ids // 4) * 2 + (ids % 4) // 2
    slot_of = jnp.sum(jnp.where(block_deal[None, :] == ids[:, None], slots[None, :], 0), axis=1)
    place = (last[:, None] * BLOCK + jnp.arange(BLOCK, dtype=jnp.int32)[None, :]).reshape(-1)
    passed = place[:, None] >= jnp.cumsum(lengths)[None, :]
    start = jnp.sum(jnp.where(passed, lengths[None, :], 0), axis=1)
    start_rows = start.reshape(-1, 1, BLOCK)
    meta = (start_rows[:, 0, 0] // BLOCK, (start_rows[:, 0, BLOCK - 1] + BLOCK - 1) // BLOCK, last, slot_of)
    start_rows = jnp.tile(start_rows, (1, 1, heads))
    offsets = (place - start).astype(F32)[:, None]
    spacing = ROPE_BASE ** (-2.0 * jnp.arange(size // 2, dtype=F32) / size)
    spacing = jnp.concatenate([spacing, spacing])[None]

    wide = tokens.astype(F32)
    normed, norm_back = jax.vjp(rms_scale, wide, norm_gain)
    normed_low = normed.astype(BF)
    depth = w_query.shape[0]
    out_pack = w_out.reshape(4, q_cols, depth).transpose(2, 0, 1).reshape(depth, -1)
    side = lax.axis_index("head") == jnp.arange(2, dtype=jnp.int32)
    router_pack = jnp.where(side[None, :, None], w_router.T[:, None, :], 0).astype(BF).reshape(depth, experts)
    w_qkv, w_out_t, w_router_t, group_tokens, assign_low, chosen, cosine, sine = launch(
        [
            plane_gather_flow([(w_query, q_cols, 1), (key_weight, size, 2), (value_weight, size, 2)], "x", "y", ahead="zhc"),
            plane_gather_flow([(out_pack, q_cols, 1)], "y", "x", ahead="zhc"),
            plane_gather_flow([(router_pack, experts, 1)], "y", "x", ahead="z"),
            ring_gather_flow(normed_low),
            tables_flow(routes, offsets, spacing, experts, cap),
        ],
        0,
        45,
    )
    normed_group = group_tokens.reshape(group_rows, width)
    w_qkv, w_out_t = w_qkv.reshape(width, -1), w_out_t.reshape(width, -1)
    w_router_t = jnp.sum(w_router_t.reshape(-1, 2, depth, experts), axis=1).reshape(width, experts)

    q_gain, k_gain = query_gain[None], key_gain[None]
    q_raw, k_raw, keys, values = project(normed_group, w_qkv, k_gain, cosine, sine, q_cols)
    keys, values, grad_rows = launch(
        [
            plane_gather_flow([(keys, size, 1)], "x", "y", to_core=True),
            plane_gather_flow([(values, size, 1)], "y", "x", to_core=True),
            product_flow(assign_low, cotangent),
        ],
        1,
        30,
    )
    grad_rows = all_to_all(grad_rows.reshape(devices, cap, width)).reshape(-1, width)
    keys, values = keys.reshape(-1, BLOCK, size), values.reshape(-1, BLOCK, size)
    queries, attended, logs = attend_forward(meta, q_raw, q_gain, cosine, sine, keys, values, start_rows)

    residual = wide + launch([product_scatter_flow([attended], w_out_t)], 2, 25)[0]
    mixed, mix_back = jax.vjp(rms_scale, residual, mix_gain)
    mixed_low, grad_rows = lax.optimization_barrier((mixed.astype(BF), grad_rows))
    logits = dot_nn(mixed_low, w_router_t)
    gates = jax.nn.softmax(jnp.where(chosen > 0, logits, -1e30), axis=-1)
    outgoing = dot_tn(assign_low, jnp.concatenate([mixed_low, gates.astype(BF)], axis=1)).astype(BF)
    arrived = all_to_all(outgoing.reshape(devices, cap, -1)).reshape(experts * cap, -1)

    plain_grad = lax.optimization_barrier(dot_nt(grad_rows, down))
    rows, plain_grad = lax.optimization_barrier((arrived, plain_grad))
    back, hidden, gated, grad_both = expert(rows, plain_grad, gate_up)
    back = all_to_all(back.reshape(devices, cap, -1)).reshape(experts * cap, -1)
    back, expert_out = lax.optimization_barrier((back, dot_nn(hidden, down).astype(BF)))
    grad_down = dot_tn(gated, grad_rows)
    grad_gate_up = dot_tn(rows[:, :width], grad_both)

    spread = jnp.arange(experts * cap, dtype=jnp.int32)[:, None] // cap == jnp.arange(experts, dtype=jnp.int32)[None, :]
    high, low = two_parts(jnp.where(spread, jnp.sum(back[:, width : width + 2].astype(F32), axis=1, keepdims=True), 0.0))
    gate_grads = dot_nn(assign_low, high) + dot_nn(assign_low, low)
    grad_logits = (gates * (gate_grads - jnp.sum(gates * gate_grads, axis=1, keepdims=True))).astype(BF)
    grad_mixed = dot_nn(assign_low, back[:, :width]) + dot_nt(grad_logits, w_router_t)
    grad_router_t = dot_tn(mixed_low, grad_logits)
    grad_from_mix, grad_mix_gain = mix_back(grad_mixed)
    grad_residual = cotangent.astype(F32) + grad_from_mix
    grad_group = launch([ring_gather_flow(grad_residual.astype(BF))], 3, 20)[0].reshape(group_rows, width)
    grad_group, expert_out = lax.optimization_barrier((grad_group, expert_out))
    expert_out = all_to_all(expert_out.reshape(devices, cap, width)).reshape(-1, width)
    grad_q, grad_query_gain, grad_keys, grad_values = attend_backward(
        meta, q_raw, q_gain, cosine, sine, keys, values, start_rows, queries, attended, grad_group, w_out_t, logs
    )

    split = (2, 4, 4, group_rows // 2, size)
    grad_key, grad_value, grad_wq, grad_wo = launch(
        [
            plane_scatter_flow(grad_keys.reshape(split), "y", "x", from_core=True),
            plane_scatter_flow(grad_values.reshape(split), "x", "y", from_core=True),
            product_flow(normed_group, grad_q),
            product_flow(grad_group, attended),
        ],
        4,
        35,
    )
    grad_kv, grad_wkv, grad_key_gain = key_back(grad_key, grad_value, k_raw, k_gain, cosine, sine, normed_group)

    grad_kv, expert_out = lax.optimization_barrier((grad_kv, expert_out))
    plane_split = (4, 4, 4 * depth, -1)
    gains = jnp.concatenate([jnp.zeros((width,), F32), grad_mix_gain, grad_query_gain[0], grad_key_gain[0], jnp.zeros((6 * size,), F32)])
    grad_normed, gains, grad_wq, grad_wkv, grad_wo, grad_wr, output = launch(
        [
            product_scatter_flow([grad_q, grad_kv], w_qkv, normed_group, gains.reshape(-1, size)),
            plane_scatter_flow(grad_wq.reshape(plane_split), "y", "x", last_in="zhc"),
            plane_scatter_flow(grad_wkv.reshape(plane_split), "y", "x", last_in="zhc"),
            plane_scatter_flow(grad_wo.reshape(plane_split), "x", "y", last_in="zhc"),
            plane_scatter_flow(grad_router_t.astype(BF).reshape(plane_split), "x", "y", last_in="z"),
            output_flow(residual, gates, assign_low, expert_out),
        ],
        5,
        45,
    )
    grad_from_norm = norm_back(grad_normed)[0]
    grad_tokens = grad_residual + grad_from_norm
    gains = gains.reshape(-1)
    grad_w_query = grad_wq.astype(F32).transpose(1, 0, 2).reshape(depth, -1)
    grad_kv_w = jnp.sum(grad_wkv.astype(F32).reshape(2, 2, depth, 2, size), axis=1)
    grad_w_key = grad_kv_w[:, :, 0].transpose(1, 0, 2).reshape(depth, -1)
    grad_w_value = grad_kv_w[:, :, 1].transpose(1, 0, 2).reshape(depth, -1)
    grad_w_out = grad_wo.astype(F32).transpose(0, 2, 1).reshape(-1, depth)
    grad_w_router = lax.dynamic_slice_in_dim(add_up(grad_wr), lax.axis_index("head") * (experts // 2), experts // 2, 1).T
    return (
        output,
        grad_tokens,
        gains[:width] / norm_gain,
        grad_w_query,
        grad_w_key,
        grad_w_value,
        gains[2 * width : 2 * width + size],
        gains[2 * width + size : 2 * width + 2 * size],
        grad_w_out,
        gains[width : 2 * width],
        grad_w_router,
        grad_gate_up[None],
        grad_down[None],
    )


def solution(mesh):
    rows, both = P(("head", "blk"), None), P("blk", "head")
    expert, turned = P(("head", "blk"), None, None), P("head", "blk")
    in_specs = (rows, P(), both, both, both, P(), P(), turned, P(), turned, expert, expert, P(), P(), rows, rows)
    out_specs = (rows, rows, P(), both, both, both, P(), P(), turned, P(), turned, expert, expert)
    return jax.shard_map(body, mesh=mesh, in_specs=in_specs, out_specs=out_specs, check_vma=False)
```

```python
import jax
import jax.numpy as jnp
from jax import lax
from jax.experimental import pallas as pl
from jax.experimental.pallas import tpu as pltpu
from jax.sharding import PartitionSpec as P

MESH = pl.DeviceIdType.MESH
EPS = 1e-06
ROPE_BASE = 1000000.0
LOG2E = 1.4426950408889634
BF = jnp.bfloat16
F32 = jnp.float32
BLOCK = 256
VMEM_LIMIT = 60 << 20
SIZES = {"zc": 4, "c": 2, "x": 4, "y": 4, "zhc": 4, "z": 8, "yx": 16}


def peers_of(kind):
    h = lax.axis_index("head")
    b = lax.axis_index("blk")
    q, r = lax.div(b, 4), lax.rem(b, 4)
    if kind == "zc":
        return lax.div(r, 2) * 2 + h, lambda g: (lax.rem(g, 2), q * 4 + lax.div(g, 2) * 2 + lax.rem(r, 2))
    if kind == "z":
        return r * 2 + h, lambda g: (lax.rem(g, 2), q * 4 + lax.div(g, 2))
    if kind == "c":
        return lax.rem(b, 2), lambda g: (h, b - lax.rem(b, 2) + g)
    if kind == "x":
        return lax.rem(q, 4), lambda g: (h, (lax.div(q, 4) * 4 + g) * 4 + r)
    if kind == "y":
        return lax.div(q, 4), lambda g: (h, (g * 4 + lax.rem(q, 4)) * 4 + r)
    if kind == "yx":
        return q, lambda g: (h, g * 4 + r)
    return r, lambda g: (h, q * 4 + g)


def cost_of(microseconds):
    return pl.CostEstimate(flops=microseconds * 10**9, bytes_accessed=microseconds * 3 * 10**6, transcendentals=0)


class Flow:
    def __init__(self, inputs, outputs, scratch, partners, steps):
        self.inputs, self.outputs, self.scratch = inputs, outputs, scratch
        self.partners, self.steps = partners, steps


class Made:
    def __init__(self, *shape):
        self.shape, self.ref = shape, None


def launch(flows, cid, cost):
    partners = sorted({p for flow in flows for p in flow.partners})

    def kernel(*refs):
        n_in, n_out = sum(len(f.inputs) for f in flows), sum(len(f.outputs) for f in flows)
        ins, outs, rest = list(refs[:n_in]), list(refs[n_in : n_in + n_out]), list(refs[n_in + n_out :])
        barrier = pltpu.get_barrier_semaphore()
        for kind, distance in partners:
            me, member = peers_of(kind)
            to = member(lax.rem(me + distance, SIZES[kind]))
            pl.semaphore_signal(barrier, inc=1, device_id=to, device_id_type=MESH)
        running = []
        for flow in flows:
            own = [[group.pop(0) for _ in part] for group, part in ((ins, flow.inputs), (outs, flow.outputs), (rest, flow.scratch))]
            running.append(flow.steps(*own))
            next(running[-1])
        pl.semaphore_wait(barrier, len(partners))
        while running:
            going = []
            for steps in running:
                more = next(steps, running)
                if more is not running:
                    going += [steps] if more is None else [steps, more]
            running = going

    return pl.pallas_call(
        kernel,
        out_shape=tuple(jax.ShapeDtypeStruct(s, d) for f in flows for s, d, _ in f.outputs),
        in_specs=[pl.BlockSpec(memory_space=space) for f in flows for _, space in f.inputs],
        out_specs=tuple(pl.BlockSpec(memory_space=space) for f in flows for _, _, space in f.outputs),
        scratch_shapes=[x for f in flows for x in f.scratch],
        compiler_params=pltpu.CompilerParams(collective_id=cid, has_side_effects=True, vmem_limit_bytes=VMEM_LIMIT),
        cost_estimate=cost_of(cost),
        name=f"links_{cid}",
    )(*[x for f in flows for x, _ in f.inputs])


def remote(src, dst, send, recv, device):
    return pltpu.make_async_remote_copy(
        src_ref=src, dst_ref=dst, send_sem=send, recv_sem=recv, device_id=device, device_id_type=MESH
    )


def piece(ref, which):
    rows = ref.shape[0] // 2
    return ref.at[pl.ds(which * rows, rows)]


def ring_partners(kind):
    return [(kind, 1), (kind, 3)]


class RingGather:
    def __init__(self, kind, slot, src, send, recv):
        me, member = peers_of(kind)
        up, down = lax.rem(me + 1, 4), lax.rem(me + 3, 4)

        def copy(source, target, i, to):
            return remote(source, target, send.at[i], recv.at[i], member(to))

        mine = slot(me)
        self.copies = [
            copy(piece(src, 0), piece(mine, 0), 0, up),
            copy(piece(src, 1), piece(mine, 1), 1, up),
            copy(piece(src, 1), piece(mine, 1), 2, down),
            copy(piece(src, 0), piece(mine, 0), 3, down),
            copy(piece(slot(down), 0), piece(slot(down), 0), 4, up),
            copy(piece(slot(up), 1), piece(slot(up), 1), 5, down),
        ]

    def start(self):
        for i in (0, 2, 1, 3):
            self.copies[i].start()

    def forward(self):
        self.copies[0].wait_recv()
        self.copies[4].start()
        self.copies[2].wait_recv()
        self.copies[5].start()

    def near(self):
        self.copies[1].wait_recv()
        self.copies[3].wait_recv()

    def far(self):
        self.copies[4].wait_recv()
        self.copies[5].wait_recv()

    def sent(self):
        for copy in self.copies:
            copy.wait_send()


class RingScatter:
    def __init__(self, kind, chunk, bufs, send, recv, raw=None):
        raw = raw or chunk
        self.me, member = peers_of(kind)
        self.up, self.down, self.far = (lax.rem(self.me + k, 4) for k in (1, 3, 2))
        self.chunk, self.bufs = chunk, bufs

        def copy(source, target, i, to):
            return remote(source, bufs.at[target], send.at[i], recv.at[i], member(to))

        self.copies = [
            copy(piece(raw(self.far), 0), 0, 0, self.up),
            copy(piece(raw(self.far), 1), 1, 1, self.down),
            copy(piece(raw(self.up), 1), 2, 2, self.up),
            copy(piece(raw(self.down), 0), 3, 3, self.down),
            copy(bufs.at[6], 4, 4, self.up),
            copy(bufs.at[7], 5, 5, self.down),
        ]

    def start_far(self):
        self.copies[0].start()
        self.copies[1].start()

    def start_up(self):
        self.copies[2].start()

    def start_down(self):
        self.copies[3].start()

    def add(self):
        self.copies[0].wait_recv()
        self.bufs[6] = (piece(self.chunk(self.up), 0)[...].astype(F32) + self.bufs[0].astype(F32)).astype(BF)
        self.copies[4].start()
        self.copies[1].wait_recv()
        self.bufs[7] = (piece(self.chunk(self.down), 1)[...].astype(F32) + self.bufs[1].astype(F32)).astype(BF)
        self.copies[5].start()

    def total(self, which):
        first, second = ((4, 3), (2, 5))[which]
        self.copies[first].wait_recv()
        self.copies[second].wait_recv()
        return self.bufs[first].astype(F32) + self.bufs[second].astype(F32)

    def sent(self):
        for copy in self.copies:
            copy.wait_send()


def dma(*shape):
    return pltpu.SemaphoreType.DMA(shape)


def ring_gather_flow(made):
    shape = (2, 4) + made.shape

    def steps(ins, outs, scratch):
        (out,), src = outs, made.ref
        send, recv, pass_send, pass_recv, local = scratch
        yield
        me, _ = peers_of("zc")
        core, member = peers_of("c")
        ring = RingGather("zc", lambda g: out.at[core, g], src, send, recv)

        def passing(k):
            g = lax.rem(me + k, 4)
            return remote(src if k == 0 else out.at[core, g], out.at[core, g], pass_send.at[k], pass_recv.at[k], member(1 - core))

        passes = [passing(k) for k in range(4)]
        ring.start()
        passes[0].start()
        yield
        ring.forward()
        back = pltpu.make_async_copy(src, out.at[core, me], local.at[0])
        back.start()
        yield
        ring.near()
        passes[1].start()
        passes[3].start()
        yield
        ring.far()
        passes[2].start()
        yield
        back.wait()
        ring.sent()
        for copy in passes:
            copy.wait()

    return Flow(
        [],
        [(shape, BF, pl.ANY)],
        [dma(6), dma(6), dma(4), dma(4), dma(1)],
        ring_partners("zc") + [("c", 1)],
        steps,
    )


def plane_gather_flow(arrays, first, second, ahead=None):
    to_core = ahead is None
    if ahead == "zhc":
        shard = (4, arrays[0][0].shape[0], sum(columns for _, columns, _ in arrays))
    elif ahead == "z":
        shard = (8,) + arrays[0][0].shape
    else:
        shard = arrays.shape
    shape = ((2,) if to_core else ()) + (4, 4) + shard
    n_ahead = SIZES[ahead] if ahead else 1

    def steps(ins, outs, scratch):
        (out,) = outs
        stage, send, recv, pass_send, pass_recv, local, ahead_send, ahead_recv = scratch
        core, member = peers_of("c")
        here, _ = peers_of(first)
        there, _ = peers_of(second)
        view = out.at[core] if to_core else out

        def slot(a, b):
            return view.at[b, a] if first == "x" else view.at[a, b]

        if ahead:
            mine, at = peers_of(ahead)

            def parts(to):
                if ahead == "z":
                    return [(ins[0], stage.at[mine])]
                found, begin = [], 0
                for ref, (_, columns, share) in zip(ins, arrays):
                    source = ref.at[:, pl.ds(pl.multiple_of(lax.div(to, share) * columns, columns), columns)]
                    found.append((source, stage.at[mine, :, pl.ds(begin, columns)]))
                    begin += columns
                return found

            early = [pltpu.make_async_copy(source, target, local.at[i]) for i, (source, target) in enumerate(parts(mine))]
            for k in range(1, n_ahead):
                to = lax.rem(mine + k, n_ahead)
                for i, (source, target) in enumerate(parts(to)):
                    early.append(remote(source, target, ahead_send.at[i, k], ahead_recv.at[i, k], at(to)))
            local_parts = len(parts(mine))
            for copy in early[:local_parts]:
                copy.start()
            yield
            for copy in early[local_parts:]:
                copy.start()
            yield
            for copy in early:
                copy.wait()
            src = stage
        else:
            src = arrays.ref
            yield
        ring = RingGather(first, lambda g: slot(g, there), src, send.at[4], recv.at[4])
        columns = [lax.rem(here + k, 4) for k in range(4)]
        rings = [
            RingGather(second, lambda g, a=a: slot(a, g), src if k == 0 else slot(a, there), send.at[k], recv.at[k])
            for k, a in enumerate(columns)
        ]

        def passing(k, m):
            ref = slot(columns[k], lax.rem(there + m, 4))
            return remote(src if k == m == 0 else ref, ref, pass_send.at[k * 4 + m], pass_recv.at[k * 4 + m], member(1 - core))

        passes = {}

        def hand_over(k, m):
            if to_core:
                passes[k, m] = passing(k, m)
                passes[k, m].start()

        ring.start()
        rings[0].start()
        hand_over(0, 0)
        yield
        ring.forward()
        back = pltpu.make_async_copy(src, slot(here, there), local.at[0])
        back.start()
        yield
        rings[0].forward()
        yield
        ring.near()
        for k in (1, 3):
            rings[k].start()
            hand_over(k, 0)
        yield
        ring.far()
        rings[2].start()
        hand_over(2, 0)
        yield
        for k in (0, 1, 3, 2):
            if k > 0:
                rings[k].forward()
            rings[k].near()
            hand_over(k, 1)
            hand_over(k, 3)
            yield
            rings[k].far()
            hand_over(k, 2)
            yield
        back.wait()
        ring.sent()
        for one in rings:
            one.sent()
        for copy in passes.values():
            copy.wait()

    return Flow(
        [] if to_core else [(array, pl.ANY) for array, *_ in arrays],
        [(shape, BF, pl.ANY)],
        [pltpu.VMEM((8, 128) if to_core else shard, BF), dma(5, 6), dma(5, 6), dma(16), dma(16), dma(3), dma(3, 8), dma(3, 8)],
        ring_partners("x") + ring_partners("y") + ([("c", 1)] if to_core else []) + [(ahead, k) for k in range(1, n_ahead)],
        steps,
    )


def product_flow(left, right):
    columns, width = left.shape[1], right.shape[1]

    def steps(ins, outs, scratch):
        (out,) = outs
        left_ref, right_ref, local = scratch
        copies = [pltpu.make_async_copy(source, target, local.at[i]) for i, (source, target) in enumerate(zip(ins, (left_ref, right_ref)))]
        for copy in copies:
            copy.start()
        yield
        for copy in copies:
            copy.wait()
        for column in range(0, columns, 256):
            span = slice(column, column + 256)
            out[span, :] = dot_tn(left_ref[:, span], right_ref[...]).astype(BF)
            yield

    return Flow(
        [(left, pl.ANY), (right, pl.ANY)],
        [((columns, width), BF, pltpu.VMEM)],
        [pltpu.VMEM(left.shape, BF), pltpu.VMEM(right.shape, BF), dma(2)],
        [],
        steps,
    )


def output_flow(residual, gates, assign, expert_out):
    own, width = residual.shape
    experts = gates.shape[1]
    count = expert_out.shape[0]

    def steps(ins, outs, scratch):
        residual_ref, gates_ref, assign_ref, expert_hbm = ins
        (out,) = outs
        expert_ref, mixing, local = scratch
        copy = pltpu.make_async_copy(expert_hbm, expert_ref, local.at[0])
        copy.start()
        wide = (experts, count)
        cap = count // experts
        spread = (lax.broadcasted_iota(jnp.int32, wide, 1) // cap == lax.broadcasted_iota(jnp.int32, wide, 0)).astype(F32).astype(BF)
        taken = assign_ref[...].astype(F32)
        high = gates_ref[...].astype(BF)
        low = (gates_ref[...] - high.astype(F32)).astype(BF)
        mixing[0] = (dot_nn(high, spread) * taken).astype(BF)
        mixing[1] = (dot_nn(low, spread) * taken).astype(BF)
        yield
        copy.wait()
        for column in range(0, width, 512):
            span = slice(column, column + 512)
            rows = expert_ref[:, span]
            out[:, span] = (residual_ref[:, span] + dot_nn(mixing[0], rows) + dot_nn(mixing[1], rows)).astype(BF)
            yield

    return Flow(
        [(residual, pltpu.VMEM), (gates, pltpu.VMEM), (assign, pltpu.VMEM), (expert_out, pl.ANY)],
        [(residual.shape, BF, pltpu.VMEM)],
        [pltpu.VMEM(expert_out.shape, BF), pltpu.VMEM((2, own, count), BF), dma(1)],
        [],
        steps,
    )


sum_partners = [("yx", k) for k in range(1, 16)] + [("z", k) for k in range(1, 8)]


def sum_room(shape):
    return [pltpu.VMEM((16,) + shape, F32), pltpu.VMEM((8,) + shape, F32), pltpu.VMEM(shape, F32), dma(16), dma(16), dma(8), dma(8)]


def sum_steps(src, gains, out, scratch):
    wide, far, middle, sends, recvs, far_sends, far_recvs = scratch
    me, member = peers_of("yx")
    copies = []
    for k in range(1, 16):
        copies.append(remote(src, wide.at[me], sends.at[k], recvs.at[k], member(lax.rem(me + k, 16))))
        copies[-1].start()
    wide[me] = src[...]
    yield
    for copy in copies:
        copy.wait()
    middle[...] = jnp.sum(wide[...], axis=0)
    ring, ring_member = peers_of("z")
    late = []
    for k in range(1, 8):
        late.append(remote(middle, far.at[ring], far_sends.at[k], far_recvs.at[k], ring_member(lax.rem(ring + k, 8))))
        late[-1].start()
    far[ring] = middle[...]
    yield
    for copy in late:
        copy.wait()
    out[...] = jnp.sum(far[...], axis=0) / gains[1]


def product_scatter_flow(lefts, right, done, units=None, gains=None, key_gain=None):
    arrays = [left for left in lefts if not isinstance(left, Made)]
    own, wide = lefts[0].shape[0] // 8, right.shape[0]
    spans = [0]
    for left in lefts:
        spans.append(spans[-1] + left.shape[1])

    def steps(ins, outs, scratch):
        given = list(ins[: len(arrays)])
        left_refs = [left.ref if isinstance(left, Made) else given.pop(0) for left in lefts]
        right_ref = ins[len(arrays)]
        out, theirs, came, chunks, bufs, send, recv, pass_send, pass_recv, *rest = scratch
        core, member = peers_of("c")
        me, _ = peers_of("zc")
        ring = RingScatter("zc", lambda g: chunks.at[g], bufs, send, recv)

        if units is not None:
            gains_ref = ins[len(arrays) + 1]
            unit_ref = units.ref
            sums, *sum_scratch = rest
            sums[...] = gains_ref[0]
            sums[33:34, :] += key_gain.ref[...]

        def product(c, k, column):
            row = pl.multiple_of((c * 4 + lax.rem(me + k, 4)) * own, own)
            value = sum(
                dot_nt(left_ref[pl.ds(row, own), :], right_ref[column : column + 512, spans[i] : spans[i + 1]])
                for i, left_ref in enumerate(left_refs)
            )
            if units is not None:
                row_sum = jnp.sum(value * unit_ref[pl.ds(row, own), column : column + 512].astype(F32), axis=0, keepdims=True)
                for lane in range(0, 512, 128):
                    at = (column + lane) // 128
                    sums[at : at + 1, :] += row_sum[:, lane : lane + 128]
            return value

        passes = [
            remote(theirs.at[k], came.at[k], pass_send.at[k], pass_recv.at[k], member(1 - core)) for k in range(4)
        ]
        for k in (2, 1, 3, 0):
            if k == 1:
                yield
                passes[2].start()
            for column in range(0, wide, 512):
                theirs[k, :, column : column + 512] = product(1 - core, k, column).astype(BF)
            if k != 2:
                passes[k].start()
                yield
        for k in (2, 1, 3, 0):
            passes[k].wait_recv()
            g = lax.rem(me + k, 4)
            for column in range(0, wide, 512):
                span = slice(column, column + 512)
                value = product(core, k, column) + came[k, :, span].astype(F32)
                if k == 0:
                    out[:, span] = value
                else:
                    chunks[g, :, span] = value.astype(BF)
            if k == 2:
                ring.start_far()
            elif k == 1:
                ring.start_up()
            elif k == 3:
                ring.start_down()
            yield
        if units is not None:
            yield sum_steps(sums, gains_ref, outs[0], sum_scratch)
        ring.add()
        yield
        for h in range(2):
            rows = slice(h * own // 2, (h + 1) * own // 2)
            out[rows, :] += ring.total(h)
        done.ref = out
        yield
        ring.sent()
        for copy in passes:
            copy.wait_send()

    return Flow(
        [(x, pltpu.VMEM) for x in (*arrays, right)] + ([] if units is None else [(gains, pltpu.VMEM)]),
        [] if units is None else [(gains.shape[1:], F32, pltpu.VMEM)],
        [
            pltpu.VMEM((own, wide), F32),
            pltpu.VMEM((4, own, wide), BF),
            pltpu.VMEM((4, own, wide), BF),
            pltpu.VMEM((4, own, wide), BF),
            pltpu.VMEM((8, own // 2, wide), BF),
            dma(6),
            dma(6),
            dma(4),
            dma(4),
        ]
        + ([] if units is None else [pltpu.VMEM(gains.shape[1:], F32)] + sum_room(gains.shape[1:])),
        ring_partners("zc") + [("c", 1)] + ([] if units is None else sum_partners),
        steps,
    )


def plane_scatter_flow(array, first, second, from_core=False, last_in=None):
    rows, columns = array.shape[-2:]
    n_last = SIZES[last_in] if last_in else 1
    result = (n_last, rows // 4, columns) if last_in else (rows, columns)

    def steps(ins, outs, scratch):
        src, (out,) = array.ref if isinstance(array, Made) else ins[0], outs
        came, sums, middle, bufs, late_bufs, send, recv, late_send, late_recv, pass_send, pass_recv, local, cut, cut_send, cut_recv = scratch
        core, member = peers_of("c")
        me, _ = peers_of(first)

        def along(ref, g):
            return ref.at[g] if first == "y" else ref.at[:, g]

        order = [lax.rem(me + k, 4) for k in (2, 1, 3, 0)]
        loads = [
            pltpu.make_async_copy(along(src.at[core] if from_core else src, g), along(sums, g), local.at[i])
            for i, g in enumerate(order)
            if from_core or i > 0
        ]
        passes = []
        if from_core:
            ring = RingScatter(first, lambda g: along(sums, g), bufs, send, recv)
            for i, g in enumerate(order):
                loads[i].start()
                passes.append(
                    remote(along(src.at[1 - core], g), along(came, g), pass_send.at[i], pass_recv.at[i], member(1 - core))
                )
            yield
            for copy in passes:
                copy.start()
            yield
            starts = [ring.start_far, ring.start_up, ring.start_down, lambda: None]
            for i, g in enumerate(order):
                loads[i].wait()
                passes[i].wait_recv()
                for k in range(4):
                    total = along(sums, g)[k].astype(F32) + along(came, g)[k].astype(F32)
                    along(sums, g)[k] = total.astype(BF)
                starts[i]()
                yield
        else:
            ring = RingScatter(first, lambda g: along(sums, g), bufs, send, recv, raw=lambda g: along(src, g))
            for load in loads:
                load.start()
            yield
            ring.start_far()
            ring.start_up()
            ring.start_down()
            yield
            for load in loads:
                load.wait()
        ring.add()
        yield
        own = along(sums, me)
        for h in range(2):
            came_half = ring.total(h)
            for k in range(2):
                middle[h * 2 + k] = (own[h * 2 + k].astype(F32) + came_half[k]).astype(BF)
        yield
        last = RingScatter(second, lambda g: middle.at[g], late_bufs, late_send, late_recv)
        last.start_far()
        last.start_up()
        last.start_down()
        yield
        last.add()
        yield
        for h in range(2):
            total = (piece(middle.at[last.me], h)[...].astype(F32) + last.total(h)).astype(BF)
            if last_in:
                cut[2 * h] = total[: rows // 4]
                cut[2 * h + 1] = total[rows // 4 :]
            else:
                out[h * rows // 2 : (h + 1) * rows // 2, :] = total
        cuts = []
        if last_in:
            mine, at = peers_of(last_in)
            share = n_last // 4
            for k in range(1, n_last):
                to = lax.rem(mine + k, n_last)
                cuts.append(remote(cut.at[lax.div(to, share)], out.at[mine], cut_send.at[k], cut_recv.at[k], at(to)))
                cuts[-1].start()
            out[mine] = cut[lax.div(mine, share)]
        yield
        ring.sent()
        last.sent()
        for copy in passes:
            copy.wait_send()
        for copy in cuts:
            copy.wait()

    block = (4, 4, rows, columns)
    return Flow(
        [] if isinstance(array, Made) else [(array, pl.ANY)],
        [(result, BF, pltpu.VMEM)],
        [
            pltpu.VMEM(block if from_core else (8, 128), BF),
            pltpu.VMEM(block, BF),
            pltpu.VMEM((4, rows, columns), BF),
            pltpu.VMEM((8, 2, rows, columns), BF),
            pltpu.VMEM((8, rows // 2, columns), BF),
            dma(6),
            dma(6),
            dma(6),
            dma(6),
            dma(4),
            dma(4),
            dma(4),
            pltpu.VMEM((4, rows // 4, columns), BF),
            dma(8),
            dma(8),
        ],
        ring_partners("x")
        + ring_partners("y")
        + ([("c", 1)] if from_core else [])
        + [(last_in, k) for k in range(1, n_last)],
        steps,
    )


def tables_flow(routes, offsets, spacing, experts, cap):
    own, top = routes.shape
    rows, size = offsets.size, spacing.shape[1]

    def steps(ins, outs, scratch):
        routes_ref, offsets_ref, spacing_ref = ins
        assign, chosen_ref, cosine, sine = outs
        lane = lax.broadcasted_iota(jnp.int32, (own, experts), 1)
        chosen = jnp.zeros((own, experts), F32)
        for k in range(top):
            chosen += (routes_ref[:, k : k + 1] == lane).astype(F32)
        chosen_ref[...] = chosen
        before = lax.broadcasted_iota(jnp.int32, (own, own), 0) > lax.broadcasted_iota(jnp.int32, (own, own), 1)
        earlier = dot_nn(before.astype(F32).astype(BF), chosen.astype(BF))
        wide = (experts, experts * cap)
        spread = (lax.broadcasted_iota(jnp.int32, wide, 1) // cap == lax.broadcasted_iota(jnp.int32, wide, 0)).astype(F32).astype(BF)
        slot = lax.rem(lax.broadcasted_iota(jnp.int32, (own, experts * cap), 1), cap).astype(F32)
        taken = (dot_nn(chosen.astype(BF), spread) > 0.5) & (dot_nn(earlier.astype(BF), spread) == slot)
        assign[...] = taken.astype(F32).astype(BF)
        yield
        sign = jnp.where(lax.broadcasted_iota(jnp.int32, (1, size), 1) < size // 2, -1.0, 1.0)
        for row in range(0, rows, BLOCK):
            span = slice(row, row + BLOCK)
            angles = jnp.broadcast_to(offsets_ref[row // BLOCK], (size, BLOCK)).T * spacing_ref[...]
            cosine[span, :] = jnp.cos(angles)
            sine[span, :] = jnp.sin(angles) * sign
            yield

    return Flow(
        [(routes, pltpu.VMEM), (offsets, pltpu.VMEM), (spacing, pltpu.VMEM)],
        [
            ((own, experts * cap), BF, pltpu.VMEM),
            ((own, experts), F32, pltpu.VMEM),
            ((rows, size), F32, pltpu.VMEM),
            ((rows, size), F32, pltpu.VMEM),
        ],
        [],
        [],
        steps,
    )


def norm_flow(tokens, gain, made):
    def steps(ins, outs, scratch):
        tokens_ref, gain_ref = ins
        (made.ref,) = scratch
        wide = tokens_ref[...].astype(F32)
        made.ref[...] = (wide * lax.rsqrt(jnp.mean(wide * wide, axis=-1, keepdims=True) + EPS) * gain_ref[...]).astype(BF)
        yield

    return Flow([(tokens, pltpu.VMEM), (gain, pltpu.VMEM)], [], [pltpu.VMEM(tokens.shape, BF)], [], steps)


def project_flow(rows, weights, gain, cosine, sine, q_cols, keys, values):
    count, size = rows.shape[0], gain.shape[1]
    half = count // 2

    def steps(ins, outs, scratch):
        rows_hbm, w_hbm, gain_ref, cos_ref, sin_ref = ins
        q_ref, raw_ref = outs
        rows_ref, w_ref, keys.ref, values.ref, local = scratch
        core, _ = peers_of("c")
        own = pl.ds(pl.multiple_of(core * half, half), half)
        other = pl.ds(pl.multiple_of((1 - core) * half, half), half)
        kv = pl.ds(q_cols, 2 * size)
        copies = [
            pltpu.make_async_copy(w_hbm.at[:, kv], w_ref.at[:, kv], local.at[0]),
            pltpu.make_async_copy(rows_hbm.at[own], rows_ref.at[own], local.at[1]),
            pltpu.make_async_copy(w_hbm.at[:, pl.ds(0, q_cols)], w_ref.at[:, pl.ds(0, q_cols)], local.at[2]),
            pltpu.make_async_copy(rows_hbm.at[other], rows_ref.at[other], local.at[3]),
        ]
        for copy in copies:
            copy.start()
        copies[0].wait()
        copies[1].wait()
        product = dot_nn(rows_ref[own, :], w_ref[:, q_cols:])
        raw = product[:, :size]
        raw_ref[...] = raw
        keys.ref[...] = norm_rope(raw, gain_ref[...], cos_ref[own, :], sin_ref[own, :]).astype(BF)
        values.ref[...] = product[:, size:].astype(BF)
        yield
        yield
        copies[2].wait()
        copies[3].wait()
        for row in range(0, count, BLOCK):
            q_ref[row : row + BLOCK, :] = dot_nn(rows_ref[row : row + BLOCK, :], w_ref[:, :q_cols])
            yield

    return Flow(
        [(rows, pl.ANY), (weights, pl.ANY), (gain, pltpu.VMEM), (cosine, pltpu.VMEM), (sine, pltpu.VMEM)],
        [((count, q_cols), F32, pltpu.VMEM), ((half, size), F32, pltpu.VMEM)],
        [pltpu.VMEM(rows.shape, BF), pltpu.VMEM(weights.shape, BF), pltpu.VMEM((half, size), BF), pltpu.VMEM((half, size), BF), dma(4)],
        [],
        steps,
    )


def route_flow(tokens, gain, router, chosen, assign, done):
    own, width = tokens.shape
    experts, count = chosen.shape[1], assign.shape[1]

    def steps(ins, outs, scratch):
        tokens_ref, gain_ref, router_ref, chosen_ref, assign_ref = ins
        residual_ref, mixed_ref, gates_ref, rows_ref = outs
        (pick,) = scratch
        yield
        pick[...] = assign_ref[...].T
        while done.ref is None:
            yield
        residual = tokens_ref[...].astype(F32) + done.ref[...]
        residual_ref[...] = residual
        mixed_ref[...] = (residual * lax.rsqrt(jnp.mean(residual * residual, axis=-1, keepdims=True) + EPS) * gain_ref[...]).astype(BF)
        logits = jnp.where(chosen_ref[...] > 0, dot_nn(mixed_ref[...], router_ref[...]), -1e30)
        powers = jnp.exp(logits - jnp.max(logits, axis=-1, keepdims=True))
        gates = powers / jnp.sum(powers, axis=-1, keepdims=True)
        gates_ref[...] = gates
        for column in range(0, width, 512):
            span = slice(column, column + 512)
            rows_ref[:, span] = dot_nn(pick[...], mixed_ref[:, span]).astype(BF)
        rows_ref[:, width:] = dot_nn(pick[...], gates.astype(BF)).astype(BF)
        yield

    return Flow(
        [(x, pltpu.VMEM) for x in (tokens, gain, router, chosen, assign)],
        [
            ((own, width), F32, pltpu.VMEM),
            ((own, width), BF, pltpu.VMEM),
            ((own, experts), F32, pltpu.VMEM),
            ((count, width + experts), BF, pltpu.VMEM),
        ],
        [pltpu.VMEM((count, own), BF)],
        [],
        steps,
    )


def mix_back_flow(back, assign, gates, mixed, router, residual, gain, cotangent, made):
    own, width = mixed.shape
    experts, count = gates.shape[1], back.shape[0]

    def steps(ins, outs, scratch):
        back_hbm, assign_ref, gates_ref, mixed_ref, router_ref, residual_ref, gain_ref, cotangent_ref = ins
        residual_grad, gain_grad, router_grad = outs
        back_ref, mixed_grad, made.ref, local = scratch
        copy = pltpu.make_async_copy(back_hbm, back_ref, local.at[0])
        copy.start()
        copy.wait()
        sums = jnp.sum(back_ref[:, width : width + 128].astype(F32), axis=1, keepdims=True)
        shape = (count, experts)
        expert_of = lax.div(lax.broadcasted_iota(jnp.int32, shape, 0), count // experts)
        spread = jnp.where(expert_of == lax.broadcasted_iota(jnp.int32, shape, 1), sums, 0.0)
        high = spread.astype(BF)
        low = (spread - high.astype(F32)).astype(BF)
        gate_grads = dot_nn(assign_ref[...], high) + dot_nn(assign_ref[...], low)
        gates = gates_ref[...]
        logits_grad = (gates * (gate_grads - jnp.sum(gates * gate_grads, axis=1, keepdims=True))).astype(BF)
        for column in range(0, width, 512):
            span = slice(column, column + 512)
            mixed_grad[:, span] = dot_nn(assign_ref[...], back_ref[:, span]) + dot_nt(logits_grad, router_ref[span, :])
        value = residual_ref[...]
        inverse = lax.rsqrt(jnp.mean(value * value, axis=-1, keepdims=True) + EPS)
        unit = value * inverse
        grad = mixed_grad[...]
        gain_grad[...] = jnp.sum(grad * unit, axis=0, keepdims=True)
        scaled = grad * gain_ref[...]
        total = cotangent_ref[...].astype(F32) + inverse * (scaled - unit * jnp.mean(scaled * unit, axis=-1, keepdims=True))
        residual_grad[...] = total
        made.ref[...] = total.astype(BF)
        yield
        yield
        router_grad[...] = dot_tn(mixed_ref[...], logits_grad).astype(BF)
        yield

    return Flow(
        [(back, pl.ANY)] + [(x, pltpu.VMEM) for x in (assign, gates, mixed, router, residual, gain, cotangent)],
        [((own, width), F32, pltpu.VMEM), ((1, width), F32, pltpu.VMEM), ((width, experts), BF, pltpu.VMEM)],
        [pltpu.VMEM(back.shape, BF), pltpu.VMEM((own, width), F32), pltpu.VMEM((own, width), BF), dma(1)],
        [],
        steps,
    )


def key_back_flow(grad_key, grad_value, raw, gain, cosine, sine, units, kv, w_kv, rows, key_gain):
    half, size = raw.shape
    width = units.shape[1]

    def steps(ins, outs, scratch):
        dk_ref, dv_ref, raw_ref, gain_ref, cos_ref, sin_ref, units_hbm = ins
        rows.ref, kv.ref, w_kv.ref, key_gain.ref, local = scratch
        copy = pltpu.make_async_copy(units_hbm, rows.ref, local.at[0])
        copy.start()
        core, _ = peers_of("c")
        own = pl.ds(pl.multiple_of(core * half, half), half)
        grad = dk_ref[...].astype(F32)
        grad_raw, grad_gain = norm_rope_back(grad, raw_ref[...], gain_ref[...], cos_ref[own, :], sin_ref[own, :])
        kv.ref[...] = jnp.zeros(kv.shape, BF)
        kv.ref[own, :size] = grad_raw.astype(BF)
        kv.ref[own, size:] = dv_ref[...]
        key_gain.ref[...] = jnp.sum(grad_gain, axis=0, keepdims=True)
        copy.wait()
        for i in range(16):
            w_kv.ref[i // 4, i % 4] = dot_tn(rows.ref[own, i * width // 16 : (i + 1) * width // 16], kv.ref[own, :]).astype(BF)
        yield

    return Flow(
        [(x, pltpu.VMEM) for x in (grad_key, grad_value, raw, gain, cosine, sine)] + [(units, pl.ANY)],
        [],
        [pltpu.VMEM(rows.shape, BF), pltpu.VMEM(kv.shape, BF), pltpu.VMEM(w_kv.shape, BF), pltpu.VMEM((1, size), F32), dma(1)],
        [],
        steps,
    )


def tokens_grad_flow(tokens, gain, residual_grad, done):
    def steps(ins, outs, scratch):
        tokens_ref, gain_ref, residual_ref = ins
        (out,) = outs
        yield
        while done.ref is None:
            yield
        value = tokens_ref[...].astype(F32)
        inverse = lax.rsqrt(jnp.mean(value * value, axis=-1, keepdims=True) + EPS)
        unit = value * inverse
        scaled = done.ref[...] * gain_ref[...]
        out[...] = residual_ref[...] + inverse * (scaled - unit * jnp.mean(scaled * unit, axis=-1, keepdims=True))
        yield

    return Flow(
        [(x, pltpu.VMEM) for x in (tokens, gain, residual_grad)], [(tokens.shape, F32, pltpu.VMEM)], [], [], steps
    )


def add_up(stacked):
    return jnp.sum(stacked.astype(F32), axis=0)


def dot_nn(a, b):
    return lax.dot_general(a, b, (((1,), (0,)), ((), ())), preferred_element_type=F32)


def dot_nt(a, b):
    return lax.dot_general(a, b, (((1,), (1,)), ((), ())), preferred_element_type=F32)


def dot_tn(a, b):
    return lax.dot_general(a, b, (((0,), (0,)), ((), ())), preferred_element_type=F32)


def norm_rope(raw, gain, cosine, sine):
    unit = raw * lax.rsqrt(jnp.mean(raw * raw, axis=-1, keepdims=True) + EPS)
    scaled = unit * gain
    return scaled * cosine + pltpu.roll(scaled, 64, 1) * sine


def norm_rope_back(grad, raw, gain, cosine, sine):
    inverse = lax.rsqrt(jnp.mean(raw * raw, axis=-1, keepdims=True) + EPS)
    unit = raw * inverse
    turned = grad * cosine + pltpu.roll(grad * sine, 64, 1)
    scaled = turned * gain
    return inverse * (scaled - unit * jnp.mean(scaled * unit, axis=-1, keepdims=True)), turned * unit


def expert_kernel(rows_ref, plain_ref, w_ref, back_ref, hidden_ref, gated_ref, both_ref):
    width, ff = w_ref.shape[0], plain_ref.shape[1]
    own = lax.axis_index("head") * lax.axis_size("blk") + lax.axis_index("blk")
    gates = rows_ref[:, width:].astype(F32)
    lane = lax.broadcasted_iota(jnp.int32, gates.shape, 1)
    gate = jnp.sum(jnp.where(lane == own, gates, 0.0), axis=1, keepdims=True)
    gate_up = dot_nn(rows_ref[:, :width], w_ref[...])
    first, up = gate_up[:, :ff], gate_up[:, ff:]
    sigma = 1.0 / (1.0 + jnp.exp(-first))
    silu = first * sigma
    hidden = silu * up
    hidden_ref[...] = hidden.astype(BF)
    gated_ref[...] = (hidden * gate).astype(BF)
    plain = plain_ref[...]
    gate_grad = jnp.sum(hidden * plain, axis=1, keepdims=True)
    grad = plain * gate
    both_ref[:, :ff] = (grad * up * (sigma * (1.0 + first * (1.0 - sigma)))).astype(BF)
    both_ref[:, ff:] = (grad * silu).astype(BF)
    back_ref[:, :width] = dot_nt(both_ref[...], w_ref[...]).astype(BF)
    high = gate_grad.astype(BF).astype(F32)
    back_ref[:, width:] = jnp.where(lane == 0, high, jnp.where(lane == 1, gate_grad - high, 0.0)).astype(BF)


def key_tiles(lo, full, last, tile):
    middle = jnp.minimum(full, last)
    pl.loop(lo, middle)(lambda t: tile(t, True))
    pl.loop(middle, last)(lambda t: tile(t, False))
    tile(last, True)


def allowed_pairs(t, last, start, shape):
    key_place = t * BLOCK + lax.broadcasted_iota(jnp.int32, shape, 0)
    query_place = last * BLOCK + lax.rem(lax.broadcasted_iota(jnp.int32, shape, 1), BLOCK)
    return (key_place >= start) & (key_place <= query_place)


def attend_forward_kernel(
    lo_ref, full_ref, last_ref, slot_ref, raw_ref, gain_ref, cos_ref, sin_ref, k_ref, v_ref, start_ref, q_ref, o_ref, log_ref, q_t, acc, total
):
    j = pl.program_id(0)
    size = k_ref.shape[2]
    heads = raw_ref.shape[1] // size
    scale = size**-0.5 * LOG2E
    last = last_ref[j]
    for n in range(heads):
        span = slice(n * size, (n + 1) * size)
        query = norm_rope(raw_ref[:, span], gain_ref[...], cos_ref[...], sin_ref[...])
        q_ref[:, span] = query.astype(BF)
        q_t[:, n * BLOCK : (n + 1) * BLOCK] = query.T.astype(BF)
    acc[...] = jnp.zeros_like(acc)
    total[...] = jnp.zeros_like(total)
    start = start_ref[0]

    def tile(t, masked):
        slot = slot_ref[t]
        weights = jnp.exp2(dot_nn(k_ref[slot], q_t[...]) * scale)
        if masked:
            weights = jnp.where(allowed_pairs(t, last, start, weights.shape), weights, 0.0)
        total[...] += jnp.sum(weights.reshape(BLOCK // 8, 8, heads * BLOCK), axis=0)
        acc[...] += dot_nn(v_ref[slot].T, weights.astype(BF))

    key_tiles(lo_ref[j], full_ref[j], last, tile)
    row = jnp.sum(total[...], axis=0, keepdims=True)
    log_ref[0] = jnp.log2(row)
    out = acc[...] / row
    for n in range(heads):
        o_ref[:, n * size : (n + 1) * size] = out[:, n * BLOCK : (n + 1) * BLOCK].T.astype(BF)


def attend_backward_kernel(
    lo_ref,
    full_ref,
    last_ref,
    slot_ref,
    raw_ref,
    gain_ref,
    cos_ref,
    sin_ref,
    k_ref,
    v_ref,
    start_ref,
    q_ref,
    o_ref,
    g_ref,
    w_ref,
    log_ref,
    dq_ref,
    sum_ref,
    dk_ref,
    dv_ref,
    queries,
    q_t,
    grads,
    g_t,
    delta,
    acc,
    dk,
    dv,
    keys_ref,
    values_ref,
    local,
):
    j = pl.program_id(0)
    slots, _, size = keys_ref.shape
    takes = [pltpu.make_async_copy(k_ref, keys_ref, local.at[0]), pltpu.make_async_copy(v_ref, values_ref, local.at[1])]
    heads = raw_ref.shape[1] // size
    scale = size**-0.5
    last = last_ref[j]

    @pl.when(j == 0)
    def _():
        for copy in takes:
            copy.start()
        sum_ref[...] = jnp.zeros_like(sum_ref)

        @pl.loop(0, slots)
        def _(s):
            dk[s] = jnp.zeros(dk.shape[1:], F32)
            dv[s] = jnp.zeros(dv.shape[1:], F32)

    attended_grad = dot_nn(g_ref[...], w_ref[...]).astype(BF)
    for n in range(heads):
        span, rows = slice(n * size, (n + 1) * size), slice(n * BLOCK, (n + 1) * BLOCK)
        queries[rows, :] = q_ref[:, span]
        q_t[:, rows] = q_ref[:, span].T
        grads[rows, :] = attended_grad[:, span]
        grad_t = attended_grad[:, span].T
        g_t[:, rows] = grad_t
        delta[:, rows] = jnp.sum(grad_t.astype(F32) * o_ref[:, span].T.astype(F32), axis=0, keepdims=True)
    acc[...] = jnp.zeros_like(acc)
    start = start_ref[0]
    logs = log_ref[0]

    @pl.when(j == 0)
    def _():
        for copy in takes:
            copy.wait()

    def tile(t, masked):
        slot = slot_ref[t]
        keys = keys_ref[slot]
        probs = jnp.exp2(dot_nn(keys, q_t[...]) * (scale * LOG2E) - logs)
        if masked:
            probs = jnp.where(allowed_pairs(t, last, start, probs.shape), probs, 0.0)
        grad_scores = (probs * (dot_nn(values_ref[slot], g_t[...]) - delta[...])).astype(BF)
        dv[slot] += dot_nn(probs.astype(BF), grads[...])
        dk[slot] += dot_nn(grad_scores, queries[...])
        acc[...] += dot_nn(keys.T, grad_scores)

    key_tiles(lo_ref[j], full_ref[j], last, tile)
    for n in range(heads):
        span = slice(n * size, (n + 1) * size)
        grad = (acc[:, n * BLOCK : (n + 1) * BLOCK] * scale).T.astype(BF).astype(F32)
        grad_raw, grad_gain = norm_rope_back(grad, raw_ref[:, span], gain_ref[...], cos_ref[...], sin_ref[...])
        dq_ref[:, span] = grad_raw.astype(BF)
        sum_ref[...] += jnp.sum(grad_gain, axis=0, keepdims=True)

    @pl.when(j == pl.num_programs(0) - 1)
    def _():
        def out(s, n):
            span = pl.ds(s, n)
            return (
                pltpu.make_async_copy(keys_ref.at[span], dk_ref.at[span], local.at[0]),
                pltpu.make_async_copy(values_ref.at[span], dv_ref.at[span], local.at[1]),
            )

        @pl.loop(0, slots, step=8)
        def _(s):
            for i in range(8):
                keys_ref[s + i] = (dk[s + i] * scale).astype(BF)
                values_ref[s + i] = dv[s + i].astype(BF)
            for copy in out(s, 8):
                copy.start()

        for copy in out(0, slots):
            copy.wait()


def by_rows(array, rows=BLOCK):
    return pl.BlockSpec((rows,) + array.shape[1:], lambda j, *_: (j,) + (0,) * (array.ndim - 1))


def resident(array):
    return pl.BlockSpec(array.shape, lambda j, *_: (0,) * array.ndim, pipeline_mode=pl.Buffered(1))


def shaped(shape, dtype):
    return jax.ShapeDtypeStruct(shape, dtype)


def expert(rows, plain, weights, block=512):
    count, ff = plain.shape
    outs = (shaped(rows.shape, BF), shaped((count, ff), BF), shaped((count, ff), BF), shaped((count, 2 * ff), BF))
    return pl.pallas_call(
        expert_kernel,
        out_shape=outs,
        grid=(count // block,),
        in_specs=[by_rows(rows, block), by_rows(plain, block), resident(weights)],
        out_specs=tuple(by_rows(x, block) for x in outs),
        compiler_params=pltpu.CompilerParams(vmem_limit_bytes=VMEM_LIMIT),
        cost_estimate=cost_of(20),
        name="expert",
    )(rows, plain, weights)


def attend_forward(meta, raw, gain, cosine, sine, keys, values, start):
    rows, wide = raw.shape
    blocks, size = rows // BLOCK, keys.shape[2]
    lanes = wide // size * BLOCK
    outs = (shaped((rows, wide), BF), shaped((rows, wide), BF), shaped((blocks, 1, lanes), F32))
    return pl.pallas_call(
        attend_forward_kernel,
        out_shape=outs,
        grid_spec=pltpu.PrefetchScalarGridSpec(
            num_scalar_prefetch=4,
            grid=(blocks,),
            in_specs=[
                by_rows(raw),
                resident(gain),
                by_rows(cosine),
                by_rows(sine),
                resident(keys),
                resident(values),
                by_rows(start, 1),
            ],
            out_specs=(by_rows(outs[0]), by_rows(outs[1]), by_rows(outs[2], 1)),
            scratch_shapes=[pltpu.VMEM((size, lanes), BF), pltpu.VMEM((size, lanes), F32), pltpu.VMEM((8, lanes), F32)],
        ),
        compiler_params=pltpu.CompilerParams(vmem_limit_bytes=VMEM_LIMIT),
        cost_estimate=cost_of(30),
        name="attend",
    )(*meta, raw, gain, cosine, sine, keys, values, start)


def attend_backward(meta, raw, gain, cosine, sine, keys, values, start, queries, attended, grads, w_out_t, logs):
    rows, wide = raw.shape
    blocks, size = rows // BLOCK, keys.shape[2]
    lanes = wide // size * BLOCK
    outs = (shaped((rows, wide), BF), shaped((1, size), F32), shaped(keys.shape, BF), shaped(values.shape, BF))
    return pl.pallas_call(
        attend_backward_kernel,
        out_shape=outs,
        grid_spec=pltpu.PrefetchScalarGridSpec(
            num_scalar_prefetch=4,
            grid=(blocks,),
            in_specs=[
                by_rows(raw),
                resident(gain),
                by_rows(cosine),
                by_rows(sine),
                pl.BlockSpec(memory_space=pl.ANY),
                pl.BlockSpec(memory_space=pl.ANY),
                by_rows(start, 1),
                by_rows(queries),
                by_rows(attended),
                by_rows(grads),
                resident(w_out_t),
                by_rows(logs, 1),
            ],
            out_specs=(by_rows(outs[0]), resident(outs[1])) + (pl.BlockSpec(memory_space=pl.ANY),) * 2,
            scratch_shapes=[
                pltpu.VMEM((lanes, size), BF),
                pltpu.VMEM((size, lanes), BF),
                pltpu.VMEM((lanes, size), BF),
                pltpu.VMEM((size, lanes), BF),
                pltpu.VMEM((1, lanes), F32),
                pltpu.VMEM((size, lanes), F32),
                pltpu.VMEM(keys.shape, F32),
                pltpu.VMEM(values.shape, F32),
                pltpu.VMEM(keys.shape, BF),
                pltpu.VMEM(values.shape, BF),
                dma(2),
            ],
        ),
        compiler_params=pltpu.CompilerParams(vmem_limit_bytes=VMEM_LIMIT),
        cost_estimate=cost_of(40),
        name="attend_back",
    )(*meta, raw, gain, cosine, sine, keys, values, start, queries, attended, grads, w_out_t, logs)


def all_to_all(stacked):
    return lax.all_to_all(stacked, ("head", "blk"), split_axis=0, concat_axis=0, tiled=True)


def body(
    tokens,
    norm_gain,
    w_query,
    key_weight,
    value_weight,
    query_gain,
    key_gain,
    w_out,
    mix_gain,
    w_router,
    expert_gate_up,
    expert_down,
    lengths,
    block_deal,
    routes,
    cotangent,
):
    own, width = tokens.shape
    size = query_gain.shape[0]
    scale = size ** (-0.5)
    blk = lax.axis_index("blk")
    plane, core = blk // 4, blk % 2
    devices = lax.axis_size("head") * lax.axis_size("blk")
    experts = w_router.shape[0] * 2
    cap = own * routes.shape[1] // experts
    gate_up, down = expert_gate_up[0], expert_down[0]
    ff = down.shape[0]
    group_rows = 8 * own
    q_cols = w_query.shape[1] // 4
    heads = q_cols // size

    group_blocks = plane * 4 + jnp.array([0, 2, 1, 3], jnp.int32)
    ids = jnp.arange(block_deal.shape[0], dtype=jnp.int32)
    last = jnp.sum(jnp.where(group_blocks[:, None] == ids[None, :], block_deal[None, :], 0), axis=1)
    slots = (ids % 2) * (ids.shape[0] // 2) + (ids // 4) * 2 + (ids % 4) // 2
    slot_of = jnp.sum(jnp.where(block_deal[None, :] == ids[:, None], slots[None, :], 0), axis=1)
    place = (last[:, None] * BLOCK + jnp.arange(BLOCK, dtype=jnp.int32)[None, :]).reshape(-1)
    passed = place[:, None] >= jnp.cumsum(lengths)[None, :]
    start = jnp.sum(jnp.where(passed, lengths[None, :], 0), axis=1)
    start_rows = start.reshape(-1, 1, BLOCK)
    meta = (start_rows[:, 0, 0] // BLOCK, (start_rows[:, 0, BLOCK - 1] + BLOCK - 1) // BLOCK, last, slot_of)
    start_rows = jnp.tile(start_rows, (1, 1, heads))
    offsets = (place - start).astype(F32).reshape(-1, 1, BLOCK)
    spacing = ROPE_BASE ** (-2.0 * jnp.arange(size // 2, dtype=F32) / size)
    spacing = jnp.concatenate([spacing, spacing])[None]

    normed = Made(own, width)
    depth = w_query.shape[0]
    out_pack = w_out.reshape(4, q_cols, depth).transpose(2, 0, 1).reshape(depth, -1)
    side = lax.axis_index("head") == jnp.arange(2, dtype=jnp.int32)
    router_pack = jnp.where(side[None, :, None], w_router.T[:, None, :], 0).astype(BF).reshape(depth, experts)
    w_qkv, w_out_t, w_router_t, group_tokens, assign_low, chosen, cosine, sine = launch(
        [
            norm_flow(tokens, norm_gain[None], normed),
            plane_gather_flow([(w_query, q_cols, 1), (key_weight, size, 2), (value_weight, size, 2)], "x", "y", ahead="zhc"),
            plane_gather_flow([(out_pack, q_cols, 1)], "y", "x", ahead="zhc"),
            plane_gather_flow([(router_pack, experts, 1)], "y", "x", ahead="z"),
            ring_gather_flow(normed),
            tables_flow(routes, offsets, spacing, experts, cap),
        ],
        0,
        45,
    )
    normed_group = group_tokens.reshape(group_rows, width)
    w_qkv, w_out_t = w_qkv.reshape(width, -1), w_out_t.reshape(width, -1)
    w_router_t = jnp.sum(w_router_t.reshape(-1, 2, depth, experts), axis=1).reshape(width, experts)

    q_gain, k_gain = query_gain[None], key_gain[None]
    key, value = Made(group_rows // 2, size), Made(group_rows // 2, size)
    q_raw, k_raw, keys, values, grad_rows = launch(
        [
            project_flow(normed_group, w_qkv, k_gain, cosine, sine, q_cols, key, value),
            plane_gather_flow(key, "x", "y"),
            plane_gather_flow(value, "y", "x"),
            product_flow(assign_low, cotangent),
        ],
        1,
        35,
    )
    grad_rows = all_to_all(grad_rows.reshape(devices, cap, width)).reshape(-1, width)
    keys, values = keys.reshape(-1, BLOCK, size), values.reshape(-1, BLOCK, size)
    queries, attended, logs = attend_forward(meta, q_raw, q_gain, cosine, sine, keys, values, start_rows)

    attention = Made(own, width)
    residual, mixed, gates, outgoing = launch(
        [
            product_scatter_flow([attended], w_out_t, attention),
            route_flow(tokens, mix_gain[None], w_router_t, chosen, assign_low, attention),
        ],
        2,
        30,
    )
    outgoing, grad_rows = lax.optimization_barrier((outgoing, grad_rows))
    arrived = all_to_all(outgoing.reshape(devices, cap, -1)).reshape(experts * cap, -1)

    plain_grad = lax.optimization_barrier(dot_nt(grad_rows, down))
    rows, plain_grad = lax.optimization_barrier((arrived, plain_grad))
    back, hidden, gated, grad_both = expert(rows, plain_grad, gate_up)
    back = all_to_all(back.reshape(devices, cap, -1)).reshape(experts * cap, -1)
    back, expert_out = lax.optimization_barrier((back, dot_nn(hidden, down).astype(BF)))
    grad_down = dot_tn(gated, grad_rows)
    grad_gate_up = dot_tn(rows[:, :width], grad_both)

    grad_attention = Made(own, width)
    grad_residual, grad_mix_gain, grad_router_t, grad_group = launch(
        [
            mix_back_flow(back, assign_low, gates, mixed, w_router_t, residual, mix_gain[None], cotangent, grad_attention),
            ring_gather_flow(grad_attention),
        ],
        3,
        25,
    )
    grad_group = grad_group.reshape(group_rows, width)
    grad_group, expert_out = lax.optimization_barrier((grad_group, expert_out))
    expert_out = all_to_all(expert_out.reshape(devices, cap, width)).reshape(-1, width)
    grad_q, grad_query_gain, grad_keys, grad_values = attend_backward(
        meta, q_raw, q_gain, cosine, sine, keys, values, start_rows, queries, attended, grad_group, w_out_t, logs
    )

    split = (2, 4, 4, group_rows // 2, size)
    grad_key, grad_value, grad_wq, grad_wo = launch(
        [
            plane_scatter_flow(grad_keys.reshape(split), "y", "x", from_core=True),
            plane_scatter_flow(grad_values.reshape(split), "x", "y", from_core=True),
            product_flow(normed_group, grad_q),
            product_flow(grad_group, attended),
        ],
        4,
        35,
    )

    grad_key, expert_out = lax.optimization_barrier((grad_key, expert_out))
    plane_split = (4, 4, 4 * depth, -1)
    zeros, ones = jnp.zeros((width,), F32), jnp.ones((width,), F32)
    gains = jnp.concatenate([zeros, grad_mix_gain[0], grad_query_gain[0], zeros[: 7 * size], norm_gain, ones, ones[: 8 * size]])
    units, grad_kv, grad_wkv, key_gain_sum = Made(group_rows, width), Made(group_rows, 2 * size), Made(4, 4, 4 * depth, 2 * size), Made()
    grad_normed = Made(own, width)
    grad_wq, grad_wo, gains, grad_wkv, grad_wr, output, grad_tokens = launch(
        [
            key_back_flow(grad_key, grad_value, k_raw, k_gain, cosine, sine, normed_group, grad_kv, grad_wkv, units, key_gain_sum),
            plane_scatter_flow(grad_wq.reshape(plane_split), "y", "x", last_in="zhc"),
            plane_scatter_flow(grad_wo.reshape(plane_split), "x", "y", last_in="zhc"),
            product_scatter_flow([grad_q, grad_kv], w_qkv, grad_normed, units, gains.reshape(2, -1, size), key_gain_sum),
            plane_scatter_flow(grad_wkv, "y", "x", last_in="zhc"),
            plane_scatter_flow(grad_router_t.reshape(plane_split), "x", "y", last_in="z"),
            output_flow(residual, gates, assign_low, expert_out),
            tokens_grad_flow(tokens, norm_gain[None], grad_residual, grad_normed),
        ],
        5,
        50,
    )
    gains = gains.reshape(-1)
    grad_w_query = grad_wq.astype(F32).transpose(1, 0, 2).reshape(depth, -1)
    grad_kv_w = jnp.sum(grad_wkv.astype(F32).reshape(2, 2, depth, 2, size), axis=1)
    grad_w_key = grad_kv_w[:, :, 0].transpose(1, 0, 2).reshape(depth, -1)
    grad_w_value = grad_kv_w[:, :, 1].transpose(1, 0, 2).reshape(depth, -1)
    grad_w_out = grad_wo.astype(F32).transpose(0, 2, 1).reshape(-1, depth)
    grad_w_router = lax.dynamic_slice_in_dim(add_up(grad_wr), lax.axis_index("head") * (experts // 2), experts // 2, 1).T
    return (
        output,
        grad_tokens,
        gains[:width],
        grad_w_query,
        grad_w_key,
        grad_w_value,
        gains[2 * width : 2 * width + size],
        gains[2 * width + size : 2 * width + 2 * size],
        grad_w_out,
        gains[width : 2 * width],
        grad_w_router,
        grad_gate_up[None],
        grad_down[None],
    )


def solution(mesh):
    rows, both = P(("head", "blk"), None), P("blk", "head")
    expert, turned = P(("head", "blk"), None, None), P("head", "blk")
    in_specs = (rows, P(), both, both, both, P(), P(), turned, P(), turned, expert, expert, P(), P(), rows, rows)
    out_specs = (rows, rows, P(), both, both, both, P(), P(), turned, P(), turned, expert, expert)
    return jax.shard_map(body, mesh=mesh, in_specs=in_specs, out_specs=out_specs, check_vma=False)
```

```python
import math

import jax
import jax.numpy as jnp
from jax import lax
from jax.experimental import pallas as pl
from jax.experimental.pallas import tpu as pltpu
from jax.sharding import PartitionSpec as P

MESH = pl.DeviceIdType.MESH
EPS = 1e-06
ROPE_BASE = 1000000.0
LOG2E = 1.4426950408889634
BF = jnp.bfloat16
F32 = jnp.float32
BLOCK = 256
VMEM_LIMIT = 60 << 20
SIZES = {"zc": 4, "c": 2, "x": 4, "y": 4, "zhc": 4, "z": 8, "yx": 16}


def peers_of(kind):
    h = lax.axis_index("head")
    b = lax.axis_index("blk")
    q, r = lax.div(b, 4), lax.rem(b, 4)
    if kind == "zc":
        return lax.div(r, 2) * 2 + h, lambda g: (lax.rem(g, 2), q * 4 + lax.div(g, 2) * 2 + lax.rem(r, 2))
    if kind == "z":
        return r * 2 + h, lambda g: (lax.rem(g, 2), q * 4 + lax.div(g, 2))
    if kind == "c":
        return lax.rem(b, 2), lambda g: (h, b - lax.rem(b, 2) + g)
    if kind == "x":
        return lax.rem(q, 4), lambda g: (h, (lax.div(q, 4) * 4 + g) * 4 + r)
    if kind == "y":
        return lax.div(q, 4), lambda g: (h, (g * 4 + lax.rem(q, 4)) * 4 + r)
    if kind == "yx":
        return q, lambda g: (h, g * 4 + r)
    return r, lambda g: (h, q * 4 + g)


def cost_of(microseconds):
    return pl.CostEstimate(flops=microseconds * 10**9, bytes_accessed=microseconds * 3 * 10**6, transcendentals=0)


class Flow:
    def __init__(self, inputs, outputs, scratch, partners, steps):
        self.inputs, self.outputs, self.scratch = inputs, outputs, scratch
        self.partners, self.steps = partners, steps


class Filler:
    def __init__(self, cost):
        self.cost = cost


class Clock:
    now = 0.0


def in_turn(flows):
    Clock.now = 0.0
    ready, waiting, fillers = [(0.0, i, steps) for i, steps in enumerate(flows)], [], []
    count = len(flows)
    while ready or fillers or waiting:
        for entry in [e for e in waiting if e[0].ref is not None]:
            waiting.remove(entry)
            ready.append((Clock.now, entry[1], entry[2]))
        ready.sort(key=lambda e: e[:2])
        if fillers and (not ready or ready[0][0] > Clock.now + 0.5):
            cost, order, steps = fillers.pop(0)
            Clock.now += cost
        else:
            when, order, steps = ready.pop(0)
            Clock.now = max(Clock.now, when) + 0.3
        result = next(steps, steps)
        if result is steps:
            continue
        if isinstance(result, Filler):
            fillers.append((result.cost, order, steps))
        elif isinstance(result, Made):
            waiting.append((result, order, steps))
        elif result is None or isinstance(result, float):
            ready.append((Clock.now if result is None else result, order, steps))
        else:
            ready += [(Clock.now, order, steps), (Clock.now, count, result)]
            count += 1


class Made:
    def __init__(self, *shape):
        self.shape, self.ref = shape, None


HOP = 3.0
RATE = 40e3
CORE_RATE = 200e3


def launch(flows, cid, cost):
    partners = sorted({p for flow in flows for p in flow.partners})

    def kernel(*refs):
        n_in, n_out = sum(len(f.inputs) for f in flows), sum(len(f.outputs) for f in flows)
        ins, outs, rest = list(refs[:n_in]), list(refs[n_in : n_in + n_out]), list(refs[n_in + n_out :])
        barrier = pltpu.get_barrier_semaphore()
        for kind, distance in partners:
            me, member = peers_of(kind)
            to = member(lax.rem(me + distance, SIZES[kind]))
            pl.semaphore_signal(barrier, inc=1, device_id=to, device_id_type=MESH)
        running = []
        for flow in flows:
            own = [[group.pop(0) for _ in part] for group, part in ((ins, flow.inputs), (outs, flow.outputs), (rest, flow.scratch))]
            running.append(flow.steps(*own))
            next(running[-1])
        pl.semaphore_wait(barrier, len(partners))
        in_turn(running)

    return pl.pallas_call(
        kernel,
        out_shape=tuple(jax.ShapeDtypeStruct(s, d) for f in flows for s, d, _ in f.outputs),
        in_specs=[pl.BlockSpec(memory_space=space) for f in flows for _, space in f.inputs],
        out_specs=tuple(pl.BlockSpec(memory_space=space) for f in flows for _, _, space in f.outputs),
        scratch_shapes=[x for f in flows for x in f.scratch],
        compiler_params=pltpu.CompilerParams(collective_id=cid, has_side_effects=True, vmem_limit_bytes=VMEM_LIMIT),
        cost_estimate=cost_of(cost),
        name=f"links_{cid}",
    )(*[x for f in flows for x, _ in f.inputs])


def remote(src, dst, send, recv, device):
    return pltpu.make_async_remote_copy(
        src_ref=src, dst_ref=dst, send_sem=send, recv_sem=recv, device_id=device, device_id_type=MESH
    )


def piece(ref, which):
    rows = ref.shape[0] // 2
    return ref.at[pl.ds(which * rows, rows)]


def ring_partners(kind):
    return [(kind, 1), (kind, 3)]


class RingGather:
    def __init__(self, kind, slot, src, send, recv):
        me, member = peers_of(kind)
        up, down = lax.rem(me + 1, 4), lax.rem(me + 3, 4)

        def copy(source, target, i, to):
            return remote(source, target, send.at[i], recv.at[i], member(to))

        mine = slot(me)
        self.copies = [
            copy(piece(src, 0), piece(mine, 0), 0, up),
            copy(piece(src, 1), piece(mine, 1), 1, up),
            copy(piece(src, 1), piece(mine, 1), 2, down),
            copy(piece(src, 0), piece(mine, 0), 3, down),
            copy(piece(slot(down), 0), piece(slot(down), 0), 4, up),
            copy(piece(slot(up), 1), piece(slot(up), 1), 5, down),
        ]

    def start(self):
        for i in (0, 2, 1, 3):
            self.copies[i].start()

    def forward(self):
        self.copies[0].wait_recv()
        self.copies[4].start()
        self.copies[2].wait_recv()
        self.copies[5].start()

    def near(self):
        self.copies[1].wait_recv()
        self.copies[3].wait_recv()

    def far(self):
        self.copies[4].wait_recv()
        self.copies[5].wait_recv()

    def sent(self):
        for copy in self.copies:
            copy.wait_send()


class RingScatter:
    def __init__(self, kind, chunk, bufs, send, recv, raw=None):
        raw = raw or chunk
        self.me, member = peers_of(kind)
        self.up, self.down, self.far = (lax.rem(self.me + k, 4) for k in (1, 3, 2))
        self.chunk, self.bufs = chunk, bufs

        def copy(source, target, i, to):
            return remote(source, bufs.at[target], send.at[i], recv.at[i], member(to))

        self.copies = [
            copy(piece(raw(self.far), 0), 0, 0, self.up),
            copy(piece(raw(self.far), 1), 1, 1, self.down),
            copy(piece(raw(self.up), 1), 2, 2, self.up),
            copy(piece(raw(self.down), 0), 3, 3, self.down),
            copy(bufs.at[6], 4, 4, self.up),
            copy(bufs.at[7], 5, 5, self.down),
        ]

    def start_far(self):
        self.copies[0].start()
        self.copies[1].start()

    def start_up(self):
        self.copies[2].start()

    def start_down(self):
        self.copies[3].start()

    def add(self):
        self.copies[0].wait_recv()
        self.bufs[6] = (piece(self.chunk(self.up), 0)[...].astype(F32) + self.bufs[0].astype(F32)).astype(BF)
        self.copies[4].start()
        self.copies[1].wait_recv()
        self.bufs[7] = (piece(self.chunk(self.down), 1)[...].astype(F32) + self.bufs[1].astype(F32)).astype(BF)
        self.copies[5].start()

    def total(self, which):
        first, second = ((4, 3), (2, 5))[which]
        self.copies[first].wait_recv()
        self.copies[second].wait_recv()
        return self.bufs[first].astype(F32) + self.bufs[second].astype(F32)

    def sent(self):
        for copy in self.copies:
            copy.wait_send()


def dma(*shape):
    return pltpu.SemaphoreType.DMA(shape)


def ring_gather_flow(made):
    shape = (2, 4) + made.shape

    def steps(ins, outs, scratch):
        (out,), src = outs, made.ref
        send, recv, pass_send, pass_recv, local = scratch
        yield
        me, _ = peers_of("zc")
        core, member = peers_of("c")
        ring = RingGather("zc", lambda g: out.at[core, g], src, send, recv)

        def passing(k):
            g = lax.rem(me + k, 4)
            return remote(src if k == 0 else out.at[core, g], out.at[core, g], pass_send.at[k], pass_recv.at[k], member(1 - core))

        passes = [passing(k) for k in range(4)]
        unit = math.prod(made.shape) * 2 / RATE
        begun = Clock.now
        ring.start()
        passes[0].start()
        yield begun + HOP + unit / 2
        ring.forward()
        back = pltpu.make_async_copy(src, out.at[core, me], local.at[0])
        back.start()
        yield begun + HOP + unit
        ring.near()
        passes[1].start()
        passes[3].start()
        yield begun + 2 * HOP + 1.5 * unit
        ring.far()
        passes[2].start()
        yield Clock.now + HOP + 2.0
        back.wait()
        ring.sent()
        for copy in passes:
            copy.wait()

    return Flow(
        [],
        [(shape, BF, pl.ANY)],
        [dma(6), dma(6), dma(4), dma(4), dma(1)],
        ring_partners("zc") + [("c", 1)],
        steps,
    )


def plane_gather_flow(arrays, first, second, ahead=None):
    to_core = ahead is None
    if ahead == "zhc":
        shard = (4, arrays[0][0].shape[0], sum(columns for _, columns, _ in arrays))
    elif ahead == "z":
        shard = (8,) + arrays[0][0].shape
    else:
        shard = arrays.shape
    shape = ((2,) if to_core else ()) + (4, 4) + shard
    n_ahead = SIZES[ahead] if ahead else 1

    def steps(ins, outs, scratch):
        (out,) = outs
        stage, send, recv, pass_send, pass_recv, local, ahead_send, ahead_recv = scratch
        core, member = peers_of("c")
        here, _ = peers_of(first)
        there, _ = peers_of(second)
        view = out.at[core] if to_core else out

        def slot(a, b):
            return view.at[b, a] if first == "x" else view.at[a, b]

        if ahead:
            mine, at = peers_of(ahead)

            def parts(to):
                if ahead == "z":
                    return [(ins[0], stage.at[mine])]
                found, begin = [], 0
                for ref, (_, columns, share) in zip(ins, arrays):
                    source = ref.at[:, pl.ds(pl.multiple_of(lax.div(to, share) * columns, columns), columns)]
                    found.append((source, stage.at[mine, :, pl.ds(begin, columns)]))
                    begin += columns
                return found

            early = [pltpu.make_async_copy(source, target, local.at[i]) for i, (source, target) in enumerate(parts(mine))]
            for k in range(1, n_ahead):
                to = lax.rem(mine + k, n_ahead)
                for i, (source, target) in enumerate(parts(to)):
                    early.append(remote(source, target, ahead_send.at[i, k], ahead_recv.at[i, k], at(to)))
            local_parts = len(parts(mine))
            for copy in early[:local_parts]:
                copy.start()
            yield
            for copy in early[local_parts:]:
                copy.start()
            yield Clock.now + HOP + 7.0
            for copy in early:
                copy.wait()
            src = stage
        else:
            src = arrays.ref
            yield
        ring = RingGather(first, lambda g: slot(g, there), src, send.at[4], recv.at[4])
        columns = [lax.rem(here + k, 4) for k in range(4)]
        rings = [
            RingGather(second, lambda g, a=a: slot(a, g), src if k == 0 else slot(a, there), send.at[k], recv.at[k])
            for k, a in enumerate(columns)
        ]

        def passing(k, m):
            ref = slot(columns[k], lax.rem(there + m, 4))
            return remote(src if k == m == 0 else ref, ref, pass_send.at[k * 4 + m], pass_recv.at[k * 4 + m], member(1 - core))

        passes = {}

        def hand_over(k, m):
            if to_core:
                passes[k, m] = passing(k, m)
                passes[k, m].start()

        unit = math.prod(shard) * 2 / RATE
        begun = Clock.now
        ring.start()
        rings[0].start()
        hand_over(0, 0)
        yield begun + HOP + unit / 2
        ring.forward()
        back = pltpu.make_async_copy(src, slot(here, there), local.at[0])
        back.start()
        yield
        rings[0].forward()
        yield begun + HOP + unit
        ring.near()
        for k in (1, 3):
            rings[k].start()
            hand_over(k, 0)
        yield begun + 2 * HOP + 1.5 * unit
        ring.far()
        rings[2].start()
        hand_over(2, 0)
        yield
        for i, k in enumerate((0, 1, 3, 2)):
            if k > 0:
                yield begun + 2 * HOP + (1.5 * i + 0.5) * unit
                rings[k].forward()
            yield begun + 2 * HOP + (1.5 * i + 1.0) * unit
            rings[k].near()
            hand_over(k, 1)
            hand_over(k, 3)
        for i, k in enumerate((0, 1, 3, 2)):
            yield begun + 3 * HOP + (1.5 * i + 1.5) * unit
            rings[k].far()
            hand_over(k, 2)
        yield Clock.now + HOP
        back.wait()
        ring.sent()
        for one in rings:
            one.sent()
        for copy in passes.values():
            copy.wait()

    return Flow(
        [] if to_core else [(array, pl.ANY) for array, *_ in arrays],
        [(shape, BF, pl.ANY)],
        [pltpu.VMEM((8, 128) if to_core else shard, BF), dma(5, 6), dma(5, 6), dma(16), dma(16), dma(3), dma(3, 8), dma(3, 8)],
        ring_partners("x") + ring_partners("y") + ([("c", 1)] if to_core else []) + [(ahead, k) for k in range(1, n_ahead)],
        steps,
    )


def product_flow(left, right):
    columns, width = left.shape[1], right.shape[1]

    def steps(ins, outs, scratch):
        (out,) = outs
        left_ref, right_ref, local = scratch
        copies = [pltpu.make_async_copy(source, target, local.at[i]) for i, (source, target) in enumerate(zip(ins, (left_ref, right_ref)))]
        for copy in copies:
            copy.start()
        yield
        yield Filler(1.0)
        for copy in copies:
            copy.wait()
        for column in range(0, columns, 256):
            span = slice(column, column + 256)
            out[span, :] = dot_tn(left_ref[:, span], right_ref[...]).astype(BF)
            yield Filler(1.0)

    return Flow(
        [(left, pl.ANY), (right, pl.ANY)],
        [((columns, width), BF, pltpu.VMEM)],
        [pltpu.VMEM(left.shape, BF), pltpu.VMEM(right.shape, BF), dma(2)],
        [],
        steps,
    )


def output_flow(residual, gates, assign, expert_out):
    own, width = residual.shape
    experts = gates.shape[1]
    count = expert_out.shape[0]

    def steps(ins, outs, scratch):
        residual_ref, gates_ref, assign_ref, expert_hbm = ins
        (out,) = outs
        expert_ref, mixing, local = scratch
        copy = pltpu.make_async_copy(expert_hbm, expert_ref, local.at[0])
        copy.start()
        wide = (experts, count)
        cap = count // experts
        spread = (lax.broadcasted_iota(jnp.int32, wide, 1) // cap == lax.broadcasted_iota(jnp.int32, wide, 0)).astype(F32).astype(BF)
        taken = assign_ref[...].astype(F32)
        high = gates_ref[...].astype(BF)
        low = (gates_ref[...] - high.astype(F32)).astype(BF)
        mixing[0] = (dot_nn(high, spread) * taken).astype(BF)
        mixing[1] = (dot_nn(low, spread) * taken).astype(BF)
        yield
        yield Filler(1.0)
        copy.wait()
        for column in range(0, width, 512):
            span = slice(column, column + 512)
            rows = expert_ref[:, span]
            out[:, span] = (residual_ref[:, span] + dot_nn(mixing[0], rows) + dot_nn(mixing[1], rows)).astype(BF)
            yield Filler(1.0)

    return Flow(
        [(residual, pltpu.VMEM), (gates, pltpu.VMEM), (assign, pltpu.VMEM), (expert_out, pl.ANY)],
        [(residual.shape, BF, pltpu.VMEM)],
        [pltpu.VMEM(expert_out.shape, BF), pltpu.VMEM((2, own, count), BF), dma(1)],
        [],
        steps,
    )


sum_partners = [("yx", k) for k in range(1, 16)] + [("z", k) for k in range(1, 8)]


def sum_room(shape):
    return [pltpu.VMEM((16,) + shape, F32), pltpu.VMEM((8,) + shape, F32), pltpu.VMEM(shape, F32), dma(16), dma(16), dma(8), dma(8)]


def sum_steps(src, gains, out, scratch):
    wide, far, middle, sends, recvs, far_sends, far_recvs = scratch
    me, member = peers_of("yx")
    copies = []
    for k in range(1, 16):
        copies.append(remote(src, wide.at[me], sends.at[k], recvs.at[k], member(lax.rem(me + k, 16))))
        copies[-1].start()
    wide[me] = src[...]
    yield Clock.now + HOP + 4.0
    for copy in copies:
        copy.wait()
    middle[...] = jnp.sum(wide[...], axis=0)
    ring, ring_member = peers_of("z")
    late = []
    for k in range(1, 8):
        late.append(remote(middle, far.at[ring], far_sends.at[k], far_recvs.at[k], ring_member(lax.rem(ring + k, 8))))
        late[-1].start()
    far[ring] = middle[...]
    yield Clock.now + HOP + 3.0
    for copy in late:
        copy.wait()
    out[...] = jnp.sum(far[...], axis=0) / gains[1]


def product_scatter_flow(lefts, right, done, units=None, gains=None, key_gain=None):
    arrays = [left for left in lefts if not isinstance(left, Made)]
    own, wide = lefts[0].shape[0] // 8, right.shape[0]
    spans = [0]
    for left in lefts:
        spans.append(spans[-1] + left.shape[1])

    def steps(ins, outs, scratch):
        given = list(ins[: len(arrays)])
        left_refs = [left.ref if isinstance(left, Made) else given.pop(0) for left in lefts]
        right_ref = ins[len(arrays)]
        out, theirs, came, chunks, bufs, send, recv, pass_send, pass_recv, *rest = scratch
        core, member = peers_of("c")
        me, _ = peers_of("zc")
        ring = RingScatter("zc", lambda g: chunks.at[g], bufs, send, recv)

        if units is not None:
            gains_ref = ins[len(arrays) + 1]
            unit_ref = units.ref
            sums, *sum_scratch = rest
            sums[...] = gains_ref[0]
            sums[33:34, :] += key_gain.ref[...]

        def product(c, k, column):
            row = pl.multiple_of((c * 4 + lax.rem(me + k, 4)) * own, own)
            value = sum(
                dot_nt(left_ref[pl.ds(row, own), :], right_ref[column : column + 512, spans[i] : spans[i + 1]])
                for i, left_ref in enumerate(left_refs)
            )
            if units is not None:
                row_sum = jnp.sum(value * unit_ref[pl.ds(row, own), column : column + 512].astype(F32), axis=0, keepdims=True)
                for lane in range(0, 512, 128):
                    at = (column + lane) // 128
                    sums[at : at + 1, :] += row_sum[:, lane : lane + 128]
            return value

        passes = [
            remote(theirs.at[k], came.at[k], pass_send.at[k], pass_recv.at[k], member(1 - core)) for k in range(4)
        ]
        for k in (2, 1, 3, 0):
            if k == 1:
                yield
                Clock.now += 0.7
                passes[2].start()
            for column in range(0, wide, 512):
                theirs[k, :, column : column + 512] = product(1 - core, k, column).astype(BF)
            if k != 2:
                Clock.now += 0.7
                passes[k].start()
                yield
        for k in (2, 1, 3, 0):
            passes[k].wait_recv()
            g = lax.rem(me + k, 4)
            for column in range(0, wide, 512):
                span = slice(column, column + 512)
                value = product(core, k, column) + came[k, :, span].astype(F32)
                if k == 0:
                    out[:, span] = value
                else:
                    chunks[g, :, span] = value.astype(BF)
            Clock.now += 0.7
            if k == 2:
                begun = Clock.now
                ring.start_far()
            elif k == 1:
                ring.start_up()
            elif k == 3:
                ring.start_down()
            yield
        unit = own * wide * 2 / RATE
        if units is not None:
            yield sum_steps(sums, gains_ref, outs[0], sum_scratch)
        yield begun + HOP + unit / 2
        ring.add()
        yield begun + 2 * HOP + 1.5 * unit
        for h in range(2):
            rows = slice(h * own // 2, (h + 1) * own // 2)
            out[rows, :] += ring.total(h)
        done.ref = out
        yield Clock.now + 2.0
        ring.sent()
        for copy in passes:
            copy.wait_send()

    return Flow(
        [(x, pltpu.VMEM) for x in (*arrays, right)] + ([] if units is None else [(gains, pltpu.VMEM)]),
        [] if units is None else [(gains.shape[1:], F32, pltpu.VMEM)],
        [
            pltpu.VMEM((own, wide), F32),
            pltpu.VMEM((4, own, wide), BF),
            pltpu.VMEM((4, own, wide), BF),
            pltpu.VMEM((4, own, wide), BF),
            pltpu.VMEM((8, own // 2, wide), BF),
            dma(6),
            dma(6),
            dma(4),
            dma(4),
        ]
        + ([] if units is None else [pltpu.VMEM(gains.shape[1:], F32)] + sum_room(gains.shape[1:])),
        ring_partners("zc") + [("c", 1)] + ([] if units is None else sum_partners),
        steps,
    )


def plane_scatter_flow(array, first, second, from_core=False, last_in=None):
    rows, columns = array.shape[-2:]
    n_last = SIZES[last_in] if last_in else 1
    result = (n_last, rows // 4, columns) if last_in else (rows, columns)

    def steps(ins, outs, scratch):
        src, (out,) = array.ref if isinstance(array, Made) else ins[0], outs
        came, sums, middle, bufs, late_bufs, send, recv, late_send, late_recv, pass_send, pass_recv, local, cut, cut_send, cut_recv = scratch
        core, member = peers_of("c")
        me, _ = peers_of(first)

        def along(ref, g):
            return ref.at[g] if first == "y" else ref.at[:, g]

        order = [lax.rem(me + k, 4) for k in (2, 1, 3, 0)]
        unit = 4 * rows * columns * 2 / RATE
        loads = [
            pltpu.make_async_copy(along(src.at[core] if from_core else src, g), along(sums, g), local.at[i])
            for i, g in enumerate(order)
            if from_core or i > 0
        ]
        passes = []
        if from_core:
            ring = RingScatter(first, lambda g: along(sums, g), bufs, send, recv)
            for i, g in enumerate(order):
                loads[i].start()
                passes.append(
                    remote(along(src.at[1 - core], g), along(came, g), pass_send.at[i], pass_recv.at[i], member(1 - core))
                )
            yield
            for copy in passes:
                copy.start()
            yield Clock.now + HOP + unit * RATE / CORE_RATE
            starts = [ring.start_far, ring.start_up, ring.start_down, lambda: None]
            for i, g in enumerate(order):
                loads[i].wait()
                passes[i].wait_recv()
                for k in range(4):
                    total = along(sums, g)[k].astype(F32) + along(came, g)[k].astype(F32)
                    along(sums, g)[k] = total.astype(BF)
                starts[i]()
                if i == 0:
                    begun = Clock.now
                yield Clock.now + unit * RATE / CORE_RATE if i < 3 else None
        else:
            ring = RingScatter(first, lambda g: along(sums, g), bufs, send, recv, raw=lambda g: along(src, g))
            for load in loads:
                load.start()
            yield
            begun = Clock.now
            ring.start_far()
            ring.start_up()
            ring.start_down()
            yield begun + HOP + unit / 2
            for load in loads:
                load.wait()
        if from_core:
            yield begun + HOP + unit / 2
        ring.add()
        yield begun + 2 * HOP + 1.5 * unit
        own = along(sums, me)
        for h in range(2):
            came_half = ring.total(h)
            for k in range(2):
                middle[h * 2 + k] = (own[h * 2 + k].astype(F32) + came_half[k]).astype(BF)
        Clock.now += 1.0
        begun = Clock.now
        last = RingScatter(second, lambda g: middle.at[g], late_bufs, late_send, late_recv)
        last.start_far()
        last.start_up()
        last.start_down()
        yield begun + HOP + unit / 8
        last.add()
        yield begun + 2 * HOP + 0.4 * unit
        for h in range(2):
            total = (piece(middle.at[last.me], h)[...].astype(F32) + last.total(h)).astype(BF)
            if last_in:
                cut[2 * h] = total[: rows // 4]
                cut[2 * h + 1] = total[rows // 4 :]
            else:
                out[h * rows // 2 : (h + 1) * rows // 2, :] = total
        cuts = []
        if last_in:
            mine, at = peers_of(last_in)
            share = n_last // 4
            for k in range(1, n_last):
                to = lax.rem(mine + k, n_last)
                cuts.append(remote(cut.at[lax.div(to, share)], out.at[mine], cut_send.at[k], cut_recv.at[k], at(to)))
                cuts[-1].start()
            out[mine] = cut[lax.div(mine, share)]
        yield Clock.now + HOP + 3.0
        ring.sent()
        last.sent()
        for copy in passes:
            copy.wait_send()
        for copy in cuts:
            copy.wait()

    block = (4, 4, rows, columns)
    return Flow(
        [] if isinstance(array, Made) else [(array, pl.ANY)],
        [(result, BF, pltpu.VMEM)],
        [
            pltpu.VMEM(block if from_core else (8, 128), BF),
            pltpu.VMEM(block, BF),
            pltpu.VMEM((4, rows, columns), BF),
            pltpu.VMEM((8, 2, rows, columns), BF),
            pltpu.VMEM((8, rows // 2, columns), BF),
            dma(6),
            dma(6),
            dma(6),
            dma(6),
            dma(4),
            dma(4),
            dma(4),
            pltpu.VMEM((4, rows // 4, columns), BF),
            dma(8),
            dma(8),
        ],
        ring_partners("x")
        + ring_partners("y")
        + ([("c", 1)] if from_core else [])
        + [(last_in, k) for k in range(1, n_last)],
        steps,
    )


def tables_flow(routes, offsets, spacing, experts, cap):
    own, top = routes.shape
    rows, size = offsets.size, spacing.shape[1]

    def steps(ins, outs, scratch):
        routes_ref, offsets_ref, spacing_ref = ins
        assign, chosen_ref, cosine, sine = outs
        yield
        yield Filler(1.0)
        lane = lax.broadcasted_iota(jnp.int32, (own, experts), 1)
        chosen = jnp.zeros((own, experts), F32)
        for k in range(top):
            chosen += (routes_ref[:, k : k + 1] == lane).astype(F32)
        chosen_ref[...] = chosen
        before = lax.broadcasted_iota(jnp.int32, (own, own), 0) > lax.broadcasted_iota(jnp.int32, (own, own), 1)
        earlier = dot_nn(before.astype(F32).astype(BF), chosen.astype(BF))
        wide = (experts, experts * cap)
        spread = (lax.broadcasted_iota(jnp.int32, wide, 1) // cap == lax.broadcasted_iota(jnp.int32, wide, 0)).astype(F32).astype(BF)
        slot = lax.rem(lax.broadcasted_iota(jnp.int32, (own, experts * cap), 1), cap).astype(F32)
        taken = (dot_nn(chosen.astype(BF), spread) > 0.5) & (dot_nn(earlier.astype(BF), spread) == slot)
        assign[...] = taken.astype(F32).astype(BF)
        yield Filler(1.0)
        sign = jnp.where(lax.broadcasted_iota(jnp.int32, (1, size), 1) < size // 2, -1.0, 1.0)
        for row in range(0, rows, BLOCK):
            span = slice(row, row + BLOCK)
            angles = jnp.broadcast_to(offsets_ref[row // BLOCK], (size, BLOCK)).T * spacing_ref[...]
            cosine[span, :] = jnp.cos(angles)
            sine[span, :] = jnp.sin(angles) * sign
            yield Filler(1.0)

    return Flow(
        [(routes, pltpu.VMEM), (offsets, pltpu.VMEM), (spacing, pltpu.VMEM)],
        [
            ((own, experts * cap), BF, pltpu.VMEM),
            ((own, experts), F32, pltpu.VMEM),
            ((rows, size), F32, pltpu.VMEM),
            ((rows, size), F32, pltpu.VMEM),
        ],
        [],
        [],
        steps,
    )


def norm_flow(tokens, gain, made):
    def steps(ins, outs, scratch):
        tokens_ref, gain_ref = ins
        (made.ref,) = scratch
        wide = tokens_ref[...].astype(F32)
        made.ref[...] = (wide * lax.rsqrt(jnp.mean(wide * wide, axis=-1, keepdims=True) + EPS) * gain_ref[...]).astype(BF)
        yield

    return Flow([(tokens, pltpu.VMEM), (gain, pltpu.VMEM)], [], [pltpu.VMEM(tokens.shape, BF)], [], steps)


def project_flow(rows, weights, gain, cosine, sine, q_cols, keys, values):
    count, size = rows.shape[0], gain.shape[1]
    half = count // 2

    def steps(ins, outs, scratch):
        rows_hbm, w_hbm, gain_ref, cos_ref, sin_ref = ins
        q_ref, raw_ref = outs
        rows_ref, w_ref, keys.ref, values.ref, local = scratch
        core, _ = peers_of("c")
        own = pl.ds(pl.multiple_of(core * half, half), half)
        other = pl.ds(pl.multiple_of((1 - core) * half, half), half)
        kv = pl.ds(q_cols, 2 * size)
        copies = [
            pltpu.make_async_copy(w_hbm.at[:, kv], w_ref.at[:, kv], local.at[0]),
            pltpu.make_async_copy(rows_hbm.at[own], rows_ref.at[own], local.at[1]),
            pltpu.make_async_copy(w_hbm.at[:, pl.ds(0, q_cols)], w_ref.at[:, pl.ds(0, q_cols)], local.at[2]),
            pltpu.make_async_copy(rows_hbm.at[other], rows_ref.at[other], local.at[3]),
        ]
        for copy in copies:
            copy.start()
        copies[0].wait()
        copies[1].wait()
        product = dot_nn(rows_ref[own, :], w_ref[:, q_cols:])
        raw = product[:, :size]
        raw_ref[...] = raw
        keys.ref[...] = norm_rope(raw, gain_ref[...], cos_ref[own, :], sin_ref[own, :]).astype(BF)
        values.ref[...] = product[:, size:].astype(BF)
        yield
        yield Filler(1.0)
        copies[2].wait()
        copies[3].wait()
        for row in range(0, count, BLOCK):
            q_ref[row : row + BLOCK, :] = dot_nn(rows_ref[row : row + BLOCK, :], w_ref[:, :q_cols])
            yield Filler(1.2)

    return Flow(
        [(rows, pl.ANY), (weights, pl.ANY), (gain, pltpu.VMEM), (cosine, pltpu.VMEM), (sine, pltpu.VMEM)],
        [((count, q_cols), F32, pltpu.VMEM), ((half, size), F32, pltpu.VMEM)],
        [pltpu.VMEM(rows.shape, BF), pltpu.VMEM(weights.shape, BF), pltpu.VMEM((half, size), BF), pltpu.VMEM((half, size), BF), dma(4)],
        [],
        steps,
    )


def route_flow(tokens, gain, router, chosen, assign, done):
    own, width = tokens.shape
    experts, count = chosen.shape[1], assign.shape[1]

    def steps(ins, outs, scratch):
        tokens_ref, gain_ref, router_ref, chosen_ref, assign_ref = ins
        residual_ref, mixed_ref, gates_ref, rows_ref = outs
        (pick,) = scratch
        yield
        pick[...] = assign_ref[...].T
        yield done
        residual = tokens_ref[...].astype(F32) + done.ref[...]
        residual_ref[...] = residual
        mixed_ref[...] = (residual * lax.rsqrt(jnp.mean(residual * residual, axis=-1, keepdims=True) + EPS) * gain_ref[...]).astype(BF)
        logits = jnp.where(chosen_ref[...] > 0, dot_nn(mixed_ref[...], router_ref[...]), -1e30)
        powers = jnp.exp(logits - jnp.max(logits, axis=-1, keepdims=True))
        gates = powers / jnp.sum(powers, axis=-1, keepdims=True)
        gates_ref[...] = gates
        for column in range(0, width, 512):
            span = slice(column, column + 512)
            rows_ref[:, span] = dot_nn(pick[...], mixed_ref[:, span]).astype(BF)
        rows_ref[:, width:] = dot_nn(pick[...], gates.astype(BF)).astype(BF)
        yield

    return Flow(
        [(x, pltpu.VMEM) for x in (tokens, gain, router, chosen, assign)],
        [
            ((own, width), F32, pltpu.VMEM),
            ((own, width), BF, pltpu.VMEM),
            ((own, experts), F32, pltpu.VMEM),
            ((count, width + experts), BF, pltpu.VMEM),
        ],
        [pltpu.VMEM((count, own), BF)],
        [],
        steps,
    )


def mix_back_flow(back, assign, gates, mixed, router, residual, gain, cotangent, made):
    own, width = mixed.shape
    experts, count = gates.shape[1], back.shape[0]

    def steps(ins, outs, scratch):
        back_hbm, assign_ref, gates_ref, mixed_ref, router_ref, residual_ref, gain_ref, cotangent_ref = ins
        residual_grad, gain_grad, router_grad = outs
        back_ref, mixed_grad, made.ref, local = scratch
        copy = pltpu.make_async_copy(back_hbm, back_ref, local.at[0])
        copy.start()
        copy.wait()
        sums = jnp.sum(back_ref[:, width : width + 128].astype(F32), axis=1, keepdims=True)
        shape = (count, experts)
        expert_of = lax.div(lax.broadcasted_iota(jnp.int32, shape, 0), count // experts)
        spread = jnp.where(expert_of == lax.broadcasted_iota(jnp.int32, shape, 1), sums, 0.0)
        high = spread.astype(BF)
        low = (spread - high.astype(F32)).astype(BF)
        gate_grads = dot_nn(assign_ref[...], high) + dot_nn(assign_ref[...], low)
        gates = gates_ref[...]
        logits_grad = (gates * (gate_grads - jnp.sum(gates * gate_grads, axis=1, keepdims=True))).astype(BF)
        for column in range(0, width, 512):
            span = slice(column, column + 512)
            mixed_grad[:, span] = dot_nn(assign_ref[...], back_ref[:, span]) + dot_nt(logits_grad, router_ref[span, :])
        value = residual_ref[...]
        inverse = lax.rsqrt(jnp.mean(value * value, axis=-1, keepdims=True) + EPS)
        unit = value * inverse
        grad = mixed_grad[...]
        gain_grad[...] = jnp.sum(grad * unit, axis=0, keepdims=True)
        scaled = grad * gain_ref[...]
        total = cotangent_ref[...].astype(F32) + inverse * (scaled - unit * jnp.mean(scaled * unit, axis=-1, keepdims=True))
        residual_grad[...] = total
        made.ref[...] = total.astype(BF)
        yield
        yield Filler(1.0)
        router_grad[...] = dot_tn(mixed_ref[...], logits_grad).astype(BF)
        yield

    return Flow(
        [(back, pl.ANY)] + [(x, pltpu.VMEM) for x in (assign, gates, mixed, router, residual, gain, cotangent)],
        [((own, width), F32, pltpu.VMEM), ((1, width), F32, pltpu.VMEM), ((width, experts), BF, pltpu.VMEM)],
        [pltpu.VMEM(back.shape, BF), pltpu.VMEM((own, width), F32), pltpu.VMEM((own, width), BF), dma(1)],
        [],
        steps,
    )


def key_back_flow(grad_key, grad_value, raw, gain, cosine, sine, units, kv, w_kv, rows, key_gain):
    half, size = raw.shape
    width = units.shape[1]

    def steps(ins, outs, scratch):
        dk_ref, dv_ref, raw_ref, gain_ref, cos_ref, sin_ref, units_hbm = ins
        rows.ref, kv.ref, w_kv.ref, key_gain.ref, local = scratch
        copy = pltpu.make_async_copy(units_hbm, rows.ref, local.at[0])
        copy.start()
        core, _ = peers_of("c")
        own = pl.ds(pl.multiple_of(core * half, half), half)
        grad = dk_ref[...].astype(F32)
        grad_raw, grad_gain = norm_rope_back(grad, raw_ref[...], gain_ref[...], cos_ref[own, :], sin_ref[own, :])
        kv.ref[...] = jnp.zeros(kv.shape, BF)
        kv.ref[own, :size] = grad_raw.astype(BF)
        kv.ref[own, size:] = dv_ref[...]
        key_gain.ref[...] = jnp.sum(grad_gain, axis=0, keepdims=True)
        copy.wait()
        for i in range(16):
            w_kv.ref[i // 4, i % 4] = dot_tn(rows.ref[own, i * width // 16 : (i + 1) * width // 16], kv.ref[own, :]).astype(BF)
        yield

    return Flow(
        [(x, pltpu.VMEM) for x in (grad_key, grad_value, raw, gain, cosine, sine)] + [(units, pl.ANY)],
        [],
        [pltpu.VMEM(rows.shape, BF), pltpu.VMEM(kv.shape, BF), pltpu.VMEM(w_kv.shape, BF), pltpu.VMEM((1, size), F32), dma(1)],
        [],
        steps,
    )


def tokens_grad_flow(tokens, gain, residual_grad, done):
    def steps(ins, outs, scratch):
        tokens_ref, gain_ref, residual_ref = ins
        (out,) = outs
        yield
        yield done
        value = tokens_ref[...].astype(F32)
        inverse = lax.rsqrt(jnp.mean(value * value, axis=-1, keepdims=True) + EPS)
        unit = value * inverse
        scaled = done.ref[...] * gain_ref[...]
        out[...] = residual_ref[...] + inverse * (scaled - unit * jnp.mean(scaled * unit, axis=-1, keepdims=True))
        yield

    return Flow(
        [(x, pltpu.VMEM) for x in (tokens, gain, residual_grad)], [(tokens.shape, F32, pltpu.VMEM)], [], [], steps
    )


def add_up(stacked):
    return jnp.sum(stacked.astype(F32), axis=0)


def dot_nn(a, b):
    return lax.dot_general(a, b, (((1,), (0,)), ((), ())), preferred_element_type=F32)


def dot_nt(a, b):
    return lax.dot_general(a, b, (((1,), (1,)), ((), ())), preferred_element_type=F32)


def dot_tn(a, b):
    return lax.dot_general(a, b, (((0,), (0,)), ((), ())), preferred_element_type=F32)


def norm_rope(raw, gain, cosine, sine):
    unit = raw * lax.rsqrt(jnp.mean(raw * raw, axis=-1, keepdims=True) + EPS)
    scaled = unit * gain
    return scaled * cosine + pltpu.roll(scaled, 64, 1) * sine


def norm_rope_back(grad, raw, gain, cosine, sine):
    inverse = lax.rsqrt(jnp.mean(raw * raw, axis=-1, keepdims=True) + EPS)
    unit = raw * inverse
    turned = grad * cosine + pltpu.roll(grad * sine, 64, 1)
    scaled = turned * gain
    return inverse * (scaled - unit * jnp.mean(scaled * unit, axis=-1, keepdims=True)), turned * unit


def expert_kernel(rows_ref, plain_ref, w_ref, back_ref, hidden_ref, gated_ref, both_ref):
    width, ff = w_ref.shape[0], plain_ref.shape[1]
    own = lax.axis_index("head") * lax.axis_size("blk") + lax.axis_index("blk")
    gates = rows_ref[:, width:].astype(F32)
    lane = lax.broadcasted_iota(jnp.int32, gates.shape, 1)
    gate = jnp.sum(jnp.where(lane == own, gates, 0.0), axis=1, keepdims=True)
    gate_up = dot_nn(rows_ref[:, :width], w_ref[...])
    first, up = gate_up[:, :ff], gate_up[:, ff:]
    sigma = 1.0 / (1.0 + jnp.exp(-first))
    silu = first * sigma
    hidden = silu * up
    hidden_ref[...] = hidden.astype(BF)
    gated_ref[...] = (hidden * gate).astype(BF)
    plain = plain_ref[...]
    gate_grad = jnp.sum(hidden * plain, axis=1, keepdims=True)
    grad = plain * gate
    both_ref[:, :ff] = (grad * up * (sigma * (1.0 + first * (1.0 - sigma)))).astype(BF)
    both_ref[:, ff:] = (grad * silu).astype(BF)
    back_ref[:, :width] = dot_nt(both_ref[...], w_ref[...]).astype(BF)
    high = gate_grad.astype(BF).astype(F32)
    back_ref[:, width:] = jnp.where(lane == 0, high, jnp.where(lane == 1, gate_grad - high, 0.0)).astype(BF)


def key_tiles(lo, full, last, tiles):
    middle = jnp.minimum(full, last)
    fours = lax.div(last - middle, 4)
    rest = middle + 4 * fours
    pl.loop(lo, middle)(lambda t: tiles([t], True))
    pl.loop(0, fours)(lambda i: tiles([middle + 4 * i + n for n in range(4)], False))
    pl.loop(rest, last)(lambda t: tiles([t], False))
    tiles([last], True)


def stacked(ref, slots):
    return ref[slots[0]] if len(slots) == 1 else jnp.concatenate([ref[slot] for slot in slots], axis=0)


def allowed_pairs(t, last, start, shape):
    key_place = t * BLOCK + lax.broadcasted_iota(jnp.int32, shape, 0)
    query_place = last * BLOCK + lax.rem(lax.broadcasted_iota(jnp.int32, shape, 1), BLOCK)
    return (key_place >= start) & (key_place <= query_place)


def attend_forward_kernel(
    lo_ref, full_ref, last_ref, slot_ref, raw_ref, gain_ref, cos_ref, sin_ref, k_ref, v_ref, start_ref, q_ref, o_ref, log_ref, q_t, acc, total
):
    j = pl.program_id(0)
    size = k_ref.shape[2]
    heads = raw_ref.shape[1] // size
    scale = size**-0.5 * LOG2E
    last = last_ref[j]
    for n in range(heads):
        span = slice(n * size, (n + 1) * size)
        query = norm_rope(raw_ref[:, span], gain_ref[...], cos_ref[...], sin_ref[...])
        q_ref[:, span] = query.astype(BF)
        q_t[:, n * BLOCK : (n + 1) * BLOCK] = query.T.astype(BF)
    acc[...] = jnp.zeros_like(acc)
    total[...] = jnp.zeros_like(total)
    start = start_ref[0]

    def tiles(at, masked):
        slots = [slot_ref[t] for t in at]
        weights = jnp.exp2(dot_nn(stacked(k_ref, slots), q_t[...]) * scale)
        if masked:
            weights = jnp.where(allowed_pairs(at[0], last, start, weights.shape), weights, 0.0)
        total[...] += jnp.sum(weights.reshape(-1, 8, heads * BLOCK), axis=0)
        acc[...] += dot_nn(stacked(v_ref, slots).T, weights.astype(BF))

    key_tiles(lo_ref[j], full_ref[j], last, tiles)
    row = jnp.sum(total[...], axis=0, keepdims=True)
    log_ref[0] = jnp.log2(row)
    out = acc[...] / row
    for n in range(heads):
        o_ref[:, n * size : (n + 1) * size] = out[:, n * BLOCK : (n + 1) * BLOCK].T.astype(BF)


def attend_backward_kernel(
    lo_ref,
    full_ref,
    last_ref,
    slot_ref,
    raw_ref,
    gain_ref,
    cos_ref,
    sin_ref,
    k_ref,
    v_ref,
    start_ref,
    q_ref,
    o_ref,
    g_ref,
    w_ref,
    log_ref,
    dq_ref,
    sum_ref,
    dk_ref,
    dv_ref,
    queries,
    q_t,
    grads,
    g_t,
    delta,
    acc,
    dk,
    dv,
    keys_ref,
    values_ref,
    local,
):
    j = pl.program_id(0)
    slots, _, size = keys_ref.shape
    takes = [pltpu.make_async_copy(k_ref, keys_ref, local.at[0]), pltpu.make_async_copy(v_ref, values_ref, local.at[1])]
    heads = raw_ref.shape[1] // size
    scale = size**-0.5
    last = last_ref[j]

    @pl.when(j == 0)
    def _():
        for copy in takes:
            copy.start()
        sum_ref[...] = jnp.zeros_like(sum_ref)

        @pl.loop(0, slots)
        def _(s):
            dk[s] = jnp.zeros(dk.shape[1:], F32)
            dv[s] = jnp.zeros(dv.shape[1:], F32)

    attended_grad = dot_nn(g_ref[...], w_ref[...]).astype(BF)
    for n in range(heads):
        span, rows = slice(n * size, (n + 1) * size), slice(n * BLOCK, (n + 1) * BLOCK)
        queries[rows, :] = q_ref[:, span]
        q_t[:, rows] = q_ref[:, span].T
        grads[rows, :] = attended_grad[:, span]
        grad_t = attended_grad[:, span].T
        g_t[:, rows] = grad_t
        delta[:, rows] = jnp.sum(grad_t.astype(F32) * o_ref[:, span].T.astype(F32), axis=0, keepdims=True)
    acc[...] = jnp.zeros_like(acc)
    start = start_ref[0]
    logs = log_ref[0]

    @pl.when(j == 0)
    def _():
        for copy in takes:
            copy.wait()

    def tiles(at, masked):
        slots = [slot_ref[t] for t in at]
        keys = stacked(keys_ref, slots)
        probs = jnp.exp2(dot_nn(keys, q_t[...]) * (scale * LOG2E) - logs)
        if masked:
            probs = jnp.where(allowed_pairs(at[0], last, start, probs.shape), probs, 0.0)
        grad_scores = (probs * (dot_nn(stacked(values_ref, slots), g_t[...]) - delta[...])).astype(BF)
        values_part, keys_part = dot_nn(probs.astype(BF), grads[...]), dot_nn(grad_scores, queries[...])
        for n, slot in enumerate(slots):
            dv[slot] += values_part[n * BLOCK : (n + 1) * BLOCK]
            dk[slot] += keys_part[n * BLOCK : (n + 1) * BLOCK]
        acc[...] += dot_nn(keys.T, grad_scores)

    key_tiles(lo_ref[j], full_ref[j], last, tiles)
    for n in range(heads):
        span = slice(n * size, (n + 1) * size)
        grad = (acc[:, n * BLOCK : (n + 1) * BLOCK] * scale).T.astype(BF).astype(F32)
        grad_raw, grad_gain = norm_rope_back(grad, raw_ref[:, span], gain_ref[...], cos_ref[...], sin_ref[...])
        dq_ref[:, span] = grad_raw.astype(BF)
        sum_ref[...] += jnp.sum(grad_gain, axis=0, keepdims=True)

    @pl.when(j == pl.num_programs(0) - 1)
    def _():
        def out(s, n):
            span = pl.ds(s, n)
            return (
                pltpu.make_async_copy(keys_ref.at[span], dk_ref.at[span], local.at[0]),
                pltpu.make_async_copy(values_ref.at[span], dv_ref.at[span], local.at[1]),
            )

        @pl.loop(0, slots, step=8)
        def _(s):
            for i in range(8):
                keys_ref[s + i] = (dk[s + i] * scale).astype(BF)
                values_ref[s + i] = dv[s + i].astype(BF)
            for copy in out(s, 8):
                copy.start()

        for copy in out(0, slots):
            copy.wait()


def by_rows(array, rows=BLOCK):
    return pl.BlockSpec((rows,) + array.shape[1:], lambda j, *_: (j,) + (0,) * (array.ndim - 1))


def resident(array):
    return pl.BlockSpec(array.shape, lambda j, *_: (0,) * array.ndim, pipeline_mode=pl.Buffered(1))


def shaped(shape, dtype):
    return jax.ShapeDtypeStruct(shape, dtype)


def expert(rows, plain, weights, block=512):
    count, ff = plain.shape
    outs = (shaped(rows.shape, BF), shaped((count, ff), BF), shaped((count, ff), BF), shaped((count, 2 * ff), BF))
    return pl.pallas_call(
        expert_kernel,
        out_shape=outs,
        grid=(count // block,),
        in_specs=[by_rows(rows, block), by_rows(plain, block), resident(weights)],
        out_specs=tuple(by_rows(x, block) for x in outs),
        compiler_params=pltpu.CompilerParams(vmem_limit_bytes=VMEM_LIMIT),
        cost_estimate=cost_of(20),
        name="expert",
    )(rows, plain, weights)


def attend_forward(meta, raw, gain, cosine, sine, keys, values, start):
    rows, wide = raw.shape
    blocks, size = rows // BLOCK, keys.shape[2]
    lanes = wide // size * BLOCK
    outs = (shaped((rows, wide), BF), shaped((rows, wide), BF), shaped((blocks, 1, lanes), F32))
    return pl.pallas_call(
        attend_forward_kernel,
        out_shape=outs,
        grid_spec=pltpu.PrefetchScalarGridSpec(
            num_scalar_prefetch=4,
            grid=(blocks,),
            in_specs=[
                by_rows(raw),
                resident(gain),
                by_rows(cosine),
                by_rows(sine),
                resident(keys),
                resident(values),
                by_rows(start, 1),
            ],
            out_specs=(by_rows(outs[0]), by_rows(outs[1]), by_rows(outs[2], 1)),
            scratch_shapes=[pltpu.VMEM((size, lanes), BF), pltpu.VMEM((size, lanes), F32), pltpu.VMEM((8, lanes), F32)],
        ),
        compiler_params=pltpu.CompilerParams(vmem_limit_bytes=VMEM_LIMIT),
        cost_estimate=cost_of(30),
        name="attend",
    )(*meta, raw, gain, cosine, sine, keys, values, start)


def attend_backward(meta, raw, gain, cosine, sine, keys, values, start, queries, attended, grads, w_out_t, logs):
    rows, wide = raw.shape
    blocks, size = rows // BLOCK, keys.shape[2]
    lanes = wide // size * BLOCK
    outs = (shaped((rows, wide), BF), shaped((1, size), F32), shaped(keys.shape, BF), shaped(values.shape, BF))
    return pl.pallas_call(
        attend_backward_kernel,
        out_shape=outs,
        grid_spec=pltpu.PrefetchScalarGridSpec(
            num_scalar_prefetch=4,
            grid=(blocks,),
            in_specs=[
                by_rows(raw),
                resident(gain),
                by_rows(cosine),
                by_rows(sine),
                pl.BlockSpec(memory_space=pl.ANY),
                pl.BlockSpec(memory_space=pl.ANY),
                by_rows(start, 1),
                by_rows(queries),
                by_rows(attended),
                by_rows(grads),
                resident(w_out_t),
                by_rows(logs, 1),
            ],
            out_specs=(by_rows(outs[0]), resident(outs[1])) + (pl.BlockSpec(memory_space=pl.ANY),) * 2,
            scratch_shapes=[
                pltpu.VMEM((lanes, size), BF),
                pltpu.VMEM((size, lanes), BF),
                pltpu.VMEM((lanes, size), BF),
                pltpu.VMEM((size, lanes), BF),
                pltpu.VMEM((1, lanes), F32),
                pltpu.VMEM((size, lanes), F32),
                pltpu.VMEM(keys.shape, F32),
                pltpu.VMEM(values.shape, F32),
                pltpu.VMEM(keys.shape, BF),
                pltpu.VMEM(values.shape, BF),
                dma(2),
            ],
        ),
        compiler_params=pltpu.CompilerParams(vmem_limit_bytes=VMEM_LIMIT),
        cost_estimate=cost_of(40),
        name="attend_back",
    )(*meta, raw, gain, cosine, sine, keys, values, start, queries, attended, grads, w_out_t, logs)


def all_to_all(stacked):
    return lax.all_to_all(stacked, ("head", "blk"), split_axis=0, concat_axis=0, tiled=True)


def body(
    tokens,
    norm_gain,
    w_query,
    key_weight,
    value_weight,
    query_gain,
    key_gain,
    w_out,
    mix_gain,
    w_router,
    expert_gate_up,
    expert_down,
    lengths,
    block_deal,
    routes,
    cotangent,
):
    own, width = tokens.shape
    size = query_gain.shape[0]
    scale = size ** (-0.5)
    blk = lax.axis_index("blk")
    plane, core = blk // 4, blk % 2
    devices = lax.axis_size("head") * lax.axis_size("blk")
    experts = w_router.shape[0] * 2
    cap = own * routes.shape[1] // experts
    gate_up, down = expert_gate_up[0], expert_down[0]
    ff = down.shape[0]
    group_rows = 8 * own
    q_cols = w_query.shape[1] // 4
    heads = q_cols // size

    group_blocks = plane * 4 + jnp.array([0, 2, 1, 3], jnp.int32)
    ids = jnp.arange(block_deal.shape[0], dtype=jnp.int32)
    last = jnp.sum(jnp.where(group_blocks[:, None] == ids[None, :], block_deal[None, :], 0), axis=1)
    slots = (ids % 2) * (ids.shape[0] // 2) + (ids // 4) * 2 + (ids % 4) // 2
    slot_of = jnp.sum(jnp.where(block_deal[None, :] == ids[:, None], slots[None, :], 0), axis=1)
    place = (last[:, None] * BLOCK + jnp.arange(BLOCK, dtype=jnp.int32)[None, :]).reshape(-1)
    passed = place[:, None] >= jnp.cumsum(lengths)[None, :]
    start = jnp.sum(jnp.where(passed, lengths[None, :], 0), axis=1)
    start_rows = start.reshape(-1, 1, BLOCK)
    meta = (start_rows[:, 0, 0] // BLOCK, (start_rows[:, 0, BLOCK - 1] + BLOCK - 1) // BLOCK, last, slot_of)
    start_rows = jnp.tile(start_rows, (1, 1, heads))
    offsets = (place - start).astype(F32).reshape(-1, 1, BLOCK)
    spacing = ROPE_BASE ** (-2.0 * jnp.arange(size // 2, dtype=F32) / size)
    spacing = jnp.concatenate([spacing, spacing])[None]

    normed = Made(own, width)
    depth = w_query.shape[0]
    out_pack = w_out.reshape(4, q_cols, depth).transpose(2, 0, 1).reshape(depth, -1)
    side = lax.axis_index("head") == jnp.arange(2, dtype=jnp.int32)
    router_pack = jnp.where(side[None, :, None], w_router.T[:, None, :], 0).astype(BF).reshape(depth, experts)
    w_qkv, w_out_t, w_router_t, group_tokens, assign_low, chosen, cosine, sine = launch(
        [
            norm_flow(tokens, norm_gain[None], normed),
            plane_gather_flow([(w_query, q_cols, 1), (key_weight, size, 2), (value_weight, size, 2)], "x", "y", ahead="zhc"),
            plane_gather_flow([(out_pack, q_cols, 1)], "y", "x", ahead="zhc"),
            plane_gather_flow([(router_pack, experts, 1)], "y", "x", ahead="z"),
            ring_gather_flow(normed),
            tables_flow(routes, offsets, spacing, experts, cap),
        ],
        0,
        45,
    )
    normed_group = group_tokens.reshape(group_rows, width)
    w_qkv, w_out_t = w_qkv.reshape(width, -1), w_out_t.reshape(width, -1)
    w_router_t = jnp.sum(w_router_t.reshape(-1, 2, depth, experts), axis=1).reshape(width, experts)

    q_gain, k_gain = query_gain[None], key_gain[None]
    key, value = Made(group_rows // 2, size), Made(group_rows // 2, size)
    q_raw, k_raw, keys, values, grad_rows = launch(
        [
            project_flow(normed_group, w_qkv, k_gain, cosine, sine, q_cols, key, value),
            plane_gather_flow(key, "x", "y"),
            plane_gather_flow(value, "y", "x"),
            product_flow(assign_low, cotangent),
        ],
        1,
        35,
    )
    grad_rows = all_to_all(grad_rows.reshape(devices, cap, width)).reshape(-1, width)
    keys, values = keys.reshape(-1, BLOCK, size), values.reshape(-1, BLOCK, size)
    queries, attended, logs = attend_forward(meta, q_raw, q_gain, cosine, sine, keys, values, start_rows)

    attention = Made(own, width)
    residual, mixed, gates, outgoing = launch(
        [
            product_scatter_flow([attended], w_out_t, attention),
            route_flow(tokens, mix_gain[None], w_router_t, chosen, assign_low, attention),
        ],
        2,
        30,
    )
    outgoing, grad_rows = lax.optimization_barrier((outgoing, grad_rows))
    arrived = all_to_all(outgoing.reshape(devices, cap, -1)).reshape(experts * cap, -1)

    plain_grad = lax.optimization_barrier(dot_nt(grad_rows, down))
    rows, plain_grad = lax.optimization_barrier((arrived, plain_grad))
    back, hidden, gated, grad_both = expert(rows, plain_grad, gate_up)
    back = all_to_all(back.reshape(devices, cap, -1)).reshape(experts * cap, -1)
    back, expert_out = lax.optimization_barrier((back, dot_nn(hidden, down).astype(BF)))
    grad_down = dot_tn(gated, grad_rows)
    grad_gate_up = dot_tn(rows[:, :width], grad_both)

    grad_attention = Made(own, width)
    grad_residual, grad_mix_gain, grad_router_t, grad_group = launch(
        [
            mix_back_flow(back, assign_low, gates, mixed, w_router_t, residual, mix_gain[None], cotangent, grad_attention),
            ring_gather_flow(grad_attention),
        ],
        3,
        25,
    )
    grad_group = grad_group.reshape(group_rows, width)
    grad_group, expert_out = lax.optimization_barrier((grad_group, expert_out))
    expert_out = all_to_all(expert_out.reshape(devices, cap, width)).reshape(-1, width)
    grad_q, grad_query_gain, grad_keys, grad_values = attend_backward(
        meta, q_raw, q_gain, cosine, sine, keys, values, start_rows, queries, attended, grad_group, w_out_t, logs
    )

    split = (2, 4, 4, group_rows // 2, size)
    grad_key, grad_value, grad_wq, grad_wo = launch(
        [
            plane_scatter_flow(grad_keys.reshape(split), "y", "x", from_core=True),
            plane_scatter_flow(grad_values.reshape(split), "x", "y", from_core=True),
            product_flow(normed_group, grad_q),
            product_flow(grad_group, attended),
        ],
        4,
        35,
    )

    grad_key, expert_out = lax.optimization_barrier((grad_key, expert_out))
    plane_split = (4, 4, 4 * depth, -1)
    zeros, ones = jnp.zeros((width,), F32), jnp.ones((width,), F32)
    gains = jnp.concatenate([zeros, grad_mix_gain[0], grad_query_gain[0], zeros[: 7 * size], norm_gain, ones, ones[: 8 * size]])
    units, grad_kv, grad_wkv, key_gain_sum = Made(group_rows, width), Made(group_rows, 2 * size), Made(4, 4, 4 * depth, 2 * size), Made()
    grad_normed = Made(own, width)
    grad_wq, grad_wo, gains, grad_wkv, grad_wr, output, grad_tokens = launch(
        [
            key_back_flow(grad_key, grad_value, k_raw, k_gain, cosine, sine, normed_group, grad_kv, grad_wkv, units, key_gain_sum),
            plane_scatter_flow(grad_wq.reshape(plane_split), "y", "x", last_in="zhc"),
            plane_scatter_flow(grad_wo.reshape(plane_split), "x", "y", last_in="zhc"),
            product_scatter_flow([grad_q, grad_kv], w_qkv, grad_normed, units, gains.reshape(2, -1, size), key_gain_sum),
            plane_scatter_flow(grad_wkv, "y", "x", last_in="zhc"),
            plane_scatter_flow(grad_router_t.reshape(plane_split), "x", "y", last_in="z"),
            output_flow(residual, gates, assign_low, expert_out),
            tokens_grad_flow(tokens, norm_gain[None], grad_residual, grad_normed),
        ],
        5,
        50,
    )
    gains = gains.reshape(-1)
    grad_w_query = grad_wq.astype(F32).transpose(1, 0, 2).reshape(depth, -1)
    grad_kv_w = jnp.sum(grad_wkv.astype(F32).reshape(2, 2, depth, 2, size), axis=1)
    grad_w_key = grad_kv_w[:, :, 0].transpose(1, 0, 2).reshape(depth, -1)
    grad_w_value = grad_kv_w[:, :, 1].transpose(1, 0, 2).reshape(depth, -1)
    grad_w_out = grad_wo.astype(F32).transpose(0, 2, 1).reshape(-1, depth)
    grad_w_router = lax.dynamic_slice_in_dim(add_up(grad_wr), lax.axis_index("head") * (experts // 2), experts // 2, 1).T
    return (
        output,
        grad_tokens,
        gains[:width],
        grad_w_query,
        grad_w_key,
        grad_w_value,
        gains[2 * width : 2 * width + size],
        gains[2 * width + size : 2 * width + 2 * size],
        grad_w_out,
        gains[width : 2 * width],
        grad_w_router,
        grad_gate_up[None],
        grad_down[None],
    )


def solution(mesh):
    rows, both = P(("head", "blk"), None), P("blk", "head")
    expert, turned = P(("head", "blk"), None, None), P("head", "blk")
    in_specs = (rows, P(), both, both, both, P(), P(), turned, P(), turned, expert, expert, P(), P(), rows, rows)
    out_specs = (rows, rows, P(), both, both, both, P(), P(), turned, P(), turned, expert, expert)
    return jax.shard_map(body, mesh=mesh, in_specs=in_specs, out_specs=out_specs, check_vma=False)
```

```python
import math

import jax
import jax.numpy as jnp
from jax import lax
from jax.experimental import pallas as pl
from jax.experimental.pallas import tpu as pltpu
from jax.sharding import PartitionSpec as P

MESH = pl.DeviceIdType.MESH
EPS = 1e-06
ROPE_BASE = 1000000.0
LOG2E = 1.4426950408889634
BF = jnp.bfloat16
F32 = jnp.float32
BLOCK = 256
VMEM_LIMIT = 60 << 20
SIZES = {"zc": 4, "c": 2, "x": 4, "y": 4, "zhc": 4, "z": 8, "yx": 16}


def peers_of(kind):
    h = lax.axis_index("head")
    b = lax.axis_index("blk")
    q, r = lax.div(b, 4), lax.rem(b, 4)
    if kind == "zc":
        return lax.div(r, 2) * 2 + h, lambda g: (lax.rem(g, 2), q * 4 + lax.div(g, 2) * 2 + lax.rem(r, 2))
    if kind == "z":
        return r * 2 + h, lambda g: (lax.rem(g, 2), q * 4 + lax.div(g, 2))
    if kind == "c":
        return lax.rem(b, 2), lambda g: (h, b - lax.rem(b, 2) + g)
    if kind == "x":
        return lax.rem(q, 4), lambda g: (h, (lax.div(q, 4) * 4 + g) * 4 + r)
    if kind == "y":
        return lax.div(q, 4), lambda g: (h, (g * 4 + lax.rem(q, 4)) * 4 + r)
    if kind == "yx":
        return q, lambda g: (h, g * 4 + r)
    return r, lambda g: (h, q * 4 + g)


def cost_of(microseconds):
    return pl.CostEstimate(flops=microseconds * 10**9, bytes_accessed=microseconds * 3 * 10**6, transcendentals=0)


class Flow:
    def __init__(self, inputs, outputs, scratch, partners, steps):
        self.inputs, self.outputs, self.scratch = inputs, outputs, scratch
        self.partners, self.steps = partners, steps


class Filler:
    def __init__(self, cost):
        self.cost = cost


class Clock:
    now = 0.0


def in_turn(flows):
    Clock.now = 0.0
    ready, waiting, fillers = [(0.0, i, steps) for i, steps in enumerate(flows)], [], []
    count = len(flows)
    while ready or fillers or waiting:
        for entry in [e for e in waiting if e[0].ref is not None]:
            waiting.remove(entry)
            ready.append((Clock.now, entry[1], entry[2]))
        ready.sort(key=lambda e: e[:2])
        if fillers and (not ready or ready[0][0] > Clock.now + 0.5):
            cost, order, steps = fillers.pop(0)
            Clock.now += cost
        else:
            when, order, steps = ready.pop(0)
            Clock.now = max(Clock.now, when) + 0.3
        result = next(steps, steps)
        if result is steps:
            continue
        if isinstance(result, Filler):
            fillers.append((result.cost, order, steps))
        elif isinstance(result, Made):
            waiting.append((result, order, steps))
        elif result is None or isinstance(result, float):
            ready.append((Clock.now if result is None else result, order, steps))
        else:
            ready += [(Clock.now, order, steps), (Clock.now, count, result)]
            count += 1


class Made:
    def __init__(self, *shape):
        self.shape, self.ref = shape, None


HOP = 3.0
RATE = 40e3
CORE_RATE = 200e3


def launch(flows, cid, cost):
    partners = sorted({p for flow in flows for p in flow.partners})

    def kernel(*refs):
        n_in, n_out = sum(len(f.inputs) for f in flows), sum(len(f.outputs) for f in flows)
        ins, outs, rest = list(refs[:n_in]), list(refs[n_in : n_in + n_out]), list(refs[n_in + n_out :])
        barrier = pltpu.get_barrier_semaphore()
        for kind, distance in partners:
            me, member = peers_of(kind)
            to = member(lax.rem(me + distance, SIZES[kind]))
            pl.semaphore_signal(barrier, inc=1, device_id=to, device_id_type=MESH)
        running = []
        for flow in flows:
            own = [[group.pop(0) for _ in part] for group, part in ((ins, flow.inputs), (outs, flow.outputs), (rest, flow.scratch))]
            running.append(flow.steps(*own))
            next(running[-1])
        pl.semaphore_wait(barrier, len(partners))
        in_turn(running)

    return pl.pallas_call(
        kernel,
        out_shape=tuple(jax.ShapeDtypeStruct(s, d) for f in flows for s, d, _ in f.outputs),
        in_specs=[pl.BlockSpec(memory_space=space) for f in flows for _, space in f.inputs],
        out_specs=tuple(pl.BlockSpec(memory_space=space) for f in flows for _, _, space in f.outputs),
        scratch_shapes=[x for f in flows for x in f.scratch],
        compiler_params=pltpu.CompilerParams(collective_id=cid, has_side_effects=True, vmem_limit_bytes=VMEM_LIMIT),
        cost_estimate=cost_of(cost),
        name=f"links_{cid}",
    )(*[x for f in flows for x, _ in f.inputs])


def remote(src, dst, send, recv, device):
    return pltpu.make_async_remote_copy(
        src_ref=src, dst_ref=dst, send_sem=send, recv_sem=recv, device_id=device, device_id_type=MESH
    )


def piece(ref, which):
    rows = ref.shape[0] // 2
    return ref.at[pl.ds(which * rows, rows)]


def ring_partners(kind):
    return [(kind, 1), (kind, 3)]


class RingGather:
    def __init__(self, kind, slot, src, send, recv):
        me, member = peers_of(kind)
        up, down = lax.rem(me + 1, 4), lax.rem(me + 3, 4)

        def copy(source, target, i, to):
            return remote(source, target, send.at[i], recv.at[i], member(to))

        mine = slot(me)
        self.copies = [
            copy(piece(src, 0), piece(mine, 0), 0, up),
            copy(piece(src, 1), piece(mine, 1), 1, up),
            copy(piece(src, 1), piece(mine, 1), 2, down),
            copy(piece(src, 0), piece(mine, 0), 3, down),
            copy(piece(slot(down), 0), piece(slot(down), 0), 4, up),
            copy(piece(slot(up), 1), piece(slot(up), 1), 5, down),
        ]

    def start(self):
        for i in (0, 2, 1, 3):
            self.copies[i].start()

    def forward(self):
        self.copies[0].wait_recv()
        self.copies[4].start()
        self.copies[2].wait_recv()
        self.copies[5].start()

    def near(self):
        self.copies[1].wait_recv()
        self.copies[3].wait_recv()

    def far(self):
        self.copies[4].wait_recv()
        self.copies[5].wait_recv()

    def sent(self):
        for copy in self.copies:
            copy.wait_send()


class RingScatter:
    def __init__(self, kind, chunk, bufs, send, recv, raw=None):
        raw = raw or chunk
        self.me, member = peers_of(kind)
        self.up, self.down, self.far = (lax.rem(self.me + k, 4) for k in (1, 3, 2))
        self.chunk, self.bufs = chunk, bufs

        def copy(source, target, i, to):
            return remote(source, bufs.at[target], send.at[i], recv.at[i], member(to))

        self.copies = [
            copy(piece(raw(self.far), 0), 0, 0, self.up),
            copy(piece(raw(self.far), 1), 1, 1, self.down),
            copy(piece(raw(self.up), 1), 2, 2, self.up),
            copy(piece(raw(self.down), 0), 3, 3, self.down),
            copy(bufs.at[6], 4, 4, self.up),
            copy(bufs.at[7], 5, 5, self.down),
        ]

    def start_far(self):
        self.copies[0].start()
        self.copies[1].start()

    def start_up(self):
        self.copies[2].start()

    def start_down(self):
        self.copies[3].start()

    def add(self):
        self.copies[0].wait_recv()
        self.bufs[6] = (piece(self.chunk(self.up), 0)[...].astype(F32) + self.bufs[0].astype(F32)).astype(BF)
        self.copies[4].start()
        self.copies[1].wait_recv()
        self.bufs[7] = (piece(self.chunk(self.down), 1)[...].astype(F32) + self.bufs[1].astype(F32)).astype(BF)
        self.copies[5].start()

    def total(self, which):
        first, second = ((4, 3), (2, 5))[which]
        self.copies[first].wait_recv()
        self.copies[second].wait_recv()
        return self.bufs[first].astype(F32) + self.bufs[second].astype(F32)

    def sent(self):
        for copy in self.copies:
            copy.wait_send()


def dma(*shape):
    return pltpu.SemaphoreType.DMA(shape)


def ring_gather_flow(made):
    shape = (2, 4) + made.shape

    def steps(ins, outs, scratch):
        (out,), src = outs, made.ref
        send, recv, pass_send, pass_recv, local = scratch
        yield
        me, _ = peers_of("zc")
        core, member = peers_of("c")
        ring = RingGather("zc", lambda g: out.at[core, g], src, send, recv)

        def passing(k):
            g = lax.rem(me + k, 4)
            return remote(src if k == 0 else out.at[core, g], out.at[core, g], pass_send.at[k], pass_recv.at[k], member(1 - core))

        passes = [passing(k) for k in range(4)]
        unit = math.prod(made.shape) * 2 / RATE
        begun = Clock.now
        ring.start()
        passes[0].start()
        yield begun + HOP + unit / 2
        ring.forward()
        back = pltpu.make_async_copy(src, out.at[core, me], local.at[0])
        back.start()
        yield begun + HOP + unit
        ring.near()
        passes[1].start()
        passes[3].start()
        yield begun + 2 * HOP + 1.5 * unit
        ring.far()
        passes[2].start()
        yield Clock.now + HOP + 2.0
        back.wait()
        ring.sent()
        for copy in passes:
            copy.wait()

    return Flow(
        [],
        [(shape, BF, pl.ANY)],
        [dma(6), dma(6), dma(4), dma(4), dma(1)],
        ring_partners("zc") + [("c", 1)],
        steps,
    )


def plane_gather_flow(arrays, first, second, ahead=None):
    to_core = ahead is None
    if ahead == "zhc":
        shard = (4, arrays[0][0].shape[0], sum(columns for _, columns, _ in arrays))
    elif ahead == "z":
        shard = (8,) + arrays[0][0].shape
    else:
        shard = arrays.shape
    shape = ((2,) if to_core else ()) + (4, 4) + shard
    n_ahead = SIZES[ahead] if ahead else 1

    def steps(ins, outs, scratch):
        (out,) = outs
        stage, send, recv, pass_send, pass_recv, local, ahead_send, ahead_recv = scratch
        core, member = peers_of("c")
        here, _ = peers_of(first)
        there, _ = peers_of(second)
        view = out.at[core] if to_core else out

        def slot(a, b):
            return view.at[b, a] if first == "x" else view.at[a, b]

        if ahead:
            mine, at = peers_of(ahead)

            def parts(to):
                if ahead == "z":
                    return [(ins[0], stage.at[mine])]
                found, begin = [], 0
                for ref, (_, columns, share) in zip(ins, arrays):
                    source = ref.at[:, pl.ds(pl.multiple_of(lax.div(to, share) * columns, columns), columns)]
                    found.append((source, stage.at[mine, :, pl.ds(begin, columns)]))
                    begin += columns
                return found

            early = [pltpu.make_async_copy(source, target, local.at[i]) for i, (source, target) in enumerate(parts(mine))]
            for k in range(1, n_ahead):
                to = lax.rem(mine + k, n_ahead)
                for i, (source, target) in enumerate(parts(to)):
                    early.append(remote(source, target, ahead_send.at[i, k], ahead_recv.at[i, k], at(to)))
            local_parts = len(parts(mine))
            for copy in early[:local_parts]:
                copy.start()
            yield
            for copy in early[local_parts:]:
                copy.start()
            yield Clock.now + HOP + 7.0
            for copy in early:
                copy.wait()
            src = stage
        else:
            src = arrays.ref
            yield
        ring = RingGather(first, lambda g: slot(g, there), src, send.at[4], recv.at[4])
        columns = [lax.rem(here + k, 4) for k in range(4)]
        rings = [
            RingGather(second, lambda g, a=a: slot(a, g), src if k == 0 else slot(a, there), send.at[k], recv.at[k])
            for k, a in enumerate(columns)
        ]

        def passing(k, m):
            ref = slot(columns[k], lax.rem(there + m, 4))
            return remote(src if k == m == 0 else ref, ref, pass_send.at[k * 4 + m], pass_recv.at[k * 4 + m], member(1 - core))

        passes = {}

        def hand_over(k, m):
            if to_core:
                passes[k, m] = passing(k, m)
                passes[k, m].start()

        unit = math.prod(shard) * 2 / RATE
        begun = Clock.now
        ring.start()
        rings[0].start()
        hand_over(0, 0)
        yield begun + HOP + unit / 2
        ring.forward()
        back = pltpu.make_async_copy(src, slot(here, there), local.at[0])
        back.start()
        yield
        rings[0].forward()
        yield begun + HOP + unit
        ring.near()
        for k in (1, 3):
            rings[k].start()
            hand_over(k, 0)
        yield begun + 2 * HOP + 1.5 * unit
        ring.far()
        rings[2].start()
        hand_over(2, 0)
        yield
        for i, k in enumerate((0, 1, 3, 2)):
            if k > 0:
                yield begun + 2 * HOP + (1.5 * i + 0.5) * unit
                rings[k].forward()
            yield begun + 2 * HOP + (1.5 * i + 1.0) * unit
            rings[k].near()
            hand_over(k, 1)
            hand_over(k, 3)
        for i, k in enumerate((0, 1, 3, 2)):
            yield begun + 3 * HOP + (1.5 * i + 1.5) * unit
            rings[k].far()
            hand_over(k, 2)
        yield Clock.now + HOP
        back.wait()
        ring.sent()
        for one in rings:
            one.sent()
        for copy in passes.values():
            copy.wait()

    return Flow(
        [] if to_core else [(array, pl.ANY) for array, *_ in arrays],
        [(shape, BF, pl.ANY)],
        [pltpu.VMEM((8, 128) if to_core else shard, BF), dma(5, 6), dma(5, 6), dma(16), dma(16), dma(3), dma(3, 8), dma(3, 8)],
        ring_partners("x") + ring_partners("y") + ([("c", 1)] if to_core else []) + [(ahead, k) for k in range(1, n_ahead)],
        steps,
    )


def product_flow(left, right):
    columns, width = left.shape[1], right.shape[1]

    def steps(ins, outs, scratch):
        (out,) = outs
        left_ref, right_ref, local = scratch
        copies = [pltpu.make_async_copy(source, target, local.at[i]) for i, (source, target) in enumerate(zip(ins, (left_ref, right_ref)))]
        for copy in copies:
            copy.start()
        yield
        yield Filler(1.0)
        for copy in copies:
            copy.wait()
        for column in range(0, columns, 256):
            span = slice(column, column + 256)
            out[span, :] = dot_tn(left_ref[:, span], right_ref[...]).astype(BF)
            yield Filler(1.0)

    return Flow(
        [(left, pl.ANY), (right, pl.ANY)],
        [((columns, width), BF, pltpu.VMEM)],
        [pltpu.VMEM(left.shape, BF), pltpu.VMEM(right.shape, BF), dma(2)],
        [],
        steps,
    )


def output_flow(residual, gates, assign, expert_out):
    own, width = residual.shape
    experts = gates.shape[1]
    count = expert_out.shape[0]

    def steps(ins, outs, scratch):
        residual_ref, gates_ref, assign_ref, expert_hbm = ins
        (out,) = outs
        expert_ref, mixing, local = scratch
        copy = pltpu.make_async_copy(expert_hbm, expert_ref, local.at[0])
        copy.start()
        wide = (experts, count)
        cap = count // experts
        spread = (lax.broadcasted_iota(jnp.int32, wide, 1) // cap == lax.broadcasted_iota(jnp.int32, wide, 0)).astype(F32).astype(BF)
        taken = assign_ref[...].astype(F32)
        high = gates_ref[...].astype(BF)
        low = (gates_ref[...] - high.astype(F32)).astype(BF)
        mixing[0] = (dot_nn(high, spread) * taken).astype(BF)
        mixing[1] = (dot_nn(low, spread) * taken).astype(BF)
        yield
        yield Filler(1.0)
        copy.wait()
        for column in range(0, width, 512):
            span = slice(column, column + 512)
            rows = expert_ref[:, span]
            out[:, span] = (residual_ref[:, span] + dot_nn(mixing[0], rows) + dot_nn(mixing[1], rows)).astype(BF)
            yield Filler(1.0)

    return Flow(
        [(residual, pltpu.VMEM), (gates, pltpu.VMEM), (assign, pltpu.VMEM), (expert_out, pl.ANY)],
        [(residual.shape, BF, pltpu.VMEM)],
        [pltpu.VMEM(expert_out.shape, BF), pltpu.VMEM((2, own, count), BF), dma(1)],
        [],
        steps,
    )


sum_partners = [("yx", k) for k in range(1, 16)] + [("z", k) for k in range(1, 8)]


def sum_room(shape):
    return [pltpu.VMEM((16,) + shape, F32), pltpu.VMEM((8,) + shape, F32), pltpu.VMEM(shape, F32), dma(16), dma(16), dma(8), dma(8)]


def sum_steps(src, gains, out, scratch):
    wide, far, middle, sends, recvs, far_sends, far_recvs = scratch
    me, member = peers_of("yx")
    copies = []
    for k in range(1, 16):
        copies.append(remote(src, wide.at[me], sends.at[k], recvs.at[k], member(lax.rem(me + k, 16))))
        copies[-1].start()
    wide[me] = src[...]
    yield Clock.now + HOP + 4.0
    for copy in copies:
        copy.wait()
    middle[...] = jnp.sum(wide[...], axis=0)
    ring, ring_member = peers_of("z")
    late = []
    for k in range(1, 8):
        late.append(remote(middle, far.at[ring], far_sends.at[k], far_recvs.at[k], ring_member(lax.rem(ring + k, 8))))
        late[-1].start()
    far[ring] = middle[...]
    yield Clock.now + HOP + 3.0
    for copy in late:
        copy.wait()
    out[...] = jnp.sum(far[...], axis=0) / gains[1]


def product_scatter_flow(lefts, right, done, units=None, gains=None, key_gain=None):
    arrays = [left for left in lefts if not isinstance(left, Made)]
    own, wide = lefts[0].shape[0] // 8, right.shape[0]
    spans = [0]
    for left in lefts:
        spans.append(spans[-1] + left.shape[1])

    def steps(ins, outs, scratch):
        given = list(ins[: len(arrays)])
        left_refs = [left.ref if isinstance(left, Made) else given.pop(0) for left in lefts]
        right_ref = ins[len(arrays)]
        out, theirs, came, chunks, bufs, send, recv, pass_send, pass_recv, *rest = scratch
        core, member = peers_of("c")
        me, _ = peers_of("zc")
        ring = RingScatter("zc", lambda g: chunks.at[g], bufs, send, recv)

        if units is not None:
            gains_ref = ins[len(arrays) + 1]
            unit_ref = units.ref
            sums, *sum_scratch = rest
            sums[...] = gains_ref[0]
            sums[33:34, :] += key_gain.ref[...]

        def product(c, k, column):
            row = pl.multiple_of((c * 4 + lax.rem(me + k, 4)) * own, own)
            value = sum(
                dot_nt(left_ref[pl.ds(row, own), :], right_ref[column : column + 512, spans[i] : spans[i + 1]])
                for i, left_ref in enumerate(left_refs)
            )
            if units is not None:
                row_sum = jnp.sum(value * unit_ref[pl.ds(row, own), column : column + 512].astype(F32), axis=0, keepdims=True)
                for lane in range(0, 512, 128):
                    at = (column + lane) // 128
                    sums[at : at + 1, :] += row_sum[:, lane : lane + 128]
            return value

        passes = [
            remote(theirs.at[k], came.at[k], pass_send.at[k], pass_recv.at[k], member(1 - core)) for k in range(4)
        ]
        for k in (2, 1, 3, 0):
            if k == 1:
                yield
                Clock.now += 0.7
                passes[2].start()
            for column in range(0, wide, 512):
                theirs[k, :, column : column + 512] = product(1 - core, k, column).astype(BF)
            if k != 2:
                Clock.now += 0.7
                passes[k].start()
                yield
        for k in (2, 1, 3, 0):
            passes[k].wait_recv()
            g = lax.rem(me + k, 4)
            for column in range(0, wide, 512):
                span = slice(column, column + 512)
                value = product(core, k, column) + came[k, :, span].astype(F32)
                if k == 0:
                    out[:, span] = value
                else:
                    chunks[g, :, span] = value.astype(BF)
            Clock.now += 0.7
            if k == 2:
                begun = Clock.now
                ring.start_far()
            elif k == 1:
                ring.start_up()
            elif k == 3:
                ring.start_down()
            yield
        unit = own * wide * 2 / RATE
        if units is not None:
            yield sum_steps(sums, gains_ref, outs[0], sum_scratch)
        yield begun + HOP + unit / 2
        ring.add()
        yield begun + 2 * HOP + 1.5 * unit
        for h in range(2):
            rows = slice(h * own // 2, (h + 1) * own // 2)
            out[rows, :] += ring.total(h)
        done.ref = out
        yield Clock.now + 2.0
        ring.sent()
        for copy in passes:
            copy.wait_send()

    return Flow(
        [(x, pltpu.VMEM) for x in (*arrays, right)] + ([] if units is None else [(gains, pltpu.VMEM)]),
        [] if units is None else [(gains.shape[1:], F32, pltpu.VMEM)],
        [
            pltpu.VMEM((own, wide), F32),
            pltpu.VMEM((4, own, wide), BF),
            pltpu.VMEM((4, own, wide), BF),
            pltpu.VMEM((4, own, wide), BF),
            pltpu.VMEM((8, own // 2, wide), BF),
            dma(6),
            dma(6),
            dma(4),
            dma(4),
        ]
        + ([] if units is None else [pltpu.VMEM(gains.shape[1:], F32)] + sum_room(gains.shape[1:])),
        ring_partners("zc") + [("c", 1)] + ([] if units is None else sum_partners),
        steps,
    )


def plane_scatter_flow(array, first, second, from_core=False, last_in=None):
    rows, columns = array.shape[-2:]
    n_last = SIZES[last_in] if last_in else 1
    result = (n_last, rows // 4, columns) if last_in else (rows, columns)

    def steps(ins, outs, scratch):
        src, (out,) = array.ref if isinstance(array, Made) else ins[0], outs
        came, sums, middle, bufs, late_bufs, send, recv, late_send, late_recv, pass_send, pass_recv, local, cut, cut_send, cut_recv = scratch
        core, member = peers_of("c")
        me, _ = peers_of(first)

        def along(ref, g):
            return ref.at[g] if first == "y" else ref.at[:, g]

        order = [lax.rem(me + k, 4) for k in (2, 1, 3, 0)]
        unit = 4 * rows * columns * 2 / RATE
        loads = [
            pltpu.make_async_copy(along(src.at[core] if from_core else src, g), along(sums, g), local.at[i])
            for i, g in enumerate(order)
            if from_core or i > 0
        ]
        passes = []
        if from_core:
            ring = RingScatter(first, lambda g: along(sums, g), bufs, send, recv)
            for i, g in enumerate(order):
                loads[i].start()
                passes.append(
                    remote(along(src.at[1 - core], g), along(came, g), pass_send.at[i], pass_recv.at[i], member(1 - core))
                )
            yield
            for copy in passes:
                copy.start()
            yield Clock.now + HOP + unit * RATE / CORE_RATE
            starts = [ring.start_far, ring.start_up, ring.start_down, lambda: None]
            for i, g in enumerate(order):
                loads[i].wait()
                passes[i].wait_recv()
                for k in range(4):
                    total = along(sums, g)[k].astype(F32) + along(came, g)[k].astype(F32)
                    along(sums, g)[k] = total.astype(BF)
                starts[i]()
                if i == 0:
                    begun = Clock.now
                yield Clock.now + unit * RATE / CORE_RATE if i < 3 else None
        else:
            ring = RingScatter(first, lambda g: along(sums, g), bufs, send, recv, raw=lambda g: along(src, g))
            for load in loads:
                load.start()
            yield
            begun = Clock.now
            ring.start_far()
            ring.start_up()
            ring.start_down()
            yield begun + HOP + unit / 2
            for load in loads:
                load.wait()
        if from_core:
            yield begun + HOP + unit / 2
        ring.add()
        yield begun + 2 * HOP + 1.5 * unit
        own = along(sums, me)
        for h in range(2):
            came_half = ring.total(h)
            for k in range(2):
                middle[h * 2 + k] = (own[h * 2 + k].astype(F32) + came_half[k]).astype(BF)
        Clock.now += 1.0
        begun = Clock.now
        last = RingScatter(second, lambda g: middle.at[g], late_bufs, late_send, late_recv)
        last.start_far()
        last.start_up()
        last.start_down()
        yield begun + HOP + unit / 8
        last.add()
        yield begun + 2 * HOP + 0.4 * unit
        for h in range(2):
            total = (piece(middle.at[last.me], h)[...].astype(F32) + last.total(h)).astype(BF)
            if last_in:
                cut[2 * h] = total[: rows // 4]
                cut[2 * h + 1] = total[rows // 4 :]
            else:
                out[h * rows // 2 : (h + 1) * rows // 2, :] = total
        cuts = []
        if last_in:
            mine, at = peers_of(last_in)
            share = n_last // 4
            for k in range(1, n_last):
                to = lax.rem(mine + k, n_last)
                cuts.append(remote(cut.at[lax.div(to, share)], out.at[mine], cut_send.at[k], cut_recv.at[k], at(to)))
                cuts[-1].start()
            out[mine] = cut[lax.div(mine, share)]
        yield Clock.now + HOP + 3.0
        ring.sent()
        last.sent()
        for copy in passes:
            copy.wait_send()
        for copy in cuts:
            copy.wait()

    block = (4, 4, rows, columns)
    return Flow(
        [] if isinstance(array, Made) else [(array, pl.ANY)],
        [(result, BF, pltpu.VMEM)],
        [
            pltpu.VMEM(block if from_core else (8, 128), BF),
            pltpu.VMEM(block, BF),
            pltpu.VMEM((4, rows, columns), BF),
            pltpu.VMEM((8, 2, rows, columns), BF),
            pltpu.VMEM((8, rows // 2, columns), BF),
            dma(6),
            dma(6),
            dma(6),
            dma(6),
            dma(4),
            dma(4),
            dma(4),
            pltpu.VMEM((4, rows // 4, columns), BF),
            dma(8),
            dma(8),
        ],
        ring_partners("x")
        + ring_partners("y")
        + ([("c", 1)] if from_core else [])
        + [(last_in, k) for k in range(1, n_last)],
        steps,
    )


def tables_flow(routes, offsets, spacing, experts, cap):
    own, top = routes.shape
    rows, size = offsets.size, spacing.shape[1]

    def steps(ins, outs, scratch):
        routes_ref, offsets_ref, spacing_ref = ins
        assign, chosen_ref, cosine, sine = outs
        yield
        yield Filler(1.0)
        lane = lax.broadcasted_iota(jnp.int32, (own, experts), 1)
        chosen = jnp.zeros((own, experts), F32)
        for k in range(top):
            chosen += (routes_ref[:, k : k + 1] == lane).astype(F32)
        chosen_ref[...] = chosen
        before = lax.broadcasted_iota(jnp.int32, (own, own), 0) > lax.broadcasted_iota(jnp.int32, (own, own), 1)
        earlier = dot_nn(before.astype(F32).astype(BF), chosen.astype(BF))
        wide = (experts, experts * cap)
        spread = (lax.broadcasted_iota(jnp.int32, wide, 1) // cap == lax.broadcasted_iota(jnp.int32, wide, 0)).astype(F32).astype(BF)
        slot = lax.rem(lax.broadcasted_iota(jnp.int32, (own, experts * cap), 1), cap).astype(F32)
        taken = (dot_nn(chosen.astype(BF), spread) > 0.5) & (dot_nn(earlier.astype(BF), spread) == slot)
        assign[...] = taken.astype(F32).astype(BF)
        yield Filler(1.0)
        sign = jnp.where(lax.broadcasted_iota(jnp.int32, (1, size), 1) < size // 2, -1.0, 1.0)
        for row in range(0, rows, BLOCK):
            span = slice(row, row + BLOCK)
            angles = jnp.broadcast_to(offsets_ref[row // BLOCK], (size, BLOCK)).T * spacing_ref[...]
            cosine[span, :] = jnp.cos(angles)
            sine[span, :] = jnp.sin(angles) * sign
            yield Filler(1.0)

    return Flow(
        [(routes, pltpu.VMEM), (offsets, pltpu.VMEM), (spacing, pltpu.VMEM)],
        [
            ((own, experts * cap), BF, pltpu.VMEM),
            ((own, experts), F32, pltpu.VMEM),
            ((rows, size), F32, pltpu.VMEM),
            ((rows, size), F32, pltpu.VMEM),
        ],
        [],
        [],
        steps,
    )


def norm_flow(tokens, gain, made):
    def steps(ins, outs, scratch):
        tokens_ref, gain_ref = ins
        (made.ref,) = scratch
        wide = tokens_ref[...].astype(F32)
        made.ref[...] = (wide * lax.rsqrt(jnp.mean(wide * wide, axis=-1, keepdims=True) + EPS) * gain_ref[...]).astype(BF)
        yield

    return Flow([(tokens, pltpu.VMEM), (gain, pltpu.VMEM)], [], [pltpu.VMEM(tokens.shape, BF)], [], steps)


def project_flow(rows, weights, gain, cosine, sine, q_cols, keys, values):
    count, size = rows.shape[0], gain.shape[1]
    half = count // 2

    def steps(ins, outs, scratch):
        rows_hbm, w_hbm, gain_ref, cos_ref, sin_ref = ins
        q_ref, raw_ref = outs
        rows_ref, w_ref, keys.ref, values.ref, local = scratch
        core, _ = peers_of("c")
        own = pl.ds(pl.multiple_of(core * half, half), half)
        other = pl.ds(pl.multiple_of((1 - core) * half, half), half)
        kv = pl.ds(q_cols, 2 * size)
        copies = [
            pltpu.make_async_copy(w_hbm.at[:, kv], w_ref.at[:, kv], local.at[0]),
            pltpu.make_async_copy(rows_hbm.at[own], rows_ref.at[own], local.at[1]),
            pltpu.make_async_copy(w_hbm.at[:, pl.ds(0, q_cols)], w_ref.at[:, pl.ds(0, q_cols)], local.at[2]),
            pltpu.make_async_copy(rows_hbm.at[other], rows_ref.at[other], local.at[3]),
        ]
        for copy in copies:
            copy.start()
        copies[0].wait()
        copies[1].wait()
        product = dot_nn(rows_ref[own, :], w_ref[:, q_cols:])
        raw = product[:, :size]
        raw_ref[...] = raw
        keys.ref[...] = norm_rope(raw, gain_ref[...], cos_ref[own, :], sin_ref[own, :]).astype(BF)
        values.ref[...] = product[:, size:].astype(BF)
        yield
        yield Filler(1.0)
        copies[2].wait()
        copies[3].wait()
        for row in range(0, count, BLOCK):
            q_ref[row : row + BLOCK, :] = dot_nn(rows_ref[row : row + BLOCK, :], w_ref[:, :q_cols])
            yield Filler(1.2)

    return Flow(
        [(rows, pl.ANY), (weights, pl.ANY), (gain, pltpu.VMEM), (cosine, pltpu.VMEM), (sine, pltpu.VMEM)],
        [((count, q_cols), F32, pltpu.VMEM), ((half, size), F32, pltpu.VMEM)],
        [pltpu.VMEM(rows.shape, BF), pltpu.VMEM(weights.shape, BF), pltpu.VMEM((half, size), BF), pltpu.VMEM((half, size), BF), dma(4)],
        [],
        steps,
    )


def route_flow(tokens, gain, router, chosen, assign, done):
    own, width = tokens.shape
    experts, count = chosen.shape[1], assign.shape[1]

    def steps(ins, outs, scratch):
        tokens_ref, gain_ref, router_ref, chosen_ref, assign_ref = ins
        residual_ref, mixed_ref, gates_ref, rows_ref = outs
        (pick,) = scratch
        yield
        pick[...] = assign_ref[...].T
        yield done
        residual = tokens_ref[...].astype(F32) + done.ref[...]
        residual_ref[...] = residual
        mixed_ref[...] = (residual * lax.rsqrt(jnp.mean(residual * residual, axis=-1, keepdims=True) + EPS) * gain_ref[...]).astype(BF)
        logits = jnp.where(chosen_ref[...] > 0, dot_nn(mixed_ref[...], router_ref[...]), -1e30)
        powers = jnp.exp(logits - jnp.max(logits, axis=-1, keepdims=True))
        gates = powers / jnp.sum(powers, axis=-1, keepdims=True)
        gates_ref[...] = gates
        for column in range(0, width, 512):
            span = slice(column, column + 512)
            rows_ref[:, span] = dot_nn(pick[...], mixed_ref[:, span]).astype(BF)
        rows_ref[:, width:] = dot_nn(pick[...], gates.astype(BF)).astype(BF)
        yield

    return Flow(
        [(x, pltpu.VMEM) for x in (tokens, gain, router, chosen, assign)],
        [
            ((own, width), F32, pltpu.VMEM),
            ((own, width), BF, pltpu.VMEM),
            ((own, experts), F32, pltpu.VMEM),
            ((count, width + experts), BF, pltpu.VMEM),
        ],
        [pltpu.VMEM((count, own), BF)],
        [],
        steps,
    )


def mix_back_flow(back, assign, gates, mixed, router, residual, gain, cotangent, made):
    own, width = mixed.shape
    experts, count = gates.shape[1], back.shape[0]

    def steps(ins, outs, scratch):
        back_hbm, assign_ref, gates_ref, mixed_ref, router_ref, residual_ref, gain_ref, cotangent_ref = ins
        residual_grad, gain_grad, router_grad = outs
        back_ref, mixed_grad, made.ref, local = scratch
        copy = pltpu.make_async_copy(back_hbm, back_ref, local.at[0])
        copy.start()
        copy.wait()
        sums = jnp.sum(back_ref[:, width : width + 128].astype(F32), axis=1, keepdims=True)
        shape = (count, experts)
        expert_of = lax.div(lax.broadcasted_iota(jnp.int32, shape, 0), count // experts)
        spread = jnp.where(expert_of == lax.broadcasted_iota(jnp.int32, shape, 1), sums, 0.0)
        high = spread.astype(BF)
        low = (spread - high.astype(F32)).astype(BF)
        gate_grads = dot_nn(assign_ref[...], high) + dot_nn(assign_ref[...], low)
        gates = gates_ref[...]
        logits_grad = (gates * (gate_grads - jnp.sum(gates * gate_grads, axis=1, keepdims=True))).astype(BF)
        for column in range(0, width, 512):
            span = slice(column, column + 512)
            mixed_grad[:, span] = dot_nn(assign_ref[...], back_ref[:, span]) + dot_nt(logits_grad, router_ref[span, :])
        value = residual_ref[...]
        inverse = lax.rsqrt(jnp.mean(value * value, axis=-1, keepdims=True) + EPS)
        unit = value * inverse
        grad = mixed_grad[...]
        gain_grad[...] = jnp.sum(grad * unit, axis=0, keepdims=True)
        scaled = grad * gain_ref[...]
        total = cotangent_ref[...].astype(F32) + inverse * (scaled - unit * jnp.mean(scaled * unit, axis=-1, keepdims=True))
        residual_grad[...] = total
        made.ref[...] = total.astype(BF)
        yield
        yield Filler(1.0)
        router_grad[...] = dot_tn(mixed_ref[...], logits_grad).astype(BF)
        yield

    return Flow(
        [(back, pl.ANY)] + [(x, pltpu.VMEM) for x in (assign, gates, mixed, router, residual, gain, cotangent)],
        [((own, width), F32, pltpu.VMEM), ((1, width), F32, pltpu.VMEM), ((width, experts), BF, pltpu.VMEM)],
        [pltpu.VMEM(back.shape, BF), pltpu.VMEM((own, width), F32), pltpu.VMEM((own, width), BF), dma(1)],
        [],
        steps,
    )


def key_back_flow(grad_key, grad_value, raw, gain, cosine, sine, units, kv, w_kv, rows, key_gain):
    half, size = raw.shape
    width = units.shape[1]

    def steps(ins, outs, scratch):
        dk_ref, dv_ref, raw_ref, gain_ref, cos_ref, sin_ref, units_hbm = ins
        rows.ref, kv.ref, w_kv.ref, key_gain.ref, local = scratch
        copy = pltpu.make_async_copy(units_hbm, rows.ref, local.at[0])
        copy.start()
        core, _ = peers_of("c")
        own = pl.ds(pl.multiple_of(core * half, half), half)
        grad = dk_ref[...].astype(F32)
        grad_raw, grad_gain = norm_rope_back(grad, raw_ref[...], gain_ref[...], cos_ref[own, :], sin_ref[own, :])
        kv.ref[...] = jnp.zeros(kv.shape, BF)
        kv.ref[own, :size] = grad_raw.astype(BF)
        kv.ref[own, size:] = dv_ref[...]
        key_gain.ref[...] = jnp.sum(grad_gain, axis=0, keepdims=True)
        copy.wait()
        for i in range(16):
            w_kv.ref[i // 4, i % 4] = dot_tn(rows.ref[own, i * width // 16 : (i + 1) * width // 16], kv.ref[own, :]).astype(BF)
        yield

    return Flow(
        [(x, pltpu.VMEM) for x in (grad_key, grad_value, raw, gain, cosine, sine)] + [(units, pl.ANY)],
        [],
        [pltpu.VMEM(rows.shape, BF), pltpu.VMEM(kv.shape, BF), pltpu.VMEM(w_kv.shape, BF), pltpu.VMEM((1, size), F32), dma(1)],
        [],
        steps,
    )


def tokens_grad_flow(tokens, gain, residual_grad, done):
    def steps(ins, outs, scratch):
        tokens_ref, gain_ref, residual_ref = ins
        (out,) = outs
        yield
        yield done
        value = tokens_ref[...].astype(F32)
        inverse = lax.rsqrt(jnp.mean(value * value, axis=-1, keepdims=True) + EPS)
        unit = value * inverse
        scaled = done.ref[...] * gain_ref[...]
        out[...] = residual_ref[...] + inverse * (scaled - unit * jnp.mean(scaled * unit, axis=-1, keepdims=True))
        yield

    return Flow(
        [(x, pltpu.VMEM) for x in (tokens, gain, residual_grad)], [(tokens.shape, F32, pltpu.VMEM)], [], [], steps
    )


def add_up(stacked):
    return jnp.sum(stacked.astype(F32), axis=0)


def dot_nn(a, b):
    return lax.dot_general(a, b, (((1,), (0,)), ((), ())), preferred_element_type=F32)


def dot_nt(a, b):
    return lax.dot_general(a, b, (((1,), (1,)), ((), ())), preferred_element_type=F32)


def dot_tn(a, b):
    return lax.dot_general(a, b, (((0,), (0,)), ((), ())), preferred_element_type=F32)


def norm_rope(raw, gain, cosine, sine):
    unit = raw * lax.rsqrt(jnp.mean(raw * raw, axis=-1, keepdims=True) + EPS)
    scaled = unit * gain
    return scaled * cosine + pltpu.roll(scaled, 64, 1) * sine


def norm_rope_back(grad, raw, gain, cosine, sine):
    inverse = lax.rsqrt(jnp.mean(raw * raw, axis=-1, keepdims=True) + EPS)
    unit = raw * inverse
    turned = grad * cosine + pltpu.roll(grad * sine, 64, 1)
    scaled = turned * gain
    return inverse * (scaled - unit * jnp.mean(scaled * unit, axis=-1, keepdims=True)), turned * unit


def expert_kernel(rows_ref, plain_ref, w_ref, back_ref, hidden_ref, gated_ref, both_ref):
    width, ff = w_ref.shape[0], plain_ref.shape[1]
    own = lax.axis_index("head") * lax.axis_size("blk") + lax.axis_index("blk")
    gates = rows_ref[:, width:].astype(F32)
    lane = lax.broadcasted_iota(jnp.int32, gates.shape, 1)
    gate = jnp.sum(jnp.where(lane == own, gates, 0.0), axis=1, keepdims=True)
    gate_up = dot_nn(rows_ref[:, :width], w_ref[...])
    first, up = gate_up[:, :ff], gate_up[:, ff:]
    sigma = 1.0 / (1.0 + jnp.exp(-first))
    silu = first * sigma
    hidden = silu * up
    hidden_ref[...] = hidden.astype(BF)
    gated_ref[...] = (hidden * gate).astype(BF)
    plain = plain_ref[...]
    gate_grad = jnp.sum(hidden * plain, axis=1, keepdims=True)
    grad = plain * gate
    both_ref[:, :ff] = (grad * up * (sigma * (1.0 + first * (1.0 - sigma)))).astype(BF)
    both_ref[:, ff:] = (grad * silu).astype(BF)
    back_ref[:, :width] = dot_nt(both_ref[...], w_ref[...]).astype(BF)
    high = gate_grad.astype(BF).astype(F32)
    back_ref[:, width:] = jnp.where(lane == 0, high, jnp.where(lane == 1, gate_grad - high, 0.0)).astype(BF)


def key_tiles(lo, full, last, tiles):
    middle = jnp.minimum(full, last)
    twos, fours = lax.div(middle - lo, 2), lax.div(last - middle, 4)
    rest = middle + 4 * fours
    pl.loop(0, twos)(lambda i: tiles([lo + 2 * i, lo + 2 * i + 1], True))
    pl.loop(lo + 2 * twos, middle)(lambda t: tiles([t], True))
    pl.loop(0, fours)(lambda i: tiles([middle + 4 * i + n for n in range(4)], False))
    for count in range(1, 5):
        pl.when(last - rest == count - 1)(lambda count=count: tiles([rest + n for n in range(count)], True))


def stacked(ref, slots):
    return ref[slots[0]] if len(slots) == 1 else jnp.concatenate([ref[slot] for slot in slots], axis=0)


def allowed_pairs(t, last, start, shape):
    key_place = t * BLOCK + lax.broadcasted_iota(jnp.int32, shape, 0)
    query_place = last * BLOCK + lax.rem(lax.broadcasted_iota(jnp.int32, shape, 1), BLOCK)
    return (key_place >= start) & (key_place <= query_place)


def attend_forward_kernel(
    lo_ref, full_ref, last_ref, slot_ref, raw_ref, gain_ref, cos_ref, sin_ref, k_ref, v_ref, start_ref, q_ref, o_ref, log_ref, q_t, acc, total
):
    j = pl.program_id(0)
    size = k_ref.shape[2]
    heads = raw_ref.shape[1] // size
    scale = size**-0.5 * LOG2E
    last = last_ref[j]
    for n in range(heads):
        span = slice(n * size, (n + 1) * size)
        query = norm_rope(raw_ref[:, span], gain_ref[...], cos_ref[...], sin_ref[...])
        q_ref[:, span] = query.astype(BF)
        q_t[:, n * BLOCK : (n + 1) * BLOCK] = query.T.astype(BF)
    acc[...] = jnp.zeros_like(acc)
    total[...] = jnp.zeros_like(total)
    start = start_ref[0]

    def tiles(at, masked):
        slots = [slot_ref[t] for t in at]
        weights = jnp.exp2(dot_nn(stacked(k_ref, slots), q_t[...]) * scale)
        if masked:
            weights = jnp.where(allowed_pairs(at[0], last, start, weights.shape), weights, 0.0)
        total[...] += jnp.sum(weights.reshape(-1, 8, heads * BLOCK), axis=0)
        acc[...] += dot_nn(stacked(v_ref, slots).T, weights.astype(BF))

    key_tiles(lo_ref[j], full_ref[j], last, tiles)
    row = jnp.sum(total[...], axis=0, keepdims=True)
    log_ref[0] = jnp.log2(row)
    out = acc[...] / row
    for n in range(heads):
        o_ref[:, n * size : (n + 1) * size] = out[:, n * BLOCK : (n + 1) * BLOCK].T.astype(BF)


def attend_backward_kernel(
    lo_ref,
    full_ref,
    last_ref,
    slot_ref,
    block_ref,
    raw_ref,
    gain_ref,
    cos_ref,
    sin_ref,
    k_ref,
    v_ref,
    start_ref,
    q_ref,
    o_ref,
    g_ref,
    w_ref,
    log_ref,
    dq_ref,
    sum_ref,
    dk_ref,
    dv_ref,
    queries,
    q_t,
    grads,
    g_t,
    delta,
    acc,
    dk,
    dv,
    keys_ref,
    values_ref,
    local,
):
    j = pl.program_id(0)
    slots, _, size = keys_ref.shape

    def seen(s):
        block = block_ref[s]
        found = (block >= lo_ref[0]) & (block <= last_ref[0])
        for i in range(1, lo_ref.shape[0]):
            found |= (block >= lo_ref[i]) & (block <= last_ref[i])
        return found

    takes = [pltpu.make_async_copy(k_ref, keys_ref, local.at[0]), pltpu.make_async_copy(v_ref, values_ref, local.at[1])]
    heads = raw_ref.shape[1] // size
    scale = size**-0.5
    last = last_ref[j]

    @pl.when(j == 0)
    def _():
        for copy in takes:
            copy.start()
        sum_ref[...] = jnp.zeros_like(sum_ref)

        @pl.loop(0, slots)
        def _(s):
            @pl.when(seen(s))
            def _():
                dk[s] = jnp.zeros(dk.shape[1:], F32)
                dv[s] = jnp.zeros(dv.shape[1:], F32)

    attended_grad = dot_nn(g_ref[...], w_ref[...]).astype(BF)
    for n in range(heads):
        span, rows = slice(n * size, (n + 1) * size), slice(n * BLOCK, (n + 1) * BLOCK)
        queries[rows, :] = q_ref[:, span]
        q_t[:, rows] = q_ref[:, span].T
        grads[rows, :] = attended_grad[:, span]
        grad_t = attended_grad[:, span].T
        g_t[:, rows] = grad_t
        delta[:, rows] = jnp.sum(grad_t.astype(F32) * o_ref[:, span].T.astype(F32), axis=0, keepdims=True)
    acc[...] = jnp.zeros_like(acc)
    start = start_ref[0]
    logs = log_ref[0]

    @pl.when(j == 0)
    def _():
        for copy in takes:
            copy.wait()

    def tiles(at, masked):
        slots = [slot_ref[t] for t in at]
        keys = stacked(keys_ref, slots)
        probs = jnp.exp2(dot_nn(keys, q_t[...]) * (scale * LOG2E) - logs)
        if masked:
            probs = jnp.where(allowed_pairs(at[0], last, start, probs.shape), probs, 0.0)
        grad_scores = (probs * (dot_nn(stacked(values_ref, slots), g_t[...]) - delta[...])).astype(BF)
        values_part, keys_part = dot_nn(probs.astype(BF), grads[...]), dot_nn(grad_scores, queries[...])
        for n, slot in enumerate(slots):
            dv[slot] += values_part[n * BLOCK : (n + 1) * BLOCK]
            dk[slot] += keys_part[n * BLOCK : (n + 1) * BLOCK]
        acc[...] += dot_nn(keys.T, grad_scores)

    key_tiles(lo_ref[j], full_ref[j], last, tiles)
    for n in range(heads):
        span = slice(n * size, (n + 1) * size)
        grad = (acc[:, n * BLOCK : (n + 1) * BLOCK] * scale).T.astype(BF).astype(F32)
        grad_raw, grad_gain = norm_rope_back(grad, raw_ref[:, span], gain_ref[...], cos_ref[...], sin_ref[...])
        dq_ref[:, span] = grad_raw.astype(BF)
        sum_ref[...] += jnp.sum(grad_gain, axis=0, keepdims=True)

    @pl.when(j == pl.num_programs(0) - 1)
    def _():
        def out(s, n):
            span = pl.ds(s, n)
            return (
                pltpu.make_async_copy(keys_ref.at[span], dk_ref.at[span], local.at[0]),
                pltpu.make_async_copy(values_ref.at[span], dv_ref.at[span], local.at[1]),
            )

        @pl.loop(0, slots, step=8)
        def _(s):
            @pl.loop(s, s + 8)
            def _(i):
                @pl.when(seen(i))
                def _():
                    keys_ref[i] = (dk[i] * scale).astype(BF)
                    values_ref[i] = dv[i].astype(BF)

                @pl.when(jnp.logical_not(seen(i)))
                def _():
                    keys_ref[i] = jnp.zeros(keys_ref.shape[1:], BF)
                    values_ref[i] = jnp.zeros(values_ref.shape[1:], BF)

            for copy in out(s, 8):
                copy.start()

        for copy in out(0, slots):
            copy.wait()


def by_rows(array, rows=BLOCK):
    return pl.BlockSpec((rows,) + array.shape[1:], lambda j, *_: (j,) + (0,) * (array.ndim - 1))


def resident(array):
    return pl.BlockSpec(array.shape, lambda j, *_: (0,) * array.ndim, pipeline_mode=pl.Buffered(1))


def shaped(shape, dtype):
    return jax.ShapeDtypeStruct(shape, dtype)


def expert(rows, plain, weights, block=512):
    count, ff = plain.shape
    outs = (shaped(rows.shape, BF), shaped((count, ff), BF), shaped((count, ff), BF), shaped((count, 2 * ff), BF))
    return pl.pallas_call(
        expert_kernel,
        out_shape=outs,
        grid=(count // block,),
        in_specs=[by_rows(rows, block), by_rows(plain, block), resident(weights)],
        out_specs=tuple(by_rows(x, block) for x in outs),
        compiler_params=pltpu.CompilerParams(vmem_limit_bytes=VMEM_LIMIT),
        cost_estimate=cost_of(20),
        name="expert",
    )(rows, plain, weights)


def attend_forward(meta, raw, gain, cosine, sine, keys, values, start):
    rows, wide = raw.shape
    blocks, size = rows // BLOCK, keys.shape[2]
    lanes = wide // size * BLOCK
    outs = (shaped((rows, wide), BF), shaped((rows, wide), BF), shaped((blocks, 1, lanes), F32))
    return pl.pallas_call(
        attend_forward_kernel,
        out_shape=outs,
        grid_spec=pltpu.PrefetchScalarGridSpec(
            num_scalar_prefetch=4,
            grid=(blocks,),
            in_specs=[
                by_rows(raw),
                resident(gain),
                by_rows(cosine),
                by_rows(sine),
                resident(keys),
                resident(values),
                by_rows(start, 1),
            ],
            out_specs=(by_rows(outs[0]), by_rows(outs[1]), by_rows(outs[2], 1)),
            scratch_shapes=[pltpu.VMEM((size, lanes), BF), pltpu.VMEM((size, lanes), F32), pltpu.VMEM((8, lanes), F32)],
        ),
        compiler_params=pltpu.CompilerParams(vmem_limit_bytes=VMEM_LIMIT),
        cost_estimate=cost_of(30),
        name="attend",
    )(*meta, raw, gain, cosine, sine, keys, values, start)


def attend_backward(meta, raw, gain, cosine, sine, keys, values, start, queries, attended, grads, w_out_t, logs):
    rows, wide = raw.shape
    blocks, size = rows // BLOCK, keys.shape[2]
    lanes = wide // size * BLOCK
    outs = (shaped((rows, wide), BF), shaped((1, size), F32), shaped(keys.shape, BF), shaped(values.shape, BF))
    return pl.pallas_call(
        attend_backward_kernel,
        out_shape=outs,
        grid_spec=pltpu.PrefetchScalarGridSpec(
            num_scalar_prefetch=5,
            grid=(blocks,),
            in_specs=[
                by_rows(raw),
                resident(gain),
                by_rows(cosine),
                by_rows(sine),
                pl.BlockSpec(memory_space=pl.ANY),
                pl.BlockSpec(memory_space=pl.ANY),
                by_rows(start, 1),
                by_rows(queries),
                by_rows(attended),
                by_rows(grads),
                resident(w_out_t),
                by_rows(logs, 1),
            ],
            out_specs=(by_rows(outs[0]), resident(outs[1])) + (pl.BlockSpec(memory_space=pl.ANY),) * 2,
            scratch_shapes=[
                pltpu.VMEM((lanes, size), BF),
                pltpu.VMEM((size, lanes), BF),
                pltpu.VMEM((lanes, size), BF),
                pltpu.VMEM((size, lanes), BF),
                pltpu.VMEM((1, lanes), F32),
                pltpu.VMEM((size, lanes), F32),
                pltpu.VMEM(keys.shape, F32),
                pltpu.VMEM(values.shape, F32),
                pltpu.VMEM(keys.shape, BF),
                pltpu.VMEM(values.shape, BF),
                dma(2),
            ],
        ),
        compiler_params=pltpu.CompilerParams(vmem_limit_bytes=VMEM_LIMIT),
        cost_estimate=cost_of(40),
        name="attend_back",
    )(*meta, raw, gain, cosine, sine, keys, values, start, queries, attended, grads, w_out_t, logs)


def all_to_all(stacked):
    return lax.all_to_all(stacked, ("head", "blk"), split_axis=0, concat_axis=0, tiled=True)


def body(
    tokens,
    norm_gain,
    w_query,
    key_weight,
    value_weight,
    query_gain,
    key_gain,
    w_out,
    mix_gain,
    w_router,
    expert_gate_up,
    expert_down,
    lengths,
    block_deal,
    routes,
    cotangent,
):
    own, width = tokens.shape
    size = query_gain.shape[0]
    scale = size ** (-0.5)
    blk = lax.axis_index("blk")
    plane, core = blk // 4, blk % 2
    devices = lax.axis_size("head") * lax.axis_size("blk")
    experts = w_router.shape[0] * 2
    cap = own * routes.shape[1] // experts
    gate_up, down = expert_gate_up[0], expert_down[0]
    ff = down.shape[0]
    group_rows = 8 * own
    q_cols = w_query.shape[1] // 4
    heads = q_cols // size

    group_blocks = plane * 4 + jnp.array([0, 2, 1, 3], jnp.int32)
    ids = jnp.arange(block_deal.shape[0], dtype=jnp.int32)
    last = jnp.sum(jnp.where(group_blocks[:, None] == ids[None, :], block_deal[None, :], 0), axis=1)
    slots = (ids % 2) * (ids.shape[0] // 2) + (ids // 4) * 2 + (ids % 4) // 2
    slot_of = jnp.sum(jnp.where(block_deal[None, :] == ids[:, None], slots[None, :], 0), axis=1)
    place = (last[:, None] * BLOCK + jnp.arange(BLOCK, dtype=jnp.int32)[None, :]).reshape(-1)
    passed = place[:, None] >= jnp.cumsum(lengths)[None, :]
    start = jnp.sum(jnp.where(passed, lengths[None, :], 0), axis=1)
    start_rows = start.reshape(-1, 1, BLOCK)
    meta = (start_rows[:, 0, 0] // BLOCK, (start_rows[:, 0, BLOCK - 1] + BLOCK - 1) // BLOCK, last, slot_of)
    start_rows = jnp.tile(start_rows, (1, 1, heads))
    offsets = (place - start).astype(F32).reshape(-1, 1, BLOCK)
    spacing = ROPE_BASE ** (-2.0 * jnp.arange(size // 2, dtype=F32) / size)
    spacing = jnp.concatenate([spacing, spacing])[None]

    normed = Made(own, width)
    depth = w_query.shape[0]
    out_pack = w_out.reshape(4, q_cols, depth).transpose(2, 0, 1).reshape(depth, -1)
    side = lax.axis_index("head") == jnp.arange(2, dtype=jnp.int32)
    router_pack = jnp.where(side[None, :, None], w_router.T[:, None, :], 0).astype(BF).reshape(depth, experts)
    w_qkv, w_out_t, w_router_t, group_tokens, assign_low, chosen, cosine, sine = launch(
        [
            norm_flow(tokens, norm_gain[None], normed),
            plane_gather_flow([(w_query, q_cols, 1), (key_weight, size, 2), (value_weight, size, 2)], "x", "y", ahead="zhc"),
            plane_gather_flow([(out_pack, q_cols, 1)], "y", "x", ahead="zhc"),
            plane_gather_flow([(router_pack, experts, 1)], "y", "x", ahead="z"),
            ring_gather_flow(normed),
            tables_flow(routes, offsets, spacing, experts, cap),
        ],
        0,
        45,
    )
    normed_group = group_tokens.reshape(group_rows, width)
    w_qkv, w_out_t = w_qkv.reshape(width, -1), w_out_t.reshape(width, -1)
    w_router_t = jnp.sum(w_router_t.reshape(-1, 2, depth, experts), axis=1).reshape(width, experts)

    q_gain, k_gain = query_gain[None], key_gain[None]
    key, value = Made(group_rows // 2, size), Made(group_rows // 2, size)
    q_raw, k_raw, keys, values, grad_rows = launch(
        [
            project_flow(normed_group, w_qkv, k_gain, cosine, sine, q_cols, key, value),
            plane_gather_flow(key, "x", "y"),
            plane_gather_flow(value, "y", "x"),
            product_flow(assign_low, cotangent),
        ],
        1,
        35,
    )
    grad_rows = all_to_all(grad_rows.reshape(devices, cap, width)).reshape(-1, width)
    keys, values = keys.reshape(-1, BLOCK, size), values.reshape(-1, BLOCK, size)
    queries, attended, logs = attend_forward(meta, q_raw, q_gain, cosine, sine, keys, values, start_rows)

    attention = Made(own, width)
    residual, mixed, gates, outgoing = launch(
        [
            product_scatter_flow([attended], w_out_t, attention),
            route_flow(tokens, mix_gain[None], w_router_t, chosen, assign_low, attention),
        ],
        2,
        30,
    )
    outgoing, grad_rows = lax.optimization_barrier((outgoing, grad_rows))
    arrived = all_to_all(outgoing.reshape(devices, cap, -1)).reshape(experts * cap, -1)

    plain_grad = lax.optimization_barrier(dot_nt(grad_rows, down))
    rows, plain_grad = lax.optimization_barrier((arrived, plain_grad))
    back, hidden, gated, grad_both = expert(rows, plain_grad, gate_up)
    back = all_to_all(back.reshape(devices, cap, -1)).reshape(experts * cap, -1)
    back, expert_out = lax.optimization_barrier((back, dot_nn(hidden, down).astype(BF)))
    grad_down = dot_tn(gated, grad_rows)
    grad_gate_up = dot_tn(rows[:, :width], grad_both)

    grad_attention = Made(own, width)
    grad_residual, grad_mix_gain, grad_router_t, grad_group = launch(
        [
            mix_back_flow(back, assign_low, gates, mixed, w_router_t, residual, mix_gain[None], cotangent, grad_attention),
            ring_gather_flow(grad_attention),
        ],
        3,
        25,
    )
    grad_group = grad_group.reshape(group_rows, width)
    grad_group, expert_out = lax.optimization_barrier((grad_group, expert_out))
    expert_out = all_to_all(expert_out.reshape(devices, cap, width)).reshape(-1, width)
    block_of = block_deal.reshape(-1, 2, 2).transpose(2, 0, 1).reshape(-1)
    grad_q, grad_query_gain, grad_keys, grad_values = attend_backward(
        (*meta, block_of), q_raw, q_gain, cosine, sine, keys, values, start_rows, queries, attended, grad_group, w_out_t, logs
    )

    split = (2, 4, 4, group_rows // 2, size)
    grad_key, grad_value, grad_wq, grad_wo = launch(
        [
            plane_scatter_flow(grad_keys.reshape(split), "y", "x", from_core=True),
            plane_scatter_flow(grad_values.reshape(split), "x", "y", from_core=True),
            product_flow(normed_group, grad_q),
            product_flow(grad_group, attended),
        ],
        4,
        35,
    )

    grad_key, expert_out = lax.optimization_barrier((grad_key, expert_out))
    plane_split = (4, 4, 4 * depth, -1)
    zeros, ones = jnp.zeros((width,), F32), jnp.ones((width,), F32)
    gains = jnp.concatenate([zeros, grad_mix_gain[0], grad_query_gain[0], zeros[: 7 * size], norm_gain, ones, ones[: 8 * size]])
    units, grad_kv, grad_wkv, key_gain_sum = Made(group_rows, width), Made(group_rows, 2 * size), Made(4, 4, 4 * depth, 2 * size), Made()
    grad_normed = Made(own, width)
    grad_wq, grad_wo, gains, grad_wkv, grad_wr, output, grad_tokens = launch(
        [
            key_back_flow(grad_key, grad_value, k_raw, k_gain, cosine, sine, normed_group, grad_kv, grad_wkv, units, key_gain_sum),
            plane_scatter_flow(grad_wq.reshape(plane_split), "y", "x", last_in="zhc"),
            plane_scatter_flow(grad_wo.reshape(plane_split), "x", "y", last_in="zhc"),
            product_scatter_flow([grad_q, grad_kv], w_qkv, grad_normed, units, gains.reshape(2, -1, size), key_gain_sum),
            plane_scatter_flow(grad_wkv, "y", "x", last_in="zhc"),
            plane_scatter_flow(grad_router_t.reshape(plane_split), "x", "y", last_in="z"),
            output_flow(residual, gates, assign_low, expert_out),
            tokens_grad_flow(tokens, norm_gain[None], grad_residual, grad_normed),
        ],
        5,
        50,
    )
    gains = gains.reshape(-1)
    grad_w_query = grad_wq.astype(F32).transpose(1, 0, 2).reshape(depth, -1)
    grad_kv_w = jnp.sum(grad_wkv.astype(F32).reshape(2, 2, depth, 2, size), axis=1)
    grad_w_key = grad_kv_w[:, :, 0].transpose(1, 0, 2).reshape(depth, -1)
    grad_w_value = grad_kv_w[:, :, 1].transpose(1, 0, 2).reshape(depth, -1)
    grad_w_out = grad_wo.astype(F32).transpose(0, 2, 1).reshape(-1, depth)
    grad_w_router = lax.dynamic_slice_in_dim(add_up(grad_wr), lax.axis_index("head") * (experts // 2), experts // 2, 1).T
    return (
        output,
        grad_tokens,
        gains[:width],
        grad_w_query,
        grad_w_key,
        grad_w_value,
        gains[2 * width : 2 * width + size],
        gains[2 * width + size : 2 * width + 2 * size],
        grad_w_out,
        gains[width : 2 * width],
        grad_w_router,
        grad_gate_up[None],
        grad_down[None],
    )


def solution(mesh):
    rows, both = P(("head", "blk"), None), P("blk", "head")
    expert, turned = P(("head", "blk"), None, None), P("head", "blk")
    in_specs = (rows, P(), both, both, both, P(), P(), turned, P(), turned, expert, expert, P(), P(), rows, rows)
    out_specs = (rows, rows, P(), both, both, both, P(), P(), turned, P(), turned, expert, expert)
    return jax.shard_map(body, mesh=mesh, in_specs=in_specs, out_specs=out_specs, check_vma=False)
```

```python
import math

import jax
import jax.numpy as jnp
from jax import lax
from jax.experimental import pallas as pl
from jax.experimental.pallas import tpu as pltpu
from jax.sharding import PartitionSpec as P

MESH = pl.DeviceIdType.MESH
EPS = 1e-06
ROPE_BASE = 1000000.0
LOG2E = 1.4426950408889634
BF = jnp.bfloat16
F32 = jnp.float32
BLOCK = 256
VMEM_LIMIT = 60 << 20
SIZES = {"zc": 4, "c": 2, "x": 4, "y": 4, "zhc": 4, "z": 8, "yx": 16}


def peers_of(kind):
    h = lax.axis_index("head")
    b = lax.axis_index("blk")
    q, r = lax.div(b, 4), lax.rem(b, 4)
    if kind == "zc":
        return lax.div(r, 2) * 2 + h, lambda g: (lax.rem(g, 2), q * 4 + lax.div(g, 2) * 2 + lax.rem(r, 2))
    if kind == "z":
        return r * 2 + h, lambda g: (lax.rem(g, 2), q * 4 + lax.div(g, 2))
    if kind == "c":
        return lax.rem(b, 2), lambda g: (h, b - lax.rem(b, 2) + g)
    if kind == "x":
        return lax.rem(q, 4), lambda g: (h, (lax.div(q, 4) * 4 + g) * 4 + r)
    if kind == "y":
        return lax.div(q, 4), lambda g: (h, (g * 4 + lax.rem(q, 4)) * 4 + r)
    if kind == "yx":
        return q, lambda g: (h, g * 4 + r)
    return r, lambda g: (h, q * 4 + g)


def cost_of(microseconds):
    return pl.CostEstimate(flops=microseconds * 10**9, bytes_accessed=microseconds * 3 * 10**6, transcendentals=0)


class Flow:
    def __init__(self, inputs, outputs, scratch, partners, steps):
        self.inputs, self.outputs, self.scratch = inputs, outputs, scratch
        self.partners, self.steps = partners, steps


class Filler:
    def __init__(self, cost):
        self.cost = cost


class Clock:
    now = 0.0


def in_turn(flows):
    Clock.now = 0.0
    ready, waiting, fillers = [(0.0, i, steps) for i, steps in enumerate(flows)], [], []
    count = len(flows)
    while ready or fillers or waiting:
        for entry in [e for e in waiting if e[0].ref is not None]:
            waiting.remove(entry)
            ready.append((Clock.now, entry[1], entry[2]))
        ready.sort(key=lambda e: e[:2])
        if fillers and (not ready or ready[0][0] > Clock.now + 0.5):
            cost, order, steps = fillers.pop(0)
            Clock.now += cost
        else:
            when, order, steps = ready.pop(0)
            Clock.now = max(Clock.now, when) + 0.3
        result = next(steps, steps)
        if result is steps:
            continue
        if isinstance(result, Filler):
            fillers.append((result.cost, order, steps))
        elif isinstance(result, Made):
            waiting.append((result, order, steps))
        elif result is None or isinstance(result, float):
            ready.append((Clock.now if result is None else result, order, steps))
        else:
            ready += [(Clock.now, order, steps), (Clock.now, count, result)]
            count += 1


class Made:
    def __init__(self, *shape):
        self.shape, self.ref = shape, None


HOP = 3.0
RATE = 40e3
CORE_RATE = 200e3


def launch(flows, cid, cost):
    partners = sorted({p for flow in flows for p in flow.partners})

    def kernel(*refs):
        n_in, n_out = sum(len(f.inputs) for f in flows), sum(len(f.outputs) for f in flows)
        ins, outs, rest = list(refs[:n_in]), list(refs[n_in : n_in + n_out]), list(refs[n_in + n_out :])
        barrier = pltpu.get_barrier_semaphore()
        for kind, distance in partners:
            me, member = peers_of(kind)
            to = member(lax.rem(me + distance, SIZES[kind]))
            pl.semaphore_signal(barrier, inc=1, device_id=to, device_id_type=MESH)
        running = []
        for flow in flows:
            own = [[group.pop(0) for _ in part] for group, part in ((ins, flow.inputs), (outs, flow.outputs), (rest, flow.scratch))]
            running.append(flow.steps(*own))
            next(running[-1])
        pl.semaphore_wait(barrier, len(partners))
        in_turn(running)

    return pl.pallas_call(
        kernel,
        out_shape=tuple(jax.ShapeDtypeStruct(s, d) for f in flows for s, d, _ in f.outputs),
        in_specs=[pl.BlockSpec(memory_space=space) for f in flows for _, space in f.inputs],
        out_specs=tuple(pl.BlockSpec(memory_space=space) for f in flows for _, _, space in f.outputs),
        scratch_shapes=[x for f in flows for x in f.scratch],
        compiler_params=pltpu.CompilerParams(collective_id=cid, has_side_effects=True, vmem_limit_bytes=VMEM_LIMIT),
        cost_estimate=cost_of(cost),
        name=f"links_{cid}",
    )(*[x for f in flows for x, _ in f.inputs])


def remote(src, dst, send, recv, device):
    return pltpu.make_async_remote_copy(
        src_ref=src, dst_ref=dst, send_sem=send, recv_sem=recv, device_id=device, device_id_type=MESH
    )


def piece(ref, which):
    rows = ref.shape[0] // 2
    return ref.at[pl.ds(which * rows, rows)]


def ring_partners(kind):
    return [(kind, 1), (kind, 3)]


class RingGather:
    def __init__(self, kind, slot, src, send, recv):
        me, member = peers_of(kind)
        up, down = lax.rem(me + 1, 4), lax.rem(me + 3, 4)

        def copy(source, target, i, to):
            return remote(source, target, send.at[i], recv.at[i], member(to))

        mine = slot(me)
        self.copies = [
            copy(piece(src, 0), piece(mine, 0), 0, up),
            copy(piece(src, 1), piece(mine, 1), 1, up),
            copy(piece(src, 1), piece(mine, 1), 2, down),
            copy(piece(src, 0), piece(mine, 0), 3, down),
            copy(piece(slot(down), 0), piece(slot(down), 0), 4, up),
            copy(piece(slot(up), 1), piece(slot(up), 1), 5, down),
        ]

    def start(self):
        for i in (0, 2, 1, 3):
            self.copies[i].start()

    def forward(self):
        self.copies[0].wait_recv()
        self.copies[4].start()
        self.copies[2].wait_recv()
        self.copies[5].start()

    def near(self):
        self.copies[1].wait_recv()
        self.copies[3].wait_recv()

    def far(self):
        self.copies[4].wait_recv()
        self.copies[5].wait_recv()

    def sent(self):
        for copy in self.copies:
            copy.wait_send()


class RingScatter:
    def __init__(self, kind, chunk, bufs, send, recv, raw=None):
        raw = raw or chunk
        self.me, member = peers_of(kind)
        self.up, self.down, self.far = (lax.rem(self.me + k, 4) for k in (1, 3, 2))
        self.chunk, self.bufs = chunk, bufs

        def copy(source, target, i, to):
            return remote(source, bufs.at[target], send.at[i], recv.at[i], member(to))

        self.copies = [
            copy(piece(raw(self.far), 0), 0, 0, self.up),
            copy(piece(raw(self.far), 1), 1, 1, self.down),
            copy(piece(raw(self.up), 1), 2, 2, self.up),
            copy(piece(raw(self.down), 0), 3, 3, self.down),
            copy(bufs.at[6], 4, 4, self.up),
            copy(bufs.at[7], 5, 5, self.down),
        ]

    def start_far(self):
        self.copies[0].start()
        self.copies[1].start()

    def start_up(self):
        self.copies[2].start()

    def start_down(self):
        self.copies[3].start()

    def add(self):
        self.copies[0].wait_recv()
        self.bufs[6] = (piece(self.chunk(self.up), 0)[...].astype(F32) + self.bufs[0].astype(F32)).astype(BF)
        self.copies[4].start()
        self.copies[1].wait_recv()
        self.bufs[7] = (piece(self.chunk(self.down), 1)[...].astype(F32) + self.bufs[1].astype(F32)).astype(BF)
        self.copies[5].start()

    def total(self, which):
        first, second = ((4, 3), (2, 5))[which]
        self.copies[first].wait_recv()
        self.copies[second].wait_recv()
        return self.bufs[first].astype(F32) + self.bufs[second].astype(F32)

    def sent(self):
        for copy in self.copies:
            copy.wait_send()


def dma(*shape):
    return pltpu.SemaphoreType.DMA(shape)


def ring_gather_flow(made):
    shape = (2, 4) + made.shape

    def steps(ins, outs, scratch):
        (out,), src = outs, made.ref
        send, recv, pass_send, pass_recv, local = scratch
        yield
        me, _ = peers_of("zc")
        core, member = peers_of("c")
        ring = RingGather("zc", lambda g: out.at[core, g], src, send, recv)

        def passing(k):
            g = lax.rem(me + k, 4)
            return remote(src if k == 0 else out.at[core, g], out.at[core, g], pass_send.at[k], pass_recv.at[k], member(1 - core))

        passes = [passing(k) for k in range(4)]
        unit = math.prod(made.shape) * 2 / RATE
        begun = Clock.now
        ring.start()
        passes[0].start()
        yield begun + HOP + unit / 2
        ring.forward()
        back = pltpu.make_async_copy(src, out.at[core, me], local.at[0])
        back.start()
        yield begun + HOP + unit
        ring.near()
        passes[1].start()
        passes[3].start()
        yield begun + 2 * HOP + 1.5 * unit
        ring.far()
        passes[2].start()
        yield Clock.now + HOP + 2.0
        back.wait()
        ring.sent()
        for copy in passes:
            copy.wait()

    return Flow(
        [],
        [(shape, BF, pl.ANY)],
        [dma(6), dma(6), dma(4), dma(4), dma(1)],
        ring_partners("zc") + [("c", 1)],
        steps,
    )


def plane_gather_flow(arrays, first, second, ahead=None):
    to_core = ahead is None
    if ahead == "zhc":
        shard = (4, arrays[0][0].shape[0], sum(columns for _, columns, _ in arrays))
    elif ahead == "z":
        shard = (8,) + arrays[0][0].shape
    else:
        shard = arrays.shape
    shape = ((2,) if to_core else ()) + (4, 4) + shard
    n_ahead = SIZES[ahead] if ahead else 1

    def steps(ins, outs, scratch):
        (out,) = outs
        stage, send, recv, pass_send, pass_recv, local, ahead_send, ahead_recv = scratch
        core, member = peers_of("c")
        here, _ = peers_of(first)
        there, _ = peers_of(second)
        view = out.at[core] if to_core else out

        def slot(a, b):
            return view.at[b, a] if first == "x" else view.at[a, b]

        if ahead:
            mine, at = peers_of(ahead)

            def parts(to):
                if ahead == "z":
                    return [(ins[0], stage.at[mine])]
                found, begin = [], 0
                for ref, (_, columns, share) in zip(ins, arrays):
                    source = ref.at[:, pl.ds(pl.multiple_of(lax.div(to, share) * columns, columns), columns)]
                    found.append((source, stage.at[mine, :, pl.ds(begin, columns)]))
                    begin += columns
                return found

            early = [pltpu.make_async_copy(source, target, local.at[i]) for i, (source, target) in enumerate(parts(mine))]
            for k in range(1, n_ahead):
                to = lax.rem(mine + k, n_ahead)
                for i, (source, target) in enumerate(parts(to)):
                    early.append(remote(source, target, ahead_send.at[i, k], ahead_recv.at[i, k], at(to)))
            local_parts = len(parts(mine))
            for copy in early[:local_parts]:
                copy.start()
            yield
            for copy in early[local_parts:]:
                copy.start()
            yield Clock.now + HOP + 7.0
            for copy in early:
                copy.wait()
            src = stage
        else:
            src = arrays.ref
            yield
        ring = RingGather(first, lambda g: slot(g, there), src, send.at[4], recv.at[4])
        columns = [lax.rem(here + k, 4) for k in range(4)]
        rings = [
            RingGather(second, lambda g, a=a: slot(a, g), src if k == 0 else slot(a, there), send.at[k], recv.at[k])
            for k, a in enumerate(columns)
        ]

        def passing(k, m):
            ref = slot(columns[k], lax.rem(there + m, 4))
            return remote(src if k == m == 0 else ref, ref, pass_send.at[k * 4 + m], pass_recv.at[k * 4 + m], member(1 - core))

        passes = {}

        def hand_over(k, m):
            if to_core:
                passes[k, m] = passing(k, m)
                passes[k, m].start()

        unit = math.prod(shard) * 2 / RATE
        begun = Clock.now
        ring.start()
        rings[0].start()
        hand_over(0, 0)
        yield begun + HOP + unit / 2
        ring.forward()
        back = pltpu.make_async_copy(src, slot(here, there), local.at[0])
        back.start()
        yield
        rings[0].forward()
        yield begun + HOP + unit
        ring.near()
        for k in (1, 3):
            rings[k].start()
            hand_over(k, 0)
        yield begun + 2 * HOP + 1.5 * unit
        ring.far()
        rings[2].start()
        hand_over(2, 0)
        yield
        for i, k in enumerate((0, 1, 3, 2)):
            if k > 0:
                yield begun + 2 * HOP + (1.5 * i + 0.5) * unit
                rings[k].forward()
            yield begun + 2 * HOP + (1.5 * i + 1.0) * unit
            rings[k].near()
            hand_over(k, 1)
            hand_over(k, 3)
        for i, k in enumerate((0, 1, 3, 2)):
            yield begun + 3 * HOP + (1.5 * i + 1.5) * unit
            rings[k].far()
            hand_over(k, 2)
        yield Clock.now + HOP
        back.wait()
        ring.sent()
        for one in rings:
            one.sent()
        for copy in passes.values():
            copy.wait()

    return Flow(
        [] if to_core else [(array, pl.ANY) for array, *_ in arrays],
        [(shape, BF, pl.ANY)],
        [pltpu.VMEM((8, 128) if to_core else shard, BF), dma(5, 6), dma(5, 6), dma(16), dma(16), dma(3), dma(3, 8), dma(3, 8)],
        ring_partners("x") + ring_partners("y") + ([("c", 1)] if to_core else []) + [(ahead, k) for k in range(1, n_ahead)],
        steps,
    )


def ring_exchange_flow(array, columns, kind):
    n, rows = SIZES[kind], array.shape[0]

    def steps(ins, outs, scratch):
        (src,), (out,) = ins, outs
        send, recv, local = scratch
        mine, at = peers_of(kind)

        def part(to):
            return src if kind == "z" else src.at[:, pl.ds(pl.multiple_of(to * columns, columns), columns)]

        own = pltpu.make_async_copy(part(mine), out.at[mine], local.at[0])
        own.start()
        yield
        copies = []
        for k in range(1, n):
            to = lax.rem(mine + k, n)
            copies.append(remote(part(to), out.at[mine], send.at[k], recv.at[k], at(to)))
            copies[-1].start()
        yield 40.0
        own.wait()
        for copy in copies:
            copy.wait()

    return Flow(
        [(array, pl.ANY)],
        [((n, rows, columns), BF, pltpu.VMEM)],
        [dma(n), dma(n), dma(1)],
        [(kind, k) for k in range(1, n)],
        steps,
    )


def product_flow(left, right):
    columns, width = left.shape[1], right.shape[1]

    def steps(ins, outs, scratch):
        (out,) = outs
        left_ref, right_ref, local = scratch
        copies = [pltpu.make_async_copy(source, target, local.at[i]) for i, (source, target) in enumerate(zip(ins, (left_ref, right_ref)))]
        for copy in copies:
            copy.start()
        yield
        yield Filler(1.0)
        for copy in copies:
            copy.wait()
        for column in range(0, columns, 256):
            span = slice(column, column + 256)
            out[span, :] = dot_tn(left_ref[:, span], right_ref[...]).astype(BF)
            yield Filler(1.0)

    return Flow(
        [(left, pl.ANY), (right, pl.ANY)],
        [((columns, width), BF, pltpu.VMEM)],
        [pltpu.VMEM(left.shape, BF), pltpu.VMEM(right.shape, BF), dma(2)],
        [],
        steps,
    )


def output_flow(residual, gates, assign, expert_out):
    own, width = residual.shape
    experts = gates.shape[1]
    count = expert_out.shape[0]

    def steps(ins, outs, scratch):
        residual_ref, gates_ref, assign_ref, expert_hbm = ins
        (out,) = outs
        expert_ref, mixing, local = scratch
        copy = pltpu.make_async_copy(expert_hbm, expert_ref, local.at[0])
        copy.start()
        wide = (experts, count)
        cap = count // experts
        spread = (lax.broadcasted_iota(jnp.int32, wide, 1) // cap == lax.broadcasted_iota(jnp.int32, wide, 0)).astype(F32).astype(BF)
        taken = assign_ref[...].astype(F32)
        high = gates_ref[...].astype(BF)
        low = (gates_ref[...] - high.astype(F32)).astype(BF)
        mixing[0] = (dot_nn(high, spread) * taken).astype(BF)
        mixing[1] = (dot_nn(low, spread) * taken).astype(BF)
        yield
        yield Filler(1.0)
        copy.wait()
        for column in range(0, width, 512):
            span = slice(column, column + 512)
            rows = expert_ref[:, span]
            out[:, span] = (residual_ref[:, span] + dot_nn(mixing[0], rows) + dot_nn(mixing[1], rows)).astype(BF)
            yield Filler(1.0)

    return Flow(
        [(residual, pltpu.VMEM), (gates, pltpu.VMEM), (assign, pltpu.VMEM), (expert_out, pl.ANY)],
        [(residual.shape, BF, pltpu.VMEM)],
        [pltpu.VMEM(expert_out.shape, BF), pltpu.VMEM((2, own, count), BF), dma(1)],
        [],
        steps,
    )


sum_partners = [("yx", k) for k in range(1, 16)] + [("z", k) for k in range(1, 8)]


def sum_room(shape):
    return [pltpu.VMEM((16,) + shape, F32), pltpu.VMEM((8,) + shape, F32), pltpu.VMEM(shape, F32), dma(16), dma(16), dma(8), dma(8)]


def sum_steps(src, gains, out, scratch):
    wide, far, middle, sends, recvs, far_sends, far_recvs = scratch
    me, member = peers_of("yx")
    copies = []
    for k in range(1, 16):
        copies.append(remote(src, wide.at[me], sends.at[k], recvs.at[k], member(lax.rem(me + k, 16))))
        copies[-1].start()
    wide[me] = src[...]
    yield Clock.now + HOP + 4.0
    for copy in copies:
        copy.wait()
    middle[...] = jnp.sum(wide[...], axis=0)
    ring, ring_member = peers_of("z")
    late = []
    for k in range(1, 8):
        late.append(remote(middle, far.at[ring], far_sends.at[k], far_recvs.at[k], ring_member(lax.rem(ring + k, 8))))
        late[-1].start()
    far[ring] = middle[...]
    yield Clock.now + HOP + 3.0
    for copy in late:
        copy.wait()
    out[...] = jnp.sum(far[...], axis=0) / gains[1]


def product_scatter_flow(lefts, right, done, units=None, gains=None, key_gain=None, kept=None):
    arrays = [left for left in lefts if not isinstance(left, Made)]
    own, wide = lefts[0].shape[0] // 8, right.shape[0]
    spans = [0]
    for left in lefts:
        spans.append(spans[-1] + left.shape[1])

    def steps(ins, outs, scratch):
        given = list(ins[: len(arrays)])
        left_refs = [left.ref if isinstance(left, Made) else given.pop(0) for left in lefts]
        right_ref = ins[len(arrays)]
        if kept is not None:
            kept.ref = right_ref
        out, theirs, came, chunks, bufs, send, recv, pass_send, pass_recv, *rest = scratch
        core, member = peers_of("c")
        me, _ = peers_of("zc")
        ring = RingScatter("zc", lambda g: chunks.at[g], bufs, send, recv)

        if units is not None:
            gains_ref = ins[len(arrays) + 1]
            unit_ref = units.ref
            sums, *sum_scratch = rest
            sums[...] = gains_ref[0]
            sums[33:34, :] += key_gain.ref[...]

        def product(c, k, column):
            row = pl.multiple_of((c * 4 + lax.rem(me + k, 4)) * own, own)
            value = sum(
                dot_nt(left_ref[pl.ds(row, own), :], right_ref[column : column + 512, spans[i] : spans[i + 1]])
                for i, left_ref in enumerate(left_refs)
            )
            if units is not None:
                row_sum = jnp.sum(value * unit_ref[pl.ds(row, own), column : column + 512].astype(F32), axis=0, keepdims=True)
                for lane in range(0, 512, 128):
                    at = (column + lane) // 128
                    sums[at : at + 1, :] += row_sum[:, lane : lane + 128]
            return value

        passes = [
            remote(theirs.at[k], came.at[k], pass_send.at[k], pass_recv.at[k], member(1 - core)) for k in range(4)
        ]
        for k in (2, 1, 3, 0):
            if k == 1:
                yield
                Clock.now += 0.7
                passes[2].start()
            for column in range(0, wide, 512):
                theirs[k, :, column : column + 512] = product(1 - core, k, column).astype(BF)
            if k != 2:
                Clock.now += 0.7
                passes[k].start()
                yield
        for k in (2, 1, 3, 0):
            passes[k].wait_recv()
            g = lax.rem(me + k, 4)
            for column in range(0, wide, 512):
                span = slice(column, column + 512)
                value = product(core, k, column) + came[k, :, span].astype(F32)
                if k == 0:
                    out[:, span] = value
                else:
                    chunks[g, :, span] = value.astype(BF)
            Clock.now += 0.7
            if k == 2:
                begun = Clock.now
                ring.start_far()
            elif k == 1:
                ring.start_up()
            elif k == 3:
                ring.start_down()
            yield
        unit = own * wide * 2 / RATE
        if units is not None:
            yield sum_steps(sums, gains_ref, outs[0], sum_scratch)
        yield begun + HOP + unit / 2
        ring.add()
        yield begun + 2 * HOP + 1.5 * unit
        for h in range(2):
            rows = slice(h * own // 2, (h + 1) * own // 2)
            out[rows, :] += ring.total(h)
        done.ref = out
        yield Clock.now + 2.0
        ring.sent()
        for copy in passes:
            copy.wait_send()

    return Flow(
        [(x, pltpu.VMEM) for x in (*arrays, right)] + ([] if units is None else [(gains, pltpu.VMEM)]),
        [] if units is None else [(gains.shape[1:], F32, pltpu.VMEM)],
        [
            pltpu.VMEM((own, wide), F32),
            pltpu.VMEM((4, own, wide), BF),
            pltpu.VMEM((4, own, wide), BF),
            pltpu.VMEM((4, own, wide), BF),
            pltpu.VMEM((8, own // 2, wide), BF),
            dma(6),
            dma(6),
            dma(4),
            dma(4),
        ]
        + ([] if units is None else [pltpu.VMEM(gains.shape[1:], F32)] + sum_room(gains.shape[1:])),
        ring_partners("zc") + [("c", 1)] + ([] if units is None else sum_partners),
        steps,
    )


def plane_scatter_flow(array, first, second, from_core=False, last_in=None):
    rows, columns = array.shape[-2:]
    n_last = SIZES[last_in] if last_in else 1
    result = (n_last, rows // 4, columns) if last_in else (rows, columns)

    def steps(ins, outs, scratch):
        src, (out,) = array.ref if isinstance(array, Made) else ins[0], outs
        came, sums, middle, bufs, late_bufs, send, recv, late_send, late_recv, pass_send, pass_recv, local, cut, cut_send, cut_recv = scratch
        core, member = peers_of("c")
        me, _ = peers_of(first)

        def along(ref, g):
            return ref.at[g] if first == "y" else ref.at[:, g]

        order = [lax.rem(me + k, 4) for k in (2, 1, 3, 0)]
        unit = 4 * rows * columns * 2 / RATE
        loads = [
            pltpu.make_async_copy(along(src.at[core] if from_core else src, g), along(sums, g), local.at[i])
            for i, g in enumerate(order)
            if from_core or i > 0
        ]
        passes = []
        if from_core:
            ring = RingScatter(first, lambda g: along(sums, g), bufs, send, recv)
            for i, g in enumerate(order):
                loads[i].start()
                passes.append(
                    remote(along(src.at[1 - core], g), along(came, g), pass_send.at[i], pass_recv.at[i], member(1 - core))
                )
            yield
            for copy in passes:
                copy.start()
            yield Clock.now + HOP + unit * RATE / CORE_RATE
            starts = [ring.start_far, ring.start_up, ring.start_down, lambda: None]
            for i, g in enumerate(order):
                loads[i].wait()
                passes[i].wait_recv()
                for k in range(4):
                    total = along(sums, g)[k].astype(F32) + along(came, g)[k].astype(F32)
                    along(sums, g)[k] = total.astype(BF)
                starts[i]()
                if i == 0:
                    begun = Clock.now
                yield Clock.now + unit * RATE / CORE_RATE if i < 3 else None
        else:
            ring = RingScatter(first, lambda g: along(sums, g), bufs, send, recv, raw=lambda g: along(src, g))
            for load in loads:
                load.start()
            yield
            begun = Clock.now
            ring.start_far()
            ring.start_up()
            ring.start_down()
            yield begun + HOP + unit / 2
            for load in loads:
                load.wait()
        if from_core:
            yield begun + HOP + unit / 2
        ring.add()
        yield begun + 2 * HOP + 1.5 * unit
        own = along(sums, me)
        for h in range(2):
            came_half = ring.total(h)
            for k in range(2):
                middle[h * 2 + k] = (own[h * 2 + k].astype(F32) + came_half[k]).astype(BF)
        Clock.now += 1.0
        begun = Clock.now
        last = RingScatter(second, lambda g: middle.at[g], late_bufs, late_send, late_recv)
        last.start_far()
        last.start_up()
        last.start_down()
        yield begun + HOP + unit / 8
        last.add()
        yield begun + 2 * HOP + 0.4 * unit
        for h in range(2):
            total = (piece(middle.at[last.me], h)[...].astype(F32) + last.total(h)).astype(BF)
            if last_in:
                cut[2 * h] = total[: rows // 4]
                cut[2 * h + 1] = total[rows // 4 :]
            else:
                out[h * rows // 2 : (h + 1) * rows // 2, :] = total
        cuts = []
        if last_in:
            mine, at = peers_of(last_in)
            share = n_last // 4
            for k in range(1, n_last):
                to = lax.rem(mine + k, n_last)
                cuts.append(remote(cut.at[lax.div(to, share)], out.at[mine], cut_send.at[k], cut_recv.at[k], at(to)))
                cuts[-1].start()
            out[mine] = cut[lax.div(mine, share)]
        yield Clock.now + HOP + 3.0
        ring.sent()
        last.sent()
        for copy in passes:
            copy.wait_send()
        for copy in cuts:
            copy.wait()

    block = (4, 4, rows, columns)
    return Flow(
        [] if isinstance(array, Made) else [(array, pl.ANY)],
        [(result, BF, pltpu.VMEM)],
        [
            pltpu.VMEM(block if from_core else (8, 128), BF),
            pltpu.VMEM(block, BF),
            pltpu.VMEM((4, rows, columns), BF),
            pltpu.VMEM((8, 2, rows, columns), BF),
            pltpu.VMEM((8, rows // 2, columns), BF),
            dma(6),
            dma(6),
            dma(6),
            dma(6),
            dma(4),
            dma(4),
            dma(4),
            pltpu.VMEM((4, rows // 4, columns), BF),
            dma(8),
            dma(8),
        ],
        ring_partners("x")
        + ring_partners("y")
        + ([("c", 1)] if from_core else [])
        + [(last_in, k) for k in range(1, n_last)],
        steps,
    )


def tables_flow(routes, offsets, spacing, experts, cap):
    own, top = routes.shape
    rows, size = offsets.size, spacing.shape[1]

    def steps(ins, outs, scratch):
        routes_ref, offsets_ref, spacing_ref = ins
        assign, chosen_ref, cosine, sine = outs
        yield
        yield Filler(1.0)
        lane = lax.broadcasted_iota(jnp.int32, (own, experts), 1)
        chosen = jnp.zeros((own, experts), F32)
        for k in range(top):
            chosen += (routes_ref[:, k : k + 1] == lane).astype(F32)
        chosen_ref[...] = chosen
        before = lax.broadcasted_iota(jnp.int32, (own, own), 0) > lax.broadcasted_iota(jnp.int32, (own, own), 1)
        earlier = dot_nn(before.astype(F32).astype(BF), chosen.astype(BF))
        wide = (experts, experts * cap)
        spread = (lax.broadcasted_iota(jnp.int32, wide, 1) // cap == lax.broadcasted_iota(jnp.int32, wide, 0)).astype(F32).astype(BF)
        slot = lax.rem(lax.broadcasted_iota(jnp.int32, (own, experts * cap), 1), cap).astype(F32)
        taken = (dot_nn(chosen.astype(BF), spread) > 0.5) & (dot_nn(earlier.astype(BF), spread) == slot)
        assign[...] = taken.astype(F32).astype(BF)
        yield Filler(1.0)
        sign = jnp.where(lax.broadcasted_iota(jnp.int32, (1, size), 1) < size // 2, -1.0, 1.0)
        for row in range(0, rows, BLOCK):
            span = slice(row, row + BLOCK)
            angles = jnp.broadcast_to(offsets_ref[row // BLOCK], (size, BLOCK)).T * spacing_ref[...]
            cosine[span, :] = jnp.cos(angles)
            sine[span, :] = jnp.sin(angles) * sign
            yield Filler(1.0)

    return Flow(
        [(routes, pltpu.VMEM), (offsets, pltpu.VMEM), (spacing, pltpu.VMEM)],
        [
            ((own, experts * cap), BF, pltpu.VMEM),
            ((own, experts), F32, pltpu.VMEM),
            ((rows, size), F32, pltpu.VMEM),
            ((rows, size), F32, pltpu.VMEM),
        ],
        [],
        [],
        steps,
    )


def norm_flow(tokens, gain, made):
    def steps(ins, outs, scratch):
        tokens_ref, gain_ref = ins
        (made.ref,) = scratch
        wide = tokens_ref[...].astype(F32)
        made.ref[...] = (wide * lax.rsqrt(jnp.mean(wide * wide, axis=-1, keepdims=True) + EPS) * gain_ref[...]).astype(BF)
        yield

    return Flow([(tokens, pltpu.VMEM), (gain, pltpu.VMEM)], [], [pltpu.VMEM(tokens.shape, BF)], [], steps)


def project_flow(rows, weights, gain, cosine, sine, q_cols, keys, values):
    count, size = rows.shape[0], gain.shape[1]
    half = count // 2

    def steps(ins, outs, scratch):
        rows_hbm, w_hbm, gain_ref, cos_ref, sin_ref = ins
        q_ref, raw_ref = outs
        rows_ref, w_ref, keys.ref, values.ref, local = scratch
        core, _ = peers_of("c")
        own = pl.ds(pl.multiple_of(core * half, half), half)
        other = pl.ds(pl.multiple_of((1 - core) * half, half), half)
        kv = pl.ds(q_cols, 2 * size)
        copies = [
            pltpu.make_async_copy(w_hbm.at[:, kv], w_ref.at[:, kv], local.at[0]),
            pltpu.make_async_copy(rows_hbm.at[own], rows_ref.at[own], local.at[1]),
            pltpu.make_async_copy(w_hbm.at[:, pl.ds(0, q_cols)], w_ref.at[:, pl.ds(0, q_cols)], local.at[2]),
            pltpu.make_async_copy(rows_hbm.at[other], rows_ref.at[other], local.at[3]),
        ]
        for copy in copies:
            copy.start()
        copies[0].wait()
        copies[1].wait()
        product = dot_nn(rows_ref[own, :], w_ref[:, q_cols:])
        raw = product[:, :size]
        raw_ref[...] = raw
        keys.ref[...] = norm_rope(raw, gain_ref[...], cos_ref[own, :], sin_ref[own, :]).astype(BF)
        values.ref[...] = product[:, size:].astype(BF)
        yield
        yield Filler(1.0)
        copies[2].wait()
        copies[3].wait()
        for row in range(0, count, BLOCK):
            q_ref[row : row + BLOCK, :] = dot_nn(rows_ref[row : row + BLOCK, :], w_ref[:, :q_cols])
            yield Filler(1.2)

    return Flow(
        [(rows, pl.ANY), (weights, pl.ANY), (gain, pltpu.VMEM), (cosine, pltpu.VMEM), (sine, pltpu.VMEM)],
        [((count, q_cols), F32, pltpu.VMEM), ((half, size), F32, pltpu.VMEM)],
        [pltpu.VMEM(rows.shape, BF), pltpu.VMEM(weights.shape, BF), pltpu.VMEM((half, size), BF), pltpu.VMEM((half, size), BF), dma(4)],
        [],
        steps,
    )


def route_flow(tokens, gain, weights, chosen, assign, done):
    own, width = tokens.shape
    experts, count = chosen.shape[1], assign.shape[1]

    def steps(ins, outs, scratch):
        tokens_ref, gain_ref, chosen_ref, assign_ref = ins
        residual_ref, mixed_ref, gates_ref, rows_ref = outs
        (pick,) = scratch
        yield
        pick[...] = assign_ref[...].T
        yield done
        residual = tokens_ref[...].astype(F32) + done.ref[...]
        residual_ref[...] = residual
        mixed_ref[...] = (residual * lax.rsqrt(jnp.mean(residual * residual, axis=-1, keepdims=True) + EPS) * gain_ref[...]).astype(BF)
        logits = jnp.where(chosen_ref[...] > 0, dot_nn(mixed_ref[...], weights.ref[:, -experts:]), -1e30)
        powers = jnp.exp(logits - jnp.max(logits, axis=-1, keepdims=True))
        gates = powers / jnp.sum(powers, axis=-1, keepdims=True)
        gates_ref[...] = gates
        for column in range(0, width, 512):
            span = slice(column, column + 512)
            rows_ref[:, span] = dot_nn(pick[...], mixed_ref[:, span]).astype(BF)
        rows_ref[:, width:] = dot_nn(pick[...], gates.astype(BF)).astype(BF)
        yield

    return Flow(
        [(x, pltpu.VMEM) for x in (tokens, gain, chosen, assign)],
        [
            ((own, width), F32, pltpu.VMEM),
            ((own, width), BF, pltpu.VMEM),
            ((own, experts), F32, pltpu.VMEM),
            ((count, width + experts), BF, pltpu.VMEM),
        ],
        [pltpu.VMEM((count, own), BF)],
        [],
        steps,
    )


def mix_back_flow(back, assign, gates, mixed, weights, residual, gain, cotangent, made):
    own, width = mixed.shape
    experts, count = gates.shape[1], back.shape[0]

    def steps(ins, outs, scratch):
        back_hbm, weights_hbm, assign_ref, gates_ref, mixed_ref, residual_ref, gain_ref, cotangent_ref = ins
        residual_grad, gain_grad, router_grad = outs
        back_ref, mixed_grad, made.ref, router_ref, local = scratch
        last = pl.ds(weights_hbm.shape[1] - experts, experts)
        copies = [
            pltpu.make_async_copy(back_hbm, back_ref, local.at[0]),
            pltpu.make_async_copy(weights_hbm.at[:, last], router_ref, local.at[1]),
        ]
        for copy in copies:
            copy.start()
        for copy in copies:
            copy.wait()
        sums = jnp.sum(back_ref[:, width : width + 128].astype(F32), axis=1, keepdims=True)
        shape = (count, experts)
        expert_of = lax.div(lax.broadcasted_iota(jnp.int32, shape, 0), count // experts)
        spread = jnp.where(expert_of == lax.broadcasted_iota(jnp.int32, shape, 1), sums, 0.0)
        high = spread.astype(BF)
        low = (spread - high.astype(F32)).astype(BF)
        gate_grads = dot_nn(assign_ref[...], high) + dot_nn(assign_ref[...], low)
        gates = gates_ref[...]
        logits_grad = (gates * (gate_grads - jnp.sum(gates * gate_grads, axis=1, keepdims=True))).astype(BF)
        for column in range(0, width, 512):
            span = slice(column, column + 512)
            mixed_grad[:, span] = dot_nn(assign_ref[...], back_ref[:, span]) + dot_nt(logits_grad, router_ref[span, :])
        value = residual_ref[...]
        inverse = lax.rsqrt(jnp.mean(value * value, axis=-1, keepdims=True) + EPS)
        unit = value * inverse
        grad = mixed_grad[...]
        gain_grad[...] = jnp.sum(grad * unit, axis=0, keepdims=True)
        scaled = grad * gain_ref[...]
        total = cotangent_ref[...].astype(F32) + inverse * (scaled - unit * jnp.mean(scaled * unit, axis=-1, keepdims=True))
        residual_grad[...] = total
        made.ref[...] = total.astype(BF)
        yield
        yield Filler(1.0)
        router_grad[...] = dot_tn(mixed_ref[...], logits_grad).astype(BF)
        yield

    return Flow(
        [(back, pl.ANY), (weights, pl.ANY)] + [(x, pltpu.VMEM) for x in (assign, gates, mixed, residual, gain, cotangent)],
        [((own, width), F32, pltpu.VMEM), ((1, width), F32, pltpu.VMEM), ((width, experts), BF, pltpu.VMEM)],
        [
            pltpu.VMEM(back.shape, BF),
            pltpu.VMEM((own, width), F32),
            pltpu.VMEM((own, width), BF),
            pltpu.VMEM((width, experts), BF),
            dma(2),
        ],
        [],
        steps,
    )


def key_back_flow(grad_key, grad_value, raw, gain, cosine, sine, units, kv, w_kv, rows, key_gain):
    half, size = raw.shape
    width = units.shape[1]

    def steps(ins, outs, scratch):
        dk_ref, dv_ref, raw_ref, gain_ref, cos_ref, sin_ref, units_hbm = ins
        rows.ref, kv.ref, w_kv.ref, key_gain.ref, local = scratch
        copy = pltpu.make_async_copy(units_hbm, rows.ref, local.at[0])
        copy.start()
        core, _ = peers_of("c")
        own = pl.ds(pl.multiple_of(core * half, half), half)
        grad = dk_ref[...].astype(F32)
        grad_raw, grad_gain = norm_rope_back(grad, raw_ref[...], gain_ref[...], cos_ref[own, :], sin_ref[own, :])
        kv.ref[...] = jnp.zeros(kv.shape, BF)
        kv.ref[own, :size] = grad_raw.astype(BF)
        kv.ref[own, size:] = dv_ref[...]
        key_gain.ref[...] = jnp.sum(grad_gain, axis=0, keepdims=True)
        copy.wait()
        for i in range(16):
            w_kv.ref[i // 4, i % 4] = dot_tn(rows.ref[own, i * width // 16 : (i + 1) * width // 16], kv.ref[own, :]).astype(BF)
        yield

    return Flow(
        [(x, pltpu.VMEM) for x in (grad_key, grad_value, raw, gain, cosine, sine)] + [(units, pl.ANY)],
        [],
        [pltpu.VMEM(rows.shape, BF), pltpu.VMEM(kv.shape, BF), pltpu.VMEM(w_kv.shape, BF), pltpu.VMEM((1, size), F32), dma(1)],
        [],
        steps,
    )


def tokens_grad_flow(tokens, gain, residual_grad, done):
    def steps(ins, outs, scratch):
        tokens_ref, gain_ref, residual_ref = ins
        (out,) = outs
        yield
        yield done
        value = tokens_ref[...].astype(F32)
        inverse = lax.rsqrt(jnp.mean(value * value, axis=-1, keepdims=True) + EPS)
        unit = value * inverse
        scaled = done.ref[...] * gain_ref[...]
        out[...] = residual_ref[...] + inverse * (scaled - unit * jnp.mean(scaled * unit, axis=-1, keepdims=True))
        yield

    return Flow(
        [(x, pltpu.VMEM) for x in (tokens, gain, residual_grad)], [(tokens.shape, F32, pltpu.VMEM)], [], [], steps
    )


def add_up(stacked):
    return jnp.sum(stacked.astype(F32), axis=0)


def dot_nn(a, b):
    return lax.dot_general(a, b, (((1,), (0,)), ((), ())), preferred_element_type=F32)


def dot_nt(a, b):
    return lax.dot_general(a, b, (((1,), (1,)), ((), ())), preferred_element_type=F32)


def dot_tn(a, b):
    return lax.dot_general(a, b, (((0,), (0,)), ((), ())), preferred_element_type=F32)


def norm_rope(raw, gain, cosine, sine):
    unit = raw * lax.rsqrt(jnp.mean(raw * raw, axis=-1, keepdims=True) + EPS)
    scaled = unit * gain
    return scaled * cosine + pltpu.roll(scaled, 64, 1) * sine


def norm_rope_back(grad, raw, gain, cosine, sine):
    inverse = lax.rsqrt(jnp.mean(raw * raw, axis=-1, keepdims=True) + EPS)
    unit = raw * inverse
    turned = grad * cosine + pltpu.roll(grad * sine, 64, 1)
    scaled = turned * gain
    return inverse * (scaled - unit * jnp.mean(scaled * unit, axis=-1, keepdims=True)), turned * unit


def expert_kernel(rows_ref, plain_ref, w_ref, back_ref, hidden_ref, gated_ref, both_ref):
    width, ff = w_ref.shape[0], plain_ref.shape[1]
    own = lax.axis_index("head") * lax.axis_size("blk") + lax.axis_index("blk")
    gates = rows_ref[:, width:].astype(F32)
    lane = lax.broadcasted_iota(jnp.int32, gates.shape, 1)
    gate = jnp.sum(jnp.where(lane == own, gates, 0.0), axis=1, keepdims=True)
    gate_up = dot_nn(rows_ref[:, :width], w_ref[...])
    first, up = gate_up[:, :ff], gate_up[:, ff:]
    sigma = 1.0 / (1.0 + jnp.exp(-first))
    silu = first * sigma
    hidden = silu * up
    hidden_ref[...] = hidden.astype(BF)
    gated_ref[...] = (hidden * gate).astype(BF)
    plain = plain_ref[...]
    gate_grad = jnp.sum(hidden * plain, axis=1, keepdims=True)
    grad = plain * gate
    both_ref[:, :ff] = (grad * up * (sigma * (1.0 + first * (1.0 - sigma)))).astype(BF)
    both_ref[:, ff:] = (grad * silu).astype(BF)
    back_ref[:, :width] = dot_nt(both_ref[...], w_ref[...]).astype(BF)
    high = gate_grad.astype(BF).astype(F32)
    back_ref[:, width:] = jnp.where(lane == 0, high, jnp.where(lane == 1, gate_grad - high, 0.0)).astype(BF)


def key_tiles(lo, full, last, tiles):
    middle = jnp.minimum(full, last)
    twos, fours = lax.div(middle - lo, 2), lax.div(last - middle, 4)
    rest = middle + 4 * fours
    pl.loop(0, twos)(lambda i: tiles([lo + 2 * i, lo + 2 * i + 1], True))
    pl.loop(lo + 2 * twos, middle)(lambda t: tiles([t], True))
    pl.loop(0, fours)(lambda i: tiles([middle + 4 * i + n for n in range(4)], False))
    for count in range(1, 5):
        pl.when(last - rest == count - 1)(lambda count=count: tiles([rest + n for n in range(count)], True))


def stacked(ref, slots):
    return ref[slots[0]] if len(slots) == 1 else jnp.concatenate([ref[slot] for slot in slots], axis=0)


def allowed_pairs(t, last, start, shape):
    key_place = t * BLOCK + lax.broadcasted_iota(jnp.int32, shape, 0)
    query_place = last * BLOCK + lax.rem(lax.broadcasted_iota(jnp.int32, shape, 1), BLOCK)
    return (key_place >= start) & (key_place <= query_place)


def attend_forward_kernel(
    lo_ref, full_ref, last_ref, slot_ref, raw_ref, gain_ref, cos_ref, sin_ref, k_ref, v_ref, start_ref, q_ref, o_ref, log_ref, q_t, acc, total
):
    j = pl.program_id(0)
    size = k_ref.shape[2]
    heads = raw_ref.shape[1] // size
    scale = size**-0.5 * LOG2E
    last = last_ref[j]
    for n in range(heads):
        span = slice(n * size, (n + 1) * size)
        query = norm_rope(raw_ref[:, span], gain_ref[...], cos_ref[...], sin_ref[...])
        q_ref[:, span] = query.astype(BF)
        q_t[:, n * BLOCK : (n + 1) * BLOCK] = query.T.astype(BF)
    acc[...] = jnp.zeros_like(acc)
    total[...] = jnp.zeros_like(total)
    start = start_ref[0]

    def tiles(at, masked):
        slots = [slot_ref[t] for t in at]
        weights = jnp.exp2(dot_nn(stacked(k_ref, slots), q_t[...]) * scale)
        if masked:
            weights = jnp.where(allowed_pairs(at[0], last, start, weights.shape), weights, 0.0)
        total[...] += jnp.sum(weights.reshape(-1, 8, heads * BLOCK), axis=0)
        acc[...] += dot_nn(stacked(v_ref, slots).T, weights.astype(BF))

    key_tiles(lo_ref[j], full_ref[j], last, tiles)
    row = jnp.sum(total[...], axis=0, keepdims=True)
    log_ref[0] = jnp.log2(row)
    out = acc[...] / row
    for n in range(heads):
        o_ref[:, n * size : (n + 1) * size] = out[:, n * BLOCK : (n + 1) * BLOCK].T.astype(BF)


def attend_backward_kernel(
    lo_ref,
    full_ref,
    last_ref,
    slot_ref,
    block_ref,
    raw_ref,
    gain_ref,
    cos_ref,
    sin_ref,
    k_ref,
    v_ref,
    start_ref,
    q_ref,
    o_ref,
    g_ref,
    w_ref,
    log_ref,
    dq_ref,
    sum_ref,
    dk_ref,
    dv_ref,
    queries,
    q_t,
    grads,
    g_t,
    delta,
    acc,
    dk,
    dv,
    keys_ref,
    values_ref,
    local,
):
    j = pl.program_id(0)
    slots, _, size = keys_ref.shape

    def seen(s):
        block = block_ref[s]
        found = (block >= lo_ref[0]) & (block <= last_ref[0])
        for i in range(1, lo_ref.shape[0]):
            found |= (block >= lo_ref[i]) & (block <= last_ref[i])
        return found

    takes = [pltpu.make_async_copy(k_ref, keys_ref, local.at[0]), pltpu.make_async_copy(v_ref, values_ref, local.at[1])]
    heads = raw_ref.shape[1] // size
    scale = size**-0.5
    last = last_ref[j]

    @pl.when(j == 0)
    def _():
        for copy in takes:
            copy.start()
        sum_ref[...] = jnp.zeros_like(sum_ref)

        @pl.loop(0, slots)
        def _(s):
            @pl.when(seen(s))
            def _():
                dk[s] = jnp.zeros(dk.shape[1:], F32)
                dv[s] = jnp.zeros(dv.shape[1:], F32)

    attended_grad = dot_nn(g_ref[...], w_ref[...]).astype(BF)
    for n in range(heads):
        span, rows = slice(n * size, (n + 1) * size), slice(n * BLOCK, (n + 1) * BLOCK)
        queries[rows, :] = q_ref[:, span]
        q_t[:, rows] = q_ref[:, span].T
        grads[rows, :] = attended_grad[:, span]
        grad_t = attended_grad[:, span].T
        g_t[:, rows] = grad_t
        delta[:, rows] = jnp.sum(grad_t.astype(F32) * o_ref[:, span].T.astype(F32), axis=0, keepdims=True)
    acc[...] = jnp.zeros_like(acc)
    start = start_ref[0]
    logs = log_ref[0]

    @pl.when(j == 0)
    def _():
        for copy in takes:
            copy.wait()

    def tiles(at, masked):
        slots = [slot_ref[t] for t in at]
        keys = stacked(keys_ref, slots)
        probs = jnp.exp2(dot_nn(keys, q_t[...]) * (scale * LOG2E) - logs)
        if masked:
            probs = jnp.where(allowed_pairs(at[0], last, start, probs.shape), probs, 0.0)
        grad_scores = (probs * (dot_nn(stacked(values_ref, slots), g_t[...]) - delta[...])).astype(BF)
        values_part, keys_part = dot_nn(probs.astype(BF), grads[...]), dot_nn(grad_scores, queries[...])
        for n, slot in enumerate(slots):
            dv[slot] += values_part[n * BLOCK : (n + 1) * BLOCK]
            dk[slot] += keys_part[n * BLOCK : (n + 1) * BLOCK]
        acc[...] += dot_nn(keys.T, grad_scores)

    key_tiles(lo_ref[j], full_ref[j], last, tiles)
    for n in range(heads):
        span = slice(n * size, (n + 1) * size)
        grad = (acc[:, n * BLOCK : (n + 1) * BLOCK] * scale).T.astype(BF).astype(F32)
        grad_raw, grad_gain = norm_rope_back(grad, raw_ref[:, span], gain_ref[...], cos_ref[...], sin_ref[...])
        dq_ref[:, span] = grad_raw.astype(BF)
        sum_ref[...] += jnp.sum(grad_gain, axis=0, keepdims=True)

    @pl.when(j == pl.num_programs(0) - 1)
    def _():
        def out(s, n):
            span = pl.ds(s, n)
            return (
                pltpu.make_async_copy(keys_ref.at[span], dk_ref.at[span], local.at[0]),
                pltpu.make_async_copy(values_ref.at[span], dv_ref.at[span], local.at[1]),
            )

        @pl.loop(0, slots, step=8)
        def _(s):
            @pl.loop(s, s + 8)
            def _(i):
                @pl.when(seen(i))
                def _():
                    keys_ref[i] = (dk[i] * scale).astype(BF)
                    values_ref[i] = dv[i].astype(BF)

                @pl.when(jnp.logical_not(seen(i)))
                def _():
                    keys_ref[i] = jnp.zeros(keys_ref.shape[1:], BF)
                    values_ref[i] = jnp.zeros(values_ref.shape[1:], BF)

            for copy in out(s, 8):
                copy.start()

        for copy in out(0, slots):
            copy.wait()


def by_rows(array, rows=BLOCK):
    return pl.BlockSpec((rows,) + array.shape[1:], lambda j, *_: (j,) + (0,) * (array.ndim - 1))


def resident(array):
    return pl.BlockSpec(array.shape, lambda j, *_: (0,) * array.ndim, pipeline_mode=pl.Buffered(1))


def shaped(shape, dtype):
    return jax.ShapeDtypeStruct(shape, dtype)


def expert(rows, plain, weights, block=512):
    count, ff = plain.shape
    outs = (shaped(rows.shape, BF), shaped((count, ff), BF), shaped((count, ff), BF), shaped((count, 2 * ff), BF))
    return pl.pallas_call(
        expert_kernel,
        out_shape=outs,
        grid=(count // block,),
        in_specs=[by_rows(rows, block), by_rows(plain, block), resident(weights)],
        out_specs=tuple(by_rows(x, block) for x in outs),
        compiler_params=pltpu.CompilerParams(vmem_limit_bytes=VMEM_LIMIT),
        cost_estimate=cost_of(20),
        name="expert",
    )(rows, plain, weights)


def attend_forward(meta, raw, gain, cosine, sine, keys, values, start):
    rows, wide = raw.shape
    blocks, size = rows // BLOCK, keys.shape[2]
    lanes = wide // size * BLOCK
    outs = (shaped((rows, wide), BF), shaped((rows, wide), BF), shaped((blocks, 1, lanes), F32))
    return pl.pallas_call(
        attend_forward_kernel,
        out_shape=outs,
        grid_spec=pltpu.PrefetchScalarGridSpec(
            num_scalar_prefetch=4,
            grid=(blocks,),
            in_specs=[
                by_rows(raw),
                resident(gain),
                by_rows(cosine),
                by_rows(sine),
                resident(keys),
                resident(values),
                by_rows(start, 1),
            ],
            out_specs=(by_rows(outs[0]), by_rows(outs[1]), by_rows(outs[2], 1)),
            scratch_shapes=[pltpu.VMEM((size, lanes), BF), pltpu.VMEM((size, lanes), F32), pltpu.VMEM((8, lanes), F32)],
        ),
        compiler_params=pltpu.CompilerParams(vmem_limit_bytes=VMEM_LIMIT),
        cost_estimate=cost_of(30),
        name="attend",
    )(*meta, raw, gain, cosine, sine, keys, values, start)


def attend_backward(meta, raw, gain, cosine, sine, keys, values, start, queries, attended, grads, w_out_t, logs):
    rows, wide = raw.shape
    blocks, size = rows // BLOCK, keys.shape[2]
    lanes = wide // size * BLOCK
    outs = (shaped((rows, wide), BF), shaped((1, size), F32), shaped(keys.shape, BF), shaped(values.shape, BF))
    return pl.pallas_call(
        attend_backward_kernel,
        out_shape=outs,
        grid_spec=pltpu.PrefetchScalarGridSpec(
            num_scalar_prefetch=5,
            grid=(blocks,),
            in_specs=[
                by_rows(raw),
                resident(gain),
                by_rows(cosine),
                by_rows(sine),
                pl.BlockSpec(memory_space=pl.ANY),
                pl.BlockSpec(memory_space=pl.ANY),
                by_rows(start, 1),
                by_rows(queries),
                by_rows(attended),
                by_rows(grads),
                pl.BlockSpec((w_out_t.shape[0], wide), lambda j, *_: (0, 0), pipeline_mode=pl.Buffered(1)),
                by_rows(logs, 1),
            ],
            out_specs=(by_rows(outs[0]), resident(outs[1])) + (pl.BlockSpec(memory_space=pl.ANY),) * 2,
            scratch_shapes=[
                pltpu.VMEM((lanes, size), BF),
                pltpu.VMEM((size, lanes), BF),
                pltpu.VMEM((lanes, size), BF),
                pltpu.VMEM((size, lanes), BF),
                pltpu.VMEM((1, lanes), F32),
                pltpu.VMEM((size, lanes), F32),
                pltpu.VMEM(keys.shape, F32),
                pltpu.VMEM(values.shape, F32),
                pltpu.VMEM(keys.shape, BF),
                pltpu.VMEM(values.shape, BF),
                dma(2),
            ],
        ),
        compiler_params=pltpu.CompilerParams(vmem_limit_bytes=VMEM_LIMIT),
        cost_estimate=cost_of(40),
        name="attend_back",
    )(*meta, raw, gain, cosine, sine, keys, values, start, queries, attended, grads, w_out_t, logs)


def all_to_all(stacked):
    return lax.all_to_all(stacked, ("head", "blk"), split_axis=0, concat_axis=0, tiled=True)


def body(
    tokens,
    norm_gain,
    w_query,
    key_weight,
    value_weight,
    query_gain,
    key_gain,
    w_out,
    mix_gain,
    w_router,
    expert_gate_up,
    expert_down,
    lengths,
    block_deal,
    routes,
    cotangent,
):
    own, width = tokens.shape
    size = query_gain.shape[0]
    scale = size ** (-0.5)
    blk = lax.axis_index("blk")
    plane, core = blk // 4, blk % 2
    devices = lax.axis_size("head") * lax.axis_size("blk")
    experts = w_router.shape[0] * 2
    cap = own * routes.shape[1] // experts
    gate_up, down = expert_gate_up[0], expert_down[0]
    ff = down.shape[0]
    group_rows = 8 * own
    q_cols = w_query.shape[1] // 4
    heads = q_cols // size

    group_blocks = plane * 4 + jnp.array([0, 2, 1, 3], jnp.int32)
    ids = jnp.arange(block_deal.shape[0], dtype=jnp.int32)
    last = jnp.sum(jnp.where(group_blocks[:, None] == ids[None, :], block_deal[None, :], 0), axis=1)
    slots = (ids % 2) * (ids.shape[0] // 2) + (ids // 4) * 2 + (ids % 4) // 2
    slot_of = jnp.sum(jnp.where(block_deal[None, :] == ids[:, None], slots[None, :], 0), axis=1)
    place = (last[:, None] * BLOCK + jnp.arange(BLOCK, dtype=jnp.int32)[None, :]).reshape(-1)
    passed = place[:, None] >= jnp.cumsum(lengths)[None, :]
    start = jnp.sum(jnp.where(passed, lengths[None, :], 0), axis=1)
    start_rows = start.reshape(-1, 1, BLOCK)
    meta = (start_rows[:, 0, 0] // BLOCK, (start_rows[:, 0, BLOCK - 1] + BLOCK - 1) // BLOCK, last, slot_of)
    start_rows = jnp.tile(start_rows, (1, 1, heads))
    offsets = (place - start).astype(F32).reshape(-1, 1, BLOCK)
    spacing = ROPE_BASE ** (-2.0 * jnp.arange(size // 2, dtype=F32) / size)
    spacing = jnp.concatenate([spacing, spacing])[None]

    normed = Made(own, width)
    depth = w_query.shape[0]
    out_pack = w_out.reshape(4, q_cols, depth).transpose(2, 0, 1).reshape(depth, -1)
    side = lax.axis_index("head") == jnp.arange(2, dtype=jnp.int32)
    router_pack = jnp.where(side[None, :, None], w_router.T[:, None, :], 0).astype(BF).reshape(depth, experts)
    w_qkv, out_part, router_part, group_tokens, assign_low, chosen, cosine, sine = launch(
        [
            norm_flow(tokens, norm_gain[None], normed),
            plane_gather_flow([(w_query, q_cols, 1), (key_weight, size, 2), (value_weight, size, 2)], "x", "y", ahead="zhc"),
            ring_exchange_flow(out_pack, q_cols, "zhc"),
            ring_exchange_flow(router_pack, experts, "z"),
            ring_gather_flow(normed),
            tables_flow(routes, offsets, spacing, experts, cap),
        ],
        0,
        45,
    )
    normed_group = group_tokens.reshape(group_rows, width)
    w_qkv = w_qkv.reshape(width, -1)
    router_part = jnp.sum(router_part.reshape(4, 2, depth, experts), axis=1)
    w_rest = jnp.concatenate([out_part, router_part], axis=2).reshape(4 * depth, -1)
    planes = [[j * 4 + r for j in range(16)] for r in range(4)]
    w_rest = lax.all_gather(w_rest, "blk", axis_index_groups=planes, axis=0, tiled=True)

    q_gain, k_gain = query_gain[None], key_gain[None]
    key, value = Made(group_rows // 2, size), Made(group_rows // 2, size)
    q_raw, k_raw, keys, values, grad_rows = launch(
        [
            project_flow(normed_group, w_qkv, k_gain, cosine, sine, q_cols, key, value),
            plane_gather_flow(key, "x", "y"),
            plane_gather_flow(value, "y", "x"),
            product_flow(assign_low, cotangent),
        ],
        1,
        35,
    )
    grad_rows = all_to_all(grad_rows.reshape(devices, cap, width)).reshape(-1, width)
    keys, values = keys.reshape(-1, BLOCK, size), values.reshape(-1, BLOCK, size)
    queries, attended, logs = attend_forward(meta, q_raw, q_gain, cosine, sine, keys, values, start_rows)

    attention, weights_kept = Made(own, width), Made()
    residual, mixed, gates, outgoing = launch(
        [
            product_scatter_flow([attended], w_rest, attention, kept=weights_kept),
            route_flow(tokens, mix_gain[None], weights_kept, chosen, assign_low, attention),
        ],
        2,
        30,
    )
    outgoing, grad_rows = lax.optimization_barrier((outgoing, grad_rows))
    arrived = all_to_all(outgoing.reshape(devices, cap, -1)).reshape(experts * cap, -1)

    plain_grad = lax.optimization_barrier(dot_nt(grad_rows, down))
    rows, plain_grad = lax.optimization_barrier((arrived, plain_grad))
    back, hidden, gated, grad_both = expert(rows, plain_grad, gate_up)
    back = all_to_all(back.reshape(devices, cap, -1)).reshape(experts * cap, -1)
    back, expert_out = lax.optimization_barrier((back, dot_nn(hidden, down).astype(BF)))
    grad_down = dot_tn(gated, grad_rows)
    grad_gate_up = dot_tn(rows[:, :width], grad_both)

    grad_attention = Made(own, width)
    grad_residual, grad_mix_gain, grad_router_t, grad_group = launch(
        [
            mix_back_flow(back, assign_low, gates, mixed, w_rest, residual, mix_gain[None], cotangent, grad_attention),
            ring_gather_flow(grad_attention),
        ],
        3,
        25,
    )
    grad_group = grad_group.reshape(group_rows, width)
    grad_group, expert_out = lax.optimization_barrier((grad_group, expert_out))
    expert_out = all_to_all(expert_out.reshape(devices, cap, width)).reshape(-1, width)
    block_of = block_deal.reshape(-1, 2, 2).transpose(2, 0, 1).reshape(-1)
    grad_q, grad_query_gain, grad_keys, grad_values = attend_backward(
        (*meta, block_of), q_raw, q_gain, cosine, sine, keys, values, start_rows, queries, attended, grad_group, w_rest, logs
    )

    split = (2, 4, 4, group_rows // 2, size)
    grad_key, grad_value, grad_wq, grad_wo = launch(
        [
            plane_scatter_flow(grad_keys.reshape(split), "y", "x", from_core=True),
            plane_scatter_flow(grad_values.reshape(split), "x", "y", from_core=True),
            product_flow(normed_group, grad_q),
            product_flow(grad_group, attended),
        ],
        4,
        35,
    )

    grad_key, expert_out = lax.optimization_barrier((grad_key, expert_out))
    plane_split = (4, 4, 4 * depth, -1)
    zeros, ones = jnp.zeros((width,), F32), jnp.ones((width,), F32)
    gains = jnp.concatenate([zeros, grad_mix_gain[0], grad_query_gain[0], zeros[: 7 * size], norm_gain, ones, ones[: 8 * size]])
    units, grad_kv, grad_wkv, key_gain_sum = Made(group_rows, width), Made(group_rows, 2 * size), Made(4, 4, 4 * depth, 2 * size), Made()
    grad_normed = Made(own, width)
    grad_wq, grad_wo, gains, grad_wkv, grad_wr, output, grad_tokens = launch(
        [
            key_back_flow(grad_key, grad_value, k_raw, k_gain, cosine, sine, normed_group, grad_kv, grad_wkv, units, key_gain_sum),
            plane_scatter_flow(grad_wq.reshape(plane_split), "y", "x", last_in="zhc"),
            plane_scatter_flow(grad_wo.reshape(plane_split), "x", "y", last_in="zhc"),
            product_scatter_flow([grad_q, grad_kv], w_qkv, grad_normed, units, gains.reshape(2, -1, size), key_gain_sum),
            plane_scatter_flow(grad_wkv, "y", "x", last_in="zhc"),
            plane_scatter_flow(grad_router_t.reshape(plane_split), "x", "y", last_in="z"),
            output_flow(residual, gates, assign_low, expert_out),
            tokens_grad_flow(tokens, norm_gain[None], grad_residual, grad_normed),
        ],
        5,
        50,
    )
    gains = gains.reshape(-1)
    grad_w_query = grad_wq.astype(F32).transpose(1, 0, 2).reshape(depth, -1)
    grad_kv_w = jnp.sum(grad_wkv.astype(F32).reshape(2, 2, depth, 2, size), axis=1)
    grad_w_key = grad_kv_w[:, :, 0].transpose(1, 0, 2).reshape(depth, -1)
    grad_w_value = grad_kv_w[:, :, 1].transpose(1, 0, 2).reshape(depth, -1)
    grad_w_out = grad_wo.astype(F32).transpose(0, 2, 1).reshape(-1, depth)
    grad_w_router = lax.dynamic_slice_in_dim(add_up(grad_wr), lax.axis_index("head") * (experts // 2), experts // 2, 1).T
    return (
        output,
        grad_tokens,
        gains[:width],
        grad_w_query,
        grad_w_key,
        grad_w_value,
        gains[2 * width : 2 * width + size],
        gains[2 * width + size : 2 * width + 2 * size],
        grad_w_out,
        gains[width : 2 * width],
        grad_w_router,
        grad_gate_up[None],
        grad_down[None],
    )


def solution(mesh):
    rows, both = P(("head", "blk"), None), P("blk", "head")
    expert, turned = P(("head", "blk"), None, None), P("head", "blk")
    in_specs = (rows, P(), both, both, both, P(), P(), turned, P(), turned, expert, expert, P(), P(), rows, rows)
    out_specs = (rows, rows, P(), both, both, both, P(), P(), turned, P(), turned, expert, expert)
    return jax.shard_map(body, mesh=mesh, in_specs=in_specs, out_specs=out_specs, check_vma=False)
```

```python
import math

import jax
import jax.numpy as jnp
from jax import lax
from jax.experimental import pallas as pl
from jax.experimental.pallas import tpu as pltpu
from jax.sharding import PartitionSpec as P

MESH = pl.DeviceIdType.MESH
EPS = 1e-06
ROPE_BASE = 1000000.0
LOG2E = 1.4426950408889634
BF = jnp.bfloat16
F32 = jnp.float32
BLOCK = 256
VMEM_LIMIT = 60 << 20
SIZES = {"zc": 4, "c": 2, "x": 4, "y": 4, "zhc": 4, "z": 8, "yx": 16}


def peers_of(kind):
    h = lax.axis_index("head")
    b = lax.axis_index("blk")
    q, r = lax.div(b, 4), lax.rem(b, 4)
    if kind == "zc":
        return lax.div(r, 2) * 2 + h, lambda g: (lax.rem(g, 2), q * 4 + lax.div(g, 2) * 2 + lax.rem(r, 2))
    if kind == "z":
        return r * 2 + h, lambda g: (lax.rem(g, 2), q * 4 + lax.div(g, 2))
    if kind == "c":
        return lax.rem(b, 2), lambda g: (h, b - lax.rem(b, 2) + g)
    if kind == "x":
        return lax.rem(q, 4), lambda g: (h, (lax.div(q, 4) * 4 + g) * 4 + r)
    if kind == "y":
        return lax.div(q, 4), lambda g: (h, (g * 4 + lax.rem(q, 4)) * 4 + r)
    if kind == "yx":
        return q, lambda g: (h, g * 4 + r)
    return r, lambda g: (h, q * 4 + g)


def cost_of(microseconds):
    return pl.CostEstimate(flops=microseconds * 10**9, bytes_accessed=microseconds * 3 * 10**6, transcendentals=0)


class Flow:
    def __init__(self, inputs, outputs, scratch, partners, steps):
        self.inputs, self.outputs, self.scratch = inputs, outputs, scratch
        self.partners, self.steps = partners, steps


class Filler:
    def __init__(self, cost):
        self.cost = cost


class Clock:
    now = 0.0


def in_turn(flows):
    Clock.now = 0.0
    ready, waiting, fillers = [(0.0, i, steps) for i, steps in enumerate(flows)], [], []
    count = len(flows)
    while ready or fillers or waiting:
        for entry in [e for e in waiting if e[0].ref is not None]:
            waiting.remove(entry)
            ready.append((Clock.now, entry[1], entry[2]))
        ready.sort(key=lambda e: e[:2])
        if fillers and (not ready or ready[0][0] > Clock.now + 0.5):
            cost, order, steps = fillers.pop(0)
            Clock.now += cost
        else:
            when, order, steps = ready.pop(0)
            Clock.now = max(Clock.now, when) + 0.3
        result = next(steps, steps)
        if result is steps:
            continue
        if isinstance(result, Filler):
            fillers.append((result.cost, order, steps))
        elif isinstance(result, Made):
            waiting.append((result, order, steps))
        elif result is None or isinstance(result, float):
            ready.append((Clock.now if result is None else result, order, steps))
        else:
            ready += [(Clock.now, order, steps), (Clock.now, count, result)]
            count += 1


class Made:
    def __init__(self, *shape):
        self.shape, self.ref = shape, None


HOP = 3.0
RATE = 40e3
CORE_RATE = 200e3


def launch(flows, cid, cost):
    partners = sorted({p for flow in flows for p in flow.partners})

    def kernel(*refs):
        n_in, n_out = sum(len(f.inputs) for f in flows), sum(len(f.outputs) for f in flows)
        ins, outs, rest = list(refs[:n_in]), list(refs[n_in : n_in + n_out]), list(refs[n_in + n_out :])
        barrier = pltpu.get_barrier_semaphore()
        for kind, distance in partners:
            me, member = peers_of(kind)
            to = member(lax.rem(me + distance, SIZES[kind]))
            pl.semaphore_signal(barrier, inc=1, device_id=to, device_id_type=MESH)
        running = []
        for flow in flows:
            own = [[group.pop(0) for _ in part] for group, part in ((ins, flow.inputs), (outs, flow.outputs), (rest, flow.scratch))]
            running.append(flow.steps(*own))
            next(running[-1])
        pl.semaphore_wait(barrier, len(partners))
        in_turn(running)

    return pl.pallas_call(
        kernel,
        out_shape=tuple(jax.ShapeDtypeStruct(s, d) for f in flows for s, d, _ in f.outputs),
        in_specs=[pl.BlockSpec(memory_space=space) for f in flows for _, space in f.inputs],
        out_specs=tuple(pl.BlockSpec(memory_space=space) for f in flows for _, _, space in f.outputs),
        scratch_shapes=[x for f in flows for x in f.scratch],
        compiler_params=pltpu.CompilerParams(collective_id=cid, has_side_effects=True, vmem_limit_bytes=VMEM_LIMIT),
        cost_estimate=cost_of(cost),
        name=f"links_{cid}",
    )(*[x for f in flows for x, _ in f.inputs])


def remote(src, dst, send, recv, device):
    return pltpu.make_async_remote_copy(
        src_ref=src, dst_ref=dst, send_sem=send, recv_sem=recv, device_id=device, device_id_type=MESH
    )


def piece(ref, which):
    rows = ref.shape[0] // 2
    return ref.at[pl.ds(which * rows, rows)]


def ring_partners(kind):
    return [(kind, 1), (kind, 3)]


class RingGather:
    def __init__(self, kind, slot, src, send, recv):
        me, member = peers_of(kind)
        up, down = lax.rem(me + 1, 4), lax.rem(me + 3, 4)

        def copy(source, target, i, to):
            return remote(source, target, send.at[i], recv.at[i], member(to))

        mine = slot(me)
        self.copies = [
            copy(piece(src, 0), piece(mine, 0), 0, up),
            copy(piece(src, 1), piece(mine, 1), 1, up),
            copy(piece(src, 1), piece(mine, 1), 2, down),
            copy(piece(src, 0), piece(mine, 0), 3, down),
            copy(piece(slot(down), 0), piece(slot(down), 0), 4, up),
            copy(piece(slot(up), 1), piece(slot(up), 1), 5, down),
        ]

    def start(self):
        for i in (0, 2, 1, 3):
            self.copies[i].start()

    def forward(self):
        self.copies[0].wait_recv()
        self.copies[4].start()
        self.copies[2].wait_recv()
        self.copies[5].start()

    def near(self):
        self.copies[1].wait_recv()
        self.copies[3].wait_recv()

    def far(self):
        self.copies[4].wait_recv()
        self.copies[5].wait_recv()

    def sent(self):
        for copy in self.copies:
            copy.wait_send()


class RingScatter:
    def __init__(self, kind, chunk, bufs, send, recv, raw=None):
        raw = raw or chunk
        self.me, member = peers_of(kind)
        self.up, self.down, self.far = (lax.rem(self.me + k, 4) for k in (1, 3, 2))
        self.chunk, self.bufs = chunk, bufs

        def copy(source, target, i, to):
            return remote(source, bufs.at[target], send.at[i], recv.at[i], member(to))

        self.copies = [
            copy(piece(raw(self.far), 0), 0, 0, self.up),
            copy(piece(raw(self.far), 1), 1, 1, self.down),
            copy(piece(raw(self.up), 1), 2, 2, self.up),
            copy(piece(raw(self.down), 0), 3, 3, self.down),
            copy(bufs.at[6], 4, 4, self.up),
            copy(bufs.at[7], 5, 5, self.down),
        ]

    def start_far(self):
        self.copies[0].start()
        self.copies[1].start()

    def start_up(self):
        self.copies[2].start()

    def start_down(self):
        self.copies[3].start()

    def add(self):
        self.copies[0].wait_recv()
        self.bufs[6] = (piece(self.chunk(self.up), 0)[...].astype(F32) + self.bufs[0].astype(F32)).astype(BF)
        self.copies[4].start()
        self.copies[1].wait_recv()
        self.bufs[7] = (piece(self.chunk(self.down), 1)[...].astype(F32) + self.bufs[1].astype(F32)).astype(BF)
        self.copies[5].start()

    def total(self, which):
        first, second = ((4, 3), (2, 5))[which]
        self.copies[first].wait_recv()
        self.copies[second].wait_recv()
        return self.bufs[first].astype(F32) + self.bufs[second].astype(F32)

    def sent(self):
        for copy in self.copies:
            copy.wait_send()


def dma(*shape):
    return pltpu.SemaphoreType.DMA(shape)


def ring_gather_flow(made):
    shape = (2, 4) + made.shape

    def steps(ins, outs, scratch):
        (out,), src = outs, made.ref
        send, recv, pass_send, pass_recv, local = scratch
        yield
        me, _ = peers_of("zc")
        core, member = peers_of("c")
        ring = RingGather("zc", lambda g: out.at[core, g], src, send, recv)

        def passing(k):
            g = lax.rem(me + k, 4)
            return remote(src if k == 0 else out.at[core, g], out.at[core, g], pass_send.at[k], pass_recv.at[k], member(1 - core))

        passes = [passing(k) for k in range(4)]
        unit = math.prod(made.shape) * 2 / RATE
        begun = Clock.now
        ring.start()
        passes[0].start()
        yield begun + HOP + unit / 2
        ring.forward()
        back = pltpu.make_async_copy(src, out.at[core, me], local.at[0])
        back.start()
        yield begun + HOP + unit
        ring.near()
        passes[1].start()
        passes[3].start()
        yield begun + 2 * HOP + 1.5 * unit
        ring.far()
        passes[2].start()
        yield Clock.now + HOP + 2.0
        back.wait()
        ring.sent()
        for copy in passes:
            copy.wait()

    return Flow(
        [],
        [(shape, BF, pl.ANY)],
        [dma(6), dma(6), dma(4), dma(4), dma(1)],
        ring_partners("zc") + [("c", 1)],
        steps,
    )


def plane_gather_flow(arrays, first, second, ahead=None, beside=None):
    to_core = ahead is None
    if ahead == "zhc":
        shard = (4, arrays[0][0].shape[0], sum(columns for _, columns, _ in arrays) + (beside.shape[-1] if beside else 0))
    elif ahead == "z":
        shard = (8,) + arrays[0][0].shape
    else:
        shard = arrays.shape
    shape = ((2,) if to_core else ()) + (4, 4) + shard
    n_ahead = SIZES[ahead] if ahead else 1

    def steps(ins, outs, scratch):
        (out,) = outs
        stage, send, recv, pass_send, pass_recv, local, ahead_send, ahead_recv = scratch
        core, member = peers_of("c")
        here, _ = peers_of(first)
        there, _ = peers_of(second)
        view = out.at[core] if to_core else out

        def slot(a, b):
            return view.at[b, a] if first == "x" else view.at[a, b]

        if ahead:
            mine, at = peers_of(ahead)

            def parts(to):
                if ahead == "z":
                    return [(ins[0], stage.at[mine])]
                found, begin = [], 0
                for ref, (_, columns, share) in zip(ins, arrays):
                    source = ref.at[:, pl.ds(pl.multiple_of(lax.div(to, share) * columns, columns), columns)]
                    found.append((source, stage.at[mine, :, pl.ds(begin, columns)]))
                    begin += columns
                return found

            early = [pltpu.make_async_copy(source, target, local.at[i]) for i, (source, target) in enumerate(parts(mine))]
            for k in range(1, n_ahead):
                to = lax.rem(mine + k, n_ahead)
                for i, (source, target) in enumerate(parts(to)):
                    early.append(remote(source, target, ahead_send.at[i, k], ahead_recv.at[i, k], at(to)))
            local_parts = len(parts(mine))
            for copy in early[:local_parts]:
                copy.start()
            yield
            for copy in early[local_parts:]:
                copy.start()
            yield Clock.now + HOP + 7.0
            for copy in early:
                copy.wait()
            if beside:
                yield beside
                for g in range(4):
                    pair = beside.ref[2 * g].astype(F32) + beside.ref[2 * g + 1].astype(F32)
                    stage[g, :, shard[2] - beside.shape[-1] :] = pair.astype(BF)
            src = stage
        else:
            src = arrays.ref
            yield
        ring = RingGather(first, lambda g: slot(g, there), src, send.at[4], recv.at[4])
        columns = [lax.rem(here + k, 4) for k in range(4)]
        rings = [
            RingGather(second, lambda g, a=a: slot(a, g), src if k == 0 else slot(a, there), send.at[k], recv.at[k])
            for k, a in enumerate(columns)
        ]

        def passing(k, m):
            ref = slot(columns[k], lax.rem(there + m, 4))
            return remote(src if k == m == 0 else ref, ref, pass_send.at[k * 4 + m], pass_recv.at[k * 4 + m], member(1 - core))

        passes = {}

        def hand_over(k, m):
            if to_core:
                passes[k, m] = passing(k, m)
                passes[k, m].start()

        unit = math.prod(shard) * 2 / RATE
        begun = Clock.now
        ring.start()
        rings[0].start()
        hand_over(0, 0)
        yield begun + HOP + unit / 2
        ring.forward()
        back = pltpu.make_async_copy(src, slot(here, there), local.at[0])
        back.start()
        yield
        rings[0].forward()
        yield begun + HOP + unit
        ring.near()
        for k in (1, 3):
            rings[k].start()
            hand_over(k, 0)
        yield begun + 2 * HOP + 1.5 * unit
        ring.far()
        rings[2].start()
        hand_over(2, 0)
        yield
        for i, k in enumerate((0, 1, 3, 2)):
            if k > 0:
                yield begun + 2 * HOP + (1.5 * i + 0.5) * unit
                rings[k].forward()
            yield begun + 2 * HOP + (1.5 * i + 1.0) * unit
            rings[k].near()
            hand_over(k, 1)
            hand_over(k, 3)
        for i, k in enumerate((0, 1, 3, 2)):
            yield begun + 3 * HOP + (1.5 * i + 1.5) * unit
            rings[k].far()
            hand_over(k, 2)
        yield Clock.now + HOP
        back.wait()
        ring.sent()
        for one in rings:
            one.sent()
        for copy in passes.values():
            copy.wait()

    return Flow(
        [] if to_core else [(array, pl.ANY) for array, *_ in arrays],
        [(shape, BF, pl.ANY)],
        [pltpu.VMEM((8, 128) if to_core else shard, BF), dma(5, 6), dma(5, 6), dma(16), dma(16), dma(3), dma(3, 8), dma(3, 8)],
        ring_partners("x") + ring_partners("y") + ([("c", 1)] if to_core else []) + [(ahead, k) for k in range(1, n_ahead)],
        steps,
    )


def stack_flow(array, made):
    def steps(ins, outs, scratch):
        (src,) = ins
        stage, send, recv, local = scratch
        mine, at = peers_of("z")
        own = pltpu.make_async_copy(src, stage.at[mine], local.at[0])
        own.start()
        yield
        copies = []
        for k in range(1, 8):
            copies.append(remote(src, stage.at[mine], send.at[k], recv.at[k], at(lax.rem(mine + k, 8))))
            copies[-1].start()
        yield Clock.now + HOP + 6.0
        own.wait()
        for copy in copies:
            copy.wait()
        made.ref = stage

    return Flow(
        [(array, pl.ANY)], [], [pltpu.VMEM((8,) + array.shape, BF), dma(8), dma(8), dma(1)], [("z", k) for k in range(1, 8)], steps
    )


def product_flow(left, right):
    columns, width = left.shape[1], right.shape[1]

    def steps(ins, outs, scratch):
        (out,) = outs
        left_ref, right_ref, local = scratch
        copies = [pltpu.make_async_copy(source, target, local.at[i]) for i, (source, target) in enumerate(zip(ins, (left_ref, right_ref)))]
        for copy in copies:
            copy.start()
        yield
        yield Filler(1.0)
        for copy in copies:
            copy.wait()
        for column in range(0, columns, 256):
            span = slice(column, column + 256)
            out[span, :] = dot_tn(left_ref[:, span], right_ref[...]).astype(BF)
            yield Filler(1.0)

    return Flow(
        [(left, pl.ANY), (right, pl.ANY)],
        [((columns, width), BF, pltpu.VMEM)],
        [pltpu.VMEM(left.shape, BF), pltpu.VMEM(right.shape, BF), dma(2)],
        [],
        steps,
    )


def output_flow(residual, gates, assign, expert_out):
    own, width = residual.shape
    experts = gates.shape[1]
    count = expert_out.shape[0]

    def steps(ins, outs, scratch):
        residual_ref, gates_ref, assign_ref, expert_hbm = ins
        (out,) = outs
        expert_ref, mixing, local = scratch
        copy = pltpu.make_async_copy(expert_hbm, expert_ref, local.at[0])
        copy.start()
        wide = (experts, count)
        cap = count // experts
        spread = (lax.broadcasted_iota(jnp.int32, wide, 1) // cap == lax.broadcasted_iota(jnp.int32, wide, 0)).astype(F32).astype(BF)
        taken = assign_ref[...].astype(F32)
        high = gates_ref[...].astype(BF)
        low = (gates_ref[...] - high.astype(F32)).astype(BF)
        mixing[0] = (dot_nn(high, spread) * taken).astype(BF)
        mixing[1] = (dot_nn(low, spread) * taken).astype(BF)
        yield
        yield Filler(1.0)
        copy.wait()
        for column in range(0, width, 512):
            span = slice(column, column + 512)
            rows = expert_ref[:, span]
            out[:, span] = (residual_ref[:, span] + dot_nn(mixing[0], rows) + dot_nn(mixing[1], rows)).astype(BF)
            yield Filler(1.0)

    return Flow(
        [(residual, pltpu.VMEM), (gates, pltpu.VMEM), (assign, pltpu.VMEM), (expert_out, pl.ANY)],
        [(residual.shape, BF, pltpu.VMEM)],
        [pltpu.VMEM(expert_out.shape, BF), pltpu.VMEM((2, own, count), BF), dma(1)],
        [],
        steps,
    )


sum_partners = [("yx", k) for k in range(1, 16)] + [("z", k) for k in range(1, 8)]


def sum_room(shape):
    return [pltpu.VMEM((16,) + shape, F32), pltpu.VMEM((8,) + shape, F32), pltpu.VMEM(shape, F32), dma(16), dma(16), dma(8), dma(8)]


def sum_steps(src, gains, out, scratch):
    wide, far, middle, sends, recvs, far_sends, far_recvs = scratch
    me, member = peers_of("yx")
    copies = []
    for k in range(1, 16):
        copies.append(remote(src, wide.at[me], sends.at[k], recvs.at[k], member(lax.rem(me + k, 16))))
        copies[-1].start()
    wide[me] = src[...]
    yield Clock.now + HOP + 4.0
    for copy in copies:
        copy.wait()
    middle[...] = jnp.sum(wide[...], axis=0)
    ring, ring_member = peers_of("z")
    late = []
    for k in range(1, 8):
        late.append(remote(middle, far.at[ring], far_sends.at[k], far_recvs.at[k], ring_member(lax.rem(ring + k, 8))))
        late[-1].start()
    far[ring] = middle[...]
    yield Clock.now + HOP + 3.0
    for copy in late:
        copy.wait()
    out[...] = jnp.sum(far[...], axis=0) / gains[1]


def product_scatter_flow(lefts, right, done, units=None, gains=None, key_gain=None, kept=None):
    arrays = [left for left in lefts if not isinstance(left, Made)]
    own, wide = lefts[0].shape[0] // 8, right.shape[0]
    spans = [0]
    for left in lefts:
        spans.append(spans[-1] + left.shape[1])

    def steps(ins, outs, scratch):
        given = list(ins[: len(arrays)])
        left_refs = [left.ref if isinstance(left, Made) else given.pop(0) for left in lefts]
        right_ref = ins[len(arrays)]
        if kept is not None:
            kept.ref = right_ref
        out, theirs, came, chunks, bufs, send, recv, pass_send, pass_recv, *rest = scratch
        core, member = peers_of("c")
        me, _ = peers_of("zc")
        ring = RingScatter("zc", lambda g: chunks.at[g], bufs, send, recv)

        if units is not None:
            gains_ref = ins[len(arrays) + 1]
            unit_ref = units.ref
            sums, *sum_scratch = rest
            sums[...] = gains_ref[0]
            sums[33:34, :] += key_gain.ref[...]

        def product(c, k, column):
            row = pl.multiple_of((c * 4 + lax.rem(me + k, 4)) * own, own)
            value = sum(
                dot_nt(left_ref[pl.ds(row, own), :], right_ref[column : column + 512, spans[i] : spans[i + 1]])
                for i, left_ref in enumerate(left_refs)
            )
            if units is not None:
                row_sum = jnp.sum(value * unit_ref[pl.ds(row, own), column : column + 512].astype(F32), axis=0, keepdims=True)
                for lane in range(0, 512, 128):
                    at = (column + lane) // 128
                    sums[at : at + 1, :] += row_sum[:, lane : lane + 128]
            return value

        passes = [
            remote(theirs.at[k], came.at[k], pass_send.at[k], pass_recv.at[k], member(1 - core)) for k in range(4)
        ]
        for k in (2, 1, 3, 0):
            if k == 1:
                yield
                Clock.now += 0.7
                passes[2].start()
            for column in range(0, wide, 512):
                theirs[k, :, column : column + 512] = product(1 - core, k, column).astype(BF)
            if k != 2:
                Clock.now += 0.7
                passes[k].start()
                yield
        for k in (2, 1, 3, 0):
            passes[k].wait_recv()
            g = lax.rem(me + k, 4)
            for column in range(0, wide, 512):
                span = slice(column, column + 512)
                value = product(core, k, column) + came[k, :, span].astype(F32)
                if k == 0:
                    out[:, span] = value
                else:
                    chunks[g, :, span] = value.astype(BF)
            Clock.now += 0.7
            if k == 2:
                begun = Clock.now
                ring.start_far()
            elif k == 1:
                ring.start_up()
            elif k == 3:
                ring.start_down()
            yield
        unit = own * wide * 2 / RATE
        if units is not None:
            yield sum_steps(sums, gains_ref, outs[0], sum_scratch)
        yield begun + HOP + unit / 2
        ring.add()
        yield begun + 2 * HOP + 1.5 * unit
        for h in range(2):
            rows = slice(h * own // 2, (h + 1) * own // 2)
            out[rows, :] += ring.total(h)
        done.ref = out
        yield Clock.now + 2.0
        ring.sent()
        for copy in passes:
            copy.wait_send()

    return Flow(
        [(x, pltpu.VMEM) for x in (*arrays, right)] + ([] if units is None else [(gains, pltpu.VMEM)]),
        [] if units is None else [(gains.shape[1:], F32, pltpu.VMEM)],
        [
            pltpu.VMEM((own, wide), F32),
            pltpu.VMEM((4, own, wide), BF),
            pltpu.VMEM((4, own, wide), BF),
            pltpu.VMEM((4, own, wide), BF),
            pltpu.VMEM((8, own // 2, wide), BF),
            dma(6),
            dma(6),
            dma(4),
            dma(4),
        ]
        + ([] if units is None else [pltpu.VMEM(gains.shape[1:], F32)] + sum_room(gains.shape[1:])),
        ring_partners("zc") + [("c", 1)] + ([] if units is None else sum_partners),
        steps,
    )


def plane_scatter_flow(array, first, second, from_core=False, last_in=None):
    rows, columns = array.shape[-2:]
    n_last = SIZES[last_in] if last_in else 1
    result = (n_last, rows // 4, columns) if last_in else (rows, columns)

    def steps(ins, outs, scratch):
        src, (out,) = array.ref if isinstance(array, Made) else ins[0], outs
        came, sums, middle, bufs, late_bufs, send, recv, late_send, late_recv, pass_send, pass_recv, local, cut, cut_send, cut_recv = scratch
        core, member = peers_of("c")
        me, _ = peers_of(first)

        def along(ref, g):
            return ref.at[g] if first == "y" else ref.at[:, g]

        order = [lax.rem(me + k, 4) for k in (2, 1, 3, 0)]
        unit = 4 * rows * columns * 2 / RATE
        loads = [
            pltpu.make_async_copy(along(src.at[core] if from_core else src, g), along(sums, g), local.at[i])
            for i, g in enumerate(order)
            if from_core or i > 0
        ]
        passes = []
        if from_core:
            ring = RingScatter(first, lambda g: along(sums, g), bufs, send, recv)
            for i, g in enumerate(order):
                loads[i].start()
                passes.append(
                    remote(along(src.at[1 - core], g), along(came, g), pass_send.at[i], pass_recv.at[i], member(1 - core))
                )
            yield
            for copy in passes:
                copy.start()
            yield Clock.now + HOP + unit * RATE / CORE_RATE
            starts = [ring.start_far, ring.start_up, ring.start_down, lambda: None]
            for i, g in enumerate(order):
                loads[i].wait()
                passes[i].wait_recv()
                for k in range(4):
                    total = along(sums, g)[k].astype(F32) + along(came, g)[k].astype(F32)
                    along(sums, g)[k] = total.astype(BF)
                starts[i]()
                if i == 0:
                    begun = Clock.now
                yield Clock.now + unit * RATE / CORE_RATE if i < 3 else None
        else:
            ring = RingScatter(first, lambda g: along(sums, g), bufs, send, recv, raw=lambda g: along(src, g))
            for load in loads:
                load.start()
            yield
            begun = Clock.now
            ring.start_far()
            ring.start_up()
            ring.start_down()
            yield begun + HOP + unit / 2
            for load in loads:
                load.wait()
        if from_core:
            yield begun + HOP + unit / 2
        ring.add()
        yield begun + 2 * HOP + 1.5 * unit
        own = along(sums, me)
        for h in range(2):
            came_half = ring.total(h)
            for k in range(2):
                middle[h * 2 + k] = (own[h * 2 + k].astype(F32) + came_half[k]).astype(BF)
        Clock.now += 1.0
        begun = Clock.now
        last = RingScatter(second, lambda g: middle.at[g], late_bufs, late_send, late_recv)
        last.start_far()
        last.start_up()
        last.start_down()
        yield begun + HOP + unit / 8
        last.add()
        yield begun + 2 * HOP + 0.4 * unit
        for h in range(2):
            total = (piece(middle.at[last.me], h)[...].astype(F32) + last.total(h)).astype(BF)
            if last_in:
                cut[2 * h] = total[: rows // 4]
                cut[2 * h + 1] = total[rows // 4 :]
            else:
                out[h * rows // 2 : (h + 1) * rows // 2, :] = total
        cuts = []
        if last_in:
            mine, at = peers_of(last_in)
            share = n_last // 4
            for k in range(1, n_last):
                to = lax.rem(mine + k, n_last)
                cuts.append(remote(cut.at[lax.div(to, share)], out.at[mine], cut_send.at[k], cut_recv.at[k], at(to)))
                cuts[-1].start()
            out[mine] = cut[lax.div(mine, share)]
        yield Clock.now + HOP + 3.0
        ring.sent()
        last.sent()
        for copy in passes:
            copy.wait_send()
        for copy in cuts:
            copy.wait()

    block = (4, 4, rows, columns)
    return Flow(
        [] if isinstance(array, Made) else [(array, pl.ANY)],
        [(result, BF, pltpu.VMEM)],
        [
            pltpu.VMEM(block if from_core else (8, 128), BF),
            pltpu.VMEM(block, BF),
            pltpu.VMEM((4, rows, columns), BF),
            pltpu.VMEM((8, 2, rows, columns), BF),
            pltpu.VMEM((8, rows // 2, columns), BF),
            dma(6),
            dma(6),
            dma(6),
            dma(6),
            dma(4),
            dma(4),
            dma(4),
            pltpu.VMEM((4, rows // 4, columns), BF),
            dma(8),
            dma(8),
        ],
        ring_partners("x")
        + ring_partners("y")
        + ([("c", 1)] if from_core else [])
        + [(last_in, k) for k in range(1, n_last)],
        steps,
    )


def tables_flow(routes, offsets, spacing, experts, cap):
    own, top = routes.shape
    rows, size = offsets.size, spacing.shape[1]

    def steps(ins, outs, scratch):
        routes_ref, offsets_ref, spacing_ref = ins
        assign, chosen_ref, cosine, sine = outs
        yield
        yield Filler(1.0)
        lane = lax.broadcasted_iota(jnp.int32, (own, experts), 1)
        chosen = jnp.zeros((own, experts), F32)
        for k in range(top):
            chosen += (routes_ref[:, k : k + 1] == lane).astype(F32)
        chosen_ref[...] = chosen
        before = lax.broadcasted_iota(jnp.int32, (own, own), 0) > lax.broadcasted_iota(jnp.int32, (own, own), 1)
        earlier = dot_nn(before.astype(F32).astype(BF), chosen.astype(BF))
        wide = (experts, experts * cap)
        spread = (lax.broadcasted_iota(jnp.int32, wide, 1) // cap == lax.broadcasted_iota(jnp.int32, wide, 0)).astype(F32).astype(BF)
        slot = lax.rem(lax.broadcasted_iota(jnp.int32, (own, experts * cap), 1), cap).astype(F32)
        taken = (dot_nn(chosen.astype(BF), spread) > 0.5) & (dot_nn(earlier.astype(BF), spread) == slot)
        assign[...] = taken.astype(F32).astype(BF)
        yield Filler(1.0)
        sign = jnp.where(lax.broadcasted_iota(jnp.int32, (1, size), 1) < size // 2, -1.0, 1.0)
        for row in range(0, rows, BLOCK):
            span = slice(row, row + BLOCK)
            angles = jnp.broadcast_to(offsets_ref[row // BLOCK], (size, BLOCK)).T * spacing_ref[...]
            cosine[span, :] = jnp.cos(angles)
            sine[span, :] = jnp.sin(angles) * sign
            yield Filler(1.0)

    return Flow(
        [(routes, pltpu.VMEM), (offsets, pltpu.VMEM), (spacing, pltpu.VMEM)],
        [
            ((own, experts * cap), BF, pltpu.VMEM),
            ((own, experts), F32, pltpu.VMEM),
            ((rows, size), F32, pltpu.VMEM),
            ((rows, size), F32, pltpu.VMEM),
        ],
        [],
        [],
        steps,
    )


def norm_flow(tokens, gain, made):
    def steps(ins, outs, scratch):
        tokens_ref, gain_ref = ins
        (made.ref,) = scratch
        wide = tokens_ref[...].astype(F32)
        made.ref[...] = (wide * lax.rsqrt(jnp.mean(wide * wide, axis=-1, keepdims=True) + EPS) * gain_ref[...]).astype(BF)
        yield

    return Flow([(tokens, pltpu.VMEM), (gain, pltpu.VMEM)], [], [pltpu.VMEM(tokens.shape, BF)], [], steps)


def project_flow(rows, weights, gain, cosine, sine, q_cols, keys, values):
    count, size = rows.shape[0], gain.shape[1]
    half = count // 2

    def steps(ins, outs, scratch):
        rows_hbm, w_hbm, gain_ref, cos_ref, sin_ref = ins
        q_ref, raw_ref = outs
        rows_ref, w_ref, keys.ref, values.ref, local = scratch
        core, _ = peers_of("c")
        own = pl.ds(pl.multiple_of(core * half, half), half)
        other = pl.ds(pl.multiple_of((1 - core) * half, half), half)
        kv = pl.ds(q_cols, 2 * size)
        copies = [
            pltpu.make_async_copy(w_hbm.at[:, kv], w_ref.at[:, kv], local.at[0]),
            pltpu.make_async_copy(rows_hbm.at[own], rows_ref.at[own], local.at[1]),
            pltpu.make_async_copy(w_hbm.at[:, pl.ds(0, q_cols)], w_ref.at[:, pl.ds(0, q_cols)], local.at[2]),
            pltpu.make_async_copy(rows_hbm.at[other], rows_ref.at[other], local.at[3]),
        ]
        for copy in copies:
            copy.start()
        copies[0].wait()
        copies[1].wait()
        product = dot_nn(rows_ref[own, :], w_ref[:, q_cols:])
        raw = product[:, :size]
        raw_ref[...] = raw
        keys.ref[...] = norm_rope(raw, gain_ref[...], cos_ref[own, :], sin_ref[own, :]).astype(BF)
        values.ref[...] = product[:, size:].astype(BF)
        yield
        yield Filler(1.0)
        copies[2].wait()
        copies[3].wait()
        for row in range(0, count, BLOCK):
            q_ref[row : row + BLOCK, :] = dot_nn(rows_ref[row : row + BLOCK, :], w_ref[:, :q_cols])
            yield Filler(1.2)

    return Flow(
        [(rows, pl.ANY), (weights, pl.ANY), (gain, pltpu.VMEM), (cosine, pltpu.VMEM), (sine, pltpu.VMEM)],
        [((count, q_cols), F32, pltpu.VMEM), ((half, size), F32, pltpu.VMEM)],
        [pltpu.VMEM(rows.shape, BF), pltpu.VMEM(weights.shape, BF), pltpu.VMEM((half, size), BF), pltpu.VMEM((half, size), BF), dma(4)],
        [],
        steps,
    )


def route_flow(tokens, gain, weights, chosen, assign, done):
    own, width = tokens.shape
    experts, count = chosen.shape[1], assign.shape[1]

    def steps(ins, outs, scratch):
        tokens_ref, gain_ref, chosen_ref, assign_ref = ins
        residual_ref, mixed_ref, gates_ref, rows_ref = outs
        (pick,) = scratch
        yield
        pick[...] = assign_ref[...].T
        yield done
        residual = tokens_ref[...].astype(F32) + done.ref[...]
        residual_ref[...] = residual
        mixed_ref[...] = (residual * lax.rsqrt(jnp.mean(residual * residual, axis=-1, keepdims=True) + EPS) * gain_ref[...]).astype(BF)
        logits = jnp.where(chosen_ref[...] > 0, dot_nn(mixed_ref[...], weights.ref[:, -experts:]), -1e30)
        powers = jnp.exp(logits - jnp.max(logits, axis=-1, keepdims=True))
        gates = powers / jnp.sum(powers, axis=-1, keepdims=True)
        gates_ref[...] = gates
        for column in range(0, width, 512):
            span = slice(column, column + 512)
            rows_ref[:, span] = dot_nn(pick[...], mixed_ref[:, span]).astype(BF)
        rows_ref[:, width:] = dot_nn(pick[...], gates.astype(BF)).astype(BF)
        yield

    return Flow(
        [(x, pltpu.VMEM) for x in (tokens, gain, chosen, assign)],
        [
            ((own, width), F32, pltpu.VMEM),
            ((own, width), BF, pltpu.VMEM),
            ((own, experts), F32, pltpu.VMEM),
            ((count, width + experts), BF, pltpu.VMEM),
        ],
        [pltpu.VMEM((count, own), BF)],
        [],
        steps,
    )


def mix_back_flow(back, assign, gates, mixed, weights, residual, gain, cotangent, made):
    own, width = mixed.shape
    experts, count = gates.shape[1], back.shape[0]

    def steps(ins, outs, scratch):
        back_hbm, weights_hbm, assign_ref, gates_ref, mixed_ref, residual_ref, gain_ref, cotangent_ref = ins
        residual_grad, gain_grad, router_grad = outs
        back_ref, mixed_grad, made.ref, router_ref, local = scratch
        last = pl.ds(weights_hbm.shape[1] - experts, experts)
        copies = [
            pltpu.make_async_copy(back_hbm, back_ref, local.at[0]),
            pltpu.make_async_copy(weights_hbm.at[:, last], router_ref, local.at[1]),
        ]
        for copy in copies:
            copy.start()
        for copy in copies:
            copy.wait()
        sums = jnp.sum(back_ref[:, width : width + 128].astype(F32), axis=1, keepdims=True)
        shape = (count, experts)
        expert_of = lax.div(lax.broadcasted_iota(jnp.int32, shape, 0), count // experts)
        spread = jnp.where(expert_of == lax.broadcasted_iota(jnp.int32, shape, 1), sums, 0.0)
        high = spread.astype(BF)
        low = (spread - high.astype(F32)).astype(BF)
        gate_grads = dot_nn(assign_ref[...], high) + dot_nn(assign_ref[...], low)
        gates = gates_ref[...]
        logits_grad = (gates * (gate_grads - jnp.sum(gates * gate_grads, axis=1, keepdims=True))).astype(BF)
        for column in range(0, width, 512):
            span = slice(column, column + 512)
            mixed_grad[:, span] = dot_nn(assign_ref[...], back_ref[:, span]) + dot_nt(logits_grad, router_ref[span, :])
        value = residual_ref[...]
        inverse = lax.rsqrt(jnp.mean(value * value, axis=-1, keepdims=True) + EPS)
        unit = value * inverse
        grad = mixed_grad[...]
        gain_grad[...] = jnp.sum(grad * unit, axis=0, keepdims=True)
        scaled = grad * gain_ref[...]
        total = cotangent_ref[...].astype(F32) + inverse * (scaled - unit * jnp.mean(scaled * unit, axis=-1, keepdims=True))
        residual_grad[...] = total
        made.ref[...] = total.astype(BF)
        yield
        yield Filler(1.0)
        router_grad[...] = dot_tn(mixed_ref[...], logits_grad).astype(BF)
        yield

    return Flow(
        [(back, pl.ANY), (weights, pl.ANY)] + [(x, pltpu.VMEM) for x in (assign, gates, mixed, residual, gain, cotangent)],
        [((own, width), F32, pltpu.VMEM), ((1, width), F32, pltpu.VMEM), ((width, experts), BF, pltpu.VMEM)],
        [
            pltpu.VMEM(back.shape, BF),
            pltpu.VMEM((own, width), F32),
            pltpu.VMEM((own, width), BF),
            pltpu.VMEM((width, experts), BF),
            dma(2),
        ],
        [],
        steps,
    )


def key_back_flow(grad_key, grad_value, raw, gain, cosine, sine, units, kv, w_kv, rows, key_gain):
    half, size = raw.shape
    width = units.shape[1]

    def steps(ins, outs, scratch):
        dk_ref, dv_ref, raw_ref, gain_ref, cos_ref, sin_ref, units_hbm = ins
        rows.ref, kv.ref, w_kv.ref, key_gain.ref, local = scratch
        copy = pltpu.make_async_copy(units_hbm, rows.ref, local.at[0])
        copy.start()
        core, _ = peers_of("c")
        own = pl.ds(pl.multiple_of(core * half, half), half)
        grad = dk_ref[...].astype(F32)
        grad_raw, grad_gain = norm_rope_back(grad, raw_ref[...], gain_ref[...], cos_ref[own, :], sin_ref[own, :])
        kv.ref[...] = jnp.zeros(kv.shape, BF)
        kv.ref[own, :size] = grad_raw.astype(BF)
        kv.ref[own, size:] = dv_ref[...]
        key_gain.ref[...] = jnp.sum(grad_gain, axis=0, keepdims=True)
        copy.wait()
        for i in range(16):
            w_kv.ref[i // 4, i % 4] = dot_tn(rows.ref[own, i * width // 16 : (i + 1) * width // 16], kv.ref[own, :]).astype(BF)
        yield

    return Flow(
        [(x, pltpu.VMEM) for x in (grad_key, grad_value, raw, gain, cosine, sine)] + [(units, pl.ANY)],
        [],
        [pltpu.VMEM(rows.shape, BF), pltpu.VMEM(kv.shape, BF), pltpu.VMEM(w_kv.shape, BF), pltpu.VMEM((1, size), F32), dma(1)],
        [],
        steps,
    )


def tokens_grad_flow(tokens, gain, residual_grad, done):
    def steps(ins, outs, scratch):
        tokens_ref, gain_ref, residual_ref = ins
        (out,) = outs
        yield
        yield done
        value = tokens_ref[...].astype(F32)
        inverse = lax.rsqrt(jnp.mean(value * value, axis=-1, keepdims=True) + EPS)
        unit = value * inverse
        scaled = done.ref[...] * gain_ref[...]
        out[...] = residual_ref[...] + inverse * (scaled - unit * jnp.mean(scaled * unit, axis=-1, keepdims=True))
        yield

    return Flow(
        [(x, pltpu.VMEM) for x in (tokens, gain, residual_grad)], [(tokens.shape, F32, pltpu.VMEM)], [], [], steps
    )


def add_up(stacked):
    return jnp.sum(stacked.astype(F32), axis=0)


def dot_nn(a, b):
    return lax.dot_general(a, b, (((1,), (0,)), ((), ())), preferred_element_type=F32)


def dot_nt(a, b):
    return lax.dot_general(a, b, (((1,), (1,)), ((), ())), preferred_element_type=F32)


def dot_tn(a, b):
    return lax.dot_general(a, b, (((0,), (0,)), ((), ())), preferred_element_type=F32)


def norm_rope(raw, gain, cosine, sine):
    unit = raw * lax.rsqrt(jnp.mean(raw * raw, axis=-1, keepdims=True) + EPS)
    scaled = unit * gain
    return scaled * cosine + pltpu.roll(scaled, 64, 1) * sine


def norm_rope_back(grad, raw, gain, cosine, sine):
    inverse = lax.rsqrt(jnp.mean(raw * raw, axis=-1, keepdims=True) + EPS)
    unit = raw * inverse
    turned = grad * cosine + pltpu.roll(grad * sine, 64, 1)
    scaled = turned * gain
    return inverse * (scaled - unit * jnp.mean(scaled * unit, axis=-1, keepdims=True)), turned * unit


def expert_kernel(rows_ref, plain_ref, w_ref, back_ref, hidden_ref, gated_ref, both_ref):
    width, ff = w_ref.shape[0], plain_ref.shape[1]
    own = lax.axis_index("head") * lax.axis_size("blk") + lax.axis_index("blk")
    gates = rows_ref[:, width:].astype(F32)
    lane = lax.broadcasted_iota(jnp.int32, gates.shape, 1)
    gate = jnp.sum(jnp.where(lane == own, gates, 0.0), axis=1, keepdims=True)
    gate_up = dot_nn(rows_ref[:, :width], w_ref[...])
    first, up = gate_up[:, :ff], gate_up[:, ff:]
    sigma = 1.0 / (1.0 + jnp.exp(-first))
    silu = first * sigma
    hidden = silu * up
    hidden_ref[...] = hidden.astype(BF)
    gated_ref[...] = (hidden * gate).astype(BF)
    plain = plain_ref[...]
    gate_grad = jnp.sum(hidden * plain, axis=1, keepdims=True)
    grad = plain * gate
    both_ref[:, :ff] = (grad * up * (sigma * (1.0 + first * (1.0 - sigma)))).astype(BF)
    both_ref[:, ff:] = (grad * silu).astype(BF)
    back_ref[:, :width] = dot_nt(both_ref[...], w_ref[...]).astype(BF)
    high = gate_grad.astype(BF).astype(F32)
    back_ref[:, width:] = jnp.where(lane == 0, high, jnp.where(lane == 1, gate_grad - high, 0.0)).astype(BF)


def key_tiles(lo, full, last, tiles):
    middle = jnp.minimum(full, last)
    twos, fours = lax.div(middle - lo, 2), lax.div(last - middle, 4)
    rest = middle + 4 * fours
    pl.loop(0, twos)(lambda i: tiles([lo + 2 * i, lo + 2 * i + 1], True))
    pl.loop(lo + 2 * twos, middle)(lambda t: tiles([t], True))
    pl.loop(0, fours)(lambda i: tiles([middle + 4 * i + n for n in range(4)], False))
    for count in range(1, 5):
        pl.when(last - rest == count - 1)(lambda count=count: tiles([rest + n for n in range(count)], True))


def stacked(ref, slots):
    return ref[slots[0]] if len(slots) == 1 else jnp.concatenate([ref[slot] for slot in slots], axis=0)


def allowed_pairs(t, last, start, shape):
    key_place = t * BLOCK + lax.broadcasted_iota(jnp.int32, shape, 0)
    query_place = last * BLOCK + lax.rem(lax.broadcasted_iota(jnp.int32, shape, 1), BLOCK)
    return (key_place >= start) & (key_place <= query_place)


def attend_forward_kernel(
    lo_ref, full_ref, last_ref, slot_ref, raw_ref, gain_ref, cos_ref, sin_ref, k_ref, v_ref, start_ref, q_ref, o_ref, log_ref, q_t, acc, total
):
    j = pl.program_id(0)
    size = k_ref.shape[2]
    heads = raw_ref.shape[1] // size
    scale = size**-0.5 * LOG2E
    last = last_ref[j]
    for n in range(heads):
        span = slice(n * size, (n + 1) * size)
        query = norm_rope(raw_ref[:, span], gain_ref[...], cos_ref[...], sin_ref[...])
        q_ref[:, span] = query.astype(BF)
        q_t[:, n * BLOCK : (n + 1) * BLOCK] = query.T.astype(BF)
    acc[...] = jnp.zeros_like(acc)
    total[...] = jnp.zeros_like(total)
    start = start_ref[0]

    def tiles(at, masked):
        slots = [slot_ref[t] for t in at]
        weights = jnp.exp2(dot_nn(stacked(k_ref, slots), q_t[...]) * scale)
        if masked:
            weights = jnp.where(allowed_pairs(at[0], last, start, weights.shape), weights, 0.0)
        total[...] += jnp.sum(weights.reshape(-1, 8, heads * BLOCK), axis=0)
        acc[...] += dot_nn(stacked(v_ref, slots).T, weights.astype(BF))

    key_tiles(lo_ref[j], full_ref[j], last, tiles)
    row = jnp.sum(total[...], axis=0, keepdims=True)
    log_ref[0] = jnp.log2(row)
    out = acc[...] / row
    for n in range(heads):
        o_ref[:, n * size : (n + 1) * size] = out[:, n * BLOCK : (n + 1) * BLOCK].T.astype(BF)


def attend_backward_kernel(
    lo_ref,
    full_ref,
    last_ref,
    slot_ref,
    block_ref,
    raw_ref,
    gain_ref,
    cos_ref,
    sin_ref,
    k_ref,
    v_ref,
    start_ref,
    q_ref,
    o_ref,
    g_ref,
    w_ref,
    log_ref,
    dq_ref,
    sum_ref,
    dk_ref,
    dv_ref,
    queries,
    q_t,
    grads,
    g_t,
    delta,
    acc,
    dk,
    dv,
    keys_ref,
    values_ref,
    local,
):
    j = pl.program_id(0)
    slots, _, size = keys_ref.shape

    def seen(s):
        block = block_ref[s]
        found = (block >= lo_ref[0]) & (block <= last_ref[0])
        for i in range(1, lo_ref.shape[0]):
            found |= (block >= lo_ref[i]) & (block <= last_ref[i])
        return found

    takes = [pltpu.make_async_copy(k_ref, keys_ref, local.at[0]), pltpu.make_async_copy(v_ref, values_ref, local.at[1])]
    heads = raw_ref.shape[1] // size
    scale = size**-0.5
    last = last_ref[j]

    @pl.when(j == 0)
    def _():
        for copy in takes:
            copy.start()
        sum_ref[...] = jnp.zeros_like(sum_ref)

        @pl.loop(0, slots)
        def _(s):
            @pl.when(seen(s))
            def _():
                dk[s] = jnp.zeros(dk.shape[1:], F32)
                dv[s] = jnp.zeros(dv.shape[1:], F32)

    attended_grad = dot_nn(g_ref[...], w_ref[...]).astype(BF)
    for n in range(heads):
        span, rows = slice(n * size, (n + 1) * size), slice(n * BLOCK, (n + 1) * BLOCK)
        queries[rows, :] = q_ref[:, span]
        q_t[:, rows] = q_ref[:, span].T
        grads[rows, :] = attended_grad[:, span]
        grad_t = attended_grad[:, span].T
        g_t[:, rows] = grad_t
        delta[:, rows] = jnp.sum(grad_t.astype(F32) * o_ref[:, span].T.astype(F32), axis=0, keepdims=True)
    acc[...] = jnp.zeros_like(acc)
    start = start_ref[0]
    logs = log_ref[0]

    @pl.when(j == 0)
    def _():
        for copy in takes:
            copy.wait()

    def tiles(at, masked):
        slots = [slot_ref[t] for t in at]
        keys = stacked(keys_ref, slots)
        probs = jnp.exp2(dot_nn(keys, q_t[...]) * (scale * LOG2E) - logs)
        if masked:
            probs = jnp.where(allowed_pairs(at[0], last, start, probs.shape), probs, 0.0)
        grad_scores = (probs * (dot_nn(stacked(values_ref, slots), g_t[...]) - delta[...])).astype(BF)
        values_part, keys_part = dot_nn(probs.astype(BF), grads[...]), dot_nn(grad_scores, queries[...])
        for n, slot in enumerate(slots):
            dv[slot] += values_part[n * BLOCK : (n + 1) * BLOCK]
            dk[slot] += keys_part[n * BLOCK : (n + 1) * BLOCK]
        acc[...] += dot_nn(keys.T, grad_scores)

    key_tiles(lo_ref[j], full_ref[j], last, tiles)
    for n in range(heads):
        span = slice(n * size, (n + 1) * size)
        grad = (acc[:, n * BLOCK : (n + 1) * BLOCK] * scale).T.astype(BF).astype(F32)
        grad_raw, grad_gain = norm_rope_back(grad, raw_ref[:, span], gain_ref[...], cos_ref[...], sin_ref[...])
        dq_ref[:, span] = grad_raw.astype(BF)
        sum_ref[...] += jnp.sum(grad_gain, axis=0, keepdims=True)

    @pl.when(j == pl.num_programs(0) - 1)
    def _():
        def out(s, n):
            span = pl.ds(s, n)
            return (
                pltpu.make_async_copy(keys_ref.at[span], dk_ref.at[span], local.at[0]),
                pltpu.make_async_copy(values_ref.at[span], dv_ref.at[span], local.at[1]),
            )

        @pl.loop(0, slots, step=8)
        def _(s):
            @pl.loop(s, s + 8)
            def _(i):
                @pl.when(seen(i))
                def _():
                    keys_ref[i] = (dk[i] * scale).astype(BF)
                    values_ref[i] = dv[i].astype(BF)

                @pl.when(jnp.logical_not(seen(i)))
                def _():
                    keys_ref[i] = jnp.zeros(keys_ref.shape[1:], BF)
                    values_ref[i] = jnp.zeros(values_ref.shape[1:], BF)

            for copy in out(s, 8):
                copy.start()

        for copy in out(0, slots):
            copy.wait()


def by_rows(array, rows=BLOCK):
    return pl.BlockSpec((rows,) + array.shape[1:], lambda j, *_: (j,) + (0,) * (array.ndim - 1))


def resident(array):
    return pl.BlockSpec(array.shape, lambda j, *_: (0,) * array.ndim, pipeline_mode=pl.Buffered(1))


def shaped(shape, dtype):
    return jax.ShapeDtypeStruct(shape, dtype)


def expert(rows, plain, weights, block=512):
    count, ff = plain.shape
    outs = (shaped(rows.shape, BF), shaped((count, ff), BF), shaped((count, ff), BF), shaped((count, 2 * ff), BF))
    return pl.pallas_call(
        expert_kernel,
        out_shape=outs,
        grid=(count // block,),
        in_specs=[by_rows(rows, block), by_rows(plain, block), resident(weights)],
        out_specs=tuple(by_rows(x, block) for x in outs),
        compiler_params=pltpu.CompilerParams(vmem_limit_bytes=VMEM_LIMIT),
        cost_estimate=cost_of(20),
        name="expert",
    )(rows, plain, weights)


def attend_forward(meta, raw, gain, cosine, sine, keys, values, start):
    rows, wide = raw.shape
    blocks, size = rows // BLOCK, keys.shape[2]
    lanes = wide // size * BLOCK
    outs = (shaped((rows, wide), BF), shaped((rows, wide), BF), shaped((blocks, 1, lanes), F32))
    return pl.pallas_call(
        attend_forward_kernel,
        out_shape=outs,
        grid_spec=pltpu.PrefetchScalarGridSpec(
            num_scalar_prefetch=4,
            grid=(blocks,),
            in_specs=[
                by_rows(raw),
                resident(gain),
                by_rows(cosine),
                by_rows(sine),
                resident(keys),
                resident(values),
                by_rows(start, 1),
            ],
            out_specs=(by_rows(outs[0]), by_rows(outs[1]), by_rows(outs[2], 1)),
            scratch_shapes=[pltpu.VMEM((size, lanes), BF), pltpu.VMEM((size, lanes), F32), pltpu.VMEM((8, lanes), F32)],
        ),
        compiler_params=pltpu.CompilerParams(vmem_limit_bytes=VMEM_LIMIT),
        cost_estimate=cost_of(30),
        name="attend",
    )(*meta, raw, gain, cosine, sine, keys, values, start)


def attend_backward(meta, raw, gain, cosine, sine, keys, values, start, queries, attended, grads, w_out_t, logs):
    rows, wide = raw.shape
    blocks, size = rows // BLOCK, keys.shape[2]
    lanes = wide // size * BLOCK
    outs = (shaped((rows, wide), BF), shaped((1, size), F32), shaped(keys.shape, BF), shaped(values.shape, BF))
    return pl.pallas_call(
        attend_backward_kernel,
        out_shape=outs,
        grid_spec=pltpu.PrefetchScalarGridSpec(
            num_scalar_prefetch=5,
            grid=(blocks,),
            in_specs=[
                by_rows(raw),
                resident(gain),
                by_rows(cosine),
                by_rows(sine),
                pl.BlockSpec(memory_space=pl.ANY),
                pl.BlockSpec(memory_space=pl.ANY),
                by_rows(start, 1),
                by_rows(queries),
                by_rows(attended),
                by_rows(grads),
                pl.BlockSpec((w_out_t.shape[0], wide), lambda j, *_: (0, 0), pipeline_mode=pl.Buffered(1)),
                by_rows(logs, 1),
            ],
            out_specs=(by_rows(outs[0]), resident(outs[1])) + (pl.BlockSpec(memory_space=pl.ANY),) * 2,
            scratch_shapes=[
                pltpu.VMEM((lanes, size), BF),
                pltpu.VMEM((size, lanes), BF),
                pltpu.VMEM((lanes, size), BF),
                pltpu.VMEM((size, lanes), BF),
                pltpu.VMEM((1, lanes), F32),
                pltpu.VMEM((size, lanes), F32),
                pltpu.VMEM(keys.shape, F32),
                pltpu.VMEM(values.shape, F32),
                pltpu.VMEM(keys.shape, BF),
                pltpu.VMEM(values.shape, BF),
                dma(2),
            ],
        ),
        compiler_params=pltpu.CompilerParams(vmem_limit_bytes=VMEM_LIMIT),
        cost_estimate=cost_of(40),
        name="attend_back",
    )(*meta, raw, gain, cosine, sine, keys, values, start, queries, attended, grads, w_out_t, logs)


def all_to_all(stacked):
    return lax.all_to_all(stacked, ("head", "blk"), split_axis=0, concat_axis=0, tiled=True)


def body(
    tokens,
    norm_gain,
    w_query,
    key_weight,
    value_weight,
    query_gain,
    key_gain,
    w_out,
    mix_gain,
    w_router,
    expert_gate_up,
    expert_down,
    lengths,
    block_deal,
    routes,
    cotangent,
):
    own, width = tokens.shape
    size = query_gain.shape[0]
    scale = size ** (-0.5)
    blk = lax.axis_index("blk")
    plane, core = blk // 4, blk % 2
    devices = lax.axis_size("head") * lax.axis_size("blk")
    experts = w_router.shape[0] * 2
    cap = own * routes.shape[1] // experts
    gate_up, down = expert_gate_up[0], expert_down[0]
    ff = down.shape[0]
    group_rows = 8 * own
    q_cols = w_query.shape[1] // 4
    heads = q_cols // size

    group_blocks = plane * 4 + jnp.array([0, 2, 1, 3], jnp.int32)
    ids = jnp.arange(block_deal.shape[0], dtype=jnp.int32)
    last = jnp.sum(jnp.where(group_blocks[:, None] == ids[None, :], block_deal[None, :], 0), axis=1)
    slots = (ids % 2) * (ids.shape[0] // 2) + (ids // 4) * 2 + (ids % 4) // 2
    slot_of = jnp.sum(jnp.where(block_deal[None, :] == ids[:, None], slots[None, :], 0), axis=1)
    place = (last[:, None] * BLOCK + jnp.arange(BLOCK, dtype=jnp.int32)[None, :]).reshape(-1)
    passed = place[:, None] >= jnp.cumsum(lengths)[None, :]
    start = jnp.sum(jnp.where(passed, lengths[None, :], 0), axis=1)
    start_rows = start.reshape(-1, 1, BLOCK)
    meta = (start_rows[:, 0, 0] // BLOCK, (start_rows[:, 0, BLOCK - 1] + BLOCK - 1) // BLOCK, last, slot_of)
    start_rows = jnp.tile(start_rows, (1, 1, heads))
    offsets = (place - start).astype(F32).reshape(-1, 1, BLOCK)
    spacing = ROPE_BASE ** (-2.0 * jnp.arange(size // 2, dtype=F32) / size)
    spacing = jnp.concatenate([spacing, spacing])[None]

    normed = Made(own, width)
    depth = w_query.shape[0]
    out_pack = w_out.reshape(4, q_cols, depth).transpose(2, 0, 1).reshape(depth, -1)
    side = lax.axis_index("head") == jnp.arange(2, dtype=jnp.int32)
    router_pack = jnp.where(side[None, :, None], w_router.T[:, None, :], 0).astype(BF).reshape(depth, experts)
    stacked_router = Made(8, depth, experts)
    w_qkv, w_rest, group_tokens, assign_low, chosen, cosine, sine = launch(
        [
            norm_flow(tokens, norm_gain[None], normed),
            plane_gather_flow([(w_query, q_cols, 1), (key_weight, size, 2), (value_weight, size, 2)], "x", "y", ahead="zhc"),
            stack_flow(router_pack, stacked_router),
            plane_gather_flow([(out_pack, q_cols, 1)], "y", "x", ahead="zhc", beside=stacked_router),
            ring_gather_flow(normed),
            tables_flow(routes, offsets, spacing, experts, cap),
        ],
        0,
        45,
    )
    normed_group = group_tokens.reshape(group_rows, width)
    w_qkv = w_qkv.reshape(width, -1)
    w_rest = w_rest.reshape(width, -1)

    q_gain, k_gain = query_gain[None], key_gain[None]
    key, value = Made(group_rows // 2, size), Made(group_rows // 2, size)
    q_raw, k_raw, keys, values, grad_rows = launch(
        [
            project_flow(normed_group, w_qkv, k_gain, cosine, sine, q_cols, key, value),
            plane_gather_flow(key, "x", "y"),
            plane_gather_flow(value, "y", "x"),
            product_flow(assign_low, cotangent),
        ],
        1,
        35,
    )
    grad_rows = all_to_all(grad_rows.reshape(devices, cap, width)).reshape(-1, width)
    keys, values = keys.reshape(-1, BLOCK, size), values.reshape(-1, BLOCK, size)
    queries, attended, logs = attend_forward(meta, q_raw, q_gain, cosine, sine, keys, values, start_rows)

    attention, weights_kept = Made(own, width), Made()
    residual, mixed, gates, outgoing = launch(
        [
            product_scatter_flow([attended], w_rest, attention, kept=weights_kept),
            route_flow(tokens, mix_gain[None], weights_kept, chosen, assign_low, attention),
        ],
        2,
        30,
    )
    outgoing, grad_rows = lax.optimization_barrier((outgoing, grad_rows))
    arrived = all_to_all(outgoing.reshape(devices, cap, -1)).reshape(experts * cap, -1)

    plain_grad = lax.optimization_barrier(dot_nt(grad_rows, down))
    rows, plain_grad = lax.optimization_barrier((arrived, plain_grad))
    back, hidden, gated, grad_both = expert(rows, plain_grad, gate_up)
    back = all_to_all(back.reshape(devices, cap, -1)).reshape(experts * cap, -1)
    back, expert_out = lax.optimization_barrier((back, dot_nn(hidden, down).astype(BF)))
    grad_down = dot_tn(gated, grad_rows)
    grad_gate_up = dot_tn(rows[:, :width], grad_both)

    grad_attention = Made(own, width)
    grad_residual, grad_mix_gain, grad_router_t, grad_group = launch(
        [
            mix_back_flow(back, assign_low, gates, mixed, w_rest, residual, mix_gain[None], cotangent, grad_attention),
            ring_gather_flow(grad_attention),
        ],
        3,
        25,
    )
    grad_group = grad_group.reshape(group_rows, width)
    grad_group, expert_out = lax.optimization_barrier((grad_group, expert_out))
    expert_out = all_to_all(expert_out.reshape(devices, cap, width)).reshape(-1, width)
    block_of = block_deal.reshape(-1, 2, 2).transpose(2, 0, 1).reshape(-1)
    grad_q, grad_query_gain, grad_keys, grad_values = attend_backward(
        (*meta, block_of), q_raw, q_gain, cosine, sine, keys, values, start_rows, queries, attended, grad_group, w_rest, logs
    )

    split = (2, 4, 4, group_rows // 2, size)
    grad_key, grad_value, grad_wq, grad_wo = launch(
        [
            plane_scatter_flow(grad_keys.reshape(split), "y", "x", from_core=True),
            plane_scatter_flow(grad_values.reshape(split), "x", "y", from_core=True),
            product_flow(normed_group, grad_q),
            product_flow(grad_group, attended),
        ],
        4,
        35,
    )

    grad_key, expert_out = lax.optimization_barrier((grad_key, expert_out))
    plane_split = (4, 4, 4 * depth, -1)
    zeros, ones = jnp.zeros((width,), F32), jnp.ones((width,), F32)
    gains = jnp.concatenate([zeros, grad_mix_gain[0], grad_query_gain[0], zeros[: 7 * size], norm_gain, ones, ones[: 8 * size]])
    units, grad_kv, grad_wkv, key_gain_sum = Made(group_rows, width), Made(group_rows, 2 * size), Made(4, 4, 4 * depth, 2 * size), Made()
    grad_normed = Made(own, width)
    grad_wq, grad_wo, gains, grad_wkv, grad_wr, output, grad_tokens = launch(
        [
            key_back_flow(grad_key, grad_value, k_raw, k_gain, cosine, sine, normed_group, grad_kv, grad_wkv, units, key_gain_sum),
            plane_scatter_flow(grad_wq.reshape(plane_split), "y", "x", last_in="zhc"),
            plane_scatter_flow(grad_wo.reshape(plane_split), "x", "y", last_in="zhc"),
            product_scatter_flow([grad_q, grad_kv], w_qkv, grad_normed, units, gains.reshape(2, -1, size), key_gain_sum),
            plane_scatter_flow(grad_wkv, "y", "x", last_in="zhc"),
            plane_scatter_flow(grad_router_t.reshape(plane_split), "x", "y", last_in="z"),
            output_flow(residual, gates, assign_low, expert_out),
            tokens_grad_flow(tokens, norm_gain[None], grad_residual, grad_normed),
        ],
        5,
        50,
    )
    gains = gains.reshape(-1)
    grad_w_query = grad_wq.astype(F32).transpose(1, 0, 2).reshape(depth, -1)
    grad_kv_w = jnp.sum(grad_wkv.astype(F32).reshape(2, 2, depth, 2, size), axis=1)
    grad_w_key = grad_kv_w[:, :, 0].transpose(1, 0, 2).reshape(depth, -1)
    grad_w_value = grad_kv_w[:, :, 1].transpose(1, 0, 2).reshape(depth, -1)
    grad_w_out = grad_wo.astype(F32).transpose(0, 2, 1).reshape(-1, depth)
    grad_w_router = lax.dynamic_slice_in_dim(add_up(grad_wr), lax.axis_index("head") * (experts // 2), experts // 2, 1).T
    return (
        output,
        grad_tokens,
        gains[:width],
        grad_w_query,
        grad_w_key,
        grad_w_value,
        gains[2 * width : 2 * width + size],
        gains[2 * width + size : 2 * width + 2 * size],
        grad_w_out,
        gains[width : 2 * width],
        grad_w_router,
        grad_gate_up[None],
        grad_down[None],
    )


def solution(mesh):
    rows, both = P(("head", "blk"), None), P("blk", "head")
    expert, turned = P(("head", "blk"), None, None), P("head", "blk")
    in_specs = (rows, P(), both, both, both, P(), P(), turned, P(), turned, expert, expert, P(), P(), rows, rows)
    out_specs = (rows, rows, P(), both, both, both, P(), P(), turned, P(), turned, expert, expert)
    return jax.shard_map(body, mesh=mesh, in_specs=in_specs, out_specs=out_specs, check_vma=False)
```
